32 devices in a mesh: section: 2 (over core), dp: 4 (over z), mp: 4 (over y, x).
Axes of the slice: x: 2, y: 2, z: 4, core: 2. Of those that a mesh axis runs over, the one named last changes fastest.
Arguments:
- inputs: bfloat16 [8, 1024, 1024], P('dp', 'mp'), may hold values from -1 to 1
- cotangent: bfloat16 [8, 1024, 1024], P('dp', 'mp'), may hold values from -11 to 11
- doc_ids: int32 [8, 1024], P('dp'), may hold values from 0 to 3, never falling along the last dimension, each value on 1 to 512 neighbouring positions
- attention_in: float32 [2, 3, 1024, 1024], P('section', None, None, ('mp', 'dp')), may hold values from -0.1875 to 0.1875
- attention_out: float32 [2, 1024, 1024], P('section', ('mp', 'dp')), may hold values from -0.1875 to 0.1875
- feedforward_in: float32 [2, 2, 1024, 4096], P('section', None, None, ('mp', 'dp')), may hold values from -0.1875 to 0.1875
- feedforward_out: float32 [2, 4096, 1024], P('section', ('mp', 'dp')), may hold values from -0.1875 to 0.1875
- unit_scales: float32 [2, 4, 2304], P('section', 'mp', 'dp'), may hold values from 0.75 to 3
- mix_rates: float32 [2, 2, 1024], P('section', None, 'dp'), may hold values from 0.25 to 0.75
- first_attention_in: float32 [2, 3, 1024, 1024], P('section', None, None, ('mp', 'dp')), may hold values from -1 to 1
- second_attention_in: float32 [2, 3, 1024, 1024], P('section', None, None, ('mp', 'dp')), may hold values from 0 to 1
- first_attention_out: float32 [2, 1024, 1024], P('section', ('mp', 'dp')), may hold values from -1 to 1
- second_attention_out: float32 [2, 1024, 1024], P('section', ('mp', 'dp')), may hold values from 0 to 1
- first_feedforward_in: float32 [2, 2, 1024, 4096], P('section', None, None, ('mp', 'dp')), may hold values from -1 to 1
- second_feedforward_in: float32 [2, 2, 1024, 4096], P('section', None, None, ('mp', 'dp')), may hold values from 0 to 1
- first_feedforward_out: float32 [2, 4096, 1024], P('section', ('mp', 'dp')), may hold values from -1 to 1
- second_feedforward_out: float32 [2, 4096, 1024], P('section', ('mp', 'dp')), may hold values from 0 to 1
- first_unit_scales: float32 [2, 4, 2304], P('section', 'mp', 'dp'), may hold values from -1 to 1
- second_unit_scales: float32 [2, 4, 2304], P('section', 'mp', 'dp'), may hold values from 0 to 1
- first_mix_rates: float32 [2, 2, 1024], P('section', None, 'dp'), may hold values from -1 to 1
- second_mix_rates: float32 [2, 2, 1024], P('section', None, 'dp'), may hold values from 0 to 1
Outputs:
- boundary_states: float32 [2, 8, 1024, 1024], P('section', 'dp', 'mp')
- gradient_norm: float32 [], replicated
- next_first_attention_in: float32 [2, 3, 1024, 1024], P('section', None, None, ('mp', 'dp'))
- next_second_attention_in: float32 [2, 3, 1024, 1024], P('section', None, None, ('mp', 'dp'))
- next_attention_in: float32 [2, 3, 1024, 1024], P('section', None, None, ('mp', 'dp'))
- next_first_attention_out: float32 [2, 1024, 1024], P('section', ('mp', 'dp'))
- next_second_attention_out: float32 [2, 1024, 1024], P('section', ('mp', 'dp'))
- next_attention_out: float32 [2, 1024, 1024], P('section', ('mp', 'dp'))
- next_first_feedforward_in: float32 [2, 2, 1024, 4096], P('section', None, None, ('mp', 'dp'))
- next_second_feedforward_in: float32 [2, 2, 1024, 4096], P('section', None, None, ('mp', 'dp'))
- next_feedforward_in: float32 [2, 2, 1024, 4096], P('section', None, None, ('mp', 'dp'))
- next_first_feedforward_out: float32 [2, 4096, 1024], P('section', ('mp', 'dp'))
- next_second_feedforward_out: float32 [2, 4096, 1024], P('section', ('mp', 'dp'))
- next_feedforward_out: float32 [2, 4096, 1024], P('section', ('mp', 'dp'))
- next_first_unit_scales: float32 [2, 4, 2304], P('section', 'mp', 'dp')
- next_second_unit_scales: float32 [2, 4, 2304], P('section', 'mp', 'dp')
- next_unit_scales: float32 [2, 4, 2304], P('section', 'mp', 'dp')
- next_first_mix_rates: float32 [2, 2, 1024], P('section', None, 'dp')
- next_second_mix_rates: float32 [2, 2, 1024], P('section', None, 'dp')
- next_mix_rates: float32 [2, 2, 1024], P('section', None, 'dp')
The draws below stay inside these ranges and needn't reach their ends.
Inputs may be any that keep to these rules, and one draw needn't show every extreme that they name: `doc_ids`: never falls along a sequence; each document holds 1 to 512 positions and one holds exactly 512.
All inputs are finite; a program needn't handle non-finite values.
Results may differ from the reference program's by a relative error of at most 0.033.
The reference program's roundings to bfloat16 on the way count: a program that leaves them out, or rounds other values in their place, can miss the bound.
Values may be sent and summed in bfloat16 or wider, within the bound.
No kernel may reach another device: no remote copies, remote signals or barrier semaphores. Data moves between devices by JAX's collectives and lax.ppermute only.
A program may use at most 384 MiB of HBM per device.

```python
import math
import jax
import jax.numpy as jnp
import numpy as np
from jax import lax

D = 1024
FF = 4096
HEADS = 16
HD = 64
SEQ_LEN = 1024
DOCS = 4
STEP = 10
LAYERS = 2
SEQS = 8
QK_SHARD = 256
FF_SHARD = 1024
USW = 2304
PARAMS = 33576960


CLIP_NORM = 0.1


def rising_columns(count, rise_ratio):
    return jnp.exp(0.5 * math.log(rise_ratio) * jnp.arange(count, dtype=jnp.float32) / max(count - 1, 1))


def rising_entries(key, array_shape, rise_ratio):
    entries = jnp.clip(jax.random.normal(key, array_shape, jnp.float32), -6.0, 6.0)
    return entries * rising_columns(array_shape[-1], rise_ratio)


def draw_inputs(key, part):
    key = jax.random.fold_in(key, 1)
    rise_ratio = 3.0
    mean_square = (rise_ratio - 1.0) / math.log(rise_ratio)
    values = rising_entries(key, (SEQS, SEQ_LEN, D), rise_ratio) / math.sqrt(D * mean_square)
    return values.astype(jnp.bfloat16)


def draw_cotangent(key, part):
    key = jax.random.fold_in(key, 2)
    rise_ratio = 3.0
    return rising_entries(key, (SEQS, SEQ_LEN, D), rise_ratio).astype(jnp.bfloat16)


def draw_unit_scales(key, part):
    key = jax.random.fold_in(key, 3)
    ways = (D + 2 * FF) // USW
    width_qk = D // ways
    first_key, second_key = jax.random.split(key)
    array_shape = (LAYERS, ways, USW)
    low_end = 0.8
    rise_ratio = 3.0
    spread = jnp.exp(jax.random.uniform(first_key, array_shape, jnp.float32, math.log(low_end), -math.log(low_end)))
    rising = rising_columns(ways, rise_ratio)[None, :, None]
    query_part = jax.random.uniform(second_key, array_shape, jnp.float32, 1.0, 1.4)
    column = jnp.arange(USW, dtype=jnp.int32)[None, None, :]
    return jnp.where(column < width_qk, query_part, spread * rising).astype(jnp.float32)


def gradient_scale(boost):
    return boost * CLIP_NORM / math.sqrt(PARAMS)


def first_state(key, array_shape, boost):
    entries = jnp.clip(jax.random.normal(key, array_shape, jnp.float32), -6.0, 6.0)
    return (gradient_scale(boost) * (0.1 / 0.9) * entries).astype(jnp.float32)


def second_state(key, array_shape, boost):
    spread = jnp.exp(jax.random.uniform(key, array_shape, jnp.float32, 0.0, math.log(4.0)))
    return (gradient_scale(boost) ** 2 * (0.05 / 0.95) * spread).astype(jnp.float32)


def draw_first_attention_in(key, part):
    key = jax.random.fold_in(key, 11)
    return first_state(key, (LAYERS, 3, D, D), 1.0)


def draw_second_attention_in(key, part):
    key = jax.random.fold_in(key, 12)
    return second_state(key, (LAYERS, 3, D, D), 1.0)


def draw_first_attention_out(key, part):
    key = jax.random.fold_in(key, 13)
    return first_state(key, (LAYERS, D, D), 1.0)


def draw_second_attention_out(key, part):
    key = jax.random.fold_in(key, 14)
    return second_state(key, (LAYERS, D, D), 1.0)


def draw_first_feedforward_in(key, part):
    key = jax.random.fold_in(key, 15)
    return first_state(key, (LAYERS, 2, D, FF), 1.0)


def draw_second_feedforward_in(key, part):
    key = jax.random.fold_in(key, 16)
    return second_state(key, (LAYERS, 2, D, FF), 1.0)


def draw_first_feedforward_out(key, part):
    key = jax.random.fold_in(key, 17)
    return first_state(key, (LAYERS, FF, D), 1.0)


def draw_second_feedforward_out(key, part):
    key = jax.random.fold_in(key, 18)
    return second_state(key, (LAYERS, FF, D), 1.0)


def draw_first_unit_scales(key, part):
    key = jax.random.fold_in(key, 19)
    return first_state(key, (LAYERS, (D + 2 * FF) // USW, USW), 4.0)


def draw_second_unit_scales(key, part):
    key = jax.random.fold_in(key, 20)
    return second_state(key, (LAYERS, (D + 2 * FF) // USW, USW), 4.0)


def draw_first_mix_rates(key, part):
    key = jax.random.fold_in(key, 21)
    return first_state(key, (LAYERS, 2, D), 4.0)


def draw_second_mix_rates(key, part):
    key = jax.random.fold_in(key, 22)
    return second_state(key, (LAYERS, 2, D), 4.0)


def steps_of(key, dims, shards, low, high):
    level = 1.0
    for axis_at, parts in shards:
        steps = jax.random.uniform(jax.random.fold_in(jax.random.fold_in(key, 6), axis_at), (parts,), jnp.float32, low / len(shards), high / len(shards))
        level = level * jnp.repeat(jnp.exp(steps), dims[axis_at] // parts).reshape((-1,) + (1,) * (len(dims) - 1 - axis_at))
    return level


def profile(count, total, bound, lean):
    portions = [(1 << 20) // math.isqrt(grade ** lean) + 1 for grade in range(2, count + 1)]
    surplus, counts = total - bound - (count - 1), [1] * (count - 1)
    while surplus > 0:
        free = [i for i in range(count - 1) if counts[i] < bound]
        pool, left = sum([portions[i] for i in free]), surplus
        for i in free:
            extra = min(bound - counts[i], max(1, left * portions[i] // pool), surplus)
            counts[i] = counts[i] + extra
            surplus = surplus - extra
    return np.array([bound] + counts)


def uneven_parts(key, amount, total, most, skew):
    if amount == 2:
        one = jax.random.randint(key, (), max(1, total - most), min(most, total - 1) + 1)
        return jnp.stack([one, total - one])
    tallies = jnp.asarray(profile(amount, total, most, skew), jnp.int32)
    pairs = (amount - 1) // 2
    giver, taker = tallies[1:1 + 2 * pairs:2], tallies[2:2 + 2 * pairs:2]
    slack = jnp.minimum(giver - 1, most - taker)
    passed = jax.random.randint(jax.random.fold_in(key, 1), (pairs,), 0, 1 << 20) % (slack + 1)
    tallies = tallies.at[1:1 + 2 * pairs:2].set(giver - passed).at[2:2 + 2 * pairs:2].set(taker + passed)
    return tallies[jax.random.permutation(jax.random.fold_in(key, 2), amount)]


def bell_draw(key, extent, scale, reach, cuts=(), kind=jnp.bfloat16):
    factor_of = steps_of(key, extent, cuts, -0.22, 0.18) if cuts else 1.0
    values = jax.random.normal(key, extent, jnp.float32) * scale * factor_of
    return jnp.minimum(jnp.maximum(values, -reach), reach).astype(kind)


def setup_inputs(seed: int = 0) -> dict:
    splits = jax.random.split(jax.random.key(seed), 22)
    return {
        "inputs": draw_inputs(jax.random.fold_in(splits[21], 71), 0),
        "cotangent": draw_cotangent(jax.random.fold_in(splits[21], 71), 0),
        "doc_ids": jax.vmap(lambda own: jnp.searchsorted(jnp.cumsum(uneven_parts(own, DOCS, SEQ_LEN, SEQ_LEN // 2, 1)), jnp.arange(SEQ_LEN), side="right"))(jax.random.split(splits[2], SEQS)).reshape((SEQS, SEQ_LEN)).astype(jnp.int32),
        "attention_in": bell_draw(splits[3], (LAYERS, 3, D, D), D ** -0.5, 0.1875, ((0, 2), (3, 16)), jnp.float32),
        "attention_out": bell_draw(splits[4], (LAYERS, D, D), D ** -0.5, 0.1875, ((0, 2), (1, 16)), jnp.float32),
        "feedforward_in": bell_draw(splits[5], (LAYERS, 2, D, FF), D ** -0.5, 0.1875, ((0, 2), (3, 16)), jnp.float32),
        "feedforward_out": bell_draw(splits[6], (LAYERS, FF, D), D ** -0.5, 0.1875, ((0, 2), (1, 16)), jnp.float32),
        "unit_scales": draw_unit_scales(jax.random.fold_in(splits[21], 71), 0),
        "mix_rates": jnp.clip(0.25 + 0.5 * jax.random.uniform(splits[8], (LAYERS, 2, D), jnp.float32) ** steps_of(splits[8], (LAYERS, 2, D), ((0, 2), (2, 4)), -0.2, 0.2), 0.25, 0.75),
        "first_attention_in": draw_first_attention_in(jax.random.fold_in(splits[21], 71), 0),
        "second_attention_in": draw_second_attention_in(jax.random.fold_in(splits[21], 71), 0),
        "first_attention_out": draw_first_attention_out(jax.random.fold_in(splits[21], 71), 0),
        "second_attention_out": draw_second_attention_out(jax.random.fold_in(splits[21], 71), 0),
        "first_feedforward_in": draw_first_feedforward_in(jax.random.fold_in(splits[21], 71), 0),
        "second_feedforward_in": draw_second_feedforward_in(jax.random.fold_in(splits[21], 71), 0),
        "first_feedforward_out": draw_first_feedforward_out(jax.random.fold_in(splits[21], 71), 0),
        "second_feedforward_out": draw_second_feedforward_out(jax.random.fold_in(splits[21], 71), 0),
        "first_unit_scales": draw_first_unit_scales(jax.random.fold_in(splits[21], 71), 0),
        "second_unit_scales": draw_second_unit_scales(jax.random.fold_in(splits[21], 71), 0),
        "first_mix_rates": draw_first_mix_rates(jax.random.fold_in(splits[21], 71), 0),
        "second_mix_rates": draw_second_mix_rates(jax.random.fold_in(splits[21], 71), 0),
    }


@jax.custom_vjp
def low(v):
    return lax.optimization_barrier(v.astype(jnp.bfloat16)).astype(jnp.float32)

@jax.custom_vjp
def low_back(v):
    return v

def low_keep(v):
    return (low(v), None)

def low_pass(kept, grad):
    return (grad,)

def back_keep(v):
    return (v, None)

def back_low(kept, grad):
    return (low(grad),)
low.defvjp(low_keep, low_pass)
low_back.defvjp(back_keep, back_low)
NORM_EPSILON = 1e-06
ROPE_BASE = 10000.0
CLIP_NORM = 0.1
LEARN_RATE = 0.05
SCALE_RATE = 1.25
MIXING_RATE = 0.4
BETA_FIRST = 0.9
BETA_SECOND = 0.95
ADAM_EPSILON = 1e-08
MASK_VALUE = -1e+30
HIGHEST = lax.Precision.HIGHEST

def unit_norm(values):
    return values * lax.rsqrt(lax.optimization_barrier(jnp.sum(values * values, axis=-1, keepdims=True)) + NORM_EPSILON)

def rope_tables(doc_rows):
    position = jnp.arange(doc_rows.shape[-1], dtype=jnp.int32)
    change = jnp.concatenate([jnp.ones(doc_rows.shape[:-1] + (1,), dtype=jnp.bool_), doc_rows[..., 1:] != doc_rows[..., :-1]], axis=-1)
    starts = lax.cummax(jnp.where(change, position, 0), axis=doc_rows.ndim - 1)
    offsets = (position - starts).astype(jnp.float32)
    half_width = HD // 2
    inverse = 1.0 / ROPE_BASE ** (jnp.arange(half_width, dtype=jnp.float32) * (2.0 / HD))
    angles = offsets[..., None] * inverse
    angles = jnp.concatenate([angles, angles], axis=-1)
    return (jnp.cos(angles)[..., None, :], jnp.sin(angles)[..., None, :])

def turn_heads(projected, cosine, sine_table, head_gains):
    half_width = projected.shape[-1] // 2
    swapped = jnp.concatenate([-projected[..., half_width:], projected[..., :half_width]], axis=-1)
    return unit_norm(projected * cosine + swapped * sine_table) * head_gains

def mix_residual(hidden, branch, mixing):
    return unit_norm(hidden + mixing * (unit_norm(branch) - hidden))

def gated_units(up_gate, scale_up, scale_gate):
    return up_gate[0] * scale_up * jax.nn.silu(up_gate[1] * scale_gate * math.sqrt(D))

def attend_sequence(query_heads, key_heads, value_heads, doc_rows):
    length = query_heads.shape[0]
    block_rows = min(512, length)
    offsets = jnp.arange(length // block_rows, dtype=jnp.int32) * block_rows

    def one_block(offset):
        query_rows = lax.dynamic_slice_in_dim(query_heads, offset, block_rows, 0)
        query_docs = lax.dynamic_slice_in_dim(doc_rows, offset, block_rows, 0)
        scores = low_back(math.sqrt(HD) * jnp.einsum('qhe,khe->hqk', query_rows, key_heads, precision=HIGHEST))
        query_place = offset + jnp.arange(block_rows, dtype=jnp.int32)
        key_place = jnp.arange(length, dtype=jnp.int32)
        allowed = (key_place[None, :] <= query_place[:, None]) & (doc_rows[None, :] == query_docs[:, None])
        shares = jax.nn.softmax(jnp.where(allowed[None], scores, MASK_VALUE), axis=-1)
        return jnp.einsum('hqk,khe->qhe', low(shares), value_heads, precision=HIGHEST)
    blocks = lax.map(jax.checkpoint(one_block), offsets)
    return blocks.reshape(length, query_heads.shape[1], query_heads.shape[2])

def layer(hidden, doc_rows, params):
    attend_in, attend_out, feed_in, feed_out, unit_rows, mixing = params
    groups, length = (hidden.shape[0], hidden.shape[1])
    scale_qk = unit_rows[:, :QK_SHARD].reshape(HEADS, HD)
    scale_up = unit_rows[:, QK_SHARD:QK_SHARD + FF_SHARD].reshape(FF)
    scale_gate = unit_rows[:, QK_SHARD + FF_SHARD:].reshape(FF)
    cosine, sine_table = rope_tables(doc_rows)
    low_hidden = low(hidden)
    projections = low_back(jnp.einsum('gld,cde->cgle', low_hidden, attend_in, precision=HIGHEST))
    heads_raw = projections.reshape(3, groups, length, HEADS, HD)
    query_heads = low(turn_heads(heads_raw[0], cosine, sine_table, scale_qk))
    key_heads = low(turn_heads(heads_raw[1], cosine, sine_table, scale_qk))
    value_heads = low(heads_raw[2])
    attended = jax.vmap(attend_sequence)(query_heads, key_heads, value_heads, doc_rows)
    attended_low = low_back(low(attended)).reshape(groups, length, D)
    branch = low_back(jnp.einsum('glf,fd->gld', attended_low, attend_out, precision=HIGHEST))
    middle = mix_residual(hidden, branch, mixing[0])
    low_middle = low(middle)
    up_gate = low_back(jnp.einsum('gld,cdf->cglf', low_middle, feed_in, precision=HIGHEST))
    gated_out = low(gated_units(up_gate, scale_up, scale_gate))
    feed_sum = low_back(jnp.einsum('glf,fd->gld', gated_out, feed_out, precision=HIGHEST))
    return mix_residual(middle, feed_sum, mixing[1])

def network(inputs, masters, doc_rows):
    hidden = inputs
    for depth in range(LAYERS):
        params = tuple((low(weight[depth]) for weight in masters))
        hidden = layer(hidden, doc_rows, params)
        if depth + 1 < LAYERS:
            hidden = low_back(low(hidden))
    return hidden

def adam_update(weight, first, second, gradient, factor, renorm, rate):
    clipped = gradient * factor
    first_new = BETA_FIRST * first + (1.0 - BETA_FIRST) * clipped
    second_new = BETA_SECOND * second + (1.0 - BETA_SECOND) * clipped * clipped
    first_hat = first_new / (1.0 - BETA_FIRST ** STEP)
    second_hat = second_new / (1.0 - BETA_SECOND ** STEP)
    moved = weight - rate * first_hat / (jnp.sqrt(second_hat) + ADAM_EPSILON)
    if renorm:
        moved = moved * lax.rsqrt(lax.optimization_barrier(jnp.sum(moved * moved, axis=2, keepdims=True)) + NORM_EPSILON)
    return (first_new, second_new, moved)

def reference(inputs, cotangent, doc_ids, attention_in, attention_out, feedforward_in, feedforward_out, unit_scales, mix_rates, first_attention_in, second_attention_in, first_attention_out, second_attention_out, first_feedforward_in, second_feedforward_in, first_feedforward_out, second_feedforward_out, first_unit_scales, second_unit_scales, first_mix_rates, second_mix_rates):
    masters = (attention_in, attention_out, feedforward_in, feedforward_out, unit_scales, mix_rates)
    group_size = math.gcd(SEQS, max(1, 4096 // SEQ_LEN))
    group_count = SEQS // group_size
    series = (inputs.astype(jnp.float32).reshape(group_count, group_size, SEQ_LEN, D), cotangent.astype(jnp.float32).reshape(group_count, group_size, SEQ_LEN, D), doc_ids.reshape(group_count, group_size, SEQ_LEN))

    def group_step(running, batch_rows):
        group_in, group_grad, group_docs = batch_rows
        result, pull = jax.vjp(lambda values, *weights: network(values, weights, group_docs), group_in, *masters)
        pulled = pull(group_grad)
        return (tuple((earlier + latest for earlier, latest in zip(running, pulled[1:]))), (result, pulled[0]))
    starting = tuple((jnp.zeros(weight.shape, jnp.float32) for weight in masters))
    totals, (outputs, input_grads) = lax.scan(group_step, starting, series)
    boundary_states = jnp.stack([input_grads.reshape(SEQS, SEQ_LEN, D), outputs.reshape(SEQS, SEQ_LEN, D)])
    squares = jnp.sum(totals[0] * totals[0]) + jnp.sum(totals[1] * totals[1]) + jnp.sum(totals[2] * totals[2]) + jnp.sum(totals[3] * totals[3]) + jnp.sum(totals[4] * totals[4]) + jnp.sum(totals[5] * totals[5])
    gradient_norm = jnp.sqrt(squares)
    factor = CLIP_NORM / jnp.maximum(gradient_norm, CLIP_NORM)
    fa_in, sa_in, na_in = adam_update(attention_in, first_attention_in, second_attention_in, totals[0], factor, True, LEARN_RATE)
    fa_out, sa_out, na_out = adam_update(attention_out, first_attention_out, second_attention_out, totals[1], factor, True, LEARN_RATE)
    ff_in, sf_in, nf_in = adam_update(feedforward_in, first_feedforward_in, second_feedforward_in, totals[2], factor, True, LEARN_RATE)
    ff_out, sf_out, nf_out = adam_update(feedforward_out, first_feedforward_out, second_feedforward_out, totals[3], factor, True, LEARN_RATE)
    fu_sc, su_sc, nu_sc = adam_update(unit_scales, first_unit_scales, second_unit_scales, totals[4], factor, False, SCALE_RATE)
    fm_ra, sm_ra, nm_ra = adam_update(mix_rates, first_mix_rates, second_mix_rates, totals[5], factor, False, MIXING_RATE)
    return (boundary_states, gradient_norm, fa_in, sa_in, na_in, fa_out, sa_out, na_out, ff_in, sf_in, nf_in, ff_out, sf_out, nf_out, fu_sc, su_sc, nu_sc, fm_ra, sm_ra, nm_ra)
```

```python
import math

import jax
import jax.numpy as jnp
from jax import lax
from jax.sharding import PartitionSpec as P

HD = 64
STEP = 10

NORM_EPSILON = 1e-06
ROPE_BASE = 10000.0
CLIP_NORM = 0.1
LEARN_RATE = 0.05
SCALE_RATE = 1.25
MIXING_RATE = 0.4
BETA_FIRST = 0.9
BETA_SECOND = 0.95
ADAM_EPSILON = 1e-08
MASK_VALUE = -1e30

BF16 = jnp.bfloat16
F32 = jnp.float32


def exchange(block, axis, bit):
    route = [(i, i ^ bit) for i in range(lax.axis_size(axis))]
    return lax.ppermute(block, axis, route)


def spread_rows(block):
    half = block.shape[0] // 2
    first = exchange(block, "mp", 1)
    second = exchange(block, "mp", 2)
    upper = exchange(second[:half], "mp", 1)
    lower = exchange(first[half:], "mp", 2)
    return [block, first, second, jnp.concatenate([upper, lower], axis=0)]


def collect_rows(parts):
    own, first, second, far = parts
    half = far.shape[0] // 2
    far_low = far.astype(BF16)
    upper = exchange(far_low[:half], "mp", 1)
    lower = exchange(far_low[half:], "mp", 2)
    first = jnp.concatenate([first[:half], first[half:] + lower.astype(F32)], axis=0)
    second = jnp.concatenate([second[:half] + upper.astype(F32), second[half:]], axis=0)
    from_first = exchange(first.astype(BF16), "mp", 1)
    from_second = exchange(second.astype(BF16), "mp", 2)
    return own + from_first.astype(F32) + from_second.astype(F32)


def sum_over(values, axis):
    bit = 1
    while bit < lax.axis_size(axis):
        values = values + exchange(values, axis, bit)
        bit *= 2
    return values


def gather_small(values, axis):
    index = lax.axis_index(axis)
    gathered = values[None]
    bit = 1
    while bit < lax.axis_size(axis):
        other = exchange(gathered, axis, bit)
        low = (index & bit) == 0
        gathered = jnp.concatenate(
            [jnp.where(low, gathered, other), jnp.where(low, other, gathered)], axis=0
        )
        bit *= 2
    return gathered


def unit_norm(values):
    return values * lax.rsqrt(jnp.sum(values * values, axis=-1, keepdims=True) + NORM_EPSILON)


def document_starts(doc_row):
    position = jnp.arange(doc_row.shape[-1], dtype=jnp.int32)
    change = jnp.concatenate([jnp.ones((1,), dtype=jnp.bool_), doc_row[1:] != doc_row[:-1]])
    return lax.cummax(jnp.where(change, position, 0), axis=0)


def rope_tables(offsets):
    half_width = HD // 2
    inverse = 1.0 / ROPE_BASE ** (jnp.arange(half_width, dtype=F32) * (2.0 / HD))
    angles = offsets.astype(F32)[:, None] * inverse
    angles = jnp.concatenate([angles, angles], axis=-1)
    return (jnp.cos(angles)[:, None, :], jnp.sin(angles)[:, None, :])


def turn_heads(projected, cosine, sine_table, head_gains):
    half_width = projected.shape[-1] // 2
    swapped = jnp.concatenate([-projected[..., half_width:], projected[..., :half_width]], axis=-1)
    return unit_norm(projected * cosine + swapped * sine_table) * head_gains


def mix_residual(hidden, branch, mixing):
    return unit_norm(hidden + mixing * (unit_norm(branch) - hidden))


def gated_units(up, gate, scale_up, scale_gate):
    width = math.sqrt(1024)
    return up * scale_up * jax.nn.silu(gate * scale_gate * width)


def attend_block(query, keys, values, allowed):
    scores = math.sqrt(HD) * jnp.einsum("qhe,khe->hqk", query, keys, preferred_element_type=F32)
    scores = jnp.where(allowed[None], scores, MASK_VALUE)
    row_max = jnp.max(scores, axis=-1, keepdims=True)
    exponentials = jnp.exp(scores - row_max)
    row_total = jnp.sum(exponentials, axis=-1, keepdims=True)
    shares = (exponentials / row_total).astype(BF16)
    attended = jnp.einsum("hqk,khe->qhe", shares, values, preferred_element_type=F32)
    return attended.astype(BF16), row_max + jnp.log(row_total)


def attend_backward(query, keys, values, logsums, allowed, grad_out):
    length = query.shape[0]
    block_rows = min(512, length)
    score_scale = math.sqrt(HD)
    grad_keys = jnp.zeros(keys.shape, F32)
    grad_values = jnp.zeros(values.shape, F32)
    grad_queries = []
    for offset in range(0, length, block_rows):
        rows = slice(offset, offset + block_rows)
        query_rows = query[rows]
        grad_rows = grad_out[rows]
        scores = score_scale * jnp.einsum(
            "qhe,khe->hqk", query_rows, keys, preferred_element_type=F32
        )
        scores = jnp.where(allowed[rows][None], scores, MASK_VALUE)
        shares = jnp.exp(scores - logsums[:, rows])
        grad_values = grad_values + jnp.einsum(
            "hqk,qhe->khe", shares.astype(BF16), grad_rows, preferred_element_type=F32
        )
        grad_shares = jnp.einsum("qhe,khe->hqk", grad_rows, values, preferred_element_type=F32)
        grad_scores = (
            shares * (grad_shares - jnp.sum(shares * grad_shares, axis=-1, keepdims=True))
        ).astype(BF16)
        grad_queries.append(
            score_scale
            * jnp.einsum("hqk,khe->qhe", grad_scores, keys, preferred_element_type=F32)
        )
        grad_keys = grad_keys + score_scale * jnp.einsum(
            "hqk,qhe->khe", grad_scores, query_rows, preferred_element_type=F32
        )
    return (jnp.concatenate(grad_queries, axis=0), grad_keys, grad_values)


def dot(left, right):
    return jnp.dot(left, right, preferred_element_type=F32)


def dot_nt(left, right):
    return lax.dot_general(left, right, (((1,), (1,)), ((), ())), preferred_element_type=F32)


def dot_tn(left, right):
    return lax.dot_general(left, right, (((0,), (0,)), ((), ())), preferred_element_type=F32)


def layer_forward(hidden, params, tables):
    attend_in, attend_out, feed_in, feed_out, scale_qk, scale_up, scale_gate, mixing = params
    cosine, sine, allowed = tables
    rows = hidden.shape[0]
    hidden_blocks = spread_rows(hidden.astype(BF16))
    heads = attend_in.shape[2] // HD
    raw_blocks = []
    for block in hidden_blocks:
        raw = jnp.einsum("ld,cde->cle", block, attend_in, preferred_element_type=F32)
        raw_blocks.append(raw.reshape(3, rows, heads, HD))
    raw = jnp.concatenate(raw_blocks, axis=1)
    query = turn_heads(raw[0], cosine, sine, scale_qk).astype(BF16)
    keys = turn_heads(raw[1], cosine, sine, scale_qk).astype(BF16)
    values = raw[2].astype(BF16)
    attended, logsums, partial = [None] * 4, [None] * 4, [None] * 4
    for at in (3, 1, 2, 0):
        span = slice(at * rows, (at + 1) * rows)
        attended[at], logsums[at] = attend_block(query[span], keys, values, allowed[span])
        attended[at] = attended[at].reshape(rows, heads * HD)
        partial[at] = dot(attended[at], attend_out)
    branch = collect_rows(partial)
    middle = mix_residual(hidden, branch, mixing[0])
    middle_blocks = spread_rows(middle.astype(BF16))
    ups, gates, gated = [], [], []
    partial = []
    for block in middle_blocks:
        up, gate = dot(block, feed_in[0]), dot(block, feed_in[1])
        ups.append(up)
        gates.append(gate)
        gated.append(gated_units(up, gate, scale_up, scale_gate).astype(BF16))
        partial.append(dot(gated[-1], feed_out))
    mixed = collect_rows(partial)
    result = mix_residual(middle, mixed, mixing[1])
    stored = (
        hidden, hidden_blocks, raw, query, keys, values, logsums, attended, branch, middle,
        middle_blocks, ups, gates, gated, mixed,
    )
    return result, stored


def layer_backward(stored, upstream, params, tables):
    attend_in, attend_out, feed_in, feed_out, scale_qk, scale_up, scale_gate, mixing = params
    cosine, sine, allowed = tables
    (
        hidden, hidden_blocks, raw, query, keys, values, logsums, attended, branch, middle,
        middle_blocks, ups, gates, gated, mixed,
    ) = stored
    rows = hidden.shape[0]
    heads = attend_in.shape[2] // HD
    _, pull_last = jax.vjp(mix_residual, middle, mixed, mixing[1])
    grad_middle, grad_mixed, grad_rate_two = pull_last(upstream)
    mixed_blocks = spread_rows(grad_mixed.astype(BF16))
    partial, low_ups, low_gates = [], [], []
    grad_up_scale = grad_gate_scale = 0.0
    for at, block in enumerate(mixed_blocks):
        grad_gated = dot_nt(block, feed_out)
        _, pull_gate = jax.vjp(gated_units, ups[at], gates[at], scale_up, scale_gate)
        grad_up, grad_gate, part_up, part_gate = pull_gate(grad_gated)
        grad_up_scale = grad_up_scale + part_up
        grad_gate_scale = grad_gate_scale + part_gate
        low_ups.append(grad_up.astype(BF16))
        low_gates.append(grad_gate.astype(BF16))
        partial.append(dot_nt(low_ups[-1], feed_in[0]) + dot_nt(low_gates[-1], feed_in[1]))
    grad_middle = grad_middle + collect_rows(partial)
    join = lambda blocks: jnp.concatenate(blocks, axis=0)
    grad_feed_out = dot_tn(join(gated), join(mixed_blocks))
    middle_all = join(middle_blocks)
    grad_feed_in = jnp.stack([dot_tn(middle_all, join(low_ups)), dot_tn(middle_all, join(low_gates))])
    _, pull_first = jax.vjp(mix_residual, hidden, branch, mixing[0])
    grad_hidden, grad_branch, grad_rate_one = pull_first(grad_middle)
    branch_blocks = spread_rows(grad_branch.astype(BF16))
    grad_attend_out = dot_tn(join(attended), join(branch_blocks))
    grad_attended = join([dot_nt(block, attend_out).astype(BF16) for block in branch_blocks])
    grad_attended = grad_attended.reshape(raw.shape[1:])
    grad_query, grad_key, grad_value = attend_backward(
        query, keys, values, jnp.concatenate(logsums, axis=1), allowed, grad_attended
    )
    turn = lambda projected, gains: turn_heads(projected, cosine, sine, gains)
    _, pull_query = jax.vjp(turn, raw[0], scale_qk)
    grad_query_raw, gain_one = pull_query(grad_query)
    _, pull_key = jax.vjp(turn, raw[1], scale_qk)
    grad_key_raw, gain_two = pull_key(grad_key)
    low = [
        part.astype(BF16).reshape(4 * rows, heads * HD)
        for part in (grad_query_raw, grad_key_raw, grad_value)
    ]
    partial = [None] * 4
    for at in (3, 1, 2, 0):
        span = slice(at * rows, (at + 1) * rows)
        partial[at] = sum(dot_nt(low[c][span], attend_in[c]) for c in range(3))
    hidden_all = join(hidden_blocks)
    grad_attend_in = jnp.stack([dot_tn(hidden_all, low[c]) for c in range(3)])
    grad_hidden = grad_hidden + collect_rows(partial)
    grad_units = jnp.concatenate(
        [(gain_one + gain_two).reshape(-1), grad_up_scale, grad_gate_scale]
    )
    grad_rates = jnp.stack([grad_rate_one, grad_rate_two])
    return (
        grad_hidden,
        (grad_attend_in, grad_attend_out, grad_feed_in, grad_feed_out),
        (grad_units, grad_rates),
    )


def adam_update(weight, first, second, gradient, factor, renorm, rate):
    clipped = gradient * factor
    first_new = BETA_FIRST * first + (1.0 - BETA_FIRST) * clipped
    second_new = BETA_SECOND * second + (1.0 - BETA_SECOND) * clipped * clipped
    first_hat = first_new / (1.0 - BETA_FIRST**STEP)
    second_hat = second_new / (1.0 - BETA_SECOND**STEP)
    moved = weight - rate * first_hat / (jnp.sqrt(second_hat) + ADAM_EPSILON)
    if renorm:
        moved = moved * lax.rsqrt(jnp.sum(moved * moved, axis=2, keepdims=True) + NORM_EPSILON)
    return (first_new, second_new, moved)


def per_device(
    inputs,
    cotangent,
    doc_ids,
    attention_in,
    attention_out,
    feedforward_in,
    feedforward_out,
    unit_scales,
    mix_rates,
    first_attention_in,
    second_attention_in,
    first_attention_out,
    second_attention_out,
    first_feedforward_in,
    second_feedforward_in,
    first_feedforward_out,
    second_feedforward_out,
    first_unit_scales,
    second_unit_scales,
    first_mix_rates,
    second_mix_rates,
):
    section = lax.axis_index("section")
    is_first = section == 0
    mp_index = lax.axis_index("mp")
    dp_index = lax.axis_index("dp")
    local_rows = inputs.shape[1]
    matrices = (attention_in[0], attention_out[0], feedforward_in[0], feedforward_out[0])
    half_dims = (1, 1, 1, 1)
    shard_dims = (2, 0, 2, 0)

    def ordered(own, other):
        return jnp.where(is_first, own, other), jnp.where(is_first, other, own)

    def halves(array, dim):
        width = array.shape[dim] // 2
        own = lax.dynamic_slice_in_dim(array, section * width, width, dim)
        other = lax.dynamic_slice_in_dim(array, (1 - section) * width, width, dim)
        return own, other

    small = jnp.concatenate([unit_scales.reshape(-1), mix_rates.reshape(-1)]).astype(BF16)
    small = jnp.stack(ordered(small, exchange(small, "section", 1))).reshape(-1)
    small = gather_small(small, "dp").astype(F32)
    small = small.reshape(small.shape[0], 2, -1)
    units_here = unit_scales.shape[2]

    layer_halves = []
    for matrix, dim in zip(matrices, half_dims):
        own, other = halves(matrix.astype(BF16), dim)
        layer_halves.append(ordered(own, exchange(other, "section", 1)))
    layers = []
    for layer in range(2):
        params = []
        for pair, half_dim, shard_dim in zip(layer_halves, half_dims, shard_dims):
            own = lax.all_gather(pair[layer], "dp", axis=shard_dim, tiled=True)
            other = exchange(own, "section", 1)
            params.append(jnp.concatenate(ordered(own, other), axis=half_dim))
        units = small[:, layer, :units_here].reshape(-1)
        mixing = small[:, layer, units_here:].reshape(small.shape[0], 2, -1)
        mixing = jnp.swapaxes(mixing, 0, 1).reshape(2, -1)
        width_qk, width_ff = params[1].shape[0], params[3].shape[0]
        params.append(units[:width_qk].reshape(-1, HD))
        params.append(units[width_qk : width_qk + width_ff])
        params.append(units[width_qk + width_ff :])
        params.append(mixing)
        layers.append(params)

    doc_row = lax.dynamic_index_in_dim(doc_ids, section, 0, False)
    starts_all = document_starts(doc_row)
    positions, starts = [], []
    for offset in range(4):
        first_row = (mp_index ^ offset) * local_rows
        positions.append(first_row + jnp.arange(local_rows, dtype=jnp.int32))
        starts.append(lax.dynamic_slice_in_dim(starts_all, first_row, local_rows, 0))
    positions, starts = jnp.concatenate(positions), jnp.concatenate(starts)
    cosine, sine = rope_tables(positions - starts)
    allowed = (positions[None, :] <= positions[:, None]) & (positions[None, :] >= starts[:, None])
    tables = (cosine, sine, allowed)

    hidden = lax.dynamic_index_in_dim(inputs, section, 0, False).astype(F32)
    grad = lax.dynamic_index_in_dim(cotangent, section, 0, False).astype(F32)
    result, stored_first = layer_forward(hidden, layers[0], tables)
    result = result.astype(BF16).astype(F32)
    result, stored_second = layer_forward(result, layers[1], tables)
    grad, matrices_second, small_second = layer_backward(stored_second, grad, layers[1], tables)
    grad = grad.astype(BF16).astype(F32)
    grad, matrices_first, small_first = layer_backward(stored_first, grad, layers[0], tables)

    def reduce_matrix(partial, half_dim, shard_dim):
        own, other = halves(partial, half_dim)
        own = own + exchange(other.astype(BF16), "section", 1).astype(F32)
        return lax.psum_scatter(
            own.astype(BF16), "dp", scatter_dimension=shard_dim, tiled=True
        )

    reduced_second = [
        reduce_matrix(*entry) for entry in zip(matrices_second, half_dims, shard_dims)
    ]
    reduced_first = [reduce_matrix(*entry) for entry in zip(matrices_first, half_dims, shard_dims)]
    reduced = []
    for one, two, half_dim in zip(reduced_first, reduced_second, half_dims):
        own, other = jnp.where(is_first, one, two), jnp.where(is_first, two, one)
        other = exchange(other, "section", 1)
        reduced.append(jnp.concatenate(ordered(own, other), axis=half_dim).astype(F32)[None])

    units_own = jnp.where(is_first, small_first[0], small_second[0])
    units_other = jnp.where(is_first, small_second[0], small_first[0])
    rates_own = jnp.where(is_first, small_first[1], small_second[1])
    rates_other = jnp.where(is_first, small_second[1], small_first[1])
    count = units_own.shape[0]
    own = jnp.concatenate([units_own, rates_own.reshape(-1)])
    other = jnp.concatenate([units_other, rates_other.reshape(-1)])
    sums = sum_over(own + exchange(other, "section", 1), "dp")
    unit_grads = lax.dynamic_slice_in_dim(sums[:count], dp_index * units_here, units_here, 0)
    unit_grads = unit_grads[None, None]
    rate_sums = sum_over(sums[count:].reshape(2, -1), "mp")
    rates_here = mix_rates.shape[2]
    rate_grads = lax.dynamic_slice_in_dim(rate_sums, dp_index * rates_here, rates_here, 1)[None]

    leading = (mp_index == 0).astype(F32)
    squares = sum(jnp.sum(part * part) for part in reduced)
    squares = squares + jnp.sum(unit_grads * unit_grads)
    squares = squares + leading * jnp.sum(rate_grads * rate_grads)
    gradient_norm = jnp.sqrt(lax.psum(squares, ("section", "dp", "mp")))
    factor = CLIP_NORM / jnp.maximum(gradient_norm, CLIP_NORM)

    to_send = jnp.where(is_first, result, grad)
    kept = jnp.where(is_first, grad, result)
    arrived = exchange(to_send, "section", 1)
    boundary_states = jnp.stack(ordered(kept, arrived))[None]

    updates = []
    for weight, first, second, gradient in (
        (attention_in, first_attention_in, second_attention_in, reduced[0]),
        (attention_out, first_attention_out, second_attention_out, reduced[1]),
        (feedforward_in, first_feedforward_in, second_feedforward_in, reduced[2]),
        (feedforward_out, first_feedforward_out, second_feedforward_out, reduced[3]),
    ):
        updates.extend(adam_update(weight, first, second, gradient, factor, True, LEARN_RATE))
    updates.extend(
        adam_update(
            unit_scales, first_unit_scales, second_unit_scales, unit_grads, factor, False, SCALE_RATE
        )
    )
    updates.extend(
        adam_update(
            mix_rates, first_mix_rates, second_mix_rates, rate_grads, factor, False, MIXING_RATE
        )
    )
    return (boundary_states, gradient_norm, *updates)


def solution(mesh):
    in_specs = (
        P("dp", "mp", None),
        P("dp", "mp", None),
        P("dp", None),
        P("section", None, None, ("mp", "dp")),
        P("section", ("mp", "dp"), None),
        P("section", None, None, ("mp", "dp")),
        P("section", ("mp", "dp"), None),
        P("section", "mp", "dp"),
        P("section", None, "dp"),
        P("section", None, None, ("mp", "dp")),
        P("section", None, None, ("mp", "dp")),
        P("section", ("mp", "dp"), None),
        P("section", ("mp", "dp"), None),
        P("section", None, None, ("mp", "dp")),
        P("section", None, None, ("mp", "dp")),
        P("section", ("mp", "dp"), None),
        P("section", ("mp", "dp"), None),
        P("section", "mp", "dp"),
        P("section", "mp", "dp"),
        P("section", None, "dp"),
        P("section", None, "dp"),
    )
    out_specs = (
        P("section", "dp", "mp", None),
        P(),
        P("section", None, None, ("mp", "dp")),
        P("section", None, None, ("mp", "dp")),
        P("section", None, None, ("mp", "dp")),
        P("section", ("mp", "dp"), None),
        P("section", ("mp", "dp"), None),
        P("section", ("mp", "dp"), None),
        P("section", None, None, ("mp", "dp")),
        P("section", None, None, ("mp", "dp")),
        P("section", None, None, ("mp", "dp")),
        P("section", ("mp", "dp"), None),
        P("section", ("mp", "dp"), None),
        P("section", ("mp", "dp"), None),
        P("section", "mp", "dp"),
        P("section", "mp", "dp"),
        P("section", "mp", "dp"),
        P("section", None, "dp"),
        P("section", None, "dp"),
        P("section", None, "dp"),
    )
    return jax.shard_map(
        per_device, mesh=mesh, in_specs=in_specs, out_specs=out_specs, check_vma=False
    )
```

```python
import math

import jax
import jax.numpy as jnp
from jax import lax
from jax.sharding import PartitionSpec as P

HD = 64
STEP = 10

NORM_EPSILON = 1e-06
ROPE_BASE = 10000.0
CLIP_NORM = 0.1
LEARN_RATE = 0.05
SCALE_RATE = 1.25
MIXING_RATE = 0.4
BETA_FIRST = 0.9
BETA_SECOND = 0.95
ADAM_EPSILON = 1e-08
MASK_VALUE = -1e30

BF16 = jnp.bfloat16
F32 = jnp.float32


def exchange(block, axis, bit):
    route = [(i, i ^ bit) for i in range(lax.axis_size(axis))]
    return lax.ppermute(block, axis, route)


def gray(place):
    return place ^ (place >> 1)


def ring_place(index, size):
    shift = 1
    while shift < size:
        index = index ^ (index >> shift)
        shift *= 2
    return index


def ring_step(block, axis):
    size = lax.axis_size(axis)
    route = []
    for place in range(size):
        route.append((gray(place), gray((place + 1) % size)))
        route.append((size + gray(place), size + gray((place - 1) % size)))
    return lax.ppermute(block, ("section", axis), route)


def ring_sources(axis):
    size = lax.axis_size(axis)
    place = ring_place(lax.axis_index(axis), size)
    way = 1 - 2 * lax.axis_index("section")
    return [gray((place - way * step + size) % size) for step in range(size)]


def spread_rows(block, axis="mp"):
    blocks = [block]
    for _ in range(lax.axis_size(axis) - 1):
        blocks.append(ring_step(blocks[-1], axis))
    return blocks


def collect_rows(parts, axis="mp"):
    moving = parts[1]
    for part in parts[2:] + parts[:1]:
        moving = ring_step(moving.astype(BF16), axis).astype(F32) + part
    return moving


def sum_over(values, axis):
    bit, size = 1, lax.axis_size(axis)
    while bit < size:
        if 2 * bit < size:
            first, second = exchange(values, axis, bit), exchange(values, axis, 2 * bit)
            values = (values + first) + (second + exchange(values, axis, 3 * bit))
        else:
            values = values + exchange(values, axis, bit)
        bit *= 4
    return values


def gather_small(values, axis):
    index = lax.axis_index(axis)
    gathered = values[None]
    bit = 1
    while bit < lax.axis_size(axis):
        other = exchange(gathered, axis, bit)
        low = (index & bit) == 0
        gathered = jnp.concatenate(
            [jnp.where(low, gathered, other), jnp.where(low, other, gathered)], axis=0
        )
        bit *= 2
    return gathered


def unit_norm(values):
    return values * lax.rsqrt(jnp.sum(values * values, axis=-1, keepdims=True) + NORM_EPSILON)


def document_starts(doc_row):
    position = jnp.arange(doc_row.shape[-1], dtype=jnp.int32)
    change = jnp.concatenate([jnp.ones((1,), dtype=jnp.bool_), doc_row[1:] != doc_row[:-1]])
    return lax.cummax(jnp.where(change, position, 0), axis=0)


def rope_tables(offsets):
    half_width = HD // 2
    inverse = 1.0 / ROPE_BASE ** (jnp.arange(half_width, dtype=F32) * (2.0 / HD))
    angles = offsets.astype(F32)[:, None] * inverse
    angles = jnp.concatenate([angles, angles], axis=-1)
    return (jnp.cos(angles)[:, None, :], jnp.sin(angles)[:, None, :])


def turn_heads(projected, cosine, sine_table, head_gains):
    half_width = projected.shape[-1] // 2
    swapped = jnp.concatenate([-projected[..., half_width:], projected[..., :half_width]], axis=-1)
    return unit_norm(projected * cosine + swapped * sine_table) * head_gains


def mix_residual(hidden, branch, mixing):
    return unit_norm(hidden + mixing * (unit_norm(branch) - hidden))


def gated_units(up, gate, scale_up, scale_gate):
    width = math.sqrt(1024)
    return up * scale_up * jax.nn.silu(gate * scale_gate * width)


def attend_block(query, keys, values, allowed):
    scores = math.sqrt(HD) * jnp.einsum("qhe,khe->hqk", query, keys, preferred_element_type=F32)
    scores = jnp.where(allowed[None], scores, MASK_VALUE)
    row_max = jnp.max(scores, axis=-1, keepdims=True)
    exponentials = jnp.exp(scores - row_max)
    row_total = jnp.sum(exponentials, axis=-1, keepdims=True)
    shares = (exponentials / row_total).astype(BF16)
    attended = jnp.einsum("hqk,khe->qhe", shares, values, preferred_element_type=F32)
    return attended.astype(BF16), row_max + jnp.log(row_total)


def attend_backward(query, keys, values, logsums, allowed, grad_out):
    length = query.shape[0]
    block_rows = min(512, length)
    score_scale = math.sqrt(HD)
    grad_keys = jnp.zeros(keys.shape, F32)
    grad_values = jnp.zeros(values.shape, F32)
    grad_queries = []
    for offset in range(0, length, block_rows):
        rows = slice(offset, offset + block_rows)
        query_rows = query[rows]
        grad_rows = grad_out[rows]
        scores = score_scale * jnp.einsum(
            "qhe,khe->hqk", query_rows, keys, preferred_element_type=F32
        )
        scores = jnp.where(allowed[rows][None], scores, MASK_VALUE)
        shares = jnp.exp(scores - logsums[:, rows])
        grad_values = grad_values + jnp.einsum(
            "hqk,qhe->khe", shares.astype(BF16), grad_rows, preferred_element_type=F32
        )
        grad_shares = jnp.einsum("qhe,khe->hqk", grad_rows, values, preferred_element_type=F32)
        grad_scores = (
            shares * (grad_shares - jnp.sum(shares * grad_shares, axis=-1, keepdims=True))
        ).astype(BF16)
        grad_queries.append(
            score_scale
            * jnp.einsum("hqk,khe->qhe", grad_scores, keys, preferred_element_type=F32)
        )
        grad_keys = grad_keys + score_scale * jnp.einsum(
            "hqk,qhe->khe", grad_scores, query_rows, preferred_element_type=F32
        )
    return (jnp.concatenate(grad_queries, axis=0), grad_keys, grad_values)


def dot(left, right):
    return jnp.dot(left, right, preferred_element_type=F32)


def dot_nt(left, right):
    return lax.dot_general(left, right, (((1,), (1,)), ((), ())), preferred_element_type=F32)


def dot_tn(left, right):
    return lax.dot_general(left, right, (((0,), (0,)), ((), ())), preferred_element_type=F32)


def layer_forward(hidden, params, tables):
    attend_in, attend_out, feed_in, feed_out, scale_qk, scale_up, scale_gate, mixing = params
    cosine, sine, allowed = tables
    rows = hidden.shape[0]
    hidden_blocks = spread_rows(hidden.astype(BF16))
    heads = attend_in.shape[1] // HD
    raw_blocks = []
    for block in hidden_blocks:
        raw = jnp.einsum("ld,ced->cle", block, attend_in, preferred_element_type=F32)
        raw_blocks.append(raw.reshape(3, rows, heads, HD))
    raw = jnp.concatenate(raw_blocks, axis=1)
    query = turn_heads(raw[0], cosine, sine, scale_qk).astype(BF16)
    keys = turn_heads(raw[1], cosine, sine, scale_qk).astype(BF16)
    values = raw[2].astype(BF16)
    attended, logsums, partial = [None] * 4, [None] * 4, [None] * 4
    for at in (1, 2, 3, 0):
        span = slice(at * rows, (at + 1) * rows)
        attended[at], logsums[at] = attend_block(query[span], keys, values, allowed[span])
        attended[at] = attended[at].reshape(rows, heads * HD)
        partial[at] = dot(attended[at], attend_out)
    branch = collect_rows(partial)
    middle = mix_residual(hidden, branch, mixing[0])
    middle_blocks = spread_rows(middle.astype(BF16))
    ups, gates, gated = [], [], []
    partial = []
    for block in middle_blocks:
        up, gate = dot(block, feed_in[0]), dot(block, feed_in[1])
        ups.append(up)
        gates.append(gate)
        gated.append(gated_units(up, gate, scale_up, scale_gate).astype(BF16))
        partial.append(dot(gated[-1], feed_out))
    mixed = collect_rows(partial)
    result = mix_residual(middle, mixed, mixing[1])
    stored = (
        hidden, hidden_blocks, raw, query, keys, values, logsums, attended, branch, middle,
        middle_blocks, ups, gates, gated, mixed,
    )
    return result, stored


def join(blocks):
    return jnp.concatenate(blocks, axis=0)


def feed_backward(stored, upstream, params):
    attend_in, attend_out, feed_in, feed_out, scale_qk, scale_up, scale_gate, mixing = params
    middle, middle_blocks, ups, gates, gated, mixed = stored[9:]
    _, pull_last = jax.vjp(mix_residual, middle, mixed, mixing[1])
    grad_middle, grad_mixed, grad_rate = pull_last(upstream)
    mixed_blocks = spread_rows(grad_mixed.astype(BF16))
    partial, low_ups, low_gates = [], [], []
    grad_up_scale = grad_gate_scale = 0.0
    for at, block in enumerate(mixed_blocks):
        grad_gated = dot_nt(block, feed_out)
        _, pull_gate = jax.vjp(gated_units, ups[at], gates[at], scale_up, scale_gate)
        grad_up, grad_gate, part_up, part_gate = pull_gate(grad_gated)
        grad_up_scale = grad_up_scale + part_up
        grad_gate_scale = grad_gate_scale + part_gate
        low_ups.append(grad_up.astype(BF16))
        low_gates.append(grad_gate.astype(BF16))
        partial.append(dot_nt(low_ups[-1], feed_in[0]) + dot_nt(low_gates[-1], feed_in[1]))
    grad_middle = grad_middle + collect_rows(partial)
    middle_all = join(middle_blocks)
    grad_feed_in = jnp.stack(
        [dot_tn(middle_all, join(low_ups)), dot_tn(middle_all, join(low_gates))]
    )
    grad_feed_out = dot_tn(join(gated), join(mixed_blocks))
    return grad_middle, (grad_feed_in, grad_feed_out), (grad_up_scale, grad_gate_scale, grad_rate)


def attend_pull(stored, upstream, params):
    attend_in, attend_out, feed_in, feed_out, scale_qk, scale_up, scale_gate, mixing = params
    hidden, attended, branch = stored[0], stored[7], stored[8]
    _, pull_first = jax.vjp(mix_residual, hidden, branch, mixing[0])
    grad_hidden, grad_branch, grad_rate = pull_first(upstream)
    branch_blocks = spread_rows(grad_branch.astype(BF16))
    grad_attended = join([dot_nt(block, attend_out).astype(BF16) for block in branch_blocks])
    grad_attend_out = dot_tn(join(attended), join(branch_blocks))
    return grad_hidden, grad_attended, grad_attend_out, grad_rate


def attend_finish(stored, grad_hidden, grad_attended, params, tables):
    attend_in, attend_out, feed_in, feed_out, scale_qk, scale_up, scale_gate, mixing = params
    cosine, sine, allowed = tables
    hidden, hidden_blocks, raw, query, keys, values, logsums = stored[:7]
    rows = hidden.shape[0]
    heads = attend_in.shape[1] // HD
    grad_query, grad_key, grad_value = attend_backward(
        query, keys, values, jnp.concatenate(logsums, axis=1), allowed,
        grad_attended.reshape(raw.shape[1:]),
    )
    turn = lambda projected, gains: turn_heads(projected, cosine, sine, gains)
    _, pull_query = jax.vjp(turn, raw[0], scale_qk)
    grad_query_raw, gain_one = pull_query(grad_query)
    _, pull_key = jax.vjp(turn, raw[1], scale_qk)
    grad_key_raw, gain_two = pull_key(grad_key)
    low = [
        part.astype(BF16).reshape(4 * rows, heads * HD)
        for part in (grad_query_raw, grad_key_raw, grad_value)
    ]
    partial = [None] * 4
    for at in (1, 2, 3, 0):
        span = slice(at * rows, (at + 1) * rows)
        partial[at] = sum(dot(low[c][span], attend_in[c]) for c in range(3))
    hidden_all = join(hidden_blocks)
    grad_attend_in = [dot_tn(low[c], hidden_all) for c in range(3)]
    grad_hidden = grad_hidden + collect_rows(partial)
    return grad_hidden, grad_attend_in, (gain_one + gain_two).reshape(-1)


def adam_update(weight, first, second, gradient, factor, renorm, rate):
    clipped = gradient * factor
    first_new = BETA_FIRST * first + (1.0 - BETA_FIRST) * clipped
    second_new = BETA_SECOND * second + (1.0 - BETA_SECOND) * clipped * clipped
    first_hat = first_new / (1.0 - BETA_FIRST**STEP)
    second_hat = second_new / (1.0 - BETA_SECOND**STEP)
    moved = weight - rate * first_hat / (jnp.sqrt(second_hat) + ADAM_EPSILON)
    if renorm:
        moved = moved * lax.rsqrt(jnp.sum(moved * moved, axis=2, keepdims=True) + NORM_EPSILON)
    return (first_new, second_new, moved)


def per_device(
    inputs,
    cotangent,
    doc_ids,
    attention_in,
    attention_out,
    feedforward_in,
    feedforward_out,
    unit_scales,
    mix_rates,
    first_attention_in,
    second_attention_in,
    first_attention_out,
    second_attention_out,
    first_feedforward_in,
    second_feedforward_in,
    first_feedforward_out,
    second_feedforward_out,
    first_unit_scales,
    second_unit_scales,
    first_mix_rates,
    second_mix_rates,
):
    section = lax.axis_index("section")
    is_first = section == 0
    dp_index = lax.axis_index("dp")
    dp_size = lax.axis_size("dp")
    local_rows = inputs.shape[1]
    barrier = lax.optimization_barrier

    def ordered(own, other):
        return jnp.where(is_first, own, other), jnp.where(is_first, other, own)

    def halves(array, dim):
        width = array.shape[dim] // 2
        own = lax.dynamic_slice_in_dim(array, section * width, width, dim)
        other = lax.dynamic_slice_in_dim(array, (1 - section) * width, width, dim)
        return own, other

    hidden_low = lax.dynamic_index_in_dim(inputs, section, 0, False)

    attend_rows = jnp.concatenate(
        [jnp.swapaxes(attention_in[0], 1, 2), attention_out], axis=0
    ).astype(BF16)
    small = jnp.concatenate([unit_scales.reshape(-1), mix_rates.reshape(-1)]).astype(BF16)
    pieces = []
    for matrix, dim in (
        (attend_rows, 2), (feedforward_in[0].astype(BF16), 2), (feedforward_out[0].astype(BF16), 0)
    ):
        own, other = halves(matrix, dim)
        pieces.append(ordered(own, exchange(other, "section", 1)))
    small = jnp.stack(ordered(small, exchange(small, "section", 1))).reshape(-1)
    small = gather_small(small, "dp").astype(F32)
    small = small.reshape(dp_size, 2, -1)
    units_here = unit_scales.shape[2]

    def units_apart(values):
        parts = values.reshape(dp_size, 2, -1)
        own, other = ordered(parts[:, 0], parts[:, 1])
        return jnp.concatenate([own.reshape(-1), other.reshape(-1)])

    def units_back(values):
        parts = values.reshape(2, dp_size, -1)
        own, other = ordered(parts[0], parts[1])
        return jnp.stack([own, other], axis=1).reshape(-1)

    def gather_attend(half, by_ring):
        if not by_ring or dp_size > 4:
            return lax.all_gather(half, "dp", axis=1, tiled=True)
        blocks = spread_rows(half, "dp")
        count = half.shape[1]
        whole = jnp.zeros((half.shape[0], dp_size * count, half.shape[2]), BF16)
        for source, block in zip(ring_sources("dp"), blocks):
            whole = lax.dynamic_update_slice_in_dim(whole, block, source * count, 1)
        return whole

    layers = []
    for layer in range(2):
        own = gather_attend(pieces[0][layer], layer == 0)
        attend = jnp.concatenate(ordered(own, exchange(own, "section", 1)), axis=2)
        own = lax.all_gather(pieces[1][layer], "dp", axis=2, tiled=True)
        feed_in = jnp.concatenate([own, exchange(own, "section", 1)], axis=2)
        own = lax.all_gather(pieces[2][layer], "dp", axis=0, tiled=True)
        feed_out = jnp.concatenate([own, exchange(own, "section", 1)], axis=0)
        units = small[:, layer, :units_here].reshape(-1)
        mixing = small[:, layer, units_here:].reshape(dp_size, 2, -1)
        mixing = jnp.swapaxes(mixing, 0, 1).reshape(2, -1)
        width_qk, width_ff = attend.shape[1], feed_out.shape[0]
        layers.append((
            attend[:3], attend[3], feed_in, feed_out,
            units[:width_qk].reshape(-1, HD),
            units_apart(units[width_qk : width_qk + width_ff]),
            units_apart(units[width_qk + width_ff :]),
            mixing,
        ))

    doc_row = lax.dynamic_index_in_dim(doc_ids, section, 0, False)
    starts_all = document_starts(doc_row)
    positions, starts = [], []
    for source in ring_sources("mp"):
        first_row = source * local_rows
        positions.append(first_row + jnp.arange(local_rows, dtype=jnp.int32))
        starts.append(lax.dynamic_slice_in_dim(starts_all, first_row, local_rows, 0))
    positions, starts = jnp.concatenate(positions), jnp.concatenate(starts)
    cosine, sine = rope_tables(positions - starts)
    allowed = (positions[None, :] <= positions[:, None]) & (positions[None, :] >= starts[:, None])
    tables = (cosine, sine, allowed)

    def pair_sum(own, other):
        return (own + exchange(other.astype(BF16), "section", 1).astype(F32)).astype(BF16)

    def pair_feed(partials):
        grad_in, grad_out = partials
        half = grad_out.shape[0] // 2
        return (
            pair_sum(grad_in[:, :, :half], grad_in[:, :, half:]),
            pair_sum(grad_out[:half], grad_out[half:]),
        )

    def scatter_feed(sums):
        return (
            lax.psum_scatter(sums[0], "dp", scatter_dimension=2, tiled=True),
            lax.psum_scatter(sums[1], "dp", scatter_dimension=0, tiled=True),
        )

    def scatter_attend(sums, by_ring):
        if not by_ring or dp_size > 4:
            return lax.psum_scatter(sums, "dp", scatter_dimension=1, tiled=True)
        count = sums.shape[1] // dp_size
        parts = [
            lax.dynamic_slice_in_dim(sums, source * count, count, 1).astype(F32)
            for source in ring_sources("dp")
        ]
        return collect_rows(parts, "dp").astype(BF16)

    first, second = layers
    grad = lax.dynamic_index_in_dim(cotangent, section, 0, False).astype(F32)
    result, stored_first = layer_forward(hidden_low.astype(F32), first, tables)
    result = result.astype(BF16).astype(F32)
    result, stored_second = layer_forward(result, second, tables)

    grad, feed_second, scales_second = feed_backward(stored_second, grad, second)
    grad, pulled, out_second, rate_second = attend_pull(stored_second, grad, second)
    grad, in_second, gains_second = attend_finish(stored_second, grad, pulled, second, tables)
    grad = grad.astype(BF16)
    grad, feed_second = barrier((grad, pair_feed(feed_second)))
    feed_second = scatter_feed(feed_second)
    grad, feed_first, scales_first = feed_backward(stored_first, grad.astype(F32), first)
    attend_second = pair_sum(*halves(jnp.stack([*in_second, out_second]), 2))
    grad, attend_second = barrier((grad, attend_second))
    attend_second = scatter_attend(attend_second, False)
    grad, pulled, out_first, rate_first = attend_pull(stored_first, grad, first)
    pulled, feed_first = barrier((pulled, pair_feed(feed_first)))
    feed_first = scatter_feed(feed_first)
    grad, in_first, gains_first = attend_finish(stored_first, grad, pulled, first, tables)
    attend_first = pair_sum(*halves(jnp.stack([*in_first, out_first]), 2))
    attend_first = scatter_attend(attend_first, True)

    reduced_first = (attend_first, *feed_first)
    reduced_second = (attend_second, *feed_second)
    squares = sum(
        jnp.sum(jnp.square(part.astype(F32))) for part in (*reduced_first, *reduced_second)
    )
    gradients = []
    for one, two, dim in zip(reduced_first, reduced_second, (2, 2, 0)):
        own, other = jnp.where(is_first, one, two), jnp.where(is_first, two, one)
        other = exchange(other, "section", 1)
        gradients.append(jnp.concatenate(ordered(own, other), axis=dim).astype(F32))

    def small_sums(gains, scales, rate):
        grad_up_scale, grad_gate_scale, rate_two = scales
        return jnp.concatenate(
            [gains, units_back(grad_up_scale), units_back(grad_gate_scale), rate, rate_two]
        )

    small_first = small_sums(gains_first, scales_first, rate_first)
    small_second = small_sums(gains_second, scales_second, rate_second)
    own = jnp.where(is_first, small_first, small_second)
    other = jnp.where(is_first, small_second, small_first)
    sums = sum_over(own + exchange(other, "section", 1), "dp")
    count = units_here * dp_size
    unit_grads = lax.dynamic_slice_in_dim(sums[:count], dp_index * units_here, units_here, 0)
    unit_grads = unit_grads[None, None]
    rate_sums = sum_over(sums[count:].reshape(2, -1), "mp")
    rates_here = mix_rates.shape[2]
    rate_grads = lax.dynamic_slice_in_dim(rate_sums, dp_index * rates_here, rates_here, 1)[None]

    leading = (lax.axis_index("mp") == 0).astype(F32)
    squares = squares + jnp.sum(unit_grads * unit_grads)
    squares = squares + leading * jnp.sum(rate_grads * rate_grads)
    squares = squares.reshape(1)
    squares = squares + exchange(squares, "section", 1)
    squares = sum_over(sum_over(squares, "mp"), "dp")
    gradient_norm = jnp.sqrt(squares[0])
    factor = CLIP_NORM / jnp.maximum(gradient_norm, CLIP_NORM)

    to_send = jnp.where(is_first, result, grad)
    kept = jnp.where(is_first, grad, result)
    arrived = exchange(to_send, "section", 1)
    boundary_states = jnp.stack(ordered(kept, arrived))[None]

    attend_grad, feed_in_grad, feed_out_grad = gradients
    updates = []
    for weight, moment, square, gradient in (
        (attention_in, first_attention_in, second_attention_in,
         jnp.swapaxes(attend_grad[:3], 1, 2)[None]),
        (attention_out, first_attention_out, second_attention_out, attend_grad[3:]),
        (feedforward_in, first_feedforward_in, second_feedforward_in, feed_in_grad[None]),
        (feedforward_out, first_feedforward_out, second_feedforward_out, feed_out_grad[None]),
    ):
        updates.extend(adam_update(weight, moment, square, gradient, factor, True, LEARN_RATE))
    updates.extend(
        adam_update(
            unit_scales, first_unit_scales, second_unit_scales, unit_grads, factor, False, SCALE_RATE
        )
    )
    updates.extend(
        adam_update(
            mix_rates, first_mix_rates, second_mix_rates, rate_grads, factor, False, MIXING_RATE
        )
    )
    return (boundary_states, gradient_norm, *updates)


def solution(mesh):
    in_specs = (
        P("dp", "mp", None),
        P("dp", "mp", None),
        P("dp", None),
        P("section", None, None, ("mp", "dp")),
        P("section", ("mp", "dp"), None),
        P("section", None, None, ("mp", "dp")),
        P("section", ("mp", "dp"), None),
        P("section", "mp", "dp"),
        P("section", None, "dp"),
        P("section", None, None, ("mp", "dp")),
        P("section", None, None, ("mp", "dp")),
        P("section", ("mp", "dp"), None),
        P("section", ("mp", "dp"), None),
        P("section", None, None, ("mp", "dp")),
        P("section", None, None, ("mp", "dp")),
        P("section", ("mp", "dp"), None),
        P("section", ("mp", "dp"), None),
        P("section", "mp", "dp"),
        P("section", "mp", "dp"),
        P("section", None, "dp"),
        P("section", None, "dp"),
    )
    out_specs = (
        P("section", "dp", "mp", None),
        P(),
        P("section", None, None, ("mp", "dp")),
        P("section", None, None, ("mp", "dp")),
        P("section", None, None, ("mp", "dp")),
        P("section", ("mp", "dp"), None),
        P("section", ("mp", "dp"), None),
        P("section", ("mp", "dp"), None),
        P("section", None, None, ("mp", "dp")),
        P("section", None, None, ("mp", "dp")),
        P("section", None, None, ("mp", "dp")),
        P("section", ("mp", "dp"), None),
        P("section", ("mp", "dp"), None),
        P("section", ("mp", "dp"), None),
        P("section", "mp", "dp"),
        P("section", "mp", "dp"),
        P("section", "mp", "dp"),
        P("section", None, "dp"),
        P("section", None, "dp"),
        P("section", None, "dp"),
    )
    return jax.shard_map(
        per_device, mesh=mesh, in_specs=in_specs, out_specs=out_specs, check_vma=False
    )
```

```python
import functools
import math

import jax
import jax.numpy as jnp
from jax import lax
from jax.experimental import pallas as pl
from jax.experimental.pallas import tpu as pltpu
from jax.sharding import PartitionSpec as P

HD = 64
STEP = 10

NORM_EPSILON = 1e-06
ROPE_BASE = 10000.0
CLIP_NORM = 0.1
LEARN_RATE = 0.05
SCALE_RATE = 1.25
MIXING_RATE = 0.4
BETA_FIRST = 0.9
BETA_SECOND = 0.95
ADAM_EPSILON = 1e-08

BF16 = jnp.bfloat16
F32 = jnp.float32


def exchange(block, axis, bit):
    route = [(i, i ^ bit) for i in range(lax.axis_size(axis))]
    return lax.ppermute(block, axis, route)


def gray(place):
    return place ^ (place >> 1)


def ring_place(index, size):
    shift = 1
    while shift < size:
        index = index ^ (index >> shift)
        shift *= 2
    return index


def ring_step(block, axis):
    size = lax.axis_size(axis)
    route = []
    for place in range(size):
        route.append((gray(place), gray((place + 1) % size)))
        route.append((size + gray(place), size + gray((place - 1) % size)))
    return lax.ppermute(block, ("section", axis), route)


def ring_sources(axis):
    size = lax.axis_size(axis)
    place = ring_place(lax.axis_index(axis), size)
    way = 1 - 2 * lax.axis_index("section")
    return [gray((place - way * step + size) % size) for step in range(size)]


def spread_rows(block, axis="mp"):
    blocks = [block]
    for _ in range(lax.axis_size(axis) - 1):
        blocks.append(ring_step(blocks[-1], axis))
    return blocks


def collect_rows(parts, axis="mp"):
    moving = parts[1]
    for part in parts[2:] + parts[:1]:
        moving = ring_step(moving.astype(BF16), axis).astype(F32) + part
    return moving


def sum_over(values, axis):
    bit, size = 1, lax.axis_size(axis)
    while bit < size:
        if 2 * bit < size:
            first, second = exchange(values, axis, bit), exchange(values, axis, 2 * bit)
            values = (values + first) + (second + exchange(values, axis, 3 * bit))
        else:
            values = values + exchange(values, axis, bit)
        bit *= 4
    return values


def gather_small(values, axis):
    index = lax.axis_index(axis)
    gathered = values[None]
    bit = 1
    while bit < lax.axis_size(axis):
        other = exchange(gathered, axis, bit)
        low = (index & bit) == 0
        gathered = jnp.concatenate(
            [jnp.where(low, gathered, other), jnp.where(low, other, gathered)], axis=0
        )
        bit *= 2
    return gathered


def unit_norm(values):
    return values * lax.rsqrt(jnp.sum(values * values, axis=-1, keepdims=True) + NORM_EPSILON)


def document_starts(doc_row):
    position = jnp.arange(doc_row.shape[-1], dtype=jnp.int32)
    change = jnp.concatenate([jnp.ones((1,), dtype=jnp.bool_), doc_row[1:] != doc_row[:-1]])
    return lax.cummax(jnp.where(change, position, 0), axis=0)


def rope_tables(offsets):
    half_width = HD // 2
    inverse = 1.0 / ROPE_BASE ** (jnp.arange(half_width, dtype=F32) * (2.0 / HD))
    angles = inverse[:, None] * offsets.astype(F32)[..., None, :]
    angles = jnp.concatenate([angles, angles], axis=-2)
    return jnp.cos(angles), jnp.sin(angles)


def mix_residual(hidden, branch, mixing):
    return unit_norm(hidden + mixing * (unit_norm(branch) - hidden))


NT = (((1,), (1,)), ((), ()))
TN = (((0,), (0,)), ((), ()))
NN = (((1,), (0,)), ((), ()))
VMEM = pltpu.VMEM
WHOLE = pl.BlockSpec(memory_space=pltpu.VMEM)
SCALARS = pl.BlockSpec(memory_space=pltpu.SMEM)


def mul(left, right, dims=NN):
    return lax.dot_general(left, right, dims, preferred_element_type=F32)


def call(body, out_shape, in_specs, flops, moved, scratch=(), limit=32, **more):
    if "grid" not in more:
        more["out_specs"] = [WHOLE] * len(out_shape)
    return pl.pallas_call(
        body,
        out_shape=out_shape,
        in_specs=in_specs,
        scratch_shapes=list(scratch),
        compiler_params=pltpu.CompilerParams(vmem_limit_bytes=limit << 20),
        cost_estimate=pl.CostEstimate(flops=flops, bytes_accessed=moved, transcendentals=0),
        **more,
    )


def shape(dims, dtype):
    return jax.ShapeDtypeStruct(dims, dtype)


def turned(raw, cosine, sine):
    half = HD // 2
    first, second = raw[:half], raw[half:]
    return jnp.concatenate(
        [
            first * cosine[:half] - second * sine[:half],
            second * cosine[half:] + first * sine[half:],
        ],
        axis=0,
    )


def turned_back(grad, cosine, sine):
    half = HD // 2
    first, second = grad[:half], grad[half:]
    return jnp.concatenate(
        [
            first * cosine[:half] + second * sine[half:],
            second * cosine[half:] - first * sine[:half],
        ],
        axis=0,
    )


def project_kernel(x, weight, cosine, sine, gains, raw_out, query, keys, values):
    width = query.shape[0]
    raw = mul(weight[...], x[...], NT)
    raw_out[...] = raw[: 2 * width]
    values[...] = raw[2 * width :].astype(BF16)
    for part, out in ((0, query), (1, keys)):
        for top in range(0, width, HD):
            turn = turned(raw[part * width + top : part * width + top + HD], cosine[...], sine[...])
            scale = lax.rsqrt(jnp.sum(turn * turn, axis=0, keepdims=True) + NORM_EPSILON)
            head = (turn * scale * gains[top : top + HD]).astype(BF16)
            out[top : top + HD] = head * math.sqrt(HD) if part == 0 else head


def project_block(x, weight, cosine, sine, gains):
    tokens, depth = x.shape
    width = weight.shape[0] // 3
    low = shape((width, tokens), BF16)
    return call(
        project_kernel,
        [shape((2 * width, tokens), F32), low, low, low],
        [WHOLE] * 5,
        2 * tokens * depth * 3 * width,
        2 * 3 * width * depth,
    )(x, weight, cosine, sine, gains)


def near(info, at, other, tokens):
    return (info[other] <= info[at]) & ((info[other] + 1) * tokens > info[4 + at])


def seen(info, at, other, starts, tokens):
    key_place = info[other] * tokens + lax.broadcasted_iota(jnp.int32, (tokens, tokens), 0)
    query_place = info[at] * tokens + lax.broadcasted_iota(jnp.int32, (tokens, tokens), 1)
    return (key_place <= query_place) & (key_place >= starts)


def attend_kernel(at, info, starts, query, k0, k1, k2, k3, v0, v1, v2, v3, weight,
                  attended, logsums, partial, total, sums):
    width, tokens = query.shape
    total[...] = jnp.zeros_like(total)
    sums[...] = jnp.ones_like(sums)
    sums[: width // HD] = jnp.zeros((width // HD, tokens), F32)
    for other, (keys, values) in enumerate(((k0, v0), (k1, v1), (k2, v2), (k3, v3))):

        @pl.when(near(info, at, other, tokens))
        def _():
            allowed = seen(info, at, other, starts[...], tokens)
            for head in range(width // HD):
                rows = slice(head * HD, head * HD + HD)
                shares = jnp.exp(mul(keys[rows], query[rows], TN))
                shares = jnp.where(allowed, shares, 0.0)
                sums[head : head + 1] += jnp.sum(shares, axis=0, keepdims=True)
                total[rows] += mul(values[rows], shares.astype(BF16))

    logsums[...] = jnp.log(sums[...])
    inverse = 1.0 / sums[...]
    for head in range(width // HD):
        rows = slice(head * HD, head * HD + HD)
        attended[rows] = (total[rows] * inverse[head : head + 1]).astype(BF16)
    partial[...] = mul(attended[...], weight[...], TN).astype(partial.dtype)


def attend_block(at, info, starts, query, keys, values, weight, out_type):
    width, tokens = query.shape
    depth = weight.shape[1]
    return call(
        functools.partial(attend_kernel, at),
        [
            shape((width, tokens), BF16),
            shape((8, tokens), F32),
            shape((tokens, depth), out_type),
        ],
        [SCALARS] + [WHOLE] * 11,
        2 * tokens * (depth * width + 10 * tokens * 256),
        2 * depth * width,
        [VMEM((width, tokens), F32), VMEM((8, tokens), F32)],
    )(info, starts, query, *keys, *values, weight)


def attend_back_kernel(info, starts, *refs):
    query, keys, values, attended, logsums, raw, grads = (refs[4 * n : 4 * n + 4] for n in range(7))
    w_out, w_in, cosine, sine, gains = refs[28:33]
    low, partial = refs[33:37], refs[37:41]
    gain_grad = refs[41]
    pulled, deltas, grad_query, grad_keys, grad_values = refs[42:]
    width, tokens = query[0].shape
    heads = width // HD
    grad_query[...] = jnp.zeros_like(grad_query)
    grad_keys[...] = jnp.zeros_like(grad_keys)
    grad_values[...] = jnp.zeros_like(grad_values)
    deltas[...] = jnp.zeros_like(deltas)
    for at in range(4):
        grad = mul(w_out[...], grads[at][...], NT).astype(BF16)
        pulled[at] = grad
        product = grad.astype(F32) * attended[at][...].astype(F32)
        for head in range(heads):
            rows = slice(head * HD, head * HD + HD)
            deltas[at, head : head + 1] = jnp.sum(product[rows], axis=0, keepdims=True)
    for at in range(4):
        for other in range(4):

            @pl.when(near(info, at, other, tokens))
            def _():
                allowed = seen(info, at, other, starts[at : at + 1], tokens)
                for head in range(heads):
                    rows = slice(head * HD, head * HD + HD)
                    grad_rows, query_rows = pulled[at, rows], query[at][rows]
                    scores = mul(keys[other][rows], query_rows, TN) - logsums[at][head : head + 1]
                    shares = jnp.where(allowed, jnp.exp(scores), 0.0)
                    grad_shares = mul(values[other][rows], grad_rows, TN)
                    grad_scores = shares * (grad_shares - deltas[at, head : head + 1])
                    grad_scores = grad_scores.astype(BF16)
                    grad_values[other, rows] += mul(grad_rows, shares.astype(BF16), NT)
                    grad_keys[other, rows] += mul(query_rows, grad_scores, NT)
                    grad_query[at, rows] += mul(keys[other][rows], grad_scores)

    gain_total = [0.0] * heads
    for at in range(4):
        cos, sin = cosine[at], sine[at]
        for part, source, factor in ((0, grad_query, math.sqrt(HD)), (1, grad_keys, 1.0)):
            for head in range(heads):
                rows = slice(head * HD, head * HD + HD)
                turn = turned(raw[at][part * width + head * HD : part * width + head * HD + HD], cos, sin)
                scale = lax.rsqrt(jnp.sum(turn * turn, axis=0, keepdims=True) + NORM_EPSILON)
                unit = turn * scale
                grad = source[at, rows] * factor
                gain_total[head] = gain_total[head] + grad * unit
                grad = grad * gains[rows]
                grad = scale * (grad - unit * jnp.sum(unit * grad, axis=0, keepdims=True))
                low[at][part * width + head * HD : part * width + head * HD + HD] = turned_back(
                    grad, cos, sin
                ).astype(BF16)
        low[at][2 * width :] = grad_values[at].astype(BF16)
        partial[at][...] = mul(low[at][...], w_in[...], TN).astype(partial[at].dtype)
    for head in range(heads):
        gain_grad[head * HD : head * HD + HD] = jnp.sum(gain_total[head], axis=1, keepdims=True)


def attend_back(info, starts, query, keys, values, attended, logsums, raw, grads,
                w_out, w_in, cosine, sine, gains):
    width, tokens = query[0].shape
    depth = w_out.shape[1]
    low = shape((3 * width, tokens), BF16)
    block = VMEM((4, width, tokens), F32)
    outs = call(
        attend_back_kernel,
        [low] * 4
        + [shape((tokens, depth), BF16 if at == 1 else F32) for at in range(4)]
        + [shape((width, 1), F32)],
        [SCALARS] + [WHOLE] * 34,
        2 * 4 * tokens * (depth * width * 4 + 60 * tokens * 256),
        2 * depth * width * 12,
        [VMEM((4, width, tokens), BF16), VMEM((4, 8, tokens), F32), block, block, block],
        limit=40,
    )(info, starts, *query, *keys, *values, *attended, *logsums, *raw, *grads,
      w_out, w_in, cosine, sine, gains)
    return outs[:4], outs[4:8], outs[8]


def feed_kernel(x, w_in, w_out, scales, ups, gates, gated, partial, total):
    step = pl.program_id(0)
    up, gate = mul(x[...], w_in[0]), mul(x[...], w_in[1])
    ups[...] = up.astype(BF16)
    gates[...] = gate.astype(BF16)
    z = gate * (scales[1:2] * math.sqrt(1024))
    mixed = (up * scales[0:1] * (z / (1.0 + jnp.exp(-z)))).astype(BF16)
    gated[...] = mixed
    part = mul(mixed, w_out[...])

    @pl.when(step == 0)
    def _():
        total[...] = part

    @pl.when(step > 0)
    def _():
        total[...] += part

    @pl.when(step == pl.num_programs(0) - 1)
    def _():
        partial[...] = total[...].astype(partial.dtype)


CHUNK = 256


def feed_block(x, w_in, w_out, scales, out_type):
    tokens, depth = x.shape
    units = w_out.shape[0]
    chunk = min(CHUNK, units)
    kept = pl.BlockSpec((tokens, chunk), lambda i: (0, i))
    whole = pl.BlockSpec((tokens, depth), lambda i: (0, 0))
    low = shape((tokens, units), BF16)
    return call(
        feed_kernel,
        [low, low, low, shape((tokens, depth), out_type)],
        [
            whole,
            pl.BlockSpec((2, depth, chunk), lambda i: (0, 0, i)),
            pl.BlockSpec((chunk, depth), lambda i: (i, 0)),
            pl.BlockSpec((2, chunk), lambda i: (0, i)),
        ],
        2 * 3 * tokens * depth * units,
        2 * 3 * depth * units,
        [VMEM((tokens, depth), F32)],
        grid=(units // chunk,),
        out_specs=[kept, kept, kept, whole],
    )(x, w_in, w_out, scales)


def feed_back_kernel(g, w_in, w_out, scales, ups, gates, low_up, low_gate, scale_grad, partial, total):
    step = pl.program_id(0)
    grad = mul(g[...], w_out[...], NT)
    up, gate = ups[...].astype(F32), gates[...].astype(F32)
    s_up, s_gate = scales[0:1], scales[1:2] * math.sqrt(1024)
    z = gate * s_gate
    sigmoid = 1.0 / (1.0 + jnp.exp(-z))
    silu = z * sigmoid
    grad_silu = grad * silu
    scaled = up * s_up
    grad_z = grad * scaled * (sigmoid + silu * (1.0 - sigmoid))
    grad_up, grad_gate = (grad_silu * s_up).astype(BF16), (grad_z * s_gate).astype(BF16)
    low_up[...] = grad_up
    low_gate[...] = grad_gate
    scale_grad[0:1] = jnp.sum(grad_silu * up, axis=0, keepdims=True)
    scale_grad[1:2] = jnp.sum(grad_z * gate, axis=0, keepdims=True) * math.sqrt(1024)
    part = mul(grad_up, w_in[0], NT) + mul(grad_gate, w_in[1], NT)

    @pl.when(step == 0)
    def _():
        total[...] = part

    @pl.when(step > 0)
    def _():
        total[...] += part

    @pl.when(step == pl.num_programs(0) - 1)
    def _():
        partial[...] = total[...].astype(partial.dtype)


def feed_back_block(g, w_in, w_out, scales, ups, gates, out_type):
    tokens, depth = g.shape
    units = w_out.shape[0]
    chunk = min(CHUNK, units)
    kept = pl.BlockSpec((tokens, chunk), lambda i: (0, i))
    whole = pl.BlockSpec((tokens, depth), lambda i: (0, 0))
    pair = pl.BlockSpec((2, chunk), lambda i: (0, i))
    low = shape((tokens, units), BF16)
    return call(
        feed_back_kernel,
        [low, low, shape((2, units), F32), shape((tokens, depth), out_type)],
        [
            whole,
            pl.BlockSpec((2, depth, chunk), lambda i: (0, 0, i)),
            pl.BlockSpec((chunk, depth), lambda i: (i, 0)),
            pair,
            kept,
            kept,
        ],
        2 * 3 * tokens * depth * units,
        2 * 3 * depth * units,
        [VMEM((tokens, depth), F32)],
        grid=(units // chunk,),
        out_specs=[kept, kept, pair, whole],
    )(g, w_in, w_out, scales, ups, gates)


def dot(left, right):
    return jnp.dot(left, right, preferred_element_type=F32)


def dot_tn(left, right):
    return lax.dot_general(left, right, TN, preferred_element_type=F32)


def join(blocks, axis=0):
    return jnp.concatenate(blocks, axis=axis)


def tie(*values):
    return lax.optimization_barrier(values)


def passed_on(moving, part):
    return ring_step((moving.astype(F32) + part).astype(BF16), "mp")


def feed_ring(block, work):
    step = lambda moving: ring_step(moving, "mp")
    blocks, done = [block], []
    following = step(block)
    done.append(work(0, block))
    following, done[0] = tie(following, done[0])
    blocks.append(following)
    following = step(following)
    done.append(work(1, blocks[1]))
    following, done[1] = tie(following, done[1])
    blocks.append(following)
    following = step(following)
    moving = step(done[1][-1])
    done.append(work(2, blocks[2]))
    following, moving, done[2] = tie(following, moving, done[2])
    blocks.append(following)
    moving = passed_on(moving, done[2][-1])
    done.append(work(3, blocks[3]))
    moving, done[3] = tie(moving, done[3])
    moving = passed_on(moving, done[3][-1])
    return blocks, done, moving.astype(F32) + done[0][-1]


def sum_type(at):
    return BF16 if at == 1 else F32


def layer_forward(hidden, params, tables, tied):
    attend_in, attend_out, feed_in, feed_out, gains, scales, mixing = params
    cosine, sine, starts, info = tables
    blocks, heads = [hidden.astype(BF16)], []
    for at in range(4):
        if at < 3:
            following = ring_step(blocks[at], "mp")
        heads.append(project_block(blocks[at], attend_in, cosine[at], sine[at], gains))
        if at < 3:
            if tied:
                following, heads[at] = tie(following, heads[at])
            blocks.append(following)
    raw, query, keys, values = zip(*heads)
    attend = lambda at: attend_block(
        at, info, starts[at : at + 1], query[at], keys, values, attend_out, sum_type(at)
    )
    attended = [None] * 4
    attended[1] = attend(1)
    moving = ring_step(attended[1][-1], "mp")
    attended[2] = attend(2)
    moving, attended[2] = tie(moving, attended[2])
    moving = passed_on(moving, attended[2][-1])
    attended[3] = attend(3)
    moving, attended[3] = tie(moving, attended[3])
    moving = passed_on(moving, attended[3][-1])
    attended[0] = attend(0)
    branch = moving.astype(F32) + attended[0][-1]
    middle = mix_residual(hidden, branch, mixing[0])
    work = lambda at, block: feed_block(block, feed_in, feed_out, scales, sum_type(at))
    middle_blocks, fed, mixed = feed_ring(middle.astype(BF16), work)
    result = mix_residual(middle, mixed, mixing[1])
    ups, gates, gated, _ = zip(*fed)
    attended, logsums, _ = zip(*attended)
    stored = (
        (hidden, branch, blocks, raw, query, keys, values, attended, logsums),
        (middle, mixed, middle_blocks, ups, gates, gated),
    )
    return result, stored


def feed_backward(stored, upstream, params):
    attend_in, attend_out, feed_in, feed_out, gains, scales, mixing = params
    middle, mixed, middle_blocks, ups, gates, gated = stored
    _, pull = jax.vjp(mix_residual, middle, mixed, mixing[1])
    grad_middle, grad_mixed, grad_rate = pull(upstream)
    work = lambda at, block: feed_back_block(
        block, feed_in, feed_out, scales, ups[at], gates[at], sum_type(at)
    )
    blocks, done, total = feed_ring(grad_mixed.astype(BF16), work)
    low_ups, low_gates, scale_grads, _ = zip(*done)
    middle_all = join(middle_blocks)
    grad_feed_in = [dot_tn(middle_all, join(low_ups)), dot_tn(middle_all, join(low_gates))]
    grad_feed_out = dot_tn(join(gated), join(blocks))
    return grad_middle + total, (grad_feed_in, grad_feed_out), sum(scale_grads), grad_rate


def attend_pull(stored, upstream, params):
    hidden, branch = stored[:2]
    _, pull = jax.vjp(mix_residual, hidden, branch, params[-1][0])
    grad_hidden, grad_branch, grad_rate = pull(upstream)
    return grad_hidden, spread_rows(grad_branch.astype(BF16)), grad_rate


def attend_finish(stored, grad_hidden, grads, params, tables):
    attend_in, attend_out, feed_in, feed_out, gains, scales, mixing = params
    cosine, sine, starts, info = tables
    hidden, branch, blocks, raw, query, keys, values, attended, logsums = stored
    low, partial, gain_grad = attend_back(
        info, starts, query, keys, values, attended, logsums, raw, grads,
        attend_out, attend_in, cosine, sine, gains,
    )
    moving = ring_step(partial[1], "mp")
    moving = passed_on(moving, partial[2])
    moving = passed_on(moving, partial[3])
    grad_hidden = grad_hidden + (moving.astype(F32) + partial[0])
    grad_attend_in = dot(join(low, 1), join(blocks))
    grad_attend_out = dot(join(attended, 1), join(grads))
    return grad_hidden, join([grad_attend_in, grad_attend_out]), gain_grad[:, 0]


def adam_update(weight, first, second, gradient, factor, renorm, rate):
    clipped = gradient * factor
    first_new = BETA_FIRST * first + (1.0 - BETA_FIRST) * clipped
    second_new = BETA_SECOND * second + (1.0 - BETA_SECOND) * clipped * clipped
    first_hat = first_new / (1.0 - BETA_FIRST**STEP)
    second_hat = second_new / (1.0 - BETA_SECOND**STEP)
    moved = weight - rate * first_hat / (jnp.sqrt(second_hat) + ADAM_EPSILON)
    if renorm:
        moved = moved * lax.rsqrt(jnp.sum(moved * moved, axis=2, keepdims=True) + NORM_EPSILON)
    return (first_new, second_new, moved)


def per_device(
    inputs,
    cotangent,
    doc_ids,
    attention_in,
    attention_out,
    feedforward_in,
    feedforward_out,
    unit_scales,
    mix_rates,
    first_attention_in,
    second_attention_in,
    first_attention_out,
    second_attention_out,
    first_feedforward_in,
    second_feedforward_in,
    first_feedforward_out,
    second_feedforward_out,
    first_unit_scales,
    second_unit_scales,
    first_mix_rates,
    second_mix_rates,
):
    section = lax.axis_index("section")
    is_first = section == 0
    dp_index = lax.axis_index("dp")
    dp_size = lax.axis_size("dp")
    local_rows = inputs.shape[1]

    def ordered(own, other):
        return jnp.where(is_first, own, other), jnp.where(is_first, other, own)

    def halves(array, dim):
        width = array.shape[dim] // 2
        own = lax.dynamic_slice_in_dim(array, section * width, width, dim)
        other = lax.dynamic_slice_in_dim(array, (1 - section) * width, width, dim)
        return own, other

    hidden_low = lax.dynamic_index_in_dim(inputs, section, 0, False)

    attend_rows = jnp.concatenate(
        [jnp.swapaxes(attention_in[0], 1, 2), attention_out], axis=0
    ).astype(BF16)
    small = jnp.concatenate([unit_scales.reshape(-1), mix_rates.reshape(-1)]).astype(BF16)
    own, other = halves(attend_rows, 2)
    other, feed_in_here, feed_out_here = tie(
        exchange(other, "section", 1), feedforward_in[0], feedforward_out[0]
    )
    pieces = [ordered(own, other)]
    for matrix, dim in ((feed_in_here.astype(BF16), 2), (feed_out_here.astype(BF16), 0)):
        own, other = halves(matrix, dim)
        pieces.append(ordered(own, exchange(other, "section", 1)))
    small = jnp.stack(ordered(small, exchange(small, "section", 1))).reshape(-1)
    small = gather_small(small, "dp").astype(F32)
    small = small.reshape(dp_size, 2, -1)
    units_here = unit_scales.shape[2]

    def units_apart(values):
        parts = values.reshape(dp_size, 2, -1)
        own, other = ordered(parts[:, 0], parts[:, 1])
        return jnp.concatenate([own.reshape(-1), other.reshape(-1)])

    def units_back(values):
        parts = values.reshape(2, dp_size, -1)
        own, other = ordered(parts[0], parts[1])
        return jnp.stack([own, other], axis=1).reshape(-1)

    def gather_attend(half, by_ring):
        if not by_ring or dp_size > 4:
            return lax.all_gather(half, "dp", axis=1, tiled=True)
        blocks = spread_rows(half, "dp")
        count = half.shape[1]
        whole = jnp.zeros((half.shape[0], dp_size * count, half.shape[2]), BF16)
        for source, block in zip(ring_sources("dp"), blocks):
            whole = lax.dynamic_update_slice_in_dim(whole, block, source * count, 1)
        return whole

    layers = []
    for layer in range(2):
        own = gather_attend(pieces[0][layer], layer == 0)
        attend = jnp.concatenate(ordered(own, exchange(own, "section", 1)), axis=2)
        own = lax.all_gather(pieces[1][layer], "dp", axis=2, tiled=True)
        feed_in = jnp.concatenate([own, exchange(own, "section", 1)], axis=2)
        own = lax.all_gather(pieces[2][layer], "dp", axis=0, tiled=True)
        feed_out = jnp.concatenate([own, exchange(own, "section", 1)], axis=0)
        units = small[:, layer, :units_here].reshape(-1)
        mixing = small[:, layer, units_here:].reshape(dp_size, 2, -1)
        mixing = jnp.swapaxes(mixing, 0, 1).reshape(2, -1)
        width_qk, width_ff = attend.shape[1], feed_out.shape[0]
        layers.append((
            attend[:3].reshape(3 * width_qk, -1), attend[3], feed_in, feed_out,
            units[:width_qk, None],
            jnp.stack([
                units_apart(units[width_qk : width_qk + width_ff]),
                units_apart(units[width_qk + width_ff :]),
            ]),
            mixing,
        ))

    doc_row = lax.dynamic_index_in_dim(doc_ids, section, 0, False)
    starts_all = document_starts(doc_row)
    sources = ring_sources("mp")
    places = jnp.arange(local_rows, dtype=jnp.int32)
    starts = jnp.stack([
        lax.dynamic_slice_in_dim(starts_all, source * local_rows, local_rows, 0)
        for source in sources
    ])
    sources = jnp.stack(sources).astype(jnp.int32)
    cosine, sine = rope_tables(sources[:, None] * local_rows + places - starts)
    info = jnp.concatenate([sources, starts[:, 0]])
    tables = (cosine, sine, starts, info)

    def pair_sum(own, other):
        return (own + exchange(other.astype(BF16), "section", 1).astype(F32)).astype(BF16)

    def pair_feed(partials):
        grad_in, grad_out = partials
        half = grad_out.shape[0] // 2
        return (
            [pair_sum(part[:, :half], part[:, half:]) for part in grad_in],
            pair_sum(grad_out[:half], grad_out[half:]),
        )

    def scatter_feed(sums):
        return (
            lax.psum_scatter(jnp.stack(sums[0]), "dp", scatter_dimension=2, tiled=True),
            lax.psum_scatter(sums[1], "dp", scatter_dimension=0, tiled=True),
        )

    def scatter_attend(sums, by_ring):
        if not by_ring or dp_size > 4:
            return lax.psum_scatter(sums, "dp", scatter_dimension=1, tiled=True)
        count = sums.shape[1] // dp_size
        parts = [
            lax.dynamic_slice_in_dim(sums, source * count, count, 1).astype(F32)
            for source in ring_sources("dp")
        ]
        return collect_rows(parts, "dp").astype(BF16)

    def pair_attend(rows):
        return pair_sum(*halves(rows.reshape(4, -1, rows.shape[1]), 2))

    first, second = layers
    grad = lax.dynamic_index_in_dim(cotangent, section, 0, False).astype(F32)
    result, stored_first = layer_forward(hidden_low.astype(F32), first, tables, False)
    result = result.astype(BF16).astype(F32)
    result, stored_second = layer_forward(result, second, tables, True)

    grad, feed_second, scales_second, rate_two_second = feed_backward(
        stored_second[1], grad, second
    )
    grad, grads, rate_second = attend_pull(stored_second[0], grad, second)
    grad, attend_second, gains_second = attend_finish(
        stored_second[0], grad, grads, second, tables
    )
    grad, feed_second = tie(grad.astype(BF16), pair_feed(feed_second))
    feed_second = scatter_feed(feed_second)
    grad, feed_first, scales_first, rate_two_first = feed_backward(
        stored_first[1], grad.astype(F32), first
    )
    grad, attend_second = tie(grad, pair_attend(attend_second))
    attend_second = scatter_attend(attend_second, False)
    grad, grads, rate_first = attend_pull(stored_first[0], grad, first)
    grads, feed_first = tie(grads, pair_feed(feed_first))
    feed_first = scatter_feed(feed_first)
    grad, attend_first, gains_first = attend_finish(stored_first[0], grad, grads, first, tables)
    attend_first, feed_second = tie(pair_attend(attend_first), feed_second)
    attend_first = scatter_attend(attend_first, True)

    reduced_first = (attend_first, *feed_first)
    reduced_second = (attend_second, *feed_second)
    squares = sum(
        jnp.sum(jnp.square(part.astype(F32))) for part in (*reduced_first, *reduced_second)
    )
    gradients = []
    for one, two, dim in zip(reduced_first, reduced_second, (2, 2, 0)):
        own, other = jnp.where(is_first, one, two), jnp.where(is_first, two, one)
        other = exchange(other, "section", 1)
        gradients.append(jnp.concatenate(ordered(own, other), axis=dim).astype(F32))

    def small_sums(gains, scales, rate, rate_two):
        return jnp.concatenate([gains, units_back(scales[0]), units_back(scales[1]), rate, rate_two])

    small_first = small_sums(gains_first, scales_first, rate_first, rate_two_first)
    small_second = small_sums(gains_second, scales_second, rate_second, rate_two_second)
    own = jnp.where(is_first, small_first, small_second)
    other = jnp.where(is_first, small_second, small_first)
    sums = sum_over(own + exchange(other, "section", 1), "dp")
    count = units_here * dp_size
    unit_grads = lax.dynamic_slice_in_dim(sums[:count], dp_index * units_here, units_here, 0)
    unit_grads = unit_grads[None, None]
    rate_sums = sum_over(sums[count:].reshape(2, -1), "mp")
    rates_here = mix_rates.shape[2]
    rate_grads = lax.dynamic_slice_in_dim(rate_sums, dp_index * rates_here, rates_here, 1)[None]

    leading = (lax.axis_index("mp") == 0).astype(F32)
    squares = squares + jnp.sum(unit_grads * unit_grads)
    squares = squares + leading * jnp.sum(rate_grads * rate_grads)
    squares = squares.reshape(1)
    squares = squares + exchange(squares, "section", 1)
    squares = sum_over(sum_over(squares, "mp"), "dp")
    gradient_norm = jnp.sqrt(squares[0])
    factor = CLIP_NORM / jnp.maximum(gradient_norm, CLIP_NORM)

    to_send = jnp.where(is_first, result, grad)
    kept = jnp.where(is_first, grad, result)
    arrived = exchange(to_send, "section", 1)
    boundary_states = jnp.stack(ordered(kept, arrived))[None]

    attend_grad, feed_in_grad, feed_out_grad = gradients
    updates = []
    for weight, moment, square, gradient in (
        (attention_in, first_attention_in, second_attention_in,
         jnp.swapaxes(attend_grad[:3], 1, 2)[None]),
        (attention_out, first_attention_out, second_attention_out, attend_grad[3:]),
        (feedforward_in, first_feedforward_in, second_feedforward_in, feed_in_grad[None]),
        (feedforward_out, first_feedforward_out, second_feedforward_out, feed_out_grad[None]),
    ):
        updates.extend(adam_update(weight, moment, square, gradient, factor, True, LEARN_RATE))
    updates.extend(
        adam_update(
            unit_scales, first_unit_scales, second_unit_scales, unit_grads, factor, False, SCALE_RATE
        )
    )
    updates.extend(
        adam_update(
            mix_rates, first_mix_rates, second_mix_rates, rate_grads, factor, False, MIXING_RATE
        )
    )
    return (boundary_states, gradient_norm, *updates)


def solution(mesh):
    in_specs = (
        P("dp", "mp", None),
        P("dp", "mp", None),
        P("dp", None),
        P("section", None, None, ("mp", "dp")),
        P("section", ("mp", "dp"), None),
        P("section", None, None, ("mp", "dp")),
        P("section", ("mp", "dp"), None),
        P("section", "mp", "dp"),
        P("section", None, "dp"),
        P("section", None, None, ("mp", "dp")),
        P("section", None, None, ("mp", "dp")),
        P("section", ("mp", "dp"), None),
        P("section", ("mp", "dp"), None),
        P("section", None, None, ("mp", "dp")),
        P("section", None, None, ("mp", "dp")),
        P("section", ("mp", "dp"), None),
        P("section", ("mp", "dp"), None),
        P("section", "mp", "dp"),
        P("section", "mp", "dp"),
        P("section", None, "dp"),
        P("section", None, "dp"),
    )
    out_specs = (
        P("section", "dp", "mp", None),
        P(),
        P("section", None, None, ("mp", "dp")),
        P("section", None, None, ("mp", "dp")),
        P("section", None, None, ("mp", "dp")),
        P("section", ("mp", "dp"), None),
        P("section", ("mp", "dp"), None),
        P("section", ("mp", "dp"), None),
        P("section", None, None, ("mp", "dp")),
        P("section", None, None, ("mp", "dp")),
        P("section", None, None, ("mp", "dp")),
        P("section", ("mp", "dp"), None),
        P("section", ("mp", "dp"), None),
        P("section", ("mp", "dp"), None),
        P("section", "mp", "dp"),
        P("section", "mp", "dp"),
        P("section", "mp", "dp"),
        P("section", None, "dp"),
        P("section", None, "dp"),
        P("section", None, "dp"),
    )
    return jax.shard_map(
        per_device, mesh=mesh, in_specs=in_specs, out_specs=out_specs, check_vma=False
    )
```

```python
import functools
import math

import jax
import jax.numpy as jnp
from jax import lax
from jax.experimental import pallas as pl
from jax.experimental.pallas import tpu as pltpu
from jax.sharding import PartitionSpec as P

HD = 64
STEP = 10

NORM_EPSILON = 1e-06
ROPE_BASE = 10000.0
CLIP_NORM = 0.1
LEARN_RATE = 0.05
SCALE_RATE = 1.25
MIXING_RATE = 0.4
BETA_FIRST = 0.9
BETA_SECOND = 0.95
ADAM_EPSILON = 1e-08

BF16 = jnp.bfloat16
F32 = jnp.float32


def exchange(block, axis, bit):
    route = [(i, i ^ bit) for i in range(lax.axis_size(axis))]
    return lax.ppermute(block, axis, route)


def gray(place):
    return place ^ (place >> 1)


def ring_place(index, size):
    shift = 1
    while shift < size:
        index = index ^ (index >> shift)
        shift *= 2
    return index


def ring_step(block, axis):
    size = lax.axis_size(axis)
    route = []
    for place in range(size):
        route.append((gray(place), gray((place + 1) % size)))
        route.append((size + gray(place), size + gray((place - 1) % size)))
    return lax.ppermute(block, ("section", axis), route)


def ring_sources(axis):
    size = lax.axis_size(axis)
    place = ring_place(lax.axis_index(axis), size)
    way = 1 - 2 * lax.axis_index("section")
    return [gray((place - way * step + size) % size) for step in range(size)]


def spread_rows(block, axis="mp"):
    blocks = [block]
    for _ in range(lax.axis_size(axis) - 1):
        blocks.append(ring_step(blocks[-1], axis))
    return blocks


def collect_rows(parts, axis="mp"):
    moving = parts[1]
    for part in parts[2:] + parts[:1]:
        moving = ring_step(moving.astype(BF16), axis).astype(F32) + part
    return moving


def sum_over(values, axis):
    bit = 1
    while bit < lax.axis_size(axis):
        values = values + exchange(values, axis, bit)
        bit *= 2
    return values


def gather_small(values, axis):
    index = lax.axis_index(axis)
    gathered = values[None]
    bit = 1
    while bit < lax.axis_size(axis):
        other = exchange(gathered, axis, bit)
        low = (index & bit) == 0
        gathered = jnp.concatenate(
            [jnp.where(low, gathered, other), jnp.where(low, other, gathered)], axis=0
        )
        bit *= 2
    return gathered


def unit_norm(values):
    return values * lax.rsqrt(jnp.sum(values * values, axis=-1, keepdims=True) + NORM_EPSILON)


def document_starts(doc_row):
    position = jnp.arange(doc_row.shape[-1], dtype=jnp.int32)
    change = jnp.concatenate([jnp.ones((1,), dtype=jnp.bool_), doc_row[1:] != doc_row[:-1]])
    return lax.cummax(jnp.where(change, position, 0), axis=0)


def rope_tables(offsets):
    half_width = HD // 2
    inverse = 1.0 / ROPE_BASE ** (jnp.arange(half_width, dtype=F32) * (2.0 / HD))
    angles = inverse[:, None] * offsets.astype(F32)[..., None, :]
    angles = jnp.concatenate([angles, angles], axis=-2)
    return jnp.cos(angles), jnp.sin(angles)


def mix_residual(hidden, branch, mixing):
    return unit_norm(hidden + mixing * (unit_norm(branch) - hidden))


NT = (((1,), (1,)), ((), ()))
TN = (((0,), (0,)), ((), ()))
NN = (((1,), (0,)), ((), ()))
VMEM = pltpu.VMEM
WHOLE = pl.BlockSpec(memory_space=pltpu.VMEM)
SCALARS = pl.BlockSpec(memory_space=pltpu.SMEM)


def mul(left, right, dims=NN):
    return lax.dot_general(left, right, dims, preferred_element_type=F32)


def call(body, out_shape, in_specs, flops, moved, scratch=(), limit=14, **more):
    if "grid" not in more:
        more["out_specs"] = [WHOLE] * len(out_shape)
    return pl.pallas_call(
        body,
        out_shape=out_shape,
        in_specs=in_specs,
        scratch_shapes=list(scratch),
        compiler_params=pltpu.CompilerParams(vmem_limit_bytes=limit << 20),
        cost_estimate=pl.CostEstimate(flops=flops, bytes_accessed=moved, transcendentals=0),
        **more,
    )


def shape(dims, dtype):
    return jax.ShapeDtypeStruct(dims, dtype)


def turned(raw, cosine, sine):
    half = HD // 2
    first, second = raw[:half], raw[half:]
    return jnp.concatenate(
        [
            first * cosine[:half] - second * sine[:half],
            second * cosine[half:] + first * sine[half:],
        ],
        axis=0,
    )


def turned_back(grad, cosine, sine):
    half = HD // 2
    first, second = grad[:half], grad[half:]
    return jnp.concatenate(
        [
            first * cosine[:half] + second * sine[half:],
            second * cosine[half:] - first * sine[:half],
        ],
        axis=0,
    )


def project_kernel(x, weight, cosine, sine, gains, raw_out, query, keys, values):
    width = query.shape[0]
    raw = mul(weight[...], x[...], NT)
    raw_out[...] = raw[: 2 * width]
    values[...] = raw[2 * width :].astype(BF16)
    for part, out in ((0, query), (1, keys)):
        for top in range(0, width, HD):
            turn = turned(raw[part * width + top : part * width + top + HD], cosine[...], sine[...])
            scale = lax.rsqrt(jnp.sum(turn * turn, axis=0, keepdims=True) + NORM_EPSILON)
            head = (turn * scale * gains[top : top + HD]).astype(BF16)
            out[top : top + HD] = head * math.sqrt(HD) if part == 0 else head


def project_block(x, weight, cosine, sine, gains):
    tokens, depth = x.shape
    width = weight.shape[0] // 3
    low = shape((width, tokens), BF16)
    return call(
        project_kernel,
        [shape((2 * width, tokens), F32), low, low, low],
        [WHOLE] * 5,
        2 * tokens * depth * 3 * width,
        2 * 3 * width * depth,
    )(x, weight, cosine, sine, gains)


def near(info, at, other, tokens):
    return (info[other] <= info[at]) & ((info[other] + 1) * tokens > info[4 + at])


def seen(info, at, other, starts, tokens):
    key_place = info[other] * tokens + lax.broadcasted_iota(jnp.int32, (tokens, tokens), 0)
    query_place = info[at] * tokens + lax.broadcasted_iota(jnp.int32, (tokens, tokens), 1)
    return (key_place <= query_place) & (key_place >= starts)


def share_out(partial, value):
    if len(partial) == 1:
        partial[0][...] = value
    else:
        half = value.shape[0] // 2
        partial[0][...] = value[:half].astype(BF16)
        partial[1][...] = value[half:].astype(BF16)


def partial_shapes(at, tokens, depth):
    if at == 3:
        return [shape((tokens // 2, depth), BF16)] * 2
    return [shape((tokens, depth), F32)]


def attend_kernel(at, info, starts, query, k0, k1, k2, k3, v0, v1, v2, v3, weight, *refs):
    attended, logsums, *partial = refs[:-2]
    total, sums = refs[-2:]
    width, tokens = query.shape
    total[...] = jnp.zeros_like(total)
    sums[...] = jnp.ones_like(sums)
    sums[: width // HD] = jnp.zeros((width // HD, tokens), F32)
    for other, (keys, values) in enumerate(((k0, v0), (k1, v1), (k2, v2), (k3, v3))):

        @pl.when(near(info, at, other, tokens))
        def _():
            allowed = seen(info, at, other, starts[...], tokens)
            for head in range(width // HD):
                rows = slice(head * HD, head * HD + HD)
                shares = jnp.exp(mul(keys[rows], query[rows], TN))
                shares = jnp.where(allowed, shares, 0.0)
                sums[head : head + 1] += jnp.sum(shares, axis=0, keepdims=True)
                total[rows] += mul(values[rows], shares.astype(BF16))

    logsums[...] = jnp.log(sums[...])
    inverse = 1.0 / sums[...]
    for head in range(width // HD):
        rows = slice(head * HD, head * HD + HD)
        attended[rows] = (total[rows] * inverse[head : head + 1]).astype(BF16)
    share_out(partial, mul(attended[...], weight[...], TN))


def attend_block(at, info, starts, query, keys, values, weight):
    width, tokens = query.shape
    depth = weight.shape[1]
    attended, logsums, *partial = call(
        functools.partial(attend_kernel, at),
        [shape((width, tokens), BF16), shape((8, tokens), F32)] + partial_shapes(at, tokens, depth),
        [SCALARS] + [WHOLE] * 11,
        2 * tokens * (depth * width + 10 * tokens * 256),
        2 * depth * width,
        [VMEM((width, tokens), F32), VMEM((8, tokens), F32)],
    )(info, starts, query, *keys, *values, weight)
    return attended, logsums, partial


def attend_back_kernel(info, starts, *refs):
    query, keys, values, attended, logsums, raw, grads = (refs[4 * n : 4 * n + 4] for n in range(7))
    w_out, w_in, cosine, sine, gains = refs[28:33]
    low = refs[33:37]
    partial = [refs[37:38], refs[38:39], refs[39:40], refs[40:42]]
    gain_grad = refs[42]
    pulled, deltas, grad_query, grad_keys, grad_values = refs[43:]
    width, tokens = query[0].shape
    heads = width // HD
    grad_query[...] = jnp.zeros_like(grad_query)
    grad_keys[...] = jnp.zeros_like(grad_keys)
    grad_values[...] = jnp.zeros_like(grad_values)
    deltas[...] = jnp.zeros_like(deltas)
    for at in range(4):
        grad = mul(w_out[...], grads[at][...], NT).astype(BF16)
        pulled[at] = grad
        product = grad.astype(F32) * attended[at][...].astype(F32)
        for head in range(heads):
            rows = slice(head * HD, head * HD + HD)
            deltas[at, head : head + 1] = jnp.sum(product[rows], axis=0, keepdims=True)
    for at in range(4):
        for other in range(4):

            @pl.when(near(info, at, other, tokens))
            def _():
                allowed = seen(info, at, other, starts[at : at + 1], tokens)
                for head in range(heads):
                    rows = slice(head * HD, head * HD + HD)
                    grad_rows, query_rows = pulled[at, rows], query[at][rows]
                    scores = mul(keys[other][rows], query_rows, TN) - logsums[at][head : head + 1]
                    shares = jnp.where(allowed, jnp.exp(scores), 0.0)
                    grad_shares = mul(values[other][rows], grad_rows, TN)
                    grad_scores = shares * (grad_shares - deltas[at, head : head + 1])
                    grad_scores = grad_scores.astype(BF16)
                    grad_values[other, rows] += mul(grad_rows, shares.astype(BF16), NT)
                    grad_keys[other, rows] += mul(query_rows, grad_scores, NT)
                    grad_query[at, rows] += mul(keys[other][rows], grad_scores)

    gain_total = [0.0] * heads
    for at in range(4):
        cos, sin = cosine[at], sine[at]
        for part, source, factor in ((0, grad_query, math.sqrt(HD)), (1, grad_keys, 1.0)):
            for head in range(heads):
                rows = slice(head * HD, head * HD + HD)
                turn = turned(raw[at][part * width + head * HD : part * width + head * HD + HD], cos, sin)
                scale = lax.rsqrt(jnp.sum(turn * turn, axis=0, keepdims=True) + NORM_EPSILON)
                unit = turn * scale
                grad = source[at, rows] * factor
                gain_total[head] = gain_total[head] + grad * unit
                grad = grad * gains[rows]
                grad = scale * (grad - unit * jnp.sum(unit * grad, axis=0, keepdims=True))
                low[at][part * width + head * HD : part * width + head * HD + HD] = turned_back(
                    grad, cos, sin
                ).astype(BF16)
        low[at][2 * width :] = grad_values[at].astype(BF16)
        share_out(partial[at], mul(low[at][...], w_in[...], TN))
    for head in range(heads):
        gain_grad[head * HD : head * HD + HD] = jnp.sum(gain_total[head], axis=1, keepdims=True)


def attend_back(info, starts, query, keys, values, attended, logsums, raw, grads,
                w_out, w_in, cosine, sine, gains):
    width, tokens = query[0].shape
    depth = w_out.shape[1]
    low = shape((3 * width, tokens), BF16)
    block = VMEM((4, width, tokens), F32)
    outs = call(
        attend_back_kernel,
        [low] * 4
        + [out for at in range(4) for out in partial_shapes(at, tokens, depth)]
        + [shape((width, 1), F32)],
        [SCALARS] + [WHOLE] * 34,
        2 * 4 * tokens * (depth * width * 4 + 60 * tokens * 256),
        2 * depth * width * 12,
        [VMEM((4, width, tokens), BF16), VMEM((4, 8, tokens), F32), block, block, block],
        limit=28,
    )(info, starts, *query, *keys, *values, *attended, *logsums, *raw, *grads,
      w_out, w_in, cosine, sine, gains)
    return outs[:4], [outs[4:5], outs[5:6], outs[6:7], outs[7:9]], outs[9]


CHUNK = 256
GATE_WIDTH = math.sqrt(1024)


def by_halves(own, other, work):
    steps = pl.num_programs(0) // 2
    pl.when(pl.program_id(0) < steps)(lambda: work(own))
    pl.when(pl.program_id(0) >= steps)(lambda: work(other))


def add_up(total, part):
    @pl.when(pl.program_id(0) == 0)
    def _():
        total[...] = part

    @pl.when(pl.program_id(0) > 0)
    def _():
        total[...] += part


def feed_kernel(x, own, other, scales, ups, gates, gated, *refs):
    partial, total = refs[:-1], refs[-1]

    def work(weights):
        up, gate = mul(x[...], weights[0], NT), mul(x[...], weights[1], NT)
        ups[...] = up.astype(BF16)
        gates[...] = gate.astype(BF16)
        z = gate * (scales[1:2] * GATE_WIDTH)
        mixed = (up * scales[0:1] * (z * (0.5 + 0.5 * jnp.tanh(0.5 * z)))).astype(BF16)
        gated[...] = mixed
        add_up(total, mul(mixed, weights[2]))

    by_halves(own, other, work)

    @pl.when(pl.program_id(0) == pl.num_programs(0) - 1)
    def _():
        share_out(partial, total[...])


def feed_back_kernel(g, own, other, scales, ups, gates, low_up, low_gate, scale_grad, *refs):
    partial, total = refs[:-1], refs[-1]

    def work(weights):
        grad = mul(g[...], weights[2], NT)
        up, gate = ups[...].astype(F32), gates[...].astype(F32)
        s_up, s_gate = scales[0:1], scales[1:2] * GATE_WIDTH
        z = gate * s_gate
        sigmoid = 0.5 + 0.5 * jnp.tanh(0.5 * z)
        silu = z * sigmoid
        grad_silu = grad * silu
        grad_z = grad * (up * s_up) * (sigmoid + silu * (1.0 - sigmoid))
        grad_up, grad_gate = (grad_silu * s_up).astype(BF16), (grad_z * s_gate).astype(BF16)
        low_up[...] = grad_up
        low_gate[...] = grad_gate
        scale_grad[0:1] = jnp.sum(grad_silu * up, axis=0, keepdims=True)
        scale_grad[1:2] = jnp.sum(grad_z * gate, axis=0, keepdims=True) * GATE_WIDTH
        add_up(total, mul(grad_up, weights[0]) + mul(grad_gate, weights[1]))

    by_halves(own, other, work)

    @pl.when(pl.program_id(0) == pl.num_programs(0) - 1)
    def _():
        share_out(partial, total[...])


def feed_call(body, at, x, weights, scales, kept_in, kept_out, pair_out):
    tokens, depth = x.shape
    half = weights[0].shape[1]
    chunk = min(CHUNK, half)
    steps = half // chunk
    kept = pl.BlockSpec((tokens, chunk), lambda i: (0, i))
    pair = pl.BlockSpec((2, chunk), lambda i: (0, i))
    partial = partial_shapes(at, tokens, depth)
    outs = call(
        body,
        [shape((tokens, 2 * half), BF16)] * kept_out
        + [shape((2, 2 * half), F32)] * pair_out
        + partial,
        [
            pl.BlockSpec((tokens, depth), lambda i: (0, 0)),
            pl.BlockSpec((3, chunk, depth), lambda i: (0, jnp.minimum(i, steps - 1), 0)),
            pl.BlockSpec((3, chunk, depth), lambda i: (0, jnp.maximum(i - steps, 0), 0)),
            pair,
        ]
        + [kept] * len(kept_in),
        2 * 6 * tokens * depth * half,
        2 * 6 * depth * half,
        [VMEM((tokens, depth), F32)],
        limit=20,
        grid=(2 * steps,),
        out_specs=[kept] * kept_out
        + [pair] * pair_out
        + [pl.BlockSpec(out.shape, lambda i: (0, 0)) for out in partial],
    )(x, *weights, scales, *kept_in)
    return [*outs[: kept_out + pair_out], outs[kept_out + pair_out :]]


def feed_block(at, x, weights, scales):
    return feed_call(feed_kernel, at, x, weights, scales, (), 3, 0)


def feed_back_block(at, g, weights, scales, ups, gates):
    return feed_call(feed_back_kernel, at, g, weights, scales, (ups, gates), 2, 1)


def add_parts(parts):
    total = parts[0][...].astype(F32)
    for part in parts[1:]:
        total = total + part[...].astype(F32)
    return total


def mix_kernel(count, hidden, rate, *refs):
    branch_out, result, result_low = refs[count:]
    branch = add_parts(refs[:count])
    branch_out[...] = branch
    mixed = mix_residual(hidden[...].astype(F32), branch, rate[...])
    result[...] = mixed
    result_low[...] = mixed.astype(BF16)


def mix_block(hidden, rate, parts):
    dims = hidden.shape
    return call(
        functools.partial(mix_kernel, len(parts)),
        [shape(dims, F32), shape(dims, F32), shape(dims, BF16)],
        [WHOLE] * (2 + len(parts)),
        10 * dims[0] * dims[1],
        8 * dims[0] * dims[1],
    )(hidden, rate, *parts)


def mix_back_kernel(count, rounded, hidden, branch, rate, *refs):
    grad_hidden, grad_branch, grad_rate = refs[count:]
    upstream = add_parts(refs[:count])
    if rounded:
        upstream = upstream.astype(BF16).astype(F32)
    h, b, r = hidden[...].astype(F32), branch[...], rate[...]
    scale = lax.rsqrt(jnp.sum(b * b, axis=-1, keepdims=True) + NORM_EPSILON)
    unit = b * scale
    apart = unit - h
    mixed = h + r * apart
    mixed_scale = lax.rsqrt(jnp.sum(mixed * mixed, axis=-1, keepdims=True) + NORM_EPSILON)
    mixed = mixed * mixed_scale
    grad = mixed_scale * (upstream - mixed * jnp.sum(mixed * upstream, axis=-1, keepdims=True))
    grad_rate[...] = jnp.sum(grad * apart, axis=0, keepdims=True)
    grad_unit = grad * r
    grad_hidden[...] = grad - grad_unit
    grad_unit = scale * (grad_unit - unit * jnp.sum(unit * grad_unit, axis=-1, keepdims=True))
    grad_branch[...] = grad_unit.astype(BF16)


def mix_back_block(hidden, branch, rate, parts, rounded=False):
    dims = hidden.shape
    return call(
        functools.partial(mix_back_kernel, len(parts), rounded),
        [shape(dims, F32), shape(dims, BF16), shape((1, dims[1]), F32)],
        [WHOLE] * (3 + len(parts)),
        20 * dims[0] * dims[1],
        12 * dims[0] * dims[1],
    )(hidden, branch, rate, *parts)


def dot(left, right):
    return jnp.dot(left, right, preferred_element_type=F32)


def dot_tn(left, right):
    return lax.dot_general(left, right, TN, preferred_element_type=F32)


def join(blocks, axis=0):
    return jnp.concatenate(blocks, axis=axis)


def tie(*values):
    return lax.optimization_barrier(values)


def to_neighbours(block):
    return exchange(block, "mp", 1), exchange(block, "mp", 2)


def pass_halves(first, second):
    half = first.shape[0] // 2
    return exchange(second[:half], "mp", 1), exchange(first[half:], "mp", 2)


def send_far(partial):
    return exchange(partial[0], "mp", 1), exchange(partial[1], "mp", 2)


def send_near(partial_first, partial_second, upper, lower):
    half = upper.shape[0]
    zero = jnp.zeros((), F32)
    first = partial_first + lax.pad(lower.astype(F32), zero, ((half, 0, 0), (0, 0, 0)))
    second = partial_second + lax.pad(upper.astype(F32), zero, ((0, half, 0), (0, 0, 0)))
    return exchange(first.astype(BF16), "mp", 1), exchange(second.astype(BF16), "mp", 2)


def feed_exchange(block, work):
    first, second = to_neighbours(block)
    done = [None] * 4
    done[0] = work(0, block)
    first, second, done[0] = tie(first, second, done[0])
    upper, lower = pass_halves(first, second)
    done[1] = work(1, first)
    upper, lower, done[1] = tie(upper, lower, done[1])
    far = join([upper, lower])
    done[3] = work(3, far)
    upper, lower = send_far(done[3][-1])
    done[2] = work(2, second)
    upper, lower, done[2] = tie(upper, lower, done[2])
    from_first, from_second = send_near(done[1][-1][0], done[2][-1][0], upper, lower)
    return [block, first, second, far], done, (done[0][-1][0], from_first, from_second)


def layer_forward(hidden, low, params, tables, tied):
    attend_in, attend_out, feed_weights, gains, scales, mixing = params
    cosine, sine, starts, info = tables
    project = lambda at, block: project_block(block, attend_in, cosine[at], sine[at], gains)
    heads = [None] * 4
    first, second = to_neighbours(low)
    if tied:
        heads[0] = project(0, low)
        first, second, heads[0] = tie(first, second, heads[0])
    upper, lower = pass_halves(first, second)
    if tied:
        heads[1], heads[2] = project(1, first), project(2, second)
        upper, lower, heads[1], heads[2] = tie(upper, lower, heads[1], heads[2])
    else:
        heads[0], heads[1], heads[2] = project(0, low), project(1, first), project(2, second)
    far = join([upper, lower])
    heads[3] = project(3, far)
    raw, query, keys, values = zip(*heads)
    attend = lambda at: attend_block(
        at, info, starts[at : at + 1], query[at], keys, values, attend_out
    )
    attended = [None] * 4
    attended[3] = attend(3)
    upper, lower = send_far(attended[3][-1])
    attended[1], attended[2] = attend(1), attend(2)
    upper, lower, attended[1], attended[2] = tie(upper, lower, attended[1], attended[2])
    from_first, from_second = send_near(attended[1][-1][0], attended[2][-1][0], upper, lower)
    attended[0] = attend(0)
    from_first, from_second, attended[0] = tie(from_first, from_second, attended[0])
    branch, middle, middle_low = mix_block(
        hidden, mixing[:1], (attended[0][-1][0], from_first, from_second)
    )
    work = lambda at, block: feed_block(at, block, feed_weights, scales)
    middle_blocks, fed, parts = feed_exchange(middle_low, work)
    mixed, result, result_low = mix_block(middle, mixing[1:], parts)
    ups, gates, gated, _ = zip(*fed)
    attended, logsums, _ = zip(*attended)
    stored = (
        (hidden, branch, [low, first, second, far], raw, query, keys, values, attended, logsums),
        (middle, mixed, middle_blocks, ups, gates, gated),
    )
    return result, result_low, stored


def columns(blocks, start, stop):
    return join([block[:, start:stop] for block in blocks])


def layer_backward(stored, upstream, rounded, params, tables):
    attend_in, attend_out, feed_weights, gains, scales, mixing = params
    cosine, sine, starts, info = tables
    attend_stored, (middle, mixed, middle_blocks, ups, gates, gated) = stored
    hidden, branch, hidden_blocks, raw, query, keys, values, attended, logsums = attend_stored
    half = feed_weights[0].shape[1]
    grad_middle, grad_mixed, rate_two = mix_back_block(
        middle, mixed, mixing[1:], upstream, rounded
    )
    work = lambda at, block: feed_back_block(at, block, feed_weights, scales, ups[at], gates[at])
    mixed_blocks, done, parts = feed_exchange(grad_mixed, work)
    low_ups, low_gates, scale_grads, _ = zip(*done)
    middle_all, mixed_all = join(middle_blocks), join(mixed_blocks)

    def feed_grads(start, stop):
        return jnp.stack([
            dot_tn(columns(low_ups, start, stop), middle_all),
            dot_tn(columns(low_gates, start, stop), middle_all),
            dot_tn(columns(gated, start, stop), mixed_all),
        ])

    other = feed_grads(half, 2 * half).astype(BF16)
    own, from_first, from_second, other = tie(*parts, other)
    grad_hidden, grad_branch, rate_one = mix_back_block(
        hidden, branch, mixing[:1], (grad_middle, own, from_first, from_second)
    )
    first, second = to_neighbours(grad_branch)
    feed_sums = feed_grads(0, half)
    other, first, second, feed_sums = tie(exchange(other, "section", 1), first, second, feed_sums)
    upper, lower = pass_halves(first, second)
    feed_sums = (feed_sums + other.astype(F32)).astype(BF16)
    upper, lower, feed_sums = tie(upper, lower, feed_sums)
    grads = [grad_branch, first, second, join([upper, lower])]
    low, partial, gain_grad = attend_back(
        info, starts, query, keys, values, attended, logsums, raw, grads,
        attend_out, attend_in, cosine, sine, gains,
    )
    upper, lower = send_far(partial[3])
    attend_grads = [dot(join(low, 1), join(hidden_blocks)), dot(join(attended, 1), join(grads))]
    upper, lower, attend_grads = tie(upper, lower, attend_grads)
    from_first, from_second = send_near(partial[1][0], partial[2][0], upper, lower)
    attend_grads = join(attend_grads).reshape(4, -1, hidden.shape[1])
    parts = (grad_hidden, partial[0][0], from_first, from_second)
    return parts, feed_sums, attend_grads, (gain_grad[:, 0], sum(scale_grads), rate_one[0], rate_two[0])


def adam_update(weight, first, second, gradient, factor, renorm, rate):
    clipped = gradient * factor
    first_new = BETA_FIRST * first + (1.0 - BETA_FIRST) * clipped
    second_new = BETA_SECOND * second + (1.0 - BETA_SECOND) * clipped * clipped
    first_hat = first_new / (1.0 - BETA_FIRST**STEP)
    second_hat = second_new / (1.0 - BETA_SECOND**STEP)
    moved = weight - rate * first_hat / (jnp.sqrt(second_hat) + ADAM_EPSILON)
    if renorm:
        moved = moved * lax.rsqrt(jnp.sum(moved * moved, axis=2, keepdims=True) + NORM_EPSILON)
    return (first_new, second_new, moved)


def per_device(
    inputs,
    cotangent,
    doc_ids,
    attention_in,
    attention_out,
    feedforward_in,
    feedforward_out,
    unit_scales,
    mix_rates,
    first_attention_in,
    second_attention_in,
    first_attention_out,
    second_attention_out,
    first_feedforward_in,
    second_feedforward_in,
    first_feedforward_out,
    second_feedforward_out,
    first_unit_scales,
    second_unit_scales,
    first_mix_rates,
    second_mix_rates,
):
    section = lax.axis_index("section")
    is_first = section == 0
    dp_index = lax.axis_index("dp")
    dp_size = lax.axis_size("dp")
    local_rows = inputs.shape[1]

    def ordered(own, other):
        return jnp.where(is_first, own, other), jnp.where(is_first, other, own)

    def halves(array, dim):
        width = array.shape[dim] // 2
        own = lax.dynamic_slice_in_dim(array, section * width, width, dim)
        other = lax.dynamic_slice_in_dim(array, (1 - section) * width, width, dim)
        return own, other

    hidden_low = lax.dynamic_index_in_dim(inputs, section, 0, False)

    attend_rows = jnp.concatenate(
        [jnp.swapaxes(attention_in[0], 1, 2), attention_out], axis=0
    ).astype(BF16)
    small = jnp.concatenate([unit_scales.reshape(-1), mix_rates.reshape(-1)]).astype(BF16)
    feed_rows = jnp.concatenate(
        [jnp.swapaxes(feedforward_in[0].astype(BF16), 1, 2), feedforward_out.astype(BF16)], axis=0
    )

    def gather_ring(half):
        blocks = spread_rows(half, "dp")
        count = half.shape[1]
        whole = jnp.zeros((half.shape[0], dp_size * count, half.shape[2]), BF16)
        for source, block in zip(ring_sources("dp"), blocks):
            whole = lax.dynamic_update_slice_in_dim(whole, block, source * count, 1)
        return whole, blocks[-2]

    own, other = halves(attend_rows, 2)
    attend_pieces = ordered(own, exchange(other, "section", 1))
    own, other = halves(feed_rows, 1)
    feed_pieces = ordered(own, exchange(other, "section", 1))
    if dp_size <= 4:
        attend_first, step = gather_ring(attend_pieces[0])
        attend_second, *feed_pieces, _ = tie(attend_pieces[1], *feed_pieces, step)
    else:
        attend_first = lax.all_gather(attend_pieces[0], "dp", axis=1, tiled=True)
        attend_second = attend_pieces[1]
    attend_pieces = (attend_first, lax.all_gather(attend_second, "dp", axis=1, tiled=True))
    small = jnp.stack(ordered(small, exchange(small, "section", 1))).reshape(-1)
    small = gather_small(small, "dp").astype(F32)
    small = small.reshape(dp_size, 2, -1)
    units_here = unit_scales.shape[2]

    def units_apart(values):
        parts = values.reshape(dp_size, 2, -1)
        own, other = ordered(parts[:, 0], parts[:, 1])
        return jnp.concatenate([own.reshape(-1), other.reshape(-1)])

    def units_back(values):
        parts = values.reshape(2, dp_size, -1)
        own, other = ordered(parts[0], parts[1])
        return jnp.stack([own, other], axis=1).reshape(-1)

    layers = []
    for layer in range(2):
        own = attend_pieces[layer]
        attend = jnp.concatenate(ordered(own, exchange(own, "section", 1)), axis=2)
        own = lax.all_gather(feed_pieces[layer], "dp", axis=1, tiled=True)
        feed_weights = (own, exchange(own, "section", 1))
        units = small[:, layer, :units_here].reshape(-1)
        mixing = small[:, layer, units_here:].reshape(dp_size, 2, -1)
        mixing = jnp.swapaxes(mixing, 0, 1).reshape(2, -1)
        width_qk, width_ff = attend.shape[1], 2 * own.shape[1]
        layers.append((
            attend[:3].reshape(3 * width_qk, -1), attend[3], feed_weights,
            units[:width_qk, None],
            jnp.stack([
                units_apart(units[width_qk : width_qk + width_ff]),
                units_apart(units[width_qk + width_ff :]),
            ]),
            mixing,
        ))

    doc_row = lax.dynamic_index_in_dim(doc_ids, section, 0, False)
    starts_all = document_starts(doc_row)
    mp_index = lax.axis_index("mp")
    sources = [mp_index ^ offset for offset in range(4)]
    places = jnp.arange(local_rows, dtype=jnp.int32)
    starts = jnp.stack([
        lax.dynamic_slice_in_dim(starts_all, source * local_rows, local_rows, 0)
        for source in sources
    ])
    sources = jnp.stack(sources).astype(jnp.int32)
    cosine, sine = rope_tables(sources[:, None] * local_rows + places - starts)
    info = jnp.concatenate([sources, starts[:, 0]])
    tables = (cosine, sine, starts, info)

    def pair_attend(rows):
        own, other = halves(rows, 2)
        return (own + exchange(other.astype(BF16), "section", 1).astype(F32)).astype(BF16)

    def scatter(sums):
        return lax.psum_scatter(sums, "dp", scatter_dimension=1, tiled=True)

    def scatter_ring(sums):
        if dp_size > 4:
            return scatter(sums)
        count = sums.shape[1] // dp_size
        parts = [
            lax.dynamic_slice_in_dim(sums, source * count, count, 1).astype(F32)
            for source in ring_sources("dp")
        ]
        return collect_rows(parts, "dp").astype(BF16)

    first, second = layers
    grad = lax.dynamic_index_in_dim(cotangent, section, 0, False)
    _, hidden_second, stored_first = layer_forward(hidden_low, hidden_low, first, tables, False)
    result, _, stored_second = layer_forward(hidden_second, hidden_second, second, tables, True)

    parts, feed_second, attend_second, small_second = layer_backward(
        stored_second, (grad,), False, second, tables
    )
    feed_second = scatter(feed_second)
    *parts, attend_second = tie(*parts, pair_attend(attend_second))
    attend_second = scatter(attend_second)
    parts, feed_first, attend_first, small_first = layer_backward(
        stored_first, parts, True, first, tables
    )
    feed_first = scatter(feed_first)
    attend_first, feed_second, attend_second = tie(
        pair_attend(attend_first), feed_second, attend_second
    )
    attend_first = scatter_ring(attend_first)
    grad = sum(part.astype(F32) for part in parts)

    reduced_first = (attend_first, feed_first)
    reduced_second = (attend_second, feed_second)
    squares = sum(
        jnp.sum(jnp.square(part.astype(F32))) for part in (*reduced_first, *reduced_second)
    )
    gradients = []
    for one, two, dim in zip(reduced_first, reduced_second, (2, 1)):
        own, other = jnp.where(is_first, one, two), jnp.where(is_first, two, one)
        other = exchange(other, "section", 1)
        gradients.append(jnp.concatenate(ordered(own, other), axis=dim).astype(F32))

    def small_sums(gains, scales, rate, rate_two):
        return jnp.concatenate([gains, units_back(scales[0]), units_back(scales[1]), rate, rate_two])

    small_first = small_sums(*small_first)
    small_second = small_sums(*small_second)
    own = jnp.where(is_first, small_first, small_second)
    other = jnp.where(is_first, small_second, small_first)
    sums = sum_over(own + exchange(other, "section", 1), "dp")
    count = units_here * dp_size
    unit_grads = lax.dynamic_slice_in_dim(sums[:count], dp_index * units_here, units_here, 0)
    unit_grads = unit_grads[None, None]
    rate_sums = sum_over(sums[count:].reshape(2, -1), "mp")
    rates_here = mix_rates.shape[2]
    rate_grads = lax.dynamic_slice_in_dim(rate_sums, dp_index * rates_here, rates_here, 1)[None]

    leading = (mp_index == 0).astype(F32)
    squares = squares + jnp.sum(unit_grads * unit_grads)
    squares = squares + leading * jnp.sum(rate_grads * rate_grads)
    squares = squares.reshape(1)
    squares = squares + exchange(squares, "section", 1)
    squares = sum_over(sum_over(squares, "mp"), "dp")
    gradient_norm = jnp.sqrt(squares[0])
    factor = CLIP_NORM / jnp.maximum(gradient_norm, CLIP_NORM)

    to_send = jnp.where(is_first, result, grad)
    kept = jnp.where(is_first, grad, result)
    arrived = exchange(to_send, "section", 1)
    boundary_states = jnp.stack(ordered(kept, arrived))[None]

    attend_grad, feed_grad = gradients
    updates = []
    for weight, moment, square, gradient in (
        (attention_in, first_attention_in, second_attention_in,
         jnp.swapaxes(attend_grad[:3], 1, 2)[None]),
        (attention_out, first_attention_out, second_attention_out, attend_grad[3:]),
        (feedforward_in, first_feedforward_in, second_feedforward_in,
         jnp.swapaxes(feed_grad[:2], 1, 2)[None]),
        (feedforward_out, first_feedforward_out, second_feedforward_out, feed_grad[2:]),
    ):
        updates.extend(adam_update(weight, moment, square, gradient, factor, True, LEARN_RATE))
    updates.extend(
        adam_update(
            unit_scales, first_unit_scales, second_unit_scales, unit_grads, factor, False, SCALE_RATE
        )
    )
    updates.extend(
        adam_update(
            mix_rates, first_mix_rates, second_mix_rates, rate_grads, factor, False, MIXING_RATE
        )
    )
    return (boundary_states, gradient_norm, *updates)


def solution(mesh):
    in_specs = (
        P("dp", "mp", None),
        P("dp", "mp", None),
        P("dp", None),
        P("section", None, None, ("mp", "dp")),
        P("section", ("mp", "dp"), None),
        P("section", None, None, ("mp", "dp")),
        P("section", ("mp", "dp"), None),
        P("section", "mp", "dp"),
        P("section", None, "dp"),
        P("section", None, None, ("mp", "dp")),
        P("section", None, None, ("mp", "dp")),
        P("section", ("mp", "dp"), None),
        P("section", ("mp", "dp"), None),
        P("section", None, None, ("mp", "dp")),
        P("section", None, None, ("mp", "dp")),
        P("section", ("mp", "dp"), None),
        P("section", ("mp", "dp"), None),
        P("section", "mp", "dp"),
        P("section", "mp", "dp"),
        P("section", None, "dp"),
        P("section", None, "dp"),
    )
    out_specs = (
        P("section", "dp", "mp", None),
        P(),
        P("section", None, None, ("mp", "dp")),
        P("section", None, None, ("mp", "dp")),
        P("section", None, None, ("mp", "dp")),
        P("section", ("mp", "dp"), None),
        P("section", ("mp", "dp"), None),
        P("section", ("mp", "dp"), None),
        P("section", None, None, ("mp", "dp")),
        P("section", None, None, ("mp", "dp")),
        P("section", None, None, ("mp", "dp")),
        P("section", ("mp", "dp"), None),
        P("section", ("mp", "dp"), None),
        P("section", ("mp", "dp"), None),
        P("section", "mp", "dp"),
        P("section", "mp", "dp"),
        P("section", "mp", "dp"),
        P("section", None, "dp"),
        P("section", None, "dp"),
        P("section", None, "dp"),
    )
    return jax.shard_map(
        per_device, mesh=mesh, in_specs=in_specs, out_specs=out_specs, check_vma=False
    )
```

```python
import functools
import math

import jax
import jax.numpy as jnp
from jax import lax
from jax.experimental import pallas as pl
from jax.experimental.pallas import tpu as pltpu
from jax.sharding import PartitionSpec as P

HD = 64
STEP = 10

NORM_EPSILON = 1e-06
ROPE_BASE = 10000.0
CLIP_NORM = 0.1
LEARN_RATE = 0.05
SCALE_RATE = 1.25
MIXING_RATE = 0.4
BETA_FIRST = 0.9
BETA_SECOND = 0.95
ADAM_EPSILON = 1e-08

BF16 = jnp.bfloat16
F32 = jnp.float32


def exchange(block, axis, bit):
    route = [(i, i ^ bit) for i in range(lax.axis_size(axis))]
    return lax.ppermute(block, axis, route)


def gray(place):
    return place ^ (place >> 1)


def ring_place(index, size):
    shift = 1
    while shift < size:
        index = index ^ (index >> shift)
        shift *= 2
    return index


def ring_step(block, axis):
    size = lax.axis_size(axis)
    route = []
    for place in range(size):
        route.append((gray(place), gray((place + 1) % size)))
        route.append((size + gray(place), size + gray((place - 1) % size)))
    return lax.ppermute(block, ("section", axis), route)


def ring_sources(axis):
    size = lax.axis_size(axis)
    place = ring_place(lax.axis_index(axis), size)
    way = 1 - 2 * lax.axis_index("section")
    return [gray((place - way * step + size) % size) for step in range(size)]


def spread_rows(block, axis="mp"):
    blocks = [block]
    for _ in range(lax.axis_size(axis) - 1):
        blocks.append(ring_step(blocks[-1], axis))
    return blocks


def collect_rows(parts, axis="mp"):
    moving = parts[1]
    for part in parts[2:] + parts[:1]:
        moving = ring_step(moving.astype(BF16), axis).astype(F32) + part
    return moving


def sum_over(values, axis):
    bit = 1
    while bit < lax.axis_size(axis):
        values = values + exchange(values, axis, bit)
        bit *= 2
    return values


def gather_small(values, axis):
    index = lax.axis_index(axis)
    gathered = values[None]
    bit = 1
    while bit < lax.axis_size(axis):
        other = exchange(gathered, axis, bit)
        low = (index & bit) == 0
        gathered = jnp.concatenate(
            [jnp.where(low, gathered, other), jnp.where(low, other, gathered)], axis=0
        )
        bit *= 2
    return gathered


def unit_norm(values):
    return values * lax.rsqrt(jnp.sum(values * values, axis=-1, keepdims=True) + NORM_EPSILON)


def document_starts(doc_row):
    position = jnp.arange(doc_row.shape[-1], dtype=jnp.int32)
    change = jnp.concatenate([jnp.ones((1,), dtype=jnp.bool_), doc_row[1:] != doc_row[:-1]])
    return lax.cummax(jnp.where(change, position, 0), axis=0)


def rope_tables(offsets):
    half_width = HD // 2
    inverse = 1.0 / ROPE_BASE ** (jnp.arange(half_width, dtype=F32) * (2.0 / HD))
    angles = inverse[:, None] * offsets.astype(F32)[..., None, :]
    angles = jnp.concatenate([angles, angles], axis=-2)
    return jnp.cos(angles), jnp.sin(angles)


def mix_residual(hidden, branch, mixing):
    return unit_norm(hidden + mixing * (unit_norm(branch) - hidden))


NT = (((1,), (1,)), ((), ()))
TN = (((0,), (0,)), ((), ()))
NN = (((1,), (0,)), ((), ()))
VMEM = pltpu.VMEM
WHOLE = pl.BlockSpec(memory_space=pltpu.VMEM)
SCALARS = pl.BlockSpec(memory_space=pltpu.SMEM)


def mul(left, right, dims=NN):
    return lax.dot_general(left, right, dims, preferred_element_type=F32)


def call(body, out_shape, in_specs, flops, moved, scratch=(), limit=50, **more):
    if "grid" not in more:
        more["out_specs"] = [WHOLE] * len(out_shape)
    return pl.pallas_call(
        body,
        out_shape=out_shape,
        in_specs=in_specs,
        scratch_shapes=list(scratch),
        compiler_params=pltpu.CompilerParams(vmem_limit_bytes=limit << 20),
        cost_estimate=pl.CostEstimate(flops=flops, bytes_accessed=moved, transcendentals=0),
        **more,
    )


def shape(dims, dtype):
    return jax.ShapeDtypeStruct(dims, dtype)


def flat(blocks):
    return [part for block in blocks for part in block]


def turned(raw, cosine, sine):
    half = HD // 2
    first, second = raw[:half], raw[half:]
    return jnp.concatenate(
        [
            first * cosine[:half] - second * sine[:half],
            second * cosine[half:] + first * sine[half:],
        ],
        axis=0,
    )


def turned_back(grad, cosine, sine):
    half = HD // 2
    first, second = grad[:half], grad[half:]
    return jnp.concatenate(
        [
            first * cosine[:half] + second * sine[half:],
            second * cosine[half:] - first * sine[:half],
        ],
        axis=0,
    )


def rows_of(refs):
    return refs[0][...] if len(refs) == 1 else jnp.concatenate([ref[...] for ref in refs], axis=0)


def project_kernel(count, *refs):
    weight, cosine, sine, gains, raw_out, query, keys, values = refs[count:]
    width = query.shape[0]
    raw = mul(weight[...], rows_of(refs[:count]), NT)
    raw_out[...] = raw[: 2 * width]
    values[...] = raw[2 * width :].astype(BF16)
    for part, out in ((0, query), (1, keys)):
        for top in range(0, width, HD):
            turn = turned(raw[part * width + top : part * width + top + HD], cosine[...], sine[...])
            scale = lax.rsqrt(jnp.sum(turn * turn, axis=0, keepdims=True) + NORM_EPSILON)
            head = (turn * scale * gains[top : top + HD]).astype(BF16)
            out[top : top + HD] = head * math.sqrt(HD) if part == 0 else head


def project_block(x, weight, cosine, sine, gains):
    tokens, depth = cosine.shape[1], weight.shape[1]
    width = weight.shape[0] // 3
    low = shape((width, tokens), BF16)
    return call(
        functools.partial(project_kernel, len(x)),
        [shape((2 * width, tokens), F32), low, low, low],
        [WHOLE] * (4 + len(x)),
        2 * tokens * depth * 3 * width,
        2 * 3 * width * depth,
    )(*x, weight, cosine, sine, gains)


def near(info, at, other, tokens):
    return (info[other] <= info[at]) & ((info[other] + 1) * tokens > info[4 + at])


def seen(info, at, other, starts, tokens):
    key_place = info[other] * tokens + lax.broadcasted_iota(jnp.int32, (tokens, tokens), 0)
    query_place = info[at] * tokens + lax.broadcasted_iota(jnp.int32, (tokens, tokens), 1)
    return (key_place <= query_place) & (key_place >= starts)


def share_out(partial, value):
    if len(partial) == 1:
        partial[0][...] = value
    else:
        half = value.shape[0] // 2
        partial[0][...] = value[:half].astype(BF16)
        partial[1][...] = value[half:].astype(BF16)


def partial_shapes(at, tokens, depth):
    if at == 3:
        return [shape((tokens // 2, depth), BF16)] * 2
    return [shape((tokens, depth), F32)]


def attend_kernel(at, info, starts, query, k0, k1, k2, k3, v0, v1, v2, v3, weight, *refs):
    attended, logsums, *partial = refs[:-2]
    total, sums = refs[-2:]
    width, tokens = query.shape
    total[...] = jnp.zeros_like(total)
    sums[...] = jnp.ones_like(sums)
    sums[: width // HD] = jnp.zeros((width // HD, tokens), F32)
    for other, (keys, values) in enumerate(((k0, v0), (k1, v1), (k2, v2), (k3, v3))):

        @pl.when(near(info, at, other, tokens))
        def _():
            allowed = seen(info, at, other, starts[...], tokens)
            for head in range(width // HD):
                rows = slice(head * HD, head * HD + HD)
                shares = jnp.exp(mul(keys[rows], query[rows], TN))
                shares = jnp.where(allowed, shares, 0.0)
                sums[head : head + 1] += jnp.sum(shares, axis=0, keepdims=True)
                total[rows] += mul(values[rows], shares.astype(BF16))

    logsums[...] = jnp.log(sums[...])
    inverse = 1.0 / sums[...]
    for head in range(width // HD):
        rows = slice(head * HD, head * HD + HD)
        attended[rows] = (total[rows] * inverse[head : head + 1]).astype(BF16)
    share_out(partial, mul(attended[...], weight[...], TN))


def attend_block(at, info, starts, query, keys, values, weight):
    width, tokens = query.shape
    depth = weight.shape[1]
    attended, logsums, *partial = call(
        functools.partial(attend_kernel, at),
        [shape((width, tokens), BF16), shape((8, tokens), F32)] + partial_shapes(at, tokens, depth),
        [SCALARS] + [WHOLE] * 11,
        2 * tokens * (depth * width + 10 * tokens * 256),
        2 * depth * width,
        [VMEM((width, tokens), F32), VMEM((8, tokens), F32)],
    )(info, starts, query, *keys, *values, weight)
    return attended, logsums, partial


def attend_back_kernel(info, starts, *refs):
    query, keys, values, attended, logsums, raw = (refs[4 * n : 4 * n + 4] for n in range(6))
    grads = (refs[24:25], refs[25:26], refs[26:27], refs[27:29])
    w_out, w_in, cosine, sine, gains = refs[29:34]
    low = refs[34:38]
    partial = [refs[38:39], refs[39:40], refs[40:41], refs[41:43]]
    gain_grad = refs[43]
    pulled, deltas, grad_query, grad_keys, grad_values = refs[44:]
    width, tokens = query[0].shape
    heads = width // HD
    grad_query[...] = jnp.zeros_like(grad_query)
    grad_keys[...] = jnp.zeros_like(grad_keys)
    grad_values[...] = jnp.zeros_like(grad_values)
    deltas[...] = jnp.zeros_like(deltas)
    for at in range(4):
        grad = mul(w_out[...], rows_of(grads[at]), NT).astype(BF16)
        pulled[at] = grad
        product = grad.astype(F32) * attended[at][...].astype(F32)
        for head in range(heads):
            rows = slice(head * HD, head * HD + HD)
            deltas[at, head : head + 1] = jnp.sum(product[rows], axis=0, keepdims=True)
    for at in range(4):
        for other in range(4):

            @pl.when(near(info, at, other, tokens))
            def _():
                allowed = seen(info, at, other, starts[at : at + 1], tokens)
                for head in range(heads):
                    rows = slice(head * HD, head * HD + HD)
                    grad_rows, query_rows = pulled[at, rows], query[at][rows]
                    scores = mul(keys[other][rows], query_rows, TN) - logsums[at][head : head + 1]
                    shares = jnp.where(allowed, jnp.exp(scores), 0.0)
                    grad_shares = mul(values[other][rows], grad_rows, TN)
                    grad_scores = shares * (grad_shares - deltas[at, head : head + 1])
                    grad_scores = grad_scores.astype(BF16)
                    grad_values[other, rows] += mul(grad_rows, shares.astype(BF16), NT)
                    grad_keys[other, rows] += mul(query_rows, grad_scores, NT)
                    grad_query[at, rows] += mul(keys[other][rows], grad_scores)

    gain_total = [0.0] * heads
    for at in range(4):
        cos, sin = cosine[at], sine[at]
        for part, source, factor in ((0, grad_query, math.sqrt(HD)), (1, grad_keys, 1.0)):
            for head in range(heads):
                rows = slice(head * HD, head * HD + HD)
                turn = turned(raw[at][part * width + head * HD : part * width + head * HD + HD], cos, sin)
                scale = lax.rsqrt(jnp.sum(turn * turn, axis=0, keepdims=True) + NORM_EPSILON)
                unit = turn * scale
                grad = source[at, rows] * factor
                gain_total[head] = gain_total[head] + grad * unit
                grad = grad * gains[rows]
                grad = scale * (grad - unit * jnp.sum(unit * grad, axis=0, keepdims=True))
                low[at][part * width + head * HD : part * width + head * HD + HD] = turned_back(
                    grad, cos, sin
                ).astype(BF16)
        low[at][2 * width :] = grad_values[at].astype(BF16)
        share_out(partial[at], mul(low[at][...], w_in[...], TN))
    for head in range(heads):
        gain_grad[head * HD : head * HD + HD] = jnp.sum(gain_total[head], axis=1, keepdims=True)


def attend_back(info, starts, query, keys, values, attended, logsums, raw, grads,
                w_out, w_in, cosine, sine, gains):
    width, tokens = query[0].shape
    depth = w_out.shape[1]
    low = shape((3 * width, tokens), BF16)
    block = VMEM((4, width, tokens), F32)
    outs = call(
        attend_back_kernel,
        [low] * 4
        + [out for at in range(4) for out in partial_shapes(at, tokens, depth)]
        + [shape((width, 1), F32)],
        [SCALARS] + [WHOLE] * 35,
        2 * 4 * tokens * (depth * width * 4 + 60 * tokens * 256),
        2 * depth * width * 12,
        [VMEM((4, width, tokens), BF16), VMEM((4, 8, tokens), F32), block, block, block],
    )(info, starts, *query, *keys, *values, *attended, *logsums, *raw, *flat(grads),
      w_out, w_in, cosine, sine, gains)
    return outs[:4], [outs[4:5], outs[5:6], outs[6:7], outs[7:9]], outs[9]


CHUNK = 256
GATE_WIDTH = math.sqrt(1024)


def fetch_weights(own, other, weights, arrived):
    half = own.shape[1]
    copies = []
    for index, source in enumerate((own, other)):
        for at, start in enumerate(range(0, half, min(CHUNK, half))):
            rows = pl.ds(start, min(CHUNK, half))
            copy = pltpu.make_async_copy(
                source.at[:, rows], weights.at[index, :, rows], arrived.at[index, at]
            )
            copy.start()
            copies.append((index, start, min(CHUNK, half), copy))
    return copies


def feed_kernel(count, *refs):
    own, other, scales, ups, gates, gated = refs[count : count + 6]
    partial, (weights, arrived) = refs[count + 6 : -2], refs[-2:]
    half = own.shape[1]
    copies = fetch_weights(own, other, weights, arrived)
    x = rows_of(refs[:count])
    for index, start, size, copy in copies:
        copy.wait()
        rows = slice(start, start + size)
        units = slice(index * half + start, index * half + start + size)
        up, gate = mul(x, weights[index, 0, rows], NT), mul(x, weights[index, 1, rows], NT)
        ups[:, units] = up.astype(BF16)
        gates[:, units] = gate.astype(BF16)
        z = gate * (scales[1:2, units] * GATE_WIDTH)
        silu = z * (0.5 + 0.5 * jnp.tanh(0.5 * z))
        gated[:, units] = (up * scales[0:1, units] * silu).astype(BF16)
    share_out(
        partial, mul(gated[:, :half], weights[0, 2]) + mul(gated[:, half:], weights[1, 2])
    )


def feed_back_kernel(count, *refs):
    own, other, scales, ups, gates, low_up, low_gate, scale_grad = refs[count : count + 8]
    partial, (weights, arrived) = refs[count + 8 : -2], refs[-2:]
    half = own.shape[1]
    copies = fetch_weights(own, other, weights, arrived)
    g = rows_of(refs[:count])
    for index, start, size, copy in copies:
        copy.wait()
        rows = slice(start, start + size)
        units = slice(index * half + start, index * half + start + size)
        grad = mul(g, weights[index, 2, rows], NT)
        up, gate = ups[:, units].astype(F32), gates[:, units].astype(F32)
        s_up, s_gate = scales[0:1, units], scales[1:2, units] * GATE_WIDTH
        z = gate * s_gate
        sigmoid = 0.5 + 0.5 * jnp.tanh(0.5 * z)
        silu = z * sigmoid
        grad_silu = grad * silu
        grad_z = grad * (up * s_up) * (sigmoid + silu * (1.0 - sigmoid))
        low_up[:, units] = (grad_silu * s_up).astype(BF16)
        low_gate[:, units] = (grad_z * s_gate).astype(BF16)
        scale_grad[0:1, units] = jnp.sum(grad_silu * up, axis=0, keepdims=True)
        scale_grad[1:2, units] = jnp.sum(grad_z * gate, axis=0, keepdims=True) * GATE_WIDTH
    total = mul(low_up[:, :half], weights[0, 0]) + mul(low_up[:, half:], weights[1, 0])
    total = total + mul(low_gate[:, :half], weights[0, 1]) + mul(low_gate[:, half:], weights[1, 1])
    share_out(partial, total)


def feed_call(body, at, x, weights, scales, kept_in, kept_out, pair_out):
    tokens, depth = sum(part.shape[0] for part in x), x[0].shape[1]
    half = weights[0].shape[1]
    outs = call(
        functools.partial(body, len(x)),
        [shape((tokens, 2 * half), BF16)] * kept_out
        + [shape((2, 2 * half), F32)] * pair_out
        + partial_shapes(at, tokens, depth),
        [WHOLE] * len(x)
        + [pl.BlockSpec(memory_space=pl.ANY)] * 2
        + [WHOLE] * (1 + len(kept_in)),
        2 * 6 * tokens * depth * half,
        2 * 6 * depth * half,
        [
            VMEM((2, 3, half, depth), BF16),
            pltpu.SemaphoreType.DMA((2, half // min(CHUNK, half))),
        ],
    )(*x, *weights, scales, *kept_in)
    return [*outs[: kept_out + pair_out], outs[kept_out + pair_out :]]


def feed_block(at, x, weights, scales):
    return feed_call(feed_kernel, at, x, weights, scales, (), 3, 0)


def feed_back_block(at, g, weights, scales, ups, gates):
    return feed_call(feed_back_kernel, at, g, weights, scales, (ups, gates), 2, 1)


def feed_grad_kernel(has_other, *refs):
    middle, mixed, (ups, gates, gated) = refs[:5], refs[5:10], (refs[10:14], refs[14:18], refs[18:22])
    out = refs[-1]
    for row, (units, right) in enumerate(((ups, middle), (gates, middle), (gated, mixed))):
        blocks = (right[:1], right[1:2], right[2:3], right[3:5])
        total = sum(mul(left[...], rows_of(block), TN) for left, block in zip(units, blocks))
        if has_other:
            total = total + refs[22][row].astype(F32)
        out[row] = total.astype(BF16)


def feed_grads(half_at, middle, mixed, ups, gates, gated, other=None):
    tokens, units = ups[0].shape
    depth, half = middle[0][0].shape[1], ups[0].shape[1] // 2
    whole = lambda dims: pl.BlockSpec(dims, lambda i: (0,) * len(dims))
    part = pl.BlockSpec((tokens, half), lambda i: (0, half_at))
    rows = [whole(block.shape) for block in flat(middle) + flat(mixed)]
    more = () if other is None else (other,)
    dims = (3, half, depth)
    return call(
        functools.partial(feed_grad_kernel, bool(more)),
        [shape(dims, BF16)],
        rows + [part] * 12 + [whole(dims)] * len(more),
        2 * 3 * 4 * tokens * half * depth,
        2 * 12 * tokens * (half + depth),
        grid=(1,),
        out_specs=[whole(dims)],
    )(*flat(middle), *flat(mixed), *ups, *gates, *gated, *more)[0]


def attend_grad_kernel(section, *refs):
    low, attended, hidden, grads = refs[:4], refs[4:8], refs[8:13], refs[13:18]
    own, other = refs[18:]
    width, half = attended[0].shape[0], own.shape[1]
    for lefts, rights, top in ((low, hidden, 0), (attended, grads, 3 * width)):
        blocks = (rights[:1], rights[1:2], rights[2:3], rights[3:5])
        for start in range(0, lefts[0].shape[0], width):
            total = sum(
                mul(left[start : start + width], rows_of(block)) for left, block in zip(lefts, blocks)
            )
            rows = slice(top + start, top + start + width)
            for place in range(2):
                columns = total[:, place * half : place * half + half]

                @pl.when(section[0] == place)
                def _():
                    own[rows] = columns

                @pl.when(section[0] != place)
                def _():
                    other[rows] = columns.astype(BF16)


def attend_grads(section, low, attended, hidden, grads):
    width, tokens = attended[0].shape
    depth = hidden[0][0].shape[1]
    return call(
        attend_grad_kernel,
        [shape((4 * width, depth // 2), F32), shape((4 * width, depth // 2), BF16)],
        [SCALARS] + [WHOLE] * 18,
        2 * 4 * 4 * tokens * width * depth,
        2 * 16 * tokens * depth,
    )(section, *low, *attended, *flat(hidden), *flat(grads))


def adam_kernel(axis, factor, weight, first, second, gradient, first_out, second_out, weight_out):
    clipped = gradient[...].astype(F32) * factor[0]
    first_new = BETA_FIRST * first[...] + (1.0 - BETA_FIRST) * clipped
    second_new = BETA_SECOND * second[...] + (1.0 - BETA_SECOND) * clipped * clipped
    first_out[...] = first_new
    second_out[...] = second_new
    first_hat = first_new / (1.0 - BETA_FIRST**STEP)
    second_hat = second_new / (1.0 - BETA_SECOND**STEP)
    moved = weight[...] - LEARN_RATE * first_hat / (jnp.sqrt(second_hat) + ADAM_EPSILON)
    scale = lax.rsqrt(jnp.sum(moved * moved, axis=axis, keepdims=True) + NORM_EPSILON)
    weight_out[...] = moved * scale


def adam_matrix(factor, weight, first, second, gradient, axis, block, place, grid):
    spec = pl.BlockSpec(block, place)
    return call(
        functools.partial(adam_kernel, axis),
        [shape(weight.shape, F32)] * 3,
        [SCALARS] + [spec] * 4,
        20 * weight.size,
        28 * weight.size,
        grid=grid,
        out_specs=[spec] * 3,
    )(factor, weight, first, second, gradient)


def add_parts(parts):
    total = parts[0][...].astype(F32)
    for part in parts[1:]:
        total = total + part[...].astype(F32)
    return total


def mix_kernel(count, hidden, rate, *refs):
    branch_out, result, result_low = refs[count:]
    branch = add_parts(refs[:count])
    branch_out[...] = branch
    mixed = mix_residual(hidden[...].astype(F32), branch, rate[...])
    result[...] = mixed
    result_low[...] = mixed.astype(BF16)


def mix_block(hidden, rate, parts):
    dims = hidden.shape
    return call(
        functools.partial(mix_kernel, len(parts)),
        [shape(dims, F32), shape(dims, F32), shape(dims, BF16)],
        [WHOLE] * (2 + len(parts)),
        10 * dims[0] * dims[1],
        8 * dims[0] * dims[1],
    )(hidden, rate, *parts)


def mix_back_kernel(count, rounded, hidden, branch, rate, *refs):
    grad_hidden, grad_branch, grad_rate = refs[count:]
    upstream = add_parts(refs[:count])
    if rounded:
        upstream = upstream.astype(BF16).astype(F32)
    h, b, r = hidden[...].astype(F32), branch[...], rate[...]
    scale = lax.rsqrt(jnp.sum(b * b, axis=-1, keepdims=True) + NORM_EPSILON)
    unit = b * scale
    apart = unit - h
    mixed = h + r * apart
    mixed_scale = lax.rsqrt(jnp.sum(mixed * mixed, axis=-1, keepdims=True) + NORM_EPSILON)
    mixed = mixed * mixed_scale
    grad = mixed_scale * (upstream - mixed * jnp.sum(mixed * upstream, axis=-1, keepdims=True))
    grad_rate[...] = jnp.sum(grad * apart, axis=0, keepdims=True)
    grad_unit = grad * r
    grad_hidden[...] = grad - grad_unit
    grad_unit = scale * (grad_unit - unit * jnp.sum(unit * grad_unit, axis=-1, keepdims=True))
    grad_branch[...] = grad_unit.astype(BF16)


def mix_back_block(hidden, branch, rate, parts, rounded=False):
    dims = hidden.shape
    return call(
        functools.partial(mix_back_kernel, len(parts), rounded),
        [shape(dims, F32), shape(dims, BF16), shape((1, dims[1]), F32)],
        [WHOLE] * (3 + len(parts)),
        20 * dims[0] * dims[1],
        12 * dims[0] * dims[1],
    )(hidden, branch, rate, *parts)


def tie(*values):
    return lax.optimization_barrier(values)


def to_neighbours(block):
    return exchange(block, "mp", 1), exchange(block, "mp", 2)


def pass_halves(first, second):
    half = first.shape[0] // 2
    return exchange(second[:half], "mp", 1), exchange(first[half:], "mp", 2)


def send_far(partial):
    return exchange(partial[0], "mp", 1), exchange(partial[1], "mp", 2)


def send_near(partial_first, partial_second, upper, lower):
    half = upper.shape[0]
    zero = jnp.zeros((), F32)
    first = partial_first + lax.pad(lower.astype(F32), zero, ((half, 0, 0), (0, 0, 0)))
    second = partial_second + lax.pad(upper.astype(F32), zero, ((0, half, 0), (0, 0, 0)))
    return exchange(first.astype(BF16), "mp", 1), exchange(second.astype(BF16), "mp", 2)


def feed_exchange(block, work):
    first, second = to_neighbours(block)
    done = [None] * 4
    done[0] = work(0, (block,))
    first, second, done[0] = tie(first, second, done[0])
    far = pass_halves(first, second)
    done[1] = work(1, (first,))
    far, done[1] = tie(far, done[1])
    done[3] = work(3, far)
    upper, lower = send_far(done[3][-1])
    done[2] = work(2, (second,))
    upper, lower, done[2] = tie(upper, lower, done[2])
    from_first, from_second = send_near(done[1][-1][0], done[2][-1][0], upper, lower)
    return [(block,), (first,), (second,), far], done, (done[0][-1][0], from_first, from_second)


def layer_forward(hidden, low, params, tables, tied, feed_weights):
    attend_in, attend_out, gains, scales, mixing = params
    cosine, sine, starts, info = tables
    project = lambda at, block: project_block(block, attend_in, cosine[at], sine[at], gains)
    heads = [None] * 4
    first, second = to_neighbours(low)
    if tied:
        heads[0] = project(0, (low,))
        first, second, heads[0] = tie(first, second, heads[0])
    far = pass_halves(first, second)
    if tied:
        heads[1], heads[2] = project(1, (first,)), project(2, (second,))
        far, heads[1], heads[2] = tie(far, heads[1], heads[2])
    else:
        heads = [project(at, block) for at, block in enumerate(((low,), (first,), (second,)))] + [0]
    heads[3] = project(3, far)
    raw, query, keys, values = zip(*heads)
    attend = lambda at: attend_block(
        at, info, starts[at : at + 1], query[at], keys, values, attend_out
    )
    attended = [None] * 4
    attended[3] = attend(3)
    upper, lower = send_far(attended[3][-1])
    attended[1], attended[2] = attend(1), attend(2)
    upper, lower, attended[1], attended[2] = tie(upper, lower, attended[1], attended[2])
    from_first, from_second = send_near(attended[1][-1][0], attended[2][-1][0], upper, lower)
    attended[0] = attend(0)
    from_first, from_second, attended[0] = tie(from_first, from_second, attended[0])
    (branch, middle, middle_low), feed_weights = feed_weights(
        mix_block(hidden, mixing[:1], (attended[0][-1][0], from_first, from_second))
    )
    work = lambda at, block: feed_block(at, block, feed_weights, scales)
    middle_blocks, fed, parts = feed_exchange(middle_low, work)
    mixed, result, result_low = mix_block(middle, mixing[1:], parts)
    ups, gates, gated, _ = zip(*fed)
    attended, logsums, _ = zip(*attended)
    hidden_blocks = [(low,), (first,), (second,), far]
    stored = (
        (hidden, branch, hidden_blocks, raw, query, keys, values, attended, logsums),
        (middle, mixed, middle_blocks, ups, gates, gated),
    )
    return result, result_low, stored, feed_weights


def layer_backward(stored, upstream, rounded, params, tables, feed_weights, section):
    attend_in, attend_out, gains, scales, mixing = params
    cosine, sine, starts, info = tables
    attend_stored, (middle, mixed, middle_blocks, ups, gates, gated) = stored
    hidden, branch, hidden_blocks, raw, query, keys, values, attended, logsums = attend_stored
    grad_middle, grad_mixed, rate_two = mix_back_block(
        middle, mixed, mixing[1:], upstream, rounded
    )
    work = lambda at, block: feed_back_block(at, block, feed_weights, scales, ups[at], gates[at])
    mixed_blocks, done, parts = feed_exchange(grad_mixed, work)
    low_ups, low_gates, scale_grads, _ = zip(*done)
    operands = (middle_blocks, mixed_blocks, low_ups, low_gates, gated)
    other = feed_grads(1, *operands)
    own, from_first, from_second, other = tie(*parts, other)
    other = exchange(other, "section", 1)
    grad_hidden, grad_branch, rate_one = mix_back_block(
        hidden, branch, mixing[:1], (grad_middle, own, from_first, from_second)
    )
    first, second = to_neighbours(grad_branch)
    feed_sums = feed_grads(0, *operands, other)
    first, second, feed_sums = tie(first, second, feed_sums)
    grads = [(grad_branch,), (first,), (second,), pass_halves(first, second)]
    low, partial, gain_grad = attend_back(
        info, starts, query, keys, values, attended, logsums, raw, grads,
        attend_out, attend_in, cosine, sine, gains,
    )
    upper, lower = send_far(partial[3])
    own, other = attend_grads(section, low, attended, hidden_blocks, grads)
    upper, lower, own, other = tie(upper, lower, own, other)
    other = exchange(other, "section", 1)
    from_first, from_second = send_near(partial[1][0], partial[2][0], upper, lower)
    attend_sums = (own + other.astype(F32)).astype(BF16).reshape(4, -1, own.shape[1])
    parts = (grad_hidden, partial[0][0], from_first, from_second)
    small = (sum(scale_grads), rate_one[0], rate_two[0])
    return parts, feed_sums, attend_sums, gain_grad[:, 0], small


def adam_update(weight, first, second, gradient, factor, rate):
    clipped = gradient * factor
    first_new = BETA_FIRST * first + (1.0 - BETA_FIRST) * clipped
    second_new = BETA_SECOND * second + (1.0 - BETA_SECOND) * clipped * clipped
    first_hat = first_new / (1.0 - BETA_FIRST**STEP)
    second_hat = second_new / (1.0 - BETA_SECOND**STEP)
    moved = weight - rate * first_hat / (jnp.sqrt(second_hat) + ADAM_EPSILON)
    return (first_new, second_new, moved)


def per_device(
    inputs,
    cotangent,
    doc_ids,
    attention_in,
    attention_out,
    feedforward_in,
    feedforward_out,
    unit_scales,
    mix_rates,
    first_attention_in,
    second_attention_in,
    first_attention_out,
    second_attention_out,
    first_feedforward_in,
    second_feedforward_in,
    first_feedforward_out,
    second_feedforward_out,
    first_unit_scales,
    second_unit_scales,
    first_mix_rates,
    second_mix_rates,
):
    section = lax.axis_index("section")
    is_first = section == 0
    dp_index = lax.axis_index("dp")
    dp_size = lax.axis_size("dp")
    local_rows = inputs.shape[1]

    def ordered(own, other):
        return jnp.where(is_first, own, other), jnp.where(is_first, other, own)

    def halves(array, dim):
        width = array.shape[dim] // 2
        own = lax.dynamic_slice_in_dim(array, section * width, width, dim)
        other = lax.dynamic_slice_in_dim(array, (1 - section) * width, width, dim)
        return own, other

    hidden_low = lax.dynamic_index_in_dim(inputs, section, 0, False)

    attend_rows = jnp.concatenate(
        [jnp.swapaxes(attention_in[0], 1, 2), attention_out], axis=0
    ).astype(BF16)
    small = jnp.concatenate([unit_scales.reshape(-1), mix_rates.reshape(-1)]).astype(BF16)
    feed_rows = jnp.concatenate(
        [jnp.swapaxes(feedforward_in[0].astype(BF16), 1, 2), feedforward_out.astype(BF16)], axis=0
    )

    def gather_ring(half):
        blocks = spread_rows(half, "dp")
        count = half.shape[1]
        whole = jnp.zeros((half.shape[0], dp_size * count, half.shape[2]), BF16)
        for source, block in zip(ring_sources("dp"), blocks):
            whole = lax.dynamic_update_slice_in_dim(whole, block, source * count, 1)
        return whole, blocks[-1]

    own, other = halves(attend_rows, 2)
    attend_pieces = ordered(own, exchange(other, "section", 1))
    own, other = halves(feed_rows, 1)
    feed_pieces = ordered(own, exchange(other, "section", 1))
    if dp_size <= 4:
        attend_first, step = gather_ring(attend_pieces[0])
        attend_second, *feed_pieces, _ = tie(attend_pieces[1], *feed_pieces, step)
    else:
        attend_first = lax.all_gather(attend_pieces[0], "dp", axis=1, tiled=True)
        attend_second = attend_pieces[1]
    attend_pieces = (attend_first, lax.all_gather(attend_second, "dp", axis=1, tiled=True))
    small = jnp.stack(ordered(small, exchange(small, "section", 1))).reshape(-1)
    small = gather_small(small, "dp").astype(F32)
    small = small.reshape(dp_size, 2, -1)
    units_here = unit_scales.shape[2]

    def units_apart(values):
        parts = values.reshape(dp_size, 2, -1)
        own, other = ordered(parts[:, 0], parts[:, 1])
        return jnp.concatenate([own.reshape(-1), other.reshape(-1)])

    def units_back(values):
        parts = values.reshape(2, dp_size, -1)
        own, other = ordered(parts[0], parts[1])
        return jnp.stack([own, other], axis=1).reshape(-1)

    layers, feed_owns = [], []
    for layer in range(2):
        own = attend_pieces[layer]
        attend = jnp.concatenate(ordered(own, exchange(own, "section", 1)), axis=2)
        feed_own = lax.all_gather(feed_pieces[layer], "dp", axis=1, tiled=True)
        units = small[:, layer, :units_here].reshape(-1)
        mixing = small[:, layer, units_here:].reshape(dp_size, 2, -1)
        mixing = jnp.swapaxes(mixing, 0, 1).reshape(2, -1)
        width_qk, width_ff = attend.shape[1], 2 * feed_own.shape[1]
        layers.append((
            attend[:3].reshape(3 * width_qk, -1), attend[3],
            units[:width_qk, None],
            jnp.stack([
                units_apart(units[width_qk : width_qk + width_ff]),
                units_apart(units[width_qk + width_ff :]),
            ]),
            mixing,
        ))
        feed_owns.append(feed_own)

    doc_row = lax.dynamic_index_in_dim(doc_ids, section, 0, False)
    starts_all = document_starts(doc_row)
    mp_index = lax.axis_index("mp")
    sources = [mp_index ^ offset for offset in range(4)]
    places = jnp.arange(local_rows, dtype=jnp.int32)
    starts = jnp.stack([
        lax.dynamic_slice_in_dim(starts_all, source * local_rows, local_rows, 0)
        for source in sources
    ])
    sources = jnp.stack(sources).astype(jnp.int32)
    cosine, sine = rope_tables(sources[:, None] * local_rows + places - starts)
    info = jnp.concatenate([sources, starts[:, 0]])
    tables = (cosine, sine, starts, info)

    def scatter(sums):
        return lax.psum_scatter(sums, "dp", scatter_dimension=1, tiled=True)

    def scatter_ring(sums):
        if dp_size > 4:
            return scatter(sums)
        count = sums.shape[1] // dp_size
        parts = [
            lax.dynamic_slice_in_dim(sums, source * count, count, 1).astype(F32)
            for source in ring_sources("dp")
        ]
        return collect_rows(parts, "dp").astype(BF16)

    def weights_ready(own, value):
        value, own = tie(value, own)
        return value, (own, exchange(own, "section", 1))

    def small_vector(scales, rate_one, rate_two):
        return jnp.concatenate([units_back(scales[0]), units_back(scales[1]), rate_one, rate_two])

    first, second = layers
    section_ref = section.astype(jnp.int32).reshape(1)
    grad = lax.dynamic_index_in_dim(cotangent, section, 0, False)
    _, hidden_second, stored_first, weights_first = layer_forward(
        hidden_low, hidden_low, first, tables, False, functools.partial(weights_ready, feed_owns[0])
    )
    result, _, stored_second, weights_second = layer_forward(
        hidden_second, hidden_second, second, tables, True,
        functools.partial(weights_ready, feed_owns[1]),
    )
    parts, feed_second, attend_second, gains_second, small_second = layer_backward(
        stored_second, (grad,), False, second, tables, weights_second, section_ref
    )
    feed_second = scatter(feed_second)
    parts, attend_second = tie(parts, attend_second)
    attend_second = scatter(attend_second)
    parts, feed_first, attend_first, gains_first, small_first = layer_backward(
        stored_first, parts, True, first, tables, weights_first, section_ref
    )
    feed_first = scatter(feed_first)
    attend_first, feed_second, attend_second = tie(attend_first, feed_second, attend_second)
    attend_first = scatter_ring(attend_first)
    grad = sum(part.astype(F32) for part in parts)

    reduced_first = (attend_first, feed_first)
    reduced_second = (attend_second, feed_second)
    squares = sum(
        jnp.sum(jnp.square(part.astype(F32))) for part in (*reduced_first, *reduced_second)
    )
    gradients = []
    for one, two, dim in zip(reduced_first, reduced_second, (2, 1)):
        own, other = jnp.where(is_first, one, two), jnp.where(is_first, two, one)
        other = exchange(other, "section", 1)
        gradients.append(jnp.concatenate(ordered(own, other), axis=dim))

    sums = jnp.stack([small_vector(*small_first), small_vector(*small_second)])
    sums = sum_over(sum_over(sums, "section"), "dp")
    width_qk = gains_first.shape[0]
    scale_sums, rate_sums = sums[:, : dp_size * units_here - width_qk], sums[:, dp_size * units_here - width_qk :]
    rate_sums = sum_over(rate_sums, "mp").reshape(2, 2, -1)
    gain_sums = sum_over(sum_over(jnp.stack([gains_first, gains_second]), "section"), "dp")
    unit_grads = jnp.concatenate([gain_sums, scale_sums], axis=1)
    unit_grads = jnp.where(is_first, unit_grads[0], unit_grads[1])
    unit_grads = lax.dynamic_slice_in_dim(unit_grads, dp_index * units_here, units_here, 0)
    unit_grads = unit_grads[None, None]
    rates_here = mix_rates.shape[2]
    rate_grads = jnp.where(is_first, rate_sums[0], rate_sums[1])
    rate_grads = lax.dynamic_slice_in_dim(rate_grads, dp_index * rates_here, rates_here, 1)[None]

    leading = (mp_index == 0).astype(F32)
    squares = squares + jnp.sum(unit_grads * unit_grads)
    squares = squares + leading * jnp.sum(rate_grads * rate_grads)
    squares = squares.reshape(1)
    squares = squares + exchange(squares, "section", 1)
    squares = sum_over(sum_over(squares, "mp"), "dp")
    gradient_norm = jnp.sqrt(squares[0])
    factor = CLIP_NORM / jnp.maximum(gradient_norm, CLIP_NORM)

    to_send = jnp.where(is_first, result, grad)
    kept = jnp.where(is_first, grad, result)
    arrived = exchange(to_send, "section", 1)
    boundary_states = jnp.stack(ordered(kept, arrived))[None]

    attend_grad, feed_grad = gradients
    scalar = factor.reshape(1)
    updates = []
    turn = lambda array: jnp.swapaxes(array, 1, 2)
    new = adam_matrix(
        scalar, turn(attention_in[0]), turn(first_attention_in[0]), turn(second_attention_in[0]),
        attend_grad[:3], 2, (1, *attend_grad.shape[1:]), lambda i: (i, 0, 0), (3,),
    )
    updates.extend(turn(part)[None] for part in new)
    updates.extend(adam_matrix(
        scalar, attention_out, first_attention_out, second_attention_out, attend_grad[3:],
        2, attention_out.shape, lambda i: (0, 0, 0), (1,),
    ))
    new = adam_matrix(
        scalar, feedforward_in[0], first_feedforward_in[0], second_feedforward_in[0],
        turn(feed_grad[:2]), 1, (1, *feedforward_in.shape[2:]), lambda i: (i, 0, 0), (2,),
    )
    updates.extend(part[None] for part in new)
    steps = 4 if feedforward_out.shape[1] % 64 == 0 else 1
    updates.extend(adam_matrix(
        scalar, feedforward_out, first_feedforward_out, second_feedforward_out, feed_grad[2:],
        2, (1, feedforward_out.shape[1] // steps, feedforward_out.shape[2]),
        lambda i: (0, i, 0), (steps,),
    ))
    updates.extend(
        adam_update(
            unit_scales, first_unit_scales, second_unit_scales, unit_grads, factor, SCALE_RATE
        )
    )
    updates.extend(
        adam_update(
            mix_rates, first_mix_rates, second_mix_rates, rate_grads, factor, MIXING_RATE
        )
    )
    return (boundary_states, gradient_norm, *updates)


def solution(mesh):
    in_specs = (
        P("dp", "mp", None),
        P("dp", "mp", None),
        P("dp", None),
        P("section", None, None, ("mp", "dp")),
        P("section", ("mp", "dp"), None),
        P("section", None, None, ("mp", "dp")),
        P("section", ("mp", "dp"), None),
        P("section", "mp", "dp"),
        P("section", None, "dp"),
        P("section", None, None, ("mp", "dp")),
        P("section", None, None, ("mp", "dp")),
        P("section", ("mp", "dp"), None),
        P("section", ("mp", "dp"), None),
        P("section", None, None, ("mp", "dp")),
        P("section", None, None, ("mp", "dp")),
        P("section", ("mp", "dp"), None),
        P("section", ("mp", "dp"), None),
        P("section", "mp", "dp"),
        P("section", "mp", "dp"),
        P("section", None, "dp"),
        P("section", None, "dp"),
    )
    out_specs = (
        P("section", "dp", "mp", None),
        P(),
        P("section", None, None, ("mp", "dp")),
        P("section", None, None, ("mp", "dp")),
        P("section", None, None, ("mp", "dp")),
        P("section", ("mp", "dp"), None),
        P("section", ("mp", "dp"), None),
        P("section", ("mp", "dp"), None),
        P("section", None, None, ("mp", "dp")),
        P("section", None, None, ("mp", "dp")),
        P("section", None, None, ("mp", "dp")),
        P("section", ("mp", "dp"), None),
        P("section", ("mp", "dp"), None),
        P("section", ("mp", "dp"), None),
        P("section", "mp", "dp"),
        P("section", "mp", "dp"),
        P("section", "mp", "dp"),
        P("section", None, "dp"),
        P("section", None, "dp"),
        P("section", None, "dp"),
    )
    return jax.shard_map(
        per_device, mesh=mesh, in_specs=in_specs, out_specs=out_specs, check_vma=False
    )
```

```python
import functools
import math

import jax
import jax.numpy as jnp
from jax import lax
from jax.experimental import pallas as pl
from jax.experimental.pallas import tpu as pltpu
from jax.sharding import PartitionSpec as P

HD = 64
STEP = 10

NORM_EPSILON = 1e-06
ROPE_BASE = 10000.0
CLIP_NORM = 0.1
LEARN_RATE = 0.05
SCALE_RATE = 1.25
MIXING_RATE = 0.4
BETA_FIRST = 0.9
BETA_SECOND = 0.95
ADAM_EPSILON = 1e-08

BF16 = jnp.bfloat16
F32 = jnp.float32


def exchange(block, axis, bit):
    route = [(i, i ^ bit) for i in range(lax.axis_size(axis))]
    return lax.ppermute(block, axis, route)


def gray(place):
    return place ^ (place >> 1)


def ring_place(index, size):
    shift = 1
    while shift < size:
        index = index ^ (index >> shift)
        shift *= 2
    return index


def ring_step(block, axis):
    size = lax.axis_size(axis)
    route = []
    for place in range(size):
        route.append((gray(place), gray((place + 1) % size)))
        route.append((size + gray(place), size + gray((place - 1) % size)))
    return lax.ppermute(block, ("section", axis), route)


def ring_sources(axis):
    size = lax.axis_size(axis)
    place = ring_place(lax.axis_index(axis), size)
    way = 1 - 2 * lax.axis_index("section")
    return [gray((place - way * step + size) % size) for step in range(size)]


def spread_rows(block, axis="mp"):
    blocks = [block]
    for _ in range(lax.axis_size(axis) - 1):
        blocks.append(ring_step(blocks[-1], axis))
    return blocks


def collect_rows(parts, axis="mp"):
    moving = parts[1]
    for part in parts[2:] + parts[:1]:
        moving = ring_step(moving.astype(BF16), axis).astype(F32) + part
    return moving


def sum_over(values, axis):
    bit = 1
    while bit < lax.axis_size(axis):
        values = values + exchange(values, axis, bit)
        bit *= 2
    return values


def gather_small(values, axis):
    index = lax.axis_index(axis)
    gathered = values[None]
    bit = 1
    while bit < lax.axis_size(axis):
        other = exchange(gathered, axis, bit)
        low = (index & bit) == 0
        gathered = jnp.concatenate(
            [jnp.where(low, gathered, other), jnp.where(low, other, gathered)], axis=0
        )
        bit *= 2
    return gathered


def unit_norm(values):
    return values * lax.rsqrt(jnp.sum(values * values, axis=-1, keepdims=True) + NORM_EPSILON)


def document_starts(doc_row):
    position = jnp.arange(doc_row.shape[-1], dtype=jnp.int32)
    change = jnp.concatenate([jnp.ones((1,), dtype=jnp.bool_), doc_row[1:] != doc_row[:-1]])
    return lax.cummax(jnp.where(change, position, 0), axis=0)


def rope_tables(offsets):
    half_width = HD // 2
    inverse = 1.0 / ROPE_BASE ** (jnp.arange(half_width, dtype=F32) * (2.0 / HD))
    angles = inverse[:, None] * offsets.astype(F32)[..., None, :]
    angles = jnp.concatenate([angles, angles], axis=-2)
    return jnp.cos(angles), jnp.sin(angles)


def mix_residual(hidden, branch, mixing):
    return unit_norm(hidden + mixing * (unit_norm(branch) - hidden))


NT = (((1,), (1,)), ((), ()))
TN = (((0,), (0,)), ((), ()))
NN = (((1,), (0,)), ((), ()))
VMEM = pltpu.VMEM
WHOLE, NEAR = "whole", "near"
SCALARS = pl.BlockSpec(memory_space=pltpu.SMEM)


def mul(left, right, dims=NN):
    return lax.dot_general(left, right, dims, preferred_element_type=F32)


def block_of(array):
    zeros = (0,) * len(array.shape)
    return pl.BlockSpec(array.shape, lambda *place: zeros)


def call(body, out_shape, in_specs, flops, moved, scratch=(), grid=(1,), out_specs=None):
    def run(*args):
        specs = [
            block_of(arg) if spec in (WHOLE, NEAR) else spec for spec, arg in zip(in_specs, args)
        ]
        args = [
            arg if spec in (SCALARS, NEAR) else pltpu.with_memory_space_constraint(arg, pltpu.HBM)
            for spec, arg in zip(in_specs, args)
        ]
        return pl.pallas_call(
            body,
            out_shape=[pltpu.HBM(out.shape, out.dtype) for out in out_shape],
            grid=grid,
            in_specs=specs,
            out_specs=out_specs or [block_of(out) for out in out_shape],
            scratch_shapes=list(scratch),
            compiler_params=pltpu.CompilerParams(vmem_limit_bytes=50 << 20),
            cost_estimate=pl.CostEstimate(flops=flops, bytes_accessed=moved, transcendentals=0),
        )(*args)

    return run


def shape(dims, dtype):
    return jax.ShapeDtypeStruct(dims, dtype)


def turned(raw, cosine, sine):
    half = HD // 2
    first, second = raw[:half], raw[half:]
    return jnp.concatenate(
        [
            first * cosine[:half] - second * sine[:half],
            second * cosine[half:] + first * sine[half:],
        ],
        axis=0,
    )


def turned_back(grad, cosine, sine):
    half = HD // 2
    first, second = grad[:half], grad[half:]
    return jnp.concatenate(
        [
            first * cosine[:half] + second * sine[half:],
            second * cosine[half:] - first * sine[:half],
        ],
        axis=0,
    )


def project_kernel(x, weight, cosine, sine, gains, raw_out, query, keys, values):
    width = query.shape[0]
    raw = mul(weight[...], x[...], NT)
    raw_out[...] = raw[: 2 * width]
    values[...] = raw[2 * width :].astype(BF16)
    for part, out in ((0, query), (1, keys)):
        for top in range(0, width, HD):
            turn = turned(raw[part * width + top : part * width + top + HD], cosine[...], sine[...])
            scale = lax.rsqrt(jnp.sum(turn * turn, axis=0, keepdims=True) + NORM_EPSILON)
            head = (turn * scale * gains[top : top + HD]).astype(BF16)
            out[top : top + HD] = head * math.sqrt(HD) if part == 0 else head


def project_block(x, weight, cosine, sine, gains):
    tokens, depth = x.shape
    width = weight.shape[0] // 3
    low = shape((width, tokens), BF16)
    return call(
        project_kernel,
        [shape((2 * width, tokens), F32), low, low, low],
        [NEAR] + [WHOLE] * 4,
        2 * tokens * depth * 3 * width,
        2 * 3 * width * depth,
    )(x, weight, cosine, sine, gains)


def near(info, at, other, tokens):
    return (info[other] <= info[at]) & ((info[other] + 1) * tokens > info[4 + at])


def seen(info, at, other, starts, tokens):
    key_place = info[other] * tokens + lax.broadcasted_iota(jnp.int32, (tokens, tokens), 0)
    query_place = info[at] * tokens + lax.broadcasted_iota(jnp.int32, (tokens, tokens), 1)
    return (key_place <= query_place) & (key_place >= starts)


def share_out(partial, value):
    partial[...] = value.astype(partial.dtype)


def partial_shape(at, tokens, depth):
    return shape((tokens, depth), BF16 if at else F32)


def attend_kernel(at, info, starts, query, k0, k1, k2, k3, v0, v1, v2, v3, weight,
                  attended, logsums, partial, total, sums):
    width, tokens = query.shape
    total[...] = jnp.zeros_like(total)
    sums[...] = jnp.ones_like(sums)
    sums[: width // HD] = jnp.zeros((width // HD, tokens), F32)
    for other, (keys, values) in enumerate(((k0, v0), (k1, v1), (k2, v2), (k3, v3))):

        @pl.when(near(info, at, other, tokens))
        def _():
            allowed = seen(info, at, other, starts[...], tokens)
            for head in range(width // HD):
                rows = slice(head * HD, head * HD + HD)
                shares = jnp.exp(mul(keys[rows], query[rows], TN))
                shares = jnp.where(allowed, shares, 0.0)
                sums[head : head + 1] += jnp.sum(shares, axis=0, keepdims=True)
                total[rows] += mul(values[rows], shares.astype(BF16))

    logsums[...] = jnp.log(sums[...])
    inverse = 1.0 / sums[...]
    for head in range(width // HD):
        rows = slice(head * HD, head * HD + HD)
        attended[rows] = (total[rows] * inverse[head : head + 1]).astype(BF16)
    share_out(partial, mul(attended[...], weight[...], TN))


def attend_block(at, info, starts, query, keys, values, weight):
    width, tokens = query.shape
    depth = weight.shape[1]
    return call(
        functools.partial(attend_kernel, at),
        [shape((width, tokens), BF16), shape((8, tokens), F32), partial_shape(at, tokens, depth)],
        [SCALARS] + [WHOLE] * 11,
        2 * tokens * (depth * width + 10 * tokens * 256),
        2 * depth * width,
        [VMEM((width, tokens), F32), VMEM((8, tokens), F32)],
    )(info, starts, query, *keys, *values, weight)


def attend_back_kernel(info, starts, *refs):
    query, keys, values, attended, logsums, raw, grads = (refs[4 * n : 4 * n + 4] for n in range(7))
    w_out, w_in, cosine, sine, gains = refs[28:33]
    low, partial, gain_grad = refs[33:37], refs[37:41], refs[41]
    pulled, deltas, grad_query, grad_keys, grad_values = refs[42:]
    width, tokens = query[0].shape
    heads = width // HD
    grad_query[...] = jnp.zeros_like(grad_query)
    grad_keys[...] = jnp.zeros_like(grad_keys)
    grad_values[...] = jnp.zeros_like(grad_values)
    deltas[...] = jnp.zeros_like(deltas)
    for at in range(4):
        grad = mul(w_out[...], grads[at][...], NT).astype(BF16)
        pulled[at] = grad
        product = grad.astype(F32) * attended[at][...].astype(F32)
        for head in range(heads):
            rows = slice(head * HD, head * HD + HD)
            deltas[at, head : head + 1] = jnp.sum(product[rows], axis=0, keepdims=True)
    for at in range(4):
        for other in range(4):

            @pl.when(near(info, at, other, tokens))
            def _():
                allowed = seen(info, at, other, starts[at : at + 1], tokens)
                for head in range(heads):
                    rows = slice(head * HD, head * HD + HD)
                    grad_rows, query_rows = pulled[at, rows], query[at][rows]
                    scores = mul(keys[other][rows], query_rows, TN) - logsums[at][head : head + 1]
                    shares = jnp.where(allowed, jnp.exp(scores), 0.0)
                    grad_shares = mul(values[other][rows], grad_rows, TN)
                    grad_scores = shares * (grad_shares - deltas[at, head : head + 1])
                    grad_scores = grad_scores.astype(BF16)
                    grad_values[other, rows] += mul(grad_rows, shares.astype(BF16), NT)
                    grad_keys[other, rows] += mul(query_rows, grad_scores, NT)
                    grad_query[at, rows] += mul(keys[other][rows], grad_scores)

    gain_total = [0.0] * heads
    for at in range(4):
        cos, sin = cosine[at], sine[at]
        for part, source, factor in ((0, grad_query, math.sqrt(HD)), (1, grad_keys, 1.0)):
            for head in range(heads):
                rows = slice(head * HD, head * HD + HD)
                turn = turned(raw[at][part * width + head * HD : part * width + head * HD + HD], cos, sin)
                scale = lax.rsqrt(jnp.sum(turn * turn, axis=0, keepdims=True) + NORM_EPSILON)
                unit = turn * scale
                grad = source[at, rows] * factor
                gain_total[head] = gain_total[head] + grad * unit
                grad = grad * gains[rows]
                grad = scale * (grad - unit * jnp.sum(unit * grad, axis=0, keepdims=True))
                low[at][part * width + head * HD : part * width + head * HD + HD] = turned_back(
                    grad, cos, sin
                ).astype(BF16)
        low[at][2 * width :] = grad_values[at].astype(BF16)
        share_out(partial[at], mul(low[at][...], w_in[...], TN))
    for head in range(heads):
        gain_grad[head * HD : head * HD + HD] = jnp.sum(gain_total[head], axis=1, keepdims=True)


def attend_back(info, starts, query, keys, values, attended, logsums, raw, grads,
                w_out, w_in, cosine, sine, gains):
    width, tokens = query[0].shape
    depth = w_out.shape[1]
    low = shape((3 * width, tokens), BF16)
    block = VMEM((4, width, tokens), F32)
    outs = call(
        attend_back_kernel,
        [low] * 4
        + [partial_shape(at, tokens, depth) for at in range(4)]
        + [shape((width, 1), F32)],
        [SCALARS] + [WHOLE] * 25 + [NEAR] * 4 + [WHOLE] * 5,
        2 * 4 * tokens * (depth * width * 4 + 60 * tokens * 256),
        2 * depth * width * 12,
        [VMEM((4, width, tokens), BF16), VMEM((4, 8, tokens), F32), block, block, block],
    )(info, starts, *query, *keys, *values, *attended, *logsums, *raw, *grads,
      w_out, w_in, cosine, sine, gains)
    return outs[:4], outs[4:8], outs[8]


CHUNK = 256
GATE_WIDTH = math.sqrt(1024)


def fetch_weights(own, other, weights, arrived):
    half = own.shape[1]
    copies = []
    for index, source in enumerate((own, other)):
        for at, start in enumerate(range(0, half, min(CHUNK, half))):
            rows = pl.ds(start, min(CHUNK, half))
            copy = pltpu.make_async_copy(
                source.at[:, rows], weights.at[index, :, rows], arrived.at[index, at]
            )
            copy.start()
            copies.append((index, start, min(CHUNK, half), copy))
    return copies


def feed_kernel(x, own, other, scales, ups, gates, gated_out, partial, weights, gated, arrived):
    half = own.shape[1]
    for index, start, size, copy in fetch_weights(own, other, weights, arrived):
        copy.wait()
        rows = slice(start, start + size)
        units = slice(index * half + start, index * half + start + size)
        up, gate = mul(x[...], weights[index, 0, rows], NT), mul(x[...], weights[index, 1, rows], NT)
        ups[:, units] = up.astype(BF16)
        gates[:, units] = gate.astype(BF16)
        z = gate * (scales[1:2, units] * GATE_WIDTH)
        silu = z * (0.5 + 0.5 * jnp.tanh(0.5 * z))
        mixed = (up * scales[0:1, units] * silu).astype(BF16)
        gated[:, units] = mixed
        gated_out[units] = mixed.T
    share_out(
        partial, mul(gated[:, :half], weights[0, 2]) + mul(gated[:, half:], weights[1, 2])
    )


def feed_back_kernel(g, own, other, scales, ups, gates, up_out, gate_out, scale_grad, partial,
                     weights, low_up, low_gate, arrived):
    half = own.shape[1]
    for index, start, size, copy in fetch_weights(own, other, weights, arrived):
        copy.wait()
        rows = slice(start, start + size)
        units = slice(index * half + start, index * half + start + size)
        grad = mul(g[...], weights[index, 2, rows], NT)
        up, gate = ups[:, units].astype(F32), gates[:, units].astype(F32)
        s_up, s_gate = scales[0:1, units], scales[1:2, units] * GATE_WIDTH
        z = gate * s_gate
        sigmoid = 0.5 + 0.5 * jnp.tanh(0.5 * z)
        silu = z * sigmoid
        grad_silu = grad * silu
        grad_z = grad * (up * s_up) * (sigmoid + silu * (1.0 - sigmoid))
        grad_up, grad_gate = (grad_silu * s_up).astype(BF16), (grad_z * s_gate).astype(BF16)
        low_up[:, units], low_gate[:, units] = grad_up, grad_gate
        up_out[units], gate_out[units] = grad_up.T, grad_gate.T
        scale_grad[0:1, units] = jnp.sum(grad_silu * up, axis=0, keepdims=True)
        scale_grad[1:2, units] = jnp.sum(grad_z * gate, axis=0, keepdims=True) * GATE_WIDTH
    total = mul(low_up[:, :half], weights[0, 0]) + mul(low_up[:, half:], weights[1, 0])
    total = total + mul(low_gate[:, :half], weights[0, 1]) + mul(low_gate[:, half:], weights[1, 1])
    share_out(partial, total)


def feed_call(body, at, x, weights, scales, kept, outs, low_count):
    tokens, depth = x.shape
    half = weights[0].shape[1]
    return call(
        body,
        outs + [partial_shape(at, tokens, depth)],
        [NEAR] + [pl.BlockSpec(memory_space=pl.ANY)] * 2 + [WHOLE] * (1 + len(kept)),
        2 * 6 * tokens * depth * half,
        2 * 6 * depth * half,
        [VMEM((2, 3, half, depth), BF16)]
        + [VMEM((tokens, 2 * half), BF16)] * low_count
        + [pltpu.SemaphoreType.DMA((2, half // min(CHUNK, half)))],
    )(x, *weights, scales, *kept)


def feed_block(at, x, weights, scales):
    dims = (x.shape[0], 2 * weights[0].shape[1])
    outs = [shape(dims, BF16), shape(dims, BF16), shape(dims[::-1], BF16)]
    return feed_call(feed_kernel, at, x, weights, scales, (), outs, 1)


def feed_back_block(at, g, weights, scales, ups, gates):
    low, pair = shape(ups.shape[::-1], BF16), shape((2, ups.shape[1]), F32)
    return feed_call(feed_back_kernel, at, g, weights, scales, (ups, gates), [low, low, pair], 2)


def feed_grad_kernel(has_other, *refs):
    middle, mixed, ups, gates, gated = (refs[4 * n : 4 * n + 4] for n in range(5))
    out = refs[-1]
    rows = lambda blocks: jnp.concatenate([block[...] for block in blocks], axis=0)
    for row, (units, right) in enumerate(((ups, middle), (gates, middle), (gated, mixed))):
        left = jnp.concatenate([block[...] for block in units], axis=1)
        total = mul(left, rows(right))
        if has_other:
            total = total + refs[20][row].astype(F32)
        out[row] = total.astype(BF16)


def feed_grads(half_at, middle, mixed, ups, gates, gated, other=None):
    units, tokens = ups[0].shape
    depth, half = middle[0].shape[1], units // 2
    part = pl.BlockSpec((half, tokens), lambda i: (half_at, 0))
    more = () if other is None else (other,)
    return call(
        functools.partial(feed_grad_kernel, bool(more)),
        [shape((3, half, depth), BF16)],
        [WHOLE] * 4 + [NEAR] * 4 + [part] * 12 + [NEAR] * len(more),
        2 * 3 * 4 * tokens * half * depth,
        2 * 12 * tokens * (half + depth),
    )(*middle, *mixed, *ups, *gates, *gated, *more)[0]


def attend_grad_kernel(section, *refs):
    low, attended, hidden, grads = (refs[4 * n : 4 * n + 4] for n in range(4))
    own, other = refs[16:]
    width, half = attended[0].shape[0], own.shape[1]
    for lefts, rights, top in ((low, hidden, 0), (attended, grads, 3 * width)):
        right = jnp.concatenate([block[...] for block in rights], axis=0)
        for start in range(0, lefts[0].shape[0], width):
            total = mul(
                jnp.concatenate([left[start : start + width] for left in lefts], axis=1), right
            )
            rows = slice(top + start, top + start + width)
            for place in range(2):
                columns = total[:, place * half : place * half + half]

                @pl.when(section[0] == place)
                def _():
                    own[rows] = columns

                @pl.when(section[0] != place)
                def _():
                    other[rows] = columns.astype(BF16)


def attend_grads(section, low, attended, hidden, grads):
    width, tokens = attended[0].shape
    depth = hidden[0].shape[1]
    return call(
        attend_grad_kernel,
        [shape((4 * width, depth // 2), F32), shape((4 * width, depth // 2), BF16)],
        [SCALARS] + [WHOLE] * 12 + [NEAR] * 4,
        2 * 4 * 4 * tokens * width * depth,
        2 * 16 * tokens * depth,
    )(section, *low, *attended, *hidden, *grads)


def adam_kernel(axis, factor, weight, first, second, gradient, first_out, second_out, weight_out):
    clipped = gradient[...].astype(F32) * factor[0]
    first_new = BETA_FIRST * first[...] + (1.0 - BETA_FIRST) * clipped
    second_new = BETA_SECOND * second[...] + (1.0 - BETA_SECOND) * clipped * clipped
    first_out[...] = first_new
    second_out[...] = second_new
    first_hat = first_new / (1.0 - BETA_FIRST**STEP)
    second_hat = second_new / (1.0 - BETA_SECOND**STEP)
    moved = weight[...] - LEARN_RATE * first_hat / (jnp.sqrt(second_hat) + ADAM_EPSILON)
    scale = lax.rsqrt(jnp.sum(moved * moved, axis=axis, keepdims=True) + NORM_EPSILON)
    weight_out[...] = moved * scale


def adam_matrix(factor, weight, first, second, gradient, axis, block, place, grid):
    spec = pl.BlockSpec(block, place)
    return call(
        functools.partial(adam_kernel, axis),
        [shape(weight.shape, F32)] * 3,
        [SCALARS] + [spec] * 4,
        20 * weight.size,
        28 * weight.size,
        grid=grid,
        out_specs=[spec] * 3,
    )(factor, weight, first, second, gradient)


def add_parts(parts):
    total = parts[0][...].astype(F32)
    for part in parts[1:]:
        total = total + part[...].astype(F32)
    return total


def mix_kernel(count, hidden, rate, *refs):
    branch_out, result, result_low = refs[count:]
    branch = add_parts(refs[:count])
    branch_out[...] = branch
    mixed = mix_residual(hidden[...].astype(F32), branch, rate[...])
    result[...] = mixed
    result_low[...] = mixed.astype(BF16)


def mix_block(hidden, rate, parts):
    dims = hidden.shape
    return call(
        functools.partial(mix_kernel, len(parts)),
        [shape(dims, F32), shape(dims, F32), shape(dims, BF16)],
        [WHOLE] * 2 + [WHOLE if part.dtype == F32 else NEAR for part in parts],
        10 * dims[0] * dims[1],
        8 * dims[0] * dims[1],
    )(hidden, rate, *parts)


def mix_back_kernel(count, rounded, hidden, branch, rate, *refs):
    grad_hidden, grad_branch, grad_rate = refs[count:]
    upstream = add_parts(refs[:count])
    if rounded:
        upstream = upstream.astype(BF16).astype(F32)
    h, b, r = hidden[...].astype(F32), branch[...], rate[...]
    scale = lax.rsqrt(jnp.sum(b * b, axis=-1, keepdims=True) + NORM_EPSILON)
    unit = b * scale
    apart = unit - h
    mixed = h + r * apart
    mixed_scale = lax.rsqrt(jnp.sum(mixed * mixed, axis=-1, keepdims=True) + NORM_EPSILON)
    mixed = mixed * mixed_scale
    grad = mixed_scale * (upstream - mixed * jnp.sum(mixed * upstream, axis=-1, keepdims=True))
    grad_rate[...] = jnp.sum(grad * apart, axis=0, keepdims=True)
    grad_unit = grad * r
    grad_hidden[...] = grad - grad_unit
    grad_unit = scale * (grad_unit - unit * jnp.sum(unit * grad_unit, axis=-1, keepdims=True))
    grad_branch[...] = grad_unit.astype(BF16)


def mix_back_block(hidden, branch, rate, parts, rounded=False):
    dims = hidden.shape
    return call(
        functools.partial(mix_back_kernel, len(parts), rounded),
        [shape(dims, F32), shape(dims, BF16), shape((1, dims[1]), F32)],
        [WHOLE] * 3 + [WHOLE if part.dtype == F32 else NEAR for part in parts],
        20 * dims[0] * dims[1],
        12 * dims[0] * dims[1],
    )(hidden, branch, rate, *parts)


def tie(*values):
    return lax.optimization_barrier(values)


def to(block, at):
    return exchange(block, "mp", at)


def layer_forward(hidden, low, params, tables, tied, feed_weights):
    attend_in, attend_out, gains, scales, mixing = params
    cosine, sine, starts, info = tables
    project = lambda at: project_block(blocks[at], attend_in, cosine[at], sine[at], gains)
    blocks, heads = [low, to(low, 1), to(low, 2), None], [None] * 4
    if tied:
        heads[0] = project(0)
        low, heads[0] = tie(low, heads[0])
        blocks[3] = to(low, 3)
        blocks[1], blocks[2] = tie(blocks[1], blocks[2])
        heads[1], heads[2] = project(1), project(2)
        blocks[3], heads[1], heads[2] = tie(blocks[3], heads[1], heads[2])
        heads[3] = project(3)
    else:
        blocks[3] = to(low, 3)
        heads = [project(at) for at in range(4)]
    raw, query, keys, values = zip(*heads)
    attend = lambda at: attend_block(
        at, info, starts[at : at + 1], query[at], keys, values, attend_out
    )
    attended, sent = [None] * 4, [None] * 4
    for at in (3, 1, 2, 0):
        attended[at] = attend(at)
        if at:
            sent[at] = to(attended[at][-1], at)
    sent, attended[0] = tie(sent[1:], attended[0])
    branch, middle, middle_low = mix_block(hidden, mixing[:1], (attended[0][-1], *sent))
    blocks_middle, fed, parts, feed_weights = feed_exchange(
        middle_low, feed_weights, lambda at, block, weights: feed_block(at, block, weights, scales)
    )
    mixed, result, result_low = mix_block(middle, mixing[1:], parts)
    ups, gates, gated, _ = zip(*fed)
    attended, logsums, _ = zip(*attended)
    stored = (
        (hidden, branch, blocks, raw, query, keys, values, attended, logsums),
        (middle, mixed, blocks_middle, ups, gates, gated),
    )
    return result, result_low, stored, feed_weights


def feed_exchange(block, weights, work):
    blocks = [block, to(block, 1), to(block, 2), None]
    if callable(weights):
        block, weights = weights(block)
    done = [work(0, block, weights)] + [None] * 3
    sent = [None] * 4
    block, done[0] = tie(block, done[0])
    blocks[3] = to(block, 3)
    blocks[1], blocks[2] = tie(blocks[1], blocks[2])
    done[1] = work(1, blocks[1], weights)
    sent[1] = to(done[1][-1], 1)
    blocks[2], done[1] = tie(blocks[2], done[1])
    done[2] = work(2, blocks[2], weights)
    sent[2] = to(done[2][-1], 2)
    blocks[3], done[2] = tie(blocks[3], done[2])
    done[3] = work(3, blocks[3], weights)
    sent[3] = to(done[3][-1], 3)
    return blocks, done, (done[0][-1], *sent[1:]), weights


def layer_backward(stored, upstream, rounded, params, tables, feed_weights, section):
    attend_in, attend_out, gains, scales, mixing = params
    cosine, sine, starts, info = tables
    attend_stored, (middle, mixed, blocks_middle, ups, gates, gated) = stored
    hidden, branch, blocks_hidden, raw, query, keys, values, attended, logsums = attend_stored
    grad_middle, grad_mixed, rate_two = mix_back_block(
        middle, mixed, mixing[1:], upstream, rounded
    )
    blocks_mixed, done, parts, _ = feed_exchange(
        grad_mixed, feed_weights,
        lambda at, block, weights: feed_back_block(at, block, weights, scales, ups[at], gates[at]),
    )
    low_ups, low_gates, scale_grads, _ = zip(*done)
    operands = (blocks_middle, blocks_mixed, low_ups, low_gates, gated)
    other = feed_grads(1, *operands)
    parts, other = tie(parts, other)
    other = exchange(other, "section", 1)
    grad_hidden, grad_branch, rate_one = mix_back_block(
        hidden, branch, mixing[:1], (grad_middle, *parts)
    )
    near = [to(grad_branch, at) for at in (3, 1, 2)]
    feed_sums = feed_grads(0, *operands, other)
    near, feed_sums = tie(near, feed_sums)
    grads = [grad_branch, near[1], near[2], near[0]]
    low, partial, gain_grad = attend_back(
        info, starts, query, keys, values, attended, logsums, raw, grads,
        attend_out, attend_in, cosine, sine, gains,
    )
    sent = [to(partial[at], at) for at in (3, 1, 2)]
    own, other = attend_grads(section, low, attended, blocks_hidden, grads)
    sent[0], own, other = tie(sent[0], own, other)
    other = exchange(other, "section", 1)
    attend_sums = (own + other.astype(F32)).astype(BF16).reshape(4, -1, own.shape[1])
    small = (sum(scale_grads), rate_one[0], rate_two[0])
    return (grad_hidden, partial[0], *sent), feed_sums, attend_sums, gain_grad[:, 0], small


def adam_update(weight, first, second, gradient, factor, rate):
    clipped = gradient * factor
    first_new = BETA_FIRST * first + (1.0 - BETA_FIRST) * clipped
    second_new = BETA_SECOND * second + (1.0 - BETA_SECOND) * clipped * clipped
    first_hat = first_new / (1.0 - BETA_FIRST**STEP)
    second_hat = second_new / (1.0 - BETA_SECOND**STEP)
    moved = weight - rate * first_hat / (jnp.sqrt(second_hat) + ADAM_EPSILON)
    return (first_new, second_new, moved)


def per_device(
    inputs,
    cotangent,
    doc_ids,
    attention_in,
    attention_out,
    feedforward_in,
    feedforward_out,
    unit_scales,
    mix_rates,
    first_attention_in,
    second_attention_in,
    first_attention_out,
    second_attention_out,
    first_feedforward_in,
    second_feedforward_in,
    first_feedforward_out,
    second_feedforward_out,
    first_unit_scales,
    second_unit_scales,
    first_mix_rates,
    second_mix_rates,
):
    section = lax.axis_index("section")
    is_first = section == 0
    dp_index = lax.axis_index("dp")
    dp_size = lax.axis_size("dp")
    local_rows = inputs.shape[1]

    def ordered(own, other):
        return jnp.where(is_first, own, other), jnp.where(is_first, other, own)

    def halves(array, dim):
        width = array.shape[dim] // 2
        own = lax.dynamic_slice_in_dim(array, section * width, width, dim)
        other = lax.dynamic_slice_in_dim(array, (1 - section) * width, width, dim)
        return own, other

    hidden_low = lax.dynamic_index_in_dim(inputs, section, 0, False)

    attend_rows = jnp.concatenate(
        [jnp.swapaxes(attention_in[0], 1, 2), attention_out], axis=0
    ).astype(BF16)
    small = jnp.concatenate([unit_scales.reshape(-1), mix_rates.reshape(-1)]).astype(BF16)
    def gather_ring(half):
        blocks = spread_rows(half, "dp")
        count = half.shape[1]
        whole = jnp.zeros((half.shape[0], dp_size * count, half.shape[2]), BF16)
        for source, block in zip(ring_sources("dp"), blocks):
            whole = lax.dynamic_update_slice_in_dim(whole, block, source * count, 1)
        return whole, blocks[-2]

    own, other = halves(attend_rows, 2)
    attend_pieces = ordered(own, exchange(other, "section", 1))
    attend_pieces, feedforward_in_here, feedforward_out_here = tie(
        attend_pieces, feedforward_in, feedforward_out
    )
    feed_rows = jnp.concatenate(
        [jnp.swapaxes(feedforward_in_here[0].astype(BF16), 1, 2), feedforward_out_here.astype(BF16)], axis=0
    )
    own, other = halves(feed_rows, 1)
    feed_pieces = ordered(own, exchange(other, "section", 1))
    if dp_size <= 4:
        attend_first, step = gather_ring(attend_pieces[0])
        attend_second, *feed_pieces, _ = tie(attend_pieces[1], *feed_pieces, step)
    else:
        attend_first = lax.all_gather(attend_pieces[0], "dp", axis=1, tiled=True)
        attend_second = attend_pieces[1]
    attend_pieces = (attend_first, lax.all_gather(attend_second, "dp", axis=1, tiled=True))
    small = jnp.stack(ordered(small, exchange(small, "section", 1))).reshape(-1)
    small = gather_small(small, "dp").astype(F32)
    small = small.reshape(dp_size, 2, -1)
    units_here = unit_scales.shape[2]

    def units_apart(values):
        parts = values.reshape(dp_size, 2, -1)
        own, other = ordered(parts[:, 0], parts[:, 1])
        return jnp.concatenate([own.reshape(-1), other.reshape(-1)])

    def units_back(values):
        parts = values.reshape(2, dp_size, -1)
        own, other = ordered(parts[0], parts[1])
        return jnp.stack([own, other], axis=1).reshape(-1)

    layers, feed_owns = [], []
    for layer in range(2):
        own = attend_pieces[layer]
        attend = jnp.concatenate(ordered(own, exchange(own, "section", 1)), axis=2)
        feed_own = lax.all_gather(feed_pieces[layer], "dp", axis=1, tiled=True)
        units = small[:, layer, :units_here].reshape(-1)
        mixing = small[:, layer, units_here:].reshape(dp_size, 2, -1)
        mixing = jnp.swapaxes(mixing, 0, 1).reshape(2, -1)
        width_qk, width_ff = attend.shape[1], 2 * feed_own.shape[1]
        layers.append((
            attend[:3].reshape(3 * width_qk, -1), attend[3],
            units[:width_qk, None],
            jnp.stack([
                units_apart(units[width_qk : width_qk + width_ff]),
                units_apart(units[width_qk + width_ff :]),
            ]),
            mixing,
        ))
        feed_owns.append(feed_own)

    doc_row = lax.dynamic_index_in_dim(doc_ids, section, 0, False)
    starts_all = document_starts(doc_row)
    mp_index = lax.axis_index("mp")
    sources = [mp_index ^ offset for offset in range(4)]
    places = jnp.arange(local_rows, dtype=jnp.int32)
    starts = jnp.stack([
        lax.dynamic_slice_in_dim(starts_all, source * local_rows, local_rows, 0)
        for source in sources
    ])
    sources = jnp.stack(sources).astype(jnp.int32)
    cosine, sine = rope_tables(sources[:, None] * local_rows + places - starts)
    info = jnp.concatenate([sources, starts[:, 0]])
    tables = (cosine, sine, starts, info)

    def scatter(sums):
        return lax.psum_scatter(sums, "dp", scatter_dimension=1, tiled=True)

    def scatter_ring(sums):
        if dp_size > 4:
            return scatter(sums)
        count = sums.shape[1] // dp_size
        parts = [
            lax.dynamic_slice_in_dim(sums, source * count, count, 1).astype(F32)
            for source in ring_sources("dp")
        ]
        return collect_rows(parts, "dp").astype(BF16)

    def weights_ready(own, value):
        value, own = tie(value, own)
        return value, (own, exchange(own, "section", 1))

    def small_vector(scales, rate_one, rate_two):
        return jnp.concatenate([units_back(scales[0]), units_back(scales[1]), rate_one, rate_two])

    first, second = layers
    section_ref = section.astype(jnp.int32).reshape(1)
    grad = lax.dynamic_index_in_dim(cotangent, section, 0, False)
    _, hidden_second, stored_first, weights_first = layer_forward(
        hidden_low, hidden_low, first, tables, False, functools.partial(weights_ready, feed_owns[0])
    )
    result, _, stored_second, weights_second = layer_forward(
        hidden_second, hidden_second, second, tables, True,
        functools.partial(weights_ready, feed_owns[1]),
    )
    parts, feed_second, attend_second, gains_second, small_second = layer_backward(
        stored_second, (grad,), False, second, tables, weights_second, section_ref
    )
    feed_second = scatter(feed_second)
    parts, attend_second = tie(parts, attend_second)
    attend_second = scatter(attend_second)
    parts, feed_first, attend_first, gains_first, small_first = layer_backward(
        stored_first, parts, True, first, tables, weights_first, section_ref
    )
    feed_first = scatter(feed_first)
    attend_first, feed_second, attend_second = tie(attend_first, feed_second, attend_second)
    attend_first = scatter_ring(attend_first)
    grad = sum(part.astype(F32) for part in parts)

    reduced_first = (attend_first, feed_first)
    reduced_second = (attend_second, feed_second)
    squares = sum(
        jnp.sum(jnp.square(part.astype(F32))) for part in (*reduced_first, *reduced_second)
    )
    gradients = []
    for one, two, dim in zip(reduced_first, reduced_second, (2, 1)):
        own, other = jnp.where(is_first, one, two), jnp.where(is_first, two, one)
        other = exchange(other, "section", 1)
        gradients.append(jnp.concatenate(ordered(own, other), axis=dim))

    sums = jnp.stack([small_vector(*small_first), small_vector(*small_second)])
    sums = sum_over(sum_over(sums, "section"), "dp")
    width_qk = gains_first.shape[0]
    scale_sums, rate_sums = sums[:, : dp_size * units_here - width_qk], sums[:, dp_size * units_here - width_qk :]
    rate_sums = sum_over(rate_sums, "mp").reshape(2, 2, -1)
    gain_sums = sum_over(sum_over(jnp.stack([gains_first, gains_second]), "section"), "dp")
    unit_grads = jnp.concatenate([gain_sums, scale_sums], axis=1)
    unit_grads = jnp.where(is_first, unit_grads[0], unit_grads[1])
    unit_grads = lax.dynamic_slice_in_dim(unit_grads, dp_index * units_here, units_here, 0)
    unit_grads = unit_grads[None, None]
    rates_here = mix_rates.shape[2]
    rate_grads = jnp.where(is_first, rate_sums[0], rate_sums[1])
    rate_grads = lax.dynamic_slice_in_dim(rate_grads, dp_index * rates_here, rates_here, 1)[None]

    turn = lambda array: jnp.swapaxes(array, 1, 2)
    attend_grad, feed_grad = gradients
    feed_in_grad = turn(feed_grad[:2])
    squares, attend_grad, feed_grad, feed_in_grad = tie(
        squares, attend_grad, feed_grad, feed_in_grad
    )
    leading = (mp_index == 0).astype(F32)
    squares = squares + jnp.sum(unit_grads * unit_grads)
    squares = squares + leading * jnp.sum(rate_grads * rate_grads)
    squares = squares.reshape(1)
    squares = squares + exchange(squares, "section", 1)
    squares = sum_over(sum_over(squares, "mp"), "dp")
    gradient_norm = jnp.sqrt(squares[0])
    factor = CLIP_NORM / jnp.maximum(gradient_norm, CLIP_NORM)

    to_send = jnp.where(is_first, result, grad)
    kept = jnp.where(is_first, grad, result)
    arrived = exchange(to_send, "section", 1)
    boundary_states = jnp.stack(ordered(kept, arrived))[None]

    scalar = factor.reshape(1)
    updates = []
    new = adam_matrix(
        scalar, turn(attention_in[0]), turn(first_attention_in[0]), turn(second_attention_in[0]),
        attend_grad[:3], 2, (1, *attend_grad.shape[1:]), lambda i: (i, 0, 0), (3,),
    )
    updates.extend(turn(part)[None] for part in new)
    updates.extend(adam_matrix(
        scalar, attention_out, first_attention_out, second_attention_out, attend_grad[3:],
        2, attention_out.shape, lambda i: (0, 0, 0), (1,),
    ))
    new = adam_matrix(
        scalar, feedforward_in[0], first_feedforward_in[0], second_feedforward_in[0],
        feed_in_grad, 1, (1, *feedforward_in.shape[2:]), lambda i: (i, 0, 0), (2,),
    )
    updates.extend(part[None] for part in new)
    steps = 4 if feedforward_out.shape[1] % 64 == 0 else 1
    updates.extend(adam_matrix(
        scalar, feedforward_out, first_feedforward_out, second_feedforward_out, feed_grad[2:],
        2, (1, feedforward_out.shape[1] // steps, feedforward_out.shape[2]),
        lambda i: (0, i, 0), (steps,),
    ))
    updates.extend(
        adam_update(
            unit_scales, first_unit_scales, second_unit_scales, unit_grads, factor, SCALE_RATE
        )
    )
    updates.extend(
        adam_update(
            mix_rates, first_mix_rates, second_mix_rates, rate_grads, factor, MIXING_RATE
        )
    )
    return (boundary_states, gradient_norm, *updates)


def solution(mesh):
    in_specs = (
        P("dp", "mp", None),
        P("dp", "mp", None),
        P("dp", None),
        P("section", None, None, ("mp", "dp")),
        P("section", ("mp", "dp"), None),
        P("section", None, None, ("mp", "dp")),
        P("section", ("mp", "dp"), None),
        P("section", "mp", "dp"),
        P("section", None, "dp"),
        P("section", None, None, ("mp", "dp")),
        P("section", None, None, ("mp", "dp")),
        P("section", ("mp", "dp"), None),
        P("section", ("mp", "dp"), None),
        P("section", None, None, ("mp", "dp")),
        P("section", None, None, ("mp", "dp")),
        P("section", ("mp", "dp"), None),
        P("section", ("mp", "dp"), None),
        P("section", "mp", "dp"),
        P("section", "mp", "dp"),
        P("section", None, "dp"),
        P("section", None, "dp"),
    )
    out_specs = (
        P("section", "dp", "mp", None),
        P(),
        P("section", None, None, ("mp", "dp")),
        P("section", None, None, ("mp", "dp")),
        P("section", None, None, ("mp", "dp")),
        P("section", ("mp", "dp"), None),
        P("section", ("mp", "dp"), None),
        P("section", ("mp", "dp"), None),
        P("section", None, None, ("mp", "dp")),
        P("section", None, None, ("mp", "dp")),
        P("section", None, None, ("mp", "dp")),
        P("section", ("mp", "dp"), None),
        P("section", ("mp", "dp"), None),
        P("section", ("mp", "dp"), None),
        P("section", "mp", "dp"),
        P("section", "mp", "dp"),
        P("section", "mp", "dp"),
        P("section", None, "dp"),
        P("section", None, "dp"),
        P("section", None, "dp"),
    )
    return jax.shard_map(
        per_device, mesh=mesh, in_specs=in_specs, out_specs=out_specs, check_vma=False
    )
```

```python
import functools
import math

import jax
import jax.numpy as jnp
from jax import lax
from jax.experimental import pallas as pl
from jax.experimental.pallas import tpu as pltpu
from jax.sharding import PartitionSpec as P

HD = 64
STEP = 10

NORM_EPSILON = 1e-06
ROPE_BASE = 10000.0
CLIP_NORM = 0.1
LEARN_RATE = 0.05
SCALE_RATE = 1.25
MIXING_RATE = 0.4
BETA_FIRST = 0.9
BETA_SECOND = 0.95
ADAM_EPSILON = 1e-08

BF16 = jnp.bfloat16
F32 = jnp.float32


def exchange(block, axis, bit):
    route = [(i, i ^ bit) for i in range(lax.axis_size(axis))]
    return lax.ppermute(block, axis, route)


def gray(place):
    return place ^ (place >> 1)


def ring_place(index, size):
    shift = 1
    while shift < size:
        index = index ^ (index >> shift)
        shift *= 2
    return index


def ring_step(block, axis):
    size = lax.axis_size(axis)
    route = []
    for place in range(size):
        route.append((gray(place), gray((place + 1) % size)))
        route.append((size + gray(place), size + gray((place - 1) % size)))
    return lax.ppermute(block, ("section", axis), route)


def ring_sources(axis):
    size = lax.axis_size(axis)
    place = ring_place(lax.axis_index(axis), size)
    way = 1 - 2 * lax.axis_index("section")
    return [gray((place - way * step + size) % size) for step in range(size)]


def spread_rows(block, axis="mp"):
    blocks = [block]
    for _ in range(lax.axis_size(axis) - 1):
        blocks.append(ring_step(blocks[-1], axis))
    return blocks


def sum_over(values, axis):
    bit = 1
    while bit < lax.axis_size(axis):
        values = values + exchange(values, axis, bit)
        bit *= 2
    return values


def gather_small(values, axis):
    index = lax.axis_index(axis)
    gathered = values[None]
    bit = 1
    while bit < lax.axis_size(axis):
        other = exchange(gathered, axis, bit)
        low = (index & bit) == 0
        gathered = jnp.concatenate(
            [jnp.where(low, gathered, other), jnp.where(low, other, gathered)], axis=0
        )
        bit *= 2
    return gathered


def unit_norm(values):
    return values * lax.rsqrt(jnp.sum(values * values, axis=-1, keepdims=True) + NORM_EPSILON)


def document_starts(doc_row):
    position = jnp.arange(doc_row.shape[-1], dtype=jnp.int32)
    change = jnp.concatenate([jnp.ones((1,), dtype=jnp.bool_), doc_row[1:] != doc_row[:-1]])
    return lax.cummax(jnp.where(change, position, 0), axis=0)


def rope_tables(offsets):
    half_width = HD // 2
    inverse = 1.0 / ROPE_BASE ** (jnp.arange(half_width, dtype=F32) * (2.0 / HD))
    angles = inverse[:, None] * offsets.astype(F32)[..., None, :]
    angles = jnp.concatenate([angles, angles], axis=-2)
    return jnp.cos(angles), jnp.sin(angles)


def mix_residual(hidden, branch, mixing):
    return unit_norm(hidden + mixing * (unit_norm(branch) - hidden))


NT = (((1,), (1,)), ((), ()))
TN = (((0,), (0,)), ((), ()))
NN = (((1,), (0,)), ((), ()))
VMEM = pltpu.VMEM
WHOLE, NEAR = "whole", "near"
SCALARS = pl.BlockSpec(memory_space=pltpu.SMEM)


def mul(left, right, dims=NN):
    return lax.dot_general(left, right, dims, preferred_element_type=F32)


def block_of(array):
    zeros = (0,) * len(array.shape)
    return pl.BlockSpec(array.shape, lambda *place: zeros)


def call(body, out_shape, in_specs, flops, moved, scratch=(), grid=(1,), out_specs=None, loose=()):
    def run(*args):
        specs = [
            block_of(arg) if spec in (WHOLE, NEAR) else spec for spec, arg in zip(in_specs, args)
        ]
        args = [
            arg if spec in (SCALARS, NEAR) else pltpu.with_memory_space_constraint(arg, pltpu.HBM)
            for spec, arg in zip(in_specs, args)
        ]
        return pl.pallas_call(
            body,
            out_shape=[
                out if at in loose else pltpu.HBM(out.shape, out.dtype)
                for at, out in enumerate(out_shape)
            ],
            grid=grid,
            in_specs=specs,
            out_specs=out_specs or [block_of(out) for out in out_shape],
            scratch_shapes=list(scratch),
            compiler_params=pltpu.CompilerParams(vmem_limit_bytes=50 << 20),
            cost_estimate=pl.CostEstimate(flops=flops, bytes_accessed=moved, transcendentals=0),
        )(*args)

    return run


def shape(dims, dtype):
    return jax.ShapeDtypeStruct(dims, dtype)


def turned(raw, cosine, sine):
    half = HD // 2
    first, second = raw[:half], raw[half:]
    return jnp.concatenate(
        [
            first * cosine[:half] - second * sine[:half],
            second * cosine[half:] + first * sine[half:],
        ],
        axis=0,
    )


def turned_back(grad, cosine, sine):
    half = HD // 2
    first, second = grad[:half], grad[half:]
    return jnp.concatenate(
        [
            first * cosine[:half] + second * sine[half:],
            second * cosine[half:] - first * sine[:half],
        ],
        axis=0,
    )


def project_kernel(places, *refs):
    count = len(places)
    x, (weight, cosine, sine, gains), outs = refs[:count], refs[count : count + 4], refs[count + 4 :]
    for n, at in enumerate(places):
        raw_out, query, keys, values = outs[4 * n : 4 * n + 4]
        width = query.shape[0]
        raw = mul(weight[...], x[n][...], NT)
        raw_out[...] = raw[: 2 * width]
        values[...] = raw[2 * width :].astype(BF16)
        for part, out in ((0, query), (1, keys)):
            for top in range(0, width, HD):
                turn = turned(
                    raw[part * width + top : part * width + top + HD], cosine[at], sine[at]
                )
                scale = lax.rsqrt(jnp.sum(turn * turn, axis=0, keepdims=True) + NORM_EPSILON)
                head = (turn * scale * gains[top : top + HD]).astype(BF16)
                out[top : top + HD] = head * math.sqrt(HD) if part == 0 else head


def project_blocks(places, x, weight, cosine, sine, gains):
    tokens, depth = x[0].shape
    width = weight.shape[0] // 3
    low = shape((width, tokens), BF16)
    outs = call(
        functools.partial(project_kernel, places),
        [shape((2 * width, tokens), F32), low, low, low] * len(x),
        [NEAR] * len(x) + [WHOLE] * 4,
        2 * tokens * depth * 3 * width * len(x),
        2 * 3 * width * depth,
    )(*x, weight, cosine, sine, gains)
    return [outs[4 * n : 4 * n + 4] for n in range(len(x))]


def near(info, at, other, tokens):
    return (info[other] <= info[at]) & ((info[other] + 1) * tokens > info[4 + at])


def seen(info, at, other, starts, tokens):
    key_place = info[other] * tokens + lax.broadcasted_iota(jnp.int32, (tokens, tokens), 0)
    query_place = info[at] * tokens + lax.broadcasted_iota(jnp.int32, (tokens, tokens), 1)
    return (key_place <= query_place) & (key_place >= starts)


def share_out(partial, value):
    partial[...] = value.astype(partial.dtype)


def partial_shape(at, tokens, depth):
    return shape((tokens, depth), BF16 if at else F32)


def attend_kernel(places, info, starts, *refs):
    count = len(places)
    query, rest = refs[:count], refs[count:]
    keys, values, weight, outs, (total, sums) = rest[:4], rest[4:8], rest[8], rest[9:-2], rest[-2:]
    width, tokens = query[0].shape
    for n, at in enumerate(places):
        attended, logsums, partial = outs[3 * n : 3 * n + 3]
        total[n] = jnp.zeros((width, tokens), F32)
        sums[n] = jnp.ones((8, tokens), F32)
        sums[n, : width // HD] = jnp.zeros((width // HD, tokens), F32)
        for other in range(4):

            @pl.when(near(info, at, other, tokens))
            def _():
                allowed = seen(info, at, other, starts[at : at + 1], tokens)
                for head in range(width // HD):
                    rows = slice(head * HD, head * HD + HD)
                    shares = jnp.exp(mul(keys[other][rows], query[n][rows], TN))
                    shares = jnp.where(allowed, shares, 0.0)
                    sums[n, head : head + 1] += jnp.sum(shares, axis=0, keepdims=True)
                    total[n, rows] += mul(values[other][rows], shares.astype(BF16))

        logsums[...] = jnp.log(sums[n])
        inverse = 1.0 / sums[n]
        for head in range(width // HD):
            rows = slice(head * HD, head * HD + HD)
            attended[rows] = (total[n, rows] * inverse[head : head + 1]).astype(BF16)
        share_out(partial, mul(attended[...], weight[...], TN))


def attend_blocks(places, info, starts, query, keys, values, weight):
    width, tokens = query[0].shape
    depth, count = weight.shape[1], len(places)
    outs = call(
        functools.partial(attend_kernel, places),
        [
            out
            for at in places
            for out in (
                shape((width, tokens), BF16),
                shape((8, tokens), F32),
                partial_shape(at, tokens, depth),
            )
        ],
        [SCALARS] + [WHOLE] * (10 + count),
        2 * tokens * (depth * width + 10 * tokens * 256) * count,
        2 * depth * width,
        [VMEM((count, width, tokens), F32), VMEM((count, 8, tokens), F32)],
        loose=[3 * n + 2 for n, at in enumerate(places) if at],
    )(info, starts, *[query[at] for at in places], *keys, *values, weight)
    return [outs[3 * n : 3 * n + 3] for n in range(count)]


def attend_back_kernel(info, starts, *refs):
    query, keys, values, attended, logsums, raw, grads = (refs[4 * n : 4 * n + 4] for n in range(7))
    w_out, w_in, cosine, sine, gains = refs[28:33]
    low, partial, gain_grad = refs[33:37], refs[37:41], refs[41]
    pulled, deltas, grad_query, grad_keys, grad_values = refs[42:]
    width, tokens = query[0].shape
    heads = width // HD
    grad_query[...] = jnp.zeros_like(grad_query)
    grad_keys[...] = jnp.zeros_like(grad_keys)
    grad_values[...] = jnp.zeros_like(grad_values)
    deltas[...] = jnp.zeros_like(deltas)
    for at in range(4):
        grad = mul(w_out[...], grads[at][...], NT).astype(BF16)
        pulled[at] = grad
        product = grad.astype(F32) * attended[at][...].astype(F32)
        for head in range(heads):
            rows = slice(head * HD, head * HD + HD)
            deltas[at, head : head + 1] = jnp.sum(product[rows], axis=0, keepdims=True)
    for at in range(4):
        for other in range(4):

            @pl.when(near(info, at, other, tokens))
            def _():
                allowed = seen(info, at, other, starts[at : at + 1], tokens)
                for head in range(heads):
                    rows = slice(head * HD, head * HD + HD)
                    grad_rows, query_rows = pulled[at, rows], query[at][rows]
                    scores = mul(keys[other][rows], query_rows, TN) - logsums[at][head : head + 1]
                    shares = jnp.where(allowed, jnp.exp(scores), 0.0)
                    grad_shares = mul(values[other][rows], grad_rows, TN)
                    grad_scores = shares * (grad_shares - deltas[at, head : head + 1])
                    grad_scores = grad_scores.astype(BF16)
                    grad_values[other, rows] += mul(grad_rows, shares.astype(BF16), NT)
                    grad_keys[other, rows] += mul(query_rows, grad_scores, NT)
                    grad_query[at, rows] += mul(keys[other][rows], grad_scores)

    gain_total = [0.0] * heads
    for at in range(4):
        cos, sin = cosine[at], sine[at]
        for part, source, factor in ((0, grad_query, math.sqrt(HD)), (1, grad_keys, 1.0)):
            for head in range(heads):
                rows = slice(head * HD, head * HD + HD)
                turn = turned(raw[at][part * width + head * HD : part * width + head * HD + HD], cos, sin)
                scale = lax.rsqrt(jnp.sum(turn * turn, axis=0, keepdims=True) + NORM_EPSILON)
                unit = turn * scale
                grad = source[at, rows] * factor
                gain_total[head] = gain_total[head] + grad * unit
                grad = grad * gains[rows]
                grad = scale * (grad - unit * jnp.sum(unit * grad, axis=0, keepdims=True))
                low[at][part * width + head * HD : part * width + head * HD + HD] = turned_back(
                    grad, cos, sin
                ).astype(BF16)
        low[at][2 * width :] = grad_values[at].astype(BF16)
        share_out(partial[at], mul(low[at][...], w_in[...], TN))
    for head in range(heads):
        gain_grad[head * HD : head * HD + HD] = jnp.sum(gain_total[head], axis=1, keepdims=True)


def attend_back(info, starts, query, keys, values, attended, logsums, raw, grads,
                w_out, w_in, cosine, sine, gains):
    width, tokens = query[0].shape
    depth = w_out.shape[1]
    low = shape((3 * width, tokens), BF16)
    block = VMEM((4, width, tokens), F32)
    outs = call(
        attend_back_kernel,
        [low] * 4
        + [partial_shape(at, tokens, depth) for at in range(4)]
        + [shape((width, 1), F32)],
        [SCALARS] + [WHOLE] * 25 + [NEAR] * 4 + [WHOLE] * 5,
        2 * 4 * tokens * (depth * width * 4 + 60 * tokens * 256),
        2 * depth * width * 12,
        [VMEM((4, width, tokens), BF16), VMEM((4, 8, tokens), F32), block, block, block],
        loose=(5, 6, 7),
    )(info, starts, *query, *keys, *values, *attended, *logsums, *raw, *grads,
      w_out, w_in, cosine, sine, gains)
    return outs[:4], outs[4:8], outs[8]


CHUNK = 256
GATE_WIDTH = math.sqrt(1024)


def started(copies, arrived, first=0):
    copies = [
        pltpu.make_async_copy(source, target, arrived.at[first + n])
        for n, (source, target) in enumerate(copies)
    ]
    for copy in copies:
        copy.start()
    return copies


def fetch_weights(own, other, weights, arrived):
    half = own.shape[1]
    size = min(CHUNK, half)
    places = [(index, start) for index in range(2) for start in range(0, half, size)]
    copies = started(
        [
            ((own, other)[index].at[:, pl.ds(start, size)], weights.at[index, :, pl.ds(start, size)])
            for index, start in places
        ],
        arrived,
    )
    return [
        (copy, index, slice(start, start + size), slice(index * half + start, index * half + start + size))
        for copy, (index, start) in zip(copies, places)
    ]


def side_by_side(refs):
    return refs[0][...] if len(refs) == 1 else jnp.concatenate([ref[...] for ref in refs], axis=0)


def feed_kernel(count, *refs):
    x, (own, other, scales_in) = refs[:count], refs[count : count + 3]
    outs, partial = refs[count + 3 : 4 * count + 3], refs[4 * count + 3 : 5 * count + 3]
    weights, scales, ups, gates, gated, gated_turned, arrived, came, left = refs[5 * count + 3 :]
    half, tokens = own.shape[1], x[0].shape[0]
    (scales_copy,) = started([(scales_in, scales)], came)
    chunks = fetch_weights(own, other, weights, arrived)
    block = side_by_side(x)
    scales_copy.wait()
    leaving = []
    for copy, index, rows, units in chunks:
        copy.wait()
        up, gate = mul(block, weights[index, 0, rows], NT), mul(block, weights[index, 1, rows], NT)
        ups[:, units] = up.astype(BF16)
        gates[:, units] = gate.astype(BF16)
        z = gate * (scales[1:2, units] * GATE_WIDTH)
        silu = z * (0.5 + 0.5 * jnp.tanh(0.5 * z))
        mixed = (up * scales[0:1, units] * silu).astype(BF16)
        gated[:, units] = mixed
        gated_turned[units] = mixed.T
        if rows.stop == half:
            columns = pl.ds(index * half, half)
            for n in range(count):
                places = pl.ds(n * tokens, tokens)
                leaving += started(
                    [
                        (ups.at[places, columns], outs[3 * n].at[:, columns]),
                        (gates.at[places, columns], outs[3 * n + 1].at[:, columns]),
                        (gated_turned.at[columns, places], outs[3 * n + 2].at[columns]),
                    ],
                    left,
                    3 * (index * count + n),
                )
    total = mul(gated[:, :half], weights[0, 2]) + mul(gated[:, half:], weights[1, 2])
    for n in range(count):
        share_out(partial[n], total[n * tokens : (n + 1) * tokens])
    for copy in leaving:
        copy.wait()


def feed_back_kernel(count, *refs):
    g, (own, other, scales_in) = refs[:count], refs[count : count + 3]
    kept = refs[count + 3 : 3 * count + 3]
    outs, scale_grad = refs[3 * count + 3 : 5 * count + 3], refs[5 * count + 3]
    partial = refs[5 * count + 4 : 6 * count + 4]
    weights, scales, ups, gates, low_up, low_gate, up_turned, gate_turned = refs[6 * count + 4 : -3]
    arrived, came, left = refs[-3:]
    half, tokens = own.shape[1], g[0].shape[0]
    (scales_copy,) = started([(scales_in, scales)], came)
    chunks = fetch_weights(own, other, weights, arrived)
    coming = [
        started(
            [
                (ref.at[:, pl.ds(index * half, half)],
                 into.at[pl.ds(n * tokens, tokens), pl.ds(index * half, half)])
                for n in range(count)
                for ref, into in ((kept[2 * n], ups), (kept[2 * n + 1], gates))
            ],
            came,
            1 + 2 * count * index,
        )
        for index in range(2)
    ]
    block = side_by_side(g)
    scales_copy.wait()
    leaving = []
    for copy, index, rows, units in chunks:
        copy.wait()
        grad = mul(block, weights[index, 2, rows], NT)
        if rows.start == 0:
            for copy in coming[index]:
                copy.wait()
        up, gate = ups[:, units].astype(F32), gates[:, units].astype(F32)
        s_up, s_gate = scales[0:1, units], scales[1:2, units] * GATE_WIDTH
        z = gate * s_gate
        sigmoid = 0.5 + 0.5 * jnp.tanh(0.5 * z)
        silu = z * sigmoid
        grad_silu = grad * silu
        grad_z = grad * (up * s_up) * (sigmoid + silu * (1.0 - sigmoid))
        grad_up, grad_gate = (grad_silu * s_up).astype(BF16), (grad_z * s_gate).astype(BF16)
        low_up[:, units], low_gate[:, units] = grad_up, grad_gate
        up_turned[units], gate_turned[units] = grad_up.T, grad_gate.T
        scale_grad[0:1, units] = jnp.sum(grad_silu * up, axis=0, keepdims=True)
        scale_grad[1:2, units] = jnp.sum(grad_z * gate, axis=0, keepdims=True) * GATE_WIDTH
        if rows.stop == half:
            columns = pl.ds(index * half, half)
            for n in range(count):
                places = pl.ds(n * tokens, tokens)
                leaving += started(
                    [
                        (up_turned.at[columns, places], outs[2 * n].at[columns]),
                        (gate_turned.at[columns, places], outs[2 * n + 1].at[columns]),
                    ],
                    left,
                    2 * (index * count + n),
                )
    total = mul(low_up[:, :half], weights[0, 0]) + mul(low_up[:, half:], weights[1, 0])
    total = total + mul(low_gate[:, :half], weights[0, 1]) + mul(low_gate[:, half:], weights[1, 1])
    for n in range(count):
        share_out(partial[n], total[n * tokens : (n + 1) * tokens])
    for copy in leaving:
        copy.wait()


HELD = pl.BlockSpec(memory_space=pl.ANY)


def feed_call(body, places, x, weights, scales, kept, held, pair, low, turned_count):
    tokens, depth = x[0].shape
    half, count = weights[0].shape[1], len(x)
    partial = [partial_shape(at, tokens, depth) for at in places]
    semaphores = pltpu.SemaphoreType.DMA
    return call(
        functools.partial(body, count),
        held + pair + partial,
        [NEAR] * count + [HELD] * (3 + len(kept)),
        2 * 6 * tokens * depth * half * count,
        2 * 6 * depth * half,
        [VMEM((2, 3, half, depth), BF16), VMEM(scales.shape, F32)]
        + [VMEM((count * tokens, 2 * half), BF16)] * low
        + [VMEM((2 * half, count * tokens), BF16)] * turned_count
        + [
            semaphores((2 * half // min(CHUNK, half),)),
            semaphores((1 + 2 * len(kept),)),
            semaphores((2 * len(held),)),
        ],
        out_specs=[HELD] * len(held) + [block_of(out) for out in pair + partial],
        loose=[len(held + pair) + n for n, at in enumerate(places) if at],
    )(*x, *weights, scales, *kept)


def feed_blocks(places, x, weights, scales):
    dims, count = (x[0].shape[0], 2 * weights[0].shape[1]), len(x)
    held = [shape(dims, BF16), shape(dims, BF16), shape(dims[::-1], BF16)] * count
    outs = feed_call(feed_kernel, places, x, weights, scales, (), held, [], 3, 1)
    return [[*outs[3 * n : 3 * n + 3], outs[3 * count + n]] for n in range(count)]


def feed_back_blocks(places, g, weights, scales, ups, gates):
    count = len(g)
    held = [shape(ups[0].shape[::-1], BF16)] * (2 * count)
    pair = [shape((2, ups[0].shape[1]), F32)]
    kept = [array for at in places for array in (ups[at], gates[at])]
    outs = feed_call(feed_back_kernel, places, g, weights, scales, kept, held, pair, 4, 2)
    return [
        [*outs[2 * n : 2 * n + 2], outs[2 * count] if n == 0 else None, outs[2 * count + 1 + n]]
        for n in range(count)
    ]


def feed_grad_kernel(has_other, *refs):
    middle, mixed, ups, gates, gated = (refs[4 * n : 4 * n + 4] for n in range(5))
    out = refs[-1]
    rows = lambda blocks: jnp.concatenate([block[...] for block in blocks], axis=0)
    for row, (units, right) in enumerate(((ups, middle), (gates, middle), (gated, mixed))):
        left = jnp.concatenate([block[...] for block in units], axis=1)
        total = mul(left, rows(right))
        if has_other:
            total = total + refs[20][row].astype(F32)
        out[row] = total.astype(BF16)


def feed_grads(half_at, middle, mixed, ups, gates, gated, other=None):
    units, tokens = ups[0].shape
    depth, half = middle[0].shape[1], units // 2
    part = pl.BlockSpec((half, tokens), lambda i: (half_at, 0))
    more = () if other is None else (other,)
    return call(
        functools.partial(feed_grad_kernel, bool(more)),
        [shape((3, half, depth), BF16)],
        [WHOLE] * 4 + [NEAR] * 4 + [part] * 12 + [NEAR] * len(more),
        2 * 3 * 4 * tokens * half * depth,
        2 * 12 * tokens * (half + depth),
    )(*middle, *mixed, *ups, *gates, *gated, *more)[0]


def attend_grad_kernel(section, *refs):
    low, attended, hidden, grads = (refs[4 * n : 4 * n + 4] for n in range(4))
    own, other = refs[16:]
    width, half = attended[0].shape[0], own.shape[1]
    for lefts, rights, top in ((low, hidden, 0), (attended, grads, 3 * width)):
        right = jnp.concatenate([block[...] for block in rights], axis=0)
        for start in range(0, lefts[0].shape[0], width):
            total = mul(
                jnp.concatenate([left[start : start + width] for left in lefts], axis=1), right
            )
            rows = slice(top + start, top + start + width)
            for place in range(2):
                columns = total[:, place * half : place * half + half]

                @pl.when(section[0] == place)
                def _():
                    own[rows] = columns

                @pl.when(section[0] != place)
                def _():
                    other[rows] = columns.astype(BF16)


def attend_grads(section, low, attended, hidden, grads):
    width, tokens = attended[0].shape
    depth = hidden[0].shape[1]
    return call(
        attend_grad_kernel,
        [shape((4 * width, depth // 2), F32), shape((4 * width, depth // 2), BF16)],
        [SCALARS] + [WHOLE] * 12 + [NEAR] * 4,
        2 * 4 * 4 * tokens * width * depth,
        2 * 16 * tokens * depth,
    )(section, *low, *attended, *hidden, *grads)


def adam_kernel(axis, factor, weight, first, second, gradient, first_out, second_out, weight_out):
    clipped = gradient[...].astype(F32) * factor[0]
    first_new = BETA_FIRST * first[...] + (1.0 - BETA_FIRST) * clipped
    second_new = BETA_SECOND * second[...] + (1.0 - BETA_SECOND) * clipped * clipped
    first_out[...] = first_new
    second_out[...] = second_new
    first_hat = first_new / (1.0 - BETA_FIRST**STEP)
    second_hat = second_new / (1.0 - BETA_SECOND**STEP)
    moved = weight[...] - LEARN_RATE * first_hat / (jnp.sqrt(second_hat) + ADAM_EPSILON)
    scale = lax.rsqrt(jnp.sum(moved * moved, axis=axis, keepdims=True) + NORM_EPSILON)
    weight_out[...] = moved * scale


def adam_matrix(factor, weight, first, second, gradient, axis, block, place, grid):
    spec = pl.BlockSpec(block, place)
    return call(
        functools.partial(adam_kernel, axis),
        [shape(weight.shape, F32)] * 3,
        [SCALARS] + [spec] * 4,
        20 * weight.size,
        28 * weight.size,
        grid=grid,
        out_specs=[spec] * 3,
    )(factor, weight, first, second, gradient)


def add_parts(parts):
    total = parts[0][...].astype(F32)
    for part in parts[1:]:
        total = total + part[...].astype(F32)
    return total


def mix_kernel(count, hidden, rate, *refs):
    branch_out, result, result_low = refs[count:]
    branch = add_parts(refs[:count])
    branch_out[...] = branch
    mixed = mix_residual(hidden[...].astype(F32), branch, rate[...])
    result[...] = mixed
    result_low[...] = mixed.astype(BF16)


def mix_block(hidden, rate, parts):
    dims = hidden.shape
    return call(
        functools.partial(mix_kernel, len(parts)),
        [shape(dims, F32), shape(dims, F32), shape(dims, BF16)],
        [WHOLE] * 2 + [WHOLE if part.dtype == F32 else NEAR for part in parts],
        10 * dims[0] * dims[1],
        8 * dims[0] * dims[1],
    )(hidden, rate, *parts)


def mix_back_kernel(count, rounded, hidden, branch, rate, *refs):
    grad_hidden, grad_branch, grad_rate = refs[count:]
    upstream = add_parts(refs[:count])
    if rounded:
        upstream = upstream.astype(BF16).astype(F32)
    h, b, r = hidden[...].astype(F32), branch[...], rate[...]
    scale = lax.rsqrt(jnp.sum(b * b, axis=-1, keepdims=True) + NORM_EPSILON)
    unit = b * scale
    apart = unit - h
    mixed = h + r * apart
    mixed_scale = lax.rsqrt(jnp.sum(mixed * mixed, axis=-1, keepdims=True) + NORM_EPSILON)
    mixed = mixed * mixed_scale
    grad = mixed_scale * (upstream - mixed * jnp.sum(mixed * upstream, axis=-1, keepdims=True))
    grad_rate[...] = jnp.sum(grad * apart, axis=0, keepdims=True)
    grad_unit = grad * r
    grad_hidden[...] = grad - grad_unit
    grad_unit = scale * (grad_unit - unit * jnp.sum(unit * grad_unit, axis=-1, keepdims=True))
    grad_branch[...] = grad_unit.astype(BF16)


def mix_back_block(hidden, branch, rate, parts, rounded=False):
    dims = hidden.shape
    return call(
        functools.partial(mix_back_kernel, len(parts), rounded),
        [shape(dims, F32), shape(dims, BF16), shape((1, dims[1]), F32)],
        [WHOLE] * 3 + [WHOLE if part.dtype == F32 else NEAR for part in parts],
        20 * dims[0] * dims[1],
        12 * dims[0] * dims[1],
    )(hidden, branch, rate, *parts)


def tie(*values):
    return lax.optimization_barrier(values)


def to(block, at):
    return exchange(block, "mp", at)


def layer_forward(hidden, low, params, tables, tied, feed_own):
    attend_in, attend_out, gains, scales, mixing = params
    cosine, sine, starts, info = tables
    project = lambda *places: project_blocks(
        places, [blocks[at] for at in places], attend_in, cosine, sine, gains
    )
    blocks = [low, to(low, 1), to(low, 2), None]
    if tied:
        heads = project(0)
        low, heads = tie(low, heads)
        blocks[3] = to(low, 3)
        blocks[1], blocks[2] = tie(blocks[1], blocks[2])
        heads += project(1, 2)
        blocks[3], heads = tie(blocks[3], heads)
        heads += project(3)
    else:
        blocks[3] = to(low, 3)
        heads = project(0, 1, 2, 3)
    raw, query, keys, values = zip(*heads)
    attend = lambda *places: attend_blocks(places, info, starts, query, keys, values, attend_out)
    far = attend(3)
    sent = [to(far[0][-1], 3)]
    near_blocks = attend(1, 2)
    sent += [to(block[-1], at) for at, block in zip((1, 2), near_blocks)]
    attended = attend(0) + near_blocks + far
    sent, attended[0], feed_own = tie(sent, attended[0], feed_own)
    feed_weights = (feed_own, exchange(feed_own, "section", 1))
    branch, middle, middle_low = mix_block(hidden, mixing[:1], (attended[0][-1], *sent))
    blocks_middle, fed, parts = feed_exchange(
        middle_low, lambda places, x: feed_blocks(places, x, feed_weights, scales)
    )
    mixed, result, result_low = mix_block(middle, mixing[1:], parts)
    ups, gates, gated, _ = zip(*fed)
    attended, logsums, _ = zip(*attended)
    stored = (
        (hidden, branch, blocks, raw, query, keys, values, attended, logsums),
        (middle, mixed, blocks_middle, ups, gates, gated),
    )
    return result, result_low, stored, feed_weights


def feed_exchange(block, work):
    blocks = [block, to(block, 1), to(block, 2), None]
    done = work((0,), [block])
    block, done = tie(block, done)
    blocks[3] = to(block, 3)
    blocks[1], blocks[2] = tie(blocks[1], blocks[2])
    done += work((1, 2), blocks[1:3])
    sent = [to(done[at][-1], at) for at in (1, 2)]
    blocks[3], done = tie(blocks[3], done)
    done += work((3,), blocks[3:])
    sent.append(to(done[3][-1], 3))
    return blocks, done, (done[0][-1], *sent)


def layer_backward(stored, upstream, rounded, params, tables, feed_weights, section):
    attend_in, attend_out, gains, scales, mixing = params
    cosine, sine, starts, info = tables
    attend_stored, (middle, mixed, blocks_middle, ups, gates, gated) = stored
    hidden, branch, blocks_hidden, raw, query, keys, values, attended, logsums = attend_stored
    grad_middle, grad_mixed, rate_two = mix_back_block(
        middle, mixed, mixing[1:], upstream, rounded
    )
    blocks_mixed, done, parts = feed_exchange(
        grad_mixed, lambda places, g: feed_back_blocks(places, g, feed_weights, scales, ups, gates)
    )
    low_ups, low_gates, scale_grads, _ = zip(*done)
    operands = (blocks_middle, blocks_mixed, low_ups, low_gates, gated)
    other = feed_grads(1, *operands)
    parts, other = tie(parts, other)
    other = exchange(other, "section", 1)
    grad_hidden, grad_branch, rate_one = mix_back_block(
        hidden, branch, mixing[:1], (grad_middle, *parts)
    )
    near = [to(grad_branch, at) for at in (3, 1, 2)]
    feed_sums = feed_grads(0, *operands, other)
    near, _ = tie(near, feed_sums)
    grads = [grad_branch, near[1], near[2], near[0]]
    low, partial, gain_grad = attend_back(
        info, starts, query, keys, values, attended, logsums, raw, grads,
        attend_out, attend_in, cosine, sine, gains,
    )
    sent = [to(partial[at], at) for at in (3, 1, 2)]
    own, other = attend_grads(section, low, attended, blocks_hidden, grads)
    other = exchange(other, "section", 1)
    attend_sums = (own + other.astype(F32)).astype(BF16).reshape(4, -1, own.shape[1])
    scale_sum = scale_grads[0] + scale_grads[1] + scale_grads[3]
    small = (scale_sum, rate_one[0], rate_two[0])
    return (grad_hidden, partial[0], *sent), feed_sums, attend_sums, gain_grad[:, 0], small


def adam_update(weight, first, second, gradient, factor, rate):
    clipped = gradient * factor
    first_new = BETA_FIRST * first + (1.0 - BETA_FIRST) * clipped
    second_new = BETA_SECOND * second + (1.0 - BETA_SECOND) * clipped * clipped
    first_hat = first_new / (1.0 - BETA_FIRST**STEP)
    second_hat = second_new / (1.0 - BETA_SECOND**STEP)
    moved = weight - rate * first_hat / (jnp.sqrt(second_hat) + ADAM_EPSILON)
    return (first_new, second_new, moved)


def per_device(
    inputs,
    cotangent,
    doc_ids,
    attention_in,
    attention_out,
    feedforward_in,
    feedforward_out,
    unit_scales,
    mix_rates,
    first_attention_in,
    second_attention_in,
    first_attention_out,
    second_attention_out,
    first_feedforward_in,
    second_feedforward_in,
    first_feedforward_out,
    second_feedforward_out,
    first_unit_scales,
    second_unit_scales,
    first_mix_rates,
    second_mix_rates,
):
    section = lax.axis_index("section")
    is_first = section == 0
    dp_index = lax.axis_index("dp")
    dp_size = lax.axis_size("dp")
    local_rows = inputs.shape[1]

    def ordered(own, other):
        return jnp.where(is_first, own, other), jnp.where(is_first, other, own)

    def halves(array, dim):
        width = array.shape[dim] // 2
        own = lax.dynamic_slice_in_dim(array, section * width, width, dim)
        other = lax.dynamic_slice_in_dim(array, (1 - section) * width, width, dim)
        return own, other

    hidden_low = lax.dynamic_index_in_dim(inputs, section, 0, False)

    attend_rows = jnp.concatenate(
        [jnp.swapaxes(attention_in[0], 1, 2), attention_out], axis=0
    ).astype(BF16)
    small = jnp.concatenate([unit_scales.reshape(-1), mix_rates.reshape(-1)]).astype(BF16)
    def gather_ring(half):
        blocks = spread_rows(half, "dp")
        count = half.shape[1]
        whole = jnp.zeros((half.shape[0], dp_size * count, half.shape[2]), BF16)
        for source, block in zip(ring_sources("dp"), blocks):
            whole = lax.dynamic_update_slice_in_dim(whole, block, source * count, 1)
        return whole, blocks[-2]

    own, other = halves(attend_rows, 2)
    attend_pieces = ordered(own, exchange(other, "section", 1))
    attend_pieces, feedforward_in_here, feedforward_out_here = tie(
        attend_pieces, feedforward_in, feedforward_out
    )
    feed_rows = jnp.concatenate(
        [jnp.swapaxes(feedforward_in_here[0].astype(BF16), 1, 2), feedforward_out_here.astype(BF16)], axis=0
    )
    own, other = halves(feed_rows, 1)
    feed_pieces = ordered(own, exchange(other, "section", 1))
    if dp_size <= 4:
        attend_first, step = gather_ring(attend_pieces[0])
        attend_second, *feed_pieces, _ = tie(attend_pieces[1], *feed_pieces, step)
    else:
        attend_first = lax.all_gather(attend_pieces[0], "dp", axis=1, tiled=True)
        attend_second = attend_pieces[1]
    attend_pieces = (attend_first, lax.all_gather(attend_second, "dp", axis=1, tiled=True))
    small = jnp.stack(ordered(small, exchange(small, "section", 1))).reshape(-1)
    small = gather_small(small, "dp").astype(F32)
    small = small.reshape(dp_size, 2, -1)
    units_here = unit_scales.shape[2]

    def units_apart(values):
        parts = values.reshape(dp_size, 2, -1)
        own, other = ordered(parts[:, 0], parts[:, 1])
        return jnp.concatenate([own.reshape(-1), other.reshape(-1)])

    def units_back(values):
        parts = values.reshape(2, dp_size, -1)
        own, other = ordered(parts[0], parts[1])
        return jnp.stack([own, other], axis=1).reshape(-1)

    layers, feed_owns = [], []
    for layer in range(2):
        own = attend_pieces[layer]
        attend = jnp.concatenate(ordered(own, exchange(own, "section", 1)), axis=2)
        feed_own = lax.all_gather(feed_pieces[layer], "dp", axis=1, tiled=True)
        units = small[:, layer, :units_here].reshape(-1)
        mixing = small[:, layer, units_here:].reshape(dp_size, 2, -1)
        mixing = jnp.swapaxes(mixing, 0, 1).reshape(2, -1)
        width_qk, width_ff = attend.shape[1], 2 * feed_own.shape[1]
        layers.append((
            attend[:3].reshape(3 * width_qk, -1), attend[3],
            units[:width_qk, None],
            jnp.stack([
                units_apart(units[width_qk : width_qk + width_ff]),
                units_apart(units[width_qk + width_ff :]),
            ]),
            mixing,
        ))
        feed_owns.append(feed_own)

    doc_row = lax.dynamic_index_in_dim(doc_ids, section, 0, False)
    starts_all = document_starts(doc_row)
    mp_index = lax.axis_index("mp")
    sources = [mp_index ^ offset for offset in range(4)]
    places = jnp.arange(local_rows, dtype=jnp.int32)
    starts = jnp.stack([
        lax.dynamic_slice_in_dim(starts_all, source * local_rows, local_rows, 0)
        for source in sources
    ])
    sources = jnp.stack(sources).astype(jnp.int32)
    cosine, sine = rope_tables(sources[:, None] * local_rows + places - starts)
    info = jnp.concatenate([sources, starts[:, 0]])
    tables = (cosine, sine, starts, info)

    def scatter(sums):
        return lax.psum_scatter(sums, "dp", scatter_dimension=1, tiled=True)

    def scatter_direct(sums):
        if dp_size != 4:
            return scatter(sums)
        count = sums.shape[1] // dp_size
        parts = [
            lax.dynamic_slice_in_dim(sums, (dp_index ^ bits) * count, count, 1)
            for bits in range(dp_size)
        ]
        parts[1:] = [exchange(part, "dp", bits) for bits, part in enumerate(parts[1:], 1)]
        return sum(part.astype(F32) for part in parts).astype(BF16)

    def small_vector(scales, rate_one, rate_two):
        return jnp.concatenate([units_back(scales[0]), units_back(scales[1]), rate_one, rate_two])

    first, second = layers
    section_ref = section.astype(jnp.int32).reshape(1)
    grad = lax.dynamic_index_in_dim(cotangent, section, 0, False)
    _, hidden_second, stored_first, weights_first = layer_forward(
        hidden_low, hidden_low, first, tables, False, feed_owns[0]
    )
    result, _, stored_second, weights_second = layer_forward(
        hidden_second, hidden_second, second, tables, True,
        feed_owns[1],
    )
    parts, feed_second, attend_second, gains_second, small_second = layer_backward(
        stored_second, (grad,), False, second, tables, weights_second, section_ref
    )
    feed_second = scatter(feed_second)
    parts, attend_second = tie(parts, attend_second)
    attend_second = scatter(attend_second)
    parts, feed_first, attend_first, gains_first, small_first = layer_backward(
        stored_first, parts, True, first, tables, weights_first, section_ref
    )
    feed_first = scatter(feed_first)
    attend_first, feed_second, attend_second = tie(attend_first, feed_second, attend_second)
    attend_first = scatter_direct(attend_first)
    grad = sum(part.astype(F32) for part in parts)

    reduced_first = (attend_first, feed_first)
    reduced_second = (attend_second, feed_second)
    squares = sum(
        jnp.sum(jnp.square(part.astype(F32))) for part in (*reduced_first, *reduced_second)
    )
    gradients = []
    for one, two, dim in zip(reduced_first, reduced_second, (2, 1)):
        own, other = jnp.where(is_first, one, two), jnp.where(is_first, two, one)
        other = exchange(other, "section", 1)
        gradients.append(jnp.concatenate(ordered(own, other), axis=dim))

    sums = jnp.stack([small_vector(*small_first), small_vector(*small_second)])
    sums = sum_over(sum_over(sums, "section"), "dp")
    width_qk = gains_first.shape[0]
    scale_sums, rate_sums = sums[:, : dp_size * units_here - width_qk], sums[:, dp_size * units_here - width_qk :]
    rate_sums = sum_over(rate_sums, "mp").reshape(2, 2, -1)
    gain_sums = sum_over(sum_over(jnp.stack([gains_first, gains_second]), "section"), "dp")
    unit_grads = jnp.concatenate([gain_sums, scale_sums], axis=1)
    unit_grads = jnp.where(is_first, unit_grads[0], unit_grads[1])
    unit_grads = lax.dynamic_slice_in_dim(unit_grads, dp_index * units_here, units_here, 0)
    unit_grads = unit_grads[None, None]
    rates_here = mix_rates.shape[2]
    rate_grads = jnp.where(is_first, rate_sums[0], rate_sums[1])
    rate_grads = lax.dynamic_slice_in_dim(rate_grads, dp_index * rates_here, rates_here, 1)[None]

    turn = lambda array: jnp.swapaxes(array, 1, 2)
    attend_grad, feed_grad = gradients
    feed_in_grad = turn(feed_grad[:2])
    squares, attend_grad, feed_grad, feed_in_grad = tie(
        squares, attend_grad, feed_grad, feed_in_grad
    )
    leading = (mp_index == 0).astype(F32)
    squares = squares + jnp.sum(unit_grads * unit_grads)
    squares = squares + leading * jnp.sum(rate_grads * rate_grads)
    squares = squares.reshape(1)
    squares = squares + exchange(squares, "section", 1)
    squares = sum_over(sum_over(squares, "mp"), "dp")
    gradient_norm = jnp.sqrt(squares[0])
    factor = CLIP_NORM / jnp.maximum(gradient_norm, CLIP_NORM)

    to_send = jnp.where(is_first, result, grad)
    kept = jnp.where(is_first, grad, result)
    arrived = exchange(to_send, "section", 1)
    boundary_states = jnp.stack(ordered(kept, arrived))[None]

    scalar = factor.reshape(1)
    head_rows, width = attention_out.shape[1:]
    feed_units = feedforward_out.shape[1]
    rows, columns = min(32, head_rows), min(128, feed_units)
    updates = []
    new = adam_matrix(
        scalar, turn(attention_in[0]), turn(first_attention_in[0]), turn(second_attention_in[0]),
        attend_grad[:3], 2, (1, rows, width), lambda i, j: (i, j, 0), (3, head_rows // rows),
    )
    updates.extend(turn(part)[None] for part in new)
    updates.extend(adam_matrix(
        scalar, attention_out, first_attention_out, second_attention_out, attend_grad[3:],
        2, (1, rows, width), lambda i: (0, i, 0), (head_rows // rows,),
    ))
    new = adam_matrix(
        scalar, feedforward_in[0], first_feedforward_in[0], second_feedforward_in[0],
        feed_in_grad, 1, (1, width, columns), lambda i, j: (i, 0, j), (2, feed_units // columns),
    )
    updates.extend(part[None] for part in new)
    rows = min(64, feed_units)
    updates.extend(adam_matrix(
        scalar, feedforward_out, first_feedforward_out, second_feedforward_out, feed_grad[2:],
        2, (1, rows, width), lambda i: (0, i, 0), (feed_units // rows,),
    ))
    updates.extend(
        adam_update(
            unit_scales, first_unit_scales, second_unit_scales, unit_grads, factor, SCALE_RATE
        )
    )
    updates.extend(
        adam_update(
            mix_rates, first_mix_rates, second_mix_rates, rate_grads, factor, MIXING_RATE
        )
    )
    return (boundary_states, gradient_norm, *updates)


def solution(mesh):
    in_specs = (
        P("dp", "mp", None),
        P("dp", "mp", None),
        P("dp", None),
        P("section", None, None, ("mp", "dp")),
        P("section", ("mp", "dp"), None),
        P("section", None, None, ("mp", "dp")),
        P("section", ("mp", "dp"), None),
        P("section", "mp", "dp"),
        P("section", None, "dp"),
        P("section", None, None, ("mp", "dp")),
        P("section", None, None, ("mp", "dp")),
        P("section", ("mp", "dp"), None),
        P("section", ("mp", "dp"), None),
        P("section", None, None, ("mp", "dp")),
        P("section", None, None, ("mp", "dp")),
        P("section", ("mp", "dp"), None),
        P("section", ("mp", "dp"), None),
        P("section", "mp", "dp"),
        P("section", "mp", "dp"),
        P("section", None, "dp"),
        P("section", None, "dp"),
    )
    out_specs = (
        P("section", "dp", "mp", None),
        P(),
        P("section", None, None, ("mp", "dp")),
        P("section", None, None, ("mp", "dp")),
        P("section", None, None, ("mp", "dp")),
        P("section", ("mp", "dp"), None),
        P("section", ("mp", "dp"), None),
        P("section", ("mp", "dp"), None),
        P("section", None, None, ("mp", "dp")),
        P("section", None, None, ("mp", "dp")),
        P("section", None, None, ("mp", "dp")),
        P("section", ("mp", "dp"), None),
        P("section", ("mp", "dp"), None),
        P("section", ("mp", "dp"), None),
        P("section", "mp", "dp"),
        P("section", "mp", "dp"),
        P("section", "mp", "dp"),
        P("section", None, "dp"),
        P("section", None, "dp"),
        P("section", None, "dp"),
    )
    return jax.shard_map(
        per_device, mesh=mesh, in_specs=in_specs, out_specs=out_specs, check_vma=False
    )
```

```python
import functools
import math

import jax
import jax.numpy as jnp
from jax import lax
from jax.experimental import pallas as pl
from jax.experimental.pallas import tpu as pltpu
from jax.sharding import PartitionSpec as P

HD = 64
STEP = 10

NORM_EPSILON = 1e-06
ROPE_BASE = 10000.0
CLIP_NORM = 0.1
LEARN_RATE = 0.05
SCALE_RATE = 1.25
MIXING_RATE = 0.4
BETA_FIRST = 0.9
BETA_SECOND = 0.95
ADAM_EPSILON = 1e-08

BF16 = jnp.bfloat16
F32 = jnp.float32


def exchange(block, axis, bit):
    route = [(i, i ^ bit) for i in range(lax.axis_size(axis))]
    return lax.ppermute(block, axis, route)


def gray(place):
    return place ^ (place >> 1)


def ring_place(index, size):
    shift = 1
    while shift < size:
        index = index ^ (index >> shift)
        shift *= 2
    return index


def ring_step(block, axis):
    size = lax.axis_size(axis)
    route = []
    for place in range(size):
        route.append((gray(place), gray((place + 1) % size)))
        route.append((size + gray(place), size + gray((place - 1) % size)))
    return lax.ppermute(block, ("section", axis), route)


def ring_sources(axis):
    size = lax.axis_size(axis)
    place = ring_place(lax.axis_index(axis), size)
    way = 1 - 2 * lax.axis_index("section")
    return [gray((place - way * step + size) % size) for step in range(size)]


def spread_rows(block, axis="mp"):
    blocks = [block]
    for _ in range(lax.axis_size(axis) - 1):
        blocks.append(ring_step(blocks[-1], axis))
    return blocks


def sum_over(values, axis):
    bit = 1
    while bit < lax.axis_size(axis):
        values = values + exchange(values, axis, bit)
        bit *= 2
    return values


def gather_small(values, axis):
    index = lax.axis_index(axis)
    gathered = values[None]
    bit = 1
    while bit < lax.axis_size(axis):
        other = exchange(gathered, axis, bit)
        low = (index & bit) == 0
        gathered = jnp.concatenate(
            [jnp.where(low, gathered, other), jnp.where(low, other, gathered)], axis=0
        )
        bit *= 2
    return gathered


def unit_norm(values):
    return values * lax.rsqrt(jnp.sum(values * values, axis=-1, keepdims=True) + NORM_EPSILON)


def document_starts(doc_row):
    position = jnp.arange(doc_row.shape[-1], dtype=jnp.int32)
    change = jnp.concatenate([jnp.ones((1,), dtype=jnp.bool_), doc_row[1:] != doc_row[:-1]])
    return lax.cummax(jnp.where(change, position, 0), axis=0)


def rope_tables(offsets):
    half_width = HD // 2
    inverse = 1.0 / ROPE_BASE ** (jnp.arange(half_width, dtype=F32) * (2.0 / HD))
    angles = inverse[:, None] * offsets.astype(F32)[..., None, :]
    angles = jnp.concatenate([angles, angles], axis=-2)
    return jnp.cos(angles), jnp.sin(angles)


def mix_residual(hidden, branch, mixing):
    return unit_norm(hidden + mixing * (unit_norm(branch) - hidden))


NT = (((1,), (1,)), ((), ()))
TN = (((0,), (0,)), ((), ()))
NN = (((1,), (0,)), ((), ()))
VMEM = pltpu.VMEM
WHOLE, NEAR = "whole", "near"
SCALARS = pl.BlockSpec(memory_space=pltpu.SMEM)


def mul(left, right, dims=NN):
    return lax.dot_general(left, right, dims, preferred_element_type=F32)


def block_of(array):
    zeros = (0,) * len(array.shape)
    return pl.BlockSpec(array.shape, lambda *place: zeros)


def call(body, out_shape, in_specs, flops, moved, scratch=(), grid=(1,), out_specs=None, loose=()):
    def run(*args):
        specs = [
            block_of(arg) if spec in (WHOLE, NEAR) else spec for spec, arg in zip(in_specs, args)
        ]
        args = [
            arg if spec in (SCALARS, NEAR) else pltpu.with_memory_space_constraint(arg, pltpu.HBM)
            for spec, arg in zip(in_specs, args)
        ]
        return pl.pallas_call(
            body,
            out_shape=[
                out if at in loose else pltpu.HBM(out.shape, out.dtype)
                for at, out in enumerate(out_shape)
            ],
            grid=grid,
            in_specs=specs,
            out_specs=out_specs or [block_of(out) for out in out_shape],
            scratch_shapes=list(scratch),
            compiler_params=pltpu.CompilerParams(vmem_limit_bytes=50 << 20),
            cost_estimate=pl.CostEstimate(flops=flops, bytes_accessed=moved, transcendentals=0),
        )(*args)

    return run


def shape(dims, dtype):
    return jax.ShapeDtypeStruct(dims, dtype)


def turned(raw, cosine, sine):
    half = HD // 2
    first, second = raw[:half], raw[half:]
    return jnp.concatenate(
        [
            first * cosine[:half] - second * sine[:half],
            second * cosine[half:] + first * sine[half:],
        ],
        axis=0,
    )


def turned_back(grad, cosine, sine):
    half = HD // 2
    first, second = grad[:half], grad[half:]
    return jnp.concatenate(
        [
            first * cosine[:half] + second * sine[half:],
            second * cosine[half:] - first * sine[:half],
        ],
        axis=0,
    )


def rows_at(places):
    return [row for at in places for row in ((at,) if at < 3 else (3, 4))]


def side_by_side(refs):
    return refs[0][...] if len(refs) == 1 else jnp.concatenate([ref[...] for ref in refs], axis=0)


def project_kernel(places, *refs):
    count = len(rows_at(places))
    weight, cosine, sine, gains = refs[count : count + 4]
    tokens = cosine.shape[2]
    x, outs = side_by_side(refs[:count]), refs[count + 4 :]
    for n, at in enumerate(places):
        raw_out, query, keys, values = outs[4 * n : 4 * n + 4]
        width = query.shape[0]
        raw = mul(weight[...], x[n * tokens : (n + 1) * tokens], NT)
        raw_out[...] = raw[: 2 * width]
        values[...] = raw[2 * width :].astype(BF16)
        for part, out in ((0, query), (1, keys)):
            for top in range(0, width, HD):
                turn = turned(
                    raw[part * width + top : part * width + top + HD], cosine[at], sine[at]
                )
                scale = lax.rsqrt(jnp.sum(turn * turn, axis=0, keepdims=True) + NORM_EPSILON)
                head = (turn * scale * gains[top : top + HD]).astype(BF16)
                out[top : top + HD] = head * math.sqrt(HD) if part == 0 else head


def project_blocks(places, x, weight, cosine, sine, gains):
    tokens, depth, count = cosine.shape[2], weight.shape[1], len(places)
    width = weight.shape[0] // 3
    low = shape((width, tokens), BF16)
    outs = call(
        functools.partial(project_kernel, places),
        [shape((2 * width, tokens), F32), low, low, low] * count,
        [NEAR] * len(x) + [WHOLE] * 4,
        2 * tokens * depth * 3 * width * count,
        2 * 3 * width * depth,
    )(*x, weight, cosine, sine, gains)
    return [outs[4 * n : 4 * n + 4] for n in range(count)]


def near(info, at, other, tokens):
    return (info[other] <= info[at]) & ((info[other] + 1) * tokens > info[4 + at])


def seen(info, at, other, starts, tokens):
    key_place = info[other] * tokens + lax.broadcasted_iota(jnp.int32, (tokens, tokens), 0)
    query_place = info[at] * tokens + lax.broadcasted_iota(jnp.int32, (tokens, tokens), 1)
    return (key_place <= query_place) & (key_place >= starts)


def share_out(partial, value):
    partial[...] = value.astype(partial.dtype)


def partial_shape(at, tokens, depth):
    return shape((tokens, depth), BF16 if at else F32)


def attend_kernel(places, info, starts, *refs):
    count = len(places)
    query, rest = refs[:count], refs[count:]
    keys, values, weight, outs, (total, sums) = rest[:4], rest[4:8], rest[8], rest[9:-2], rest[-2:]
    width, tokens = query[0].shape
    for n, at in enumerate(places):
        attended, logsums, partial = outs[3 * n : 3 * n + 3]
        total[n] = jnp.zeros((width, tokens), F32)
        sums[n] = jnp.ones((8, tokens), F32)
        sums[n, : width // HD] = jnp.zeros((width // HD, tokens), F32)
        for other in range(4):

            @pl.when(near(info, at, other, tokens))
            def _():
                allowed = seen(info, at, other, starts[at : at + 1], tokens)
                for head in range(width // HD):
                    rows = slice(head * HD, head * HD + HD)
                    shares = jnp.exp(mul(keys[other][rows], query[n][rows], TN))
                    shares = jnp.where(allowed, shares, 0.0)
                    sums[n, head : head + 1] += jnp.sum(shares, axis=0, keepdims=True)
                    total[n, rows] += mul(values[other][rows], shares.astype(BF16))

        logsums[...] = jnp.log(sums[n])
        inverse = 1.0 / sums[n]
        for head in range(width // HD):
            rows = slice(head * HD, head * HD + HD)
            attended[rows] = (total[n, rows] * inverse[head : head + 1]).astype(BF16)
        share_out(partial, mul(attended[...], weight[...], TN))


def attend_blocks(places, info, starts, query, keys, values, weight):
    width, tokens = query[0].shape
    depth, count = weight.shape[1], len(places)
    outs = call(
        functools.partial(attend_kernel, places),
        [
            out
            for at in places
            for out in (
                shape((width, tokens), BF16),
                shape((8, tokens), F32),
                partial_shape(at, tokens, depth),
            )
        ],
        [SCALARS] + [WHOLE] * (10 + count),
        2 * tokens * (depth * width + 10 * tokens * 256) * count,
        2 * depth * width,
        [VMEM((count, width, tokens), F32), VMEM((count, 8, tokens), F32)],
        loose=[3 * n + 2 for n, at in enumerate(places) if at],
    )(info, starts, *[query[at] for at in places], *keys, *values, weight)
    return [outs[3 * n : 3 * n + 3] for n in range(count)]


def attend_back_kernel(info, starts, *refs):
    query, keys, values, attended, logsums, raw = (refs[4 * n : 4 * n + 4] for n in range(6))
    grads, (w_out, w_in, cosine, sine, gains) = refs[24:29], refs[29:34]
    low, partial, gain_grad = refs[34:38], refs[38:42], refs[42]
    pulled, deltas, grad_query, grad_keys, grad_values = refs[43:]
    width, tokens = query[0].shape
    heads = width // HD
    grad_query[...] = jnp.zeros_like(grad_query)
    grad_keys[...] = jnp.zeros_like(grad_keys)
    grad_values[...] = jnp.zeros_like(grad_values)
    deltas[...] = jnp.zeros_like(deltas)
    for at in range(4):
        rows = side_by_side([grads[row] for row in rows_at((at,))])
        grad = mul(w_out[...], rows, NT).astype(BF16)
        pulled[at] = grad
        product = grad.astype(F32) * attended[at][...].astype(F32)
        for head in range(heads):
            rows = slice(head * HD, head * HD + HD)
            deltas[at, head : head + 1] = jnp.sum(product[rows], axis=0, keepdims=True)
    for at in range(4):
        for other in range(4):

            @pl.when(near(info, at, other, tokens))
            def _():
                allowed = seen(info, at, other, starts[at : at + 1], tokens)
                for head in range(heads):
                    rows = slice(head * HD, head * HD + HD)
                    grad_rows, query_rows = pulled[at, rows], query[at][rows]
                    scores = mul(keys[other][rows], query_rows, TN) - logsums[at][head : head + 1]
                    shares = jnp.where(allowed, jnp.exp(scores), 0.0)
                    grad_shares = mul(values[other][rows], grad_rows, TN)
                    grad_scores = shares * (grad_shares - deltas[at, head : head + 1])
                    grad_scores = grad_scores.astype(BF16)
                    grad_values[other, rows] += mul(grad_rows, shares.astype(BF16), NT)
                    grad_keys[other, rows] += mul(query_rows, grad_scores, NT)
                    grad_query[at, rows] += mul(keys[other][rows], grad_scores)

    gain_total = [0.0] * heads
    for at in range(4):
        cos, sin = cosine[at], sine[at]
        for part, source, factor in ((0, grad_query, math.sqrt(HD)), (1, grad_keys, 1.0)):
            for head in range(heads):
                rows = slice(head * HD, head * HD + HD)
                turn = turned(raw[at][part * width + head * HD : part * width + head * HD + HD], cos, sin)
                scale = lax.rsqrt(jnp.sum(turn * turn, axis=0, keepdims=True) + NORM_EPSILON)
                unit = turn * scale
                grad = source[at, rows] * factor
                gain_total[head] = gain_total[head] + grad * unit
                grad = grad * gains[rows]
                grad = scale * (grad - unit * jnp.sum(unit * grad, axis=0, keepdims=True))
                low[at][part * width + head * HD : part * width + head * HD + HD] = turned_back(
                    grad, cos, sin
                ).astype(BF16)
        low[at][2 * width :] = grad_values[at].astype(BF16)
        share_out(partial[at], mul(low[at][...], w_in[...], TN))
    for head in range(heads):
        gain_grad[head * HD : head * HD + HD] = jnp.sum(gain_total[head], axis=1, keepdims=True)


def attend_back(info, starts, query, keys, values, attended, logsums, raw, grads,
                w_out, w_in, cosine, sine, gains):
    width, tokens = query[0].shape
    depth = w_out.shape[1]
    low = shape((3 * width, tokens), BF16)
    block = VMEM((4, width, tokens), F32)
    outs = call(
        attend_back_kernel,
        [low] * 4
        + [partial_shape(at, tokens, depth) for at in range(4)]
        + [shape((width, 1), F32)],
        [SCALARS] + [WHOLE] * 25 + [NEAR] * 5 + [WHOLE] * 5,
        2 * 4 * tokens * (depth * width * 4 + 60 * tokens * 256),
        2 * depth * width * 12,
        [VMEM((4, width, tokens), BF16), VMEM((4, 8, tokens), F32), block, block, block],
        loose=(5, 6, 7),
    )(info, starts, *query, *keys, *values, *attended, *logsums, *raw, *grads,
      w_out, w_in, cosine, sine, gains)
    return outs[:4], outs[4:8], outs[8]


CHUNK = 256
GATE_WIDTH = math.sqrt(1024)


def started(copies, arrived, first=0):
    copies = [
        pltpu.make_async_copy(source, target, arrived.at[first + n])
        for n, (source, target) in enumerate(copies)
    ]
    for copy in copies:
        copy.start()
    return copies


def fetch_weights(own, other, weights, arrived):
    half = own.shape[1]
    size = min(CHUNK, half)
    places = [(index, start) for index in range(2) for start in range(0, half, size)]
    copies = started(
        [
            ((own, other)[index].at[:, pl.ds(start, size)], weights.at[index, :, pl.ds(start, size)])
            for index, start in places
        ],
        arrived,
    )
    return [
        (copy, index, slice(start, start + size), slice(index * half + start, index * half + start + size))
        for copy, (index, start) in zip(copies, places)
    ]


def feed_kernel(given, count, *refs):
    x, refs = refs[:given], refs[given:]
    (own, other, scales_in), outs, partial = refs[:3], refs[3 : 3 * count + 3], refs[3 * count + 3 : 4 * count + 3]
    weights, scales, ups, gates, gated, gated_turned, arrived, came, left = refs[4 * count + 3 :]
    half, tokens = own.shape[1], ups.shape[0] // count
    (scales_copy,) = started([(scales_in, scales)], came)
    chunks = fetch_weights(own, other, weights, arrived)
    block = side_by_side(x)
    scales_copy.wait()
    leaving = []
    for copy, index, rows, units in chunks:
        copy.wait()
        up, gate = mul(block, weights[index, 0, rows], NT), mul(block, weights[index, 1, rows], NT)
        ups[:, units] = up.astype(BF16)
        gates[:, units] = gate.astype(BF16)
        z = gate * (scales[1:2, units] * GATE_WIDTH)
        silu = z * (0.5 + 0.5 * jnp.tanh(0.5 * z))
        mixed = (up * scales[0:1, units] * silu).astype(BF16)
        gated[:, units] = mixed
        gated_turned[units] = mixed.T
        if rows.stop == half:
            columns = pl.ds(index * half, half)
            for n in range(count):
                places = pl.ds(n * tokens, tokens)
                leaving += started(
                    [
                        (ups.at[places, columns], outs[3 * n].at[:, columns]),
                        (gates.at[places, columns], outs[3 * n + 1].at[:, columns]),
                        (gated_turned.at[columns, places], outs[3 * n + 2].at[columns]),
                    ],
                    left,
                    3 * (index * count + n),
                )
    total = mul(gated[:, :half], weights[0, 2]) + mul(gated[:, half:], weights[1, 2])
    for n in range(count):
        share_out(partial[n], total[n * tokens : (n + 1) * tokens])
    for copy in leaving:
        copy.wait()


def feed_back_kernel(given, count, *refs):
    g, refs = refs[:given], refs[given:]
    (own, other, scales_in), kept = refs[:3], refs[3 : 2 * count + 3]
    outs, scale_grad = refs[2 * count + 3 : 4 * count + 3], refs[4 * count + 3]
    partial = refs[4 * count + 4 : 5 * count + 4]
    weights, scales, ups, gates, low_up, low_gate, up_turned, gate_turned = refs[5 * count + 4 : -3]
    arrived, came, left = refs[-3:]
    half, tokens = own.shape[1], ups.shape[0] // count
    (scales_copy,) = started([(scales_in, scales)], came)
    chunks = fetch_weights(own, other, weights, arrived)
    coming = [
        started(
            [
                (ref.at[:, pl.ds(index * half, half)],
                 into.at[pl.ds(n * tokens, tokens), pl.ds(index * half, half)])
                for n in range(count)
                for ref, into in ((kept[2 * n], ups), (kept[2 * n + 1], gates))
            ],
            came,
            1 + 2 * count * index,
        )
        for index in range(2)
    ]
    block = side_by_side(g)
    scales_copy.wait()
    leaving = []
    for copy, index, rows, units in chunks:
        copy.wait()
        grad = mul(block, weights[index, 2, rows], NT)
        if rows.start == 0:
            for copy in coming[index]:
                copy.wait()
        up, gate = ups[:, units].astype(F32), gates[:, units].astype(F32)
        s_up, s_gate = scales[0:1, units], scales[1:2, units] * GATE_WIDTH
        z = gate * s_gate
        sigmoid = 0.5 + 0.5 * jnp.tanh(0.5 * z)
        silu = z * sigmoid
        grad_silu = grad * silu
        grad_z = grad * (up * s_up) * (sigmoid + silu * (1.0 - sigmoid))
        grad_up, grad_gate = (grad_silu * s_up).astype(BF16), (grad_z * s_gate).astype(BF16)
        low_up[:, units], low_gate[:, units] = grad_up, grad_gate
        up_turned[units], gate_turned[units] = grad_up.T, grad_gate.T
        scale_grad[0:1, units] = jnp.sum(grad_silu * up, axis=0, keepdims=True)
        scale_grad[1:2, units] = jnp.sum(grad_z * gate, axis=0, keepdims=True) * GATE_WIDTH
        if rows.stop == half:
            columns = pl.ds(index * half, half)
            for n in range(count):
                places = pl.ds(n * tokens, tokens)
                leaving += started(
                    [
                        (up_turned.at[columns, places], outs[2 * n].at[columns]),
                        (gate_turned.at[columns, places], outs[2 * n + 1].at[columns]),
                    ],
                    left,
                    2 * (index * count + n),
                )
    total = mul(low_up[:, :half], weights[0, 0]) + mul(low_up[:, half:], weights[1, 0])
    total = total + mul(low_gate[:, :half], weights[0, 1]) + mul(low_gate[:, half:], weights[1, 1])
    for n in range(count):
        share_out(partial[n], total[n * tokens : (n + 1) * tokens])
    for copy in leaving:
        copy.wait()


HELD = pl.BlockSpec(memory_space=pl.ANY)


def feed_call(body, places, x, weights, scales, kept, held, pair, low, turned_count):
    half, count = weights[0].shape[1], len(places)
    tokens, depth = sum(block.shape[0] for block in x) // count, x[0].shape[1]
    partial = [partial_shape(at, tokens, depth) for at in places]
    semaphores = pltpu.SemaphoreType.DMA
    return call(
        functools.partial(body, len(x), count),
        held + pair + partial,
        [NEAR] * len(x) + [HELD] * (3 + len(kept)),
        2 * 6 * tokens * depth * half * count,
        2 * 6 * depth * half,
        [VMEM((2, 3, half, depth), BF16), VMEM(scales.shape, F32)]
        + [VMEM((count * tokens, 2 * half), BF16)] * low
        + [VMEM((2 * half, count * tokens), BF16)] * turned_count
        + [
            semaphores((2 * half // min(CHUNK, half),)),
            semaphores((1 + 2 * len(kept),)),
            semaphores((2 * len(held),)),
        ],
        out_specs=[HELD] * len(held) + [block_of(out) for out in pair + partial],
        loose=[len(held + pair) + n for n, at in enumerate(places) if at],
    )(*x, *weights, scales, *kept)


def feed_blocks(places, x, weights, scales):
    count = len(places)
    dims = (sum(block.shape[0] for block in x) // count, 2 * weights[0].shape[1])
    held = [shape(dims, BF16), shape(dims, BF16), shape(dims[::-1], BF16)] * count
    outs = feed_call(feed_kernel, places, x, weights, scales, (), held, [], 3, 1)
    return [[*outs[3 * n : 3 * n + 3], outs[3 * count + n]] for n in range(count)]


def feed_back_blocks(places, g, weights, scales, ups, gates):
    count = len(places)
    held = [shape(ups[0].shape[::-1], BF16)] * (2 * count)
    pair = [shape((2, ups[0].shape[1]), F32)]
    kept = [array for at in places for array in (ups[at], gates[at])]
    outs = feed_call(feed_back_kernel, places, g, weights, scales, kept, held, pair, 4, 2)
    return [
        [*outs[2 * n : 2 * n + 2], outs[2 * count] if n == 0 else None, outs[2 * count + 1 + n]]
        for n in range(count)
    ]


def feed_grad_kernel(has_other, *refs):
    middle, mixed, (ups, gates, gated) = refs[:5], refs[5:10], (refs[10:14], refs[14:18], refs[18:22])
    out = refs[-1]
    for row, (units, right) in enumerate(((ups, middle), (gates, middle), (gated, mixed))):
        left = jnp.concatenate([block[...] for block in units], axis=1)
        total = mul(left, side_by_side(right))
        if has_other:
            total = total + refs[22][row].astype(F32)
        out[row] = total.astype(BF16)


def feed_grads(half_at, middle, mixed, ups, gates, gated, other=None):
    units, tokens = ups[0].shape
    depth, half = middle[0].shape[1], units // 2
    part = pl.BlockSpec((half, tokens), lambda i: (half_at, 0))
    more = () if other is None else (other,)
    return call(
        functools.partial(feed_grad_kernel, bool(more)),
        [shape((3, half, depth), BF16)],
        [WHOLE] * 5 + [NEAR] * 5 + [part] * 12 + [NEAR] * len(more),
        2 * 3 * 4 * tokens * half * depth,
        2 * 12 * tokens * (half + depth),
    )(*middle, *mixed, *ups, *gates, *gated, *more)[0]


def attend_grad_kernel(section, *refs):
    low, attended, hidden, grads = refs[:4], refs[4:8], refs[8:13], refs[13:18]
    own, other = refs[18:]
    width, half = attended[0].shape[0], own.shape[1]
    for lefts, rights, top in ((low, hidden, 0), (attended, grads, 3 * width)):
        right = side_by_side(rights)
        for start in range(0, lefts[0].shape[0], width):
            total = mul(
                jnp.concatenate([left[start : start + width] for left in lefts], axis=1), right
            )
            rows = slice(top + start, top + start + width)
            for place in range(2):
                columns = total[:, place * half : place * half + half]

                @pl.when(section[0] == place)
                def _():
                    own[rows] = columns

                @pl.when(section[0] != place)
                def _():
                    other[rows] = columns.astype(BF16)


def attend_grads(section, low, attended, hidden, grads):
    width, tokens = attended[0].shape
    depth = hidden[0].shape[1]
    return call(
        attend_grad_kernel,
        [shape((4 * width, depth // 2), F32), shape((4 * width, depth // 2), BF16)],
        [SCALARS] + [WHOLE] * 13 + [NEAR] * 5,
        2 * 4 * 4 * tokens * width * depth,
        2 * 16 * tokens * depth,
    )(section, *low, *attended, *hidden, *grads)


def adam_kernel(axis, factor, weight, first, second, gradient, first_out, second_out, weight_out):
    clipped = gradient[...].astype(F32) * factor[0]
    first_new = BETA_FIRST * first[...] + (1.0 - BETA_FIRST) * clipped
    second_new = BETA_SECOND * second[...] + (1.0 - BETA_SECOND) * clipped * clipped
    first_out[...] = first_new
    second_out[...] = second_new
    first_hat = first_new / (1.0 - BETA_FIRST**STEP)
    second_hat = second_new / (1.0 - BETA_SECOND**STEP)
    moved = weight[...] - LEARN_RATE * first_hat / (jnp.sqrt(second_hat) + ADAM_EPSILON)
    scale = lax.rsqrt(jnp.sum(moved * moved, axis=axis, keepdims=True) + NORM_EPSILON)
    weight_out[...] = moved * scale


def adam_matrix(factor, weight, first, second, gradient, axis, block, place, grid):
    spec = pl.BlockSpec(block, place)
    return call(
        functools.partial(adam_kernel, axis),
        [shape(weight.shape, F32)] * 3,
        [SCALARS] + [spec] * 4,
        20 * weight.size,
        28 * weight.size,
        grid=grid,
        out_specs=[spec] * 3,
    )(factor, weight, first, second, gradient)


def add_parts(parts):
    total = parts[0][...].astype(F32)
    for part in parts[1:]:
        total = total + part[...].astype(F32)
    return total


def mix_kernel(count, hidden, rate, *refs):
    branch_out, result, result_low = refs[count:]
    branch = add_parts(refs[:count])
    branch_out[...] = branch
    mixed = mix_residual(hidden[...].astype(F32), branch, rate[...])
    result[...] = mixed
    result_low[...] = mixed.astype(BF16)


def mix_block(hidden, rate, parts):
    dims = hidden.shape
    return call(
        functools.partial(mix_kernel, len(parts)),
        [shape(dims, F32), shape(dims, F32), shape(dims, BF16)],
        [WHOLE] * 2 + [WHOLE if part.dtype == F32 else NEAR for part in parts],
        10 * dims[0] * dims[1],
        8 * dims[0] * dims[1],
    )(hidden, rate, *parts)


def mix_back_kernel(count, rounded, hidden, branch, rate, *refs):
    grad_hidden, grad_branch, grad_rate = refs[count:]
    upstream = add_parts(refs[:count])
    if rounded:
        upstream = upstream.astype(BF16).astype(F32)
    h, b, r = hidden[...].astype(F32), branch[...], rate[...]
    scale = lax.rsqrt(jnp.sum(b * b, axis=-1, keepdims=True) + NORM_EPSILON)
    unit = b * scale
    apart = unit - h
    mixed = h + r * apart
    mixed_scale = lax.rsqrt(jnp.sum(mixed * mixed, axis=-1, keepdims=True) + NORM_EPSILON)
    mixed = mixed * mixed_scale
    grad = mixed_scale * (upstream - mixed * jnp.sum(mixed * upstream, axis=-1, keepdims=True))
    grad_rate[...] = jnp.sum(grad * apart, axis=0, keepdims=True)
    grad_unit = grad * r
    grad_hidden[...] = grad - grad_unit
    grad_unit = scale * (grad_unit - unit * jnp.sum(unit * grad_unit, axis=-1, keepdims=True))
    grad_branch[...] = grad_unit.astype(BF16)


def mix_back_block(hidden, branch, rate, parts, rounded=False):
    dims = hidden.shape
    return call(
        functools.partial(mix_back_kernel, len(parts), rounded),
        [shape(dims, F32), shape(dims, BF16), shape((1, dims[1]), F32)],
        [WHOLE] * 3 + [WHOLE if part.dtype == F32 else NEAR for part in parts],
        20 * dims[0] * dims[1],
        12 * dims[0] * dims[1],
    )(hidden, branch, rate, *parts)


def tie(*values):
    return lax.optimization_barrier(values)


def to(block, at):
    return exchange(block, "mp", at)


def pass_halves(first, second):
    half = first.shape[0] // 2
    return [to(second[:half], 1), to(first[half:], 2)]


def layer_forward(hidden, low, params, tables, tied, feed_own, later=None):
    attend_in, attend_out, gains, scales, mixing = params
    cosine, sine, starts, info = tables
    project = lambda *places: project_blocks(
        places, [blocks[row] for row in rows_at(places)], attend_in, cosine, sine, gains
    )
    blocks = [low, to(low, 1), to(low, 2)]
    if tied:
        heads = project(0)
        *blocks, heads = tie(*blocks, heads)
        blocks += pass_halves(*blocks[1:])
        heads += project(1, 2)
        *blocks, heads = tie(*blocks, heads)
        heads += project(3)
    else:
        blocks += pass_halves(*blocks[1:])
        heads = project(0, 1, 2, 3)
    raw, query, keys, values = zip(*heads)
    attend = lambda *places: attend_blocks(places, info, starts, query, keys, values, attend_out)
    far = attend(3)
    sent = [to(far[0][-1], 3)]
    near_blocks = attend(1, 2)
    sent += [to(block[-1], at) for at, block in zip((1, 2), near_blocks)]
    attended = attend(0) + near_blocks + far
    sent, attended[0], feed_own = tie(sent, attended[0], feed_own)
    feed_weights = (feed_own, exchange(feed_own, "section", 1))
    branch, middle, middle_low = mix_block(hidden, mixing[:1], (attended[0][-1], *sent))
    blocks_middle, fed, parts = feed_exchange(
        middle_low, lambda places, x: feed_blocks(places, x, feed_weights, scales)
    )
    fed, later = tie(fed, later)
    if later is not None:
        later = (later, exchange(later, "section", 1))
    mixed, result, result_low = mix_block(middle, mixing[1:], parts)
    ups, gates, gated, _ = zip(*fed)
    attended, logsums, _ = zip(*attended)
    stored = (
        (hidden, branch, blocks, raw, query, keys, values, attended, logsums),
        (middle, mixed, blocks_middle, ups, gates, gated),
    )
    return result, result_low, stored, feed_weights, later


def feed_exchange(block, work):
    blocks = [block, to(block, 1), to(block, 2)]
    done = work((0,), blocks[:1])
    *blocks, done = tie(*blocks, done)
    blocks += pass_halves(*blocks[1:])
    done += work((1, 2), blocks[1:3])
    sent = [to(done[at][-1], at) for at in (1, 2)]
    *blocks, done = tie(*blocks, done)
    done += work((3,), blocks[3:])
    sent.append(to(done[3][-1], 3))
    return blocks, done, (done[0][-1], *sent)


def layer_backward(stored, upstream, rounded, params, tables, feed_weights, section, hooks=()):
    attend_in, attend_out, gains, scales, mixing = params
    cosine, sine, starts, info = tables
    attend_stored, (middle, mixed, blocks_middle, ups, gates, gated) = stored
    hidden, branch, blocks_hidden, raw, query, keys, values, attended, logsums = attend_stored
    grad_middle, grad_mixed, rate_two = mix_back_block(
        middle, mixed, mixing[1:], upstream, rounded
    )
    blocks_mixed, done, parts = feed_exchange(
        grad_mixed, lambda places, g: feed_back_blocks(places, g, feed_weights, scales, ups, gates)
    )
    low_ups, low_gates, scale_grads, _ = zip(*done)
    operands = (blocks_middle, blocks_mixed, low_ups, low_gates, gated)
    other = feed_grads(1, *operands)
    parts, other = tie(parts, other)
    other = exchange(other, "section", 1)
    grad_hidden, grad_branch, rate_one = mix_back_block(
        hidden, branch, mixing[:1], (grad_middle, *parts)
    )
    grads = [grad_branch, to(grad_branch, 1), to(grad_branch, 2)]
    feed_sums = feed_grads(0, *operands, other)
    grads, _ = tie(grads, feed_sums)
    grads += pass_halves(*grads[1:])
    small = (scale_grads[0] + scale_grads[1] + scale_grads[3], rate_one[0], rate_two[0])
    if hooks:
        small = hooks[0](small)
    low, partial, gain_grad = attend_back(
        info, starts, query, keys, values, attended, logsums, raw, grads,
        attend_out, attend_in, cosine, sine, gains,
    )
    sent = [to(partial[at], at) for at in (3, 1, 2)]
    if hooks:
        low, small = hooks[1](low, small, gain_grad[:, 0])
    own, other = attend_grads(section, low, attended, blocks_hidden, grads)
    if hooks:
        other, small = hooks[2](other, small)
    other = exchange(other, "section", 1)
    attend_sums = (own + other.astype(F32)).astype(BF16).reshape(4, -1, own.shape[1])
    return (grad_hidden, partial[0], *sent), feed_sums, attend_sums, gain_grad[:, 0], small


def adam_update(weight, first, second, gradient, factor, rate):
    clipped = gradient * factor
    first_new = BETA_FIRST * first + (1.0 - BETA_FIRST) * clipped
    second_new = BETA_SECOND * second + (1.0 - BETA_SECOND) * clipped * clipped
    first_hat = first_new / (1.0 - BETA_FIRST**STEP)
    second_hat = second_new / (1.0 - BETA_SECOND**STEP)
    moved = weight - rate * first_hat / (jnp.sqrt(second_hat) + ADAM_EPSILON)
    return (first_new, second_new, moved)


def per_device(
    inputs,
    cotangent,
    doc_ids,
    attention_in,
    attention_out,
    feedforward_in,
    feedforward_out,
    unit_scales,
    mix_rates,
    first_attention_in,
    second_attention_in,
    first_attention_out,
    second_attention_out,
    first_feedforward_in,
    second_feedforward_in,
    first_feedforward_out,
    second_feedforward_out,
    first_unit_scales,
    second_unit_scales,
    first_mix_rates,
    second_mix_rates,
):
    section = lax.axis_index("section")
    is_first = section == 0
    dp_index = lax.axis_index("dp")
    dp_size = lax.axis_size("dp")
    local_rows = inputs.shape[1]

    def ordered(own, other):
        return jnp.where(is_first, own, other), jnp.where(is_first, other, own)

    def halves(array, dim):
        width = array.shape[dim] // 2
        own = lax.dynamic_slice_in_dim(array, section * width, width, dim)
        other = lax.dynamic_slice_in_dim(array, (1 - section) * width, width, dim)
        return own, other

    hidden_low = lax.dynamic_index_in_dim(inputs, section, 0, False)

    attend_rows = jnp.concatenate(
        [jnp.swapaxes(attention_in[0], 1, 2), attention_out], axis=0
    ).astype(BF16)
    small = jnp.concatenate([unit_scales.reshape(-1), mix_rates.reshape(-1)]).astype(BF16)
    def gather_direct(half):
        if dp_size != 4:
            return lax.all_gather(half, "dp", axis=1, tiled=True)
        count = half.shape[1]
        whole = jnp.zeros((half.shape[0], dp_size * count, half.shape[2]), BF16)
        for bits in range(dp_size):
            block = exchange(half, "dp", bits) if bits else half
            whole = lax.dynamic_update_slice_in_dim(whole, block, (dp_index ^ bits) * count, 1)
        return whole

    own, other = halves(attend_rows, 2)
    attend_pieces = ordered(own, exchange(other, "section", 1))
    attend_pieces, feedforward_in_here, feedforward_out_here = tie(
        attend_pieces, feedforward_in, feedforward_out
    )
    feed_rows = jnp.concatenate(
        [jnp.swapaxes(feedforward_in_here[0].astype(BF16), 1, 2), feedforward_out_here.astype(BF16)], axis=0
    )
    own, other = halves(feed_rows, 1)
    feed_pieces = ordered(own, exchange(other, "section", 1))
    attend_owns = (
        gather_direct(attend_pieces[0]),
        lax.all_gather(attend_pieces[1], "dp", axis=1, tiled=True),
    )
    small = jnp.stack(ordered(small, exchange(small, "section", 1))).reshape(-1)
    small = gather_small(small, "dp").astype(F32)
    small = small.reshape(dp_size, 2, -1)
    units_here = unit_scales.shape[2]

    def units_apart(values):
        parts = values.reshape(dp_size, 2, -1)
        own, other = ordered(parts[:, 0], parts[:, 1])
        return jnp.concatenate([own.reshape(-1), other.reshape(-1)])

    def units_back(values):
        parts = values.reshape(2, dp_size, -1)
        own, other = ordered(parts[0], parts[1])
        return jnp.stack([own, other], axis=1).reshape(-1)

    layers, feed_owns = [], []
    for layer in range(2):
        feed_own = lax.all_gather(feed_pieces[layer], "dp", axis=1, tiled=True)
        units = small[:, layer, :units_here].reshape(-1)
        mixing = small[:, layer, units_here:].reshape(dp_size, 2, -1)
        mixing = jnp.swapaxes(mixing, 0, 1).reshape(2, -1)
        width_qk, width_ff = attend_owns[0].shape[1], 2 * feed_own.shape[1]
        layers.append((
            units[:width_qk, None],
            jnp.stack([
                units_apart(units[width_qk : width_qk + width_ff]),
                units_apart(units[width_qk + width_ff :]),
            ]),
            mixing,
        ))
        feed_owns.append(feed_own)

    doc_row = lax.dynamic_index_in_dim(doc_ids, section, 0, False)
    starts_all = document_starts(doc_row)
    mp_index = lax.axis_index("mp")
    sources = [mp_index ^ offset for offset in range(4)]
    places = jnp.arange(local_rows, dtype=jnp.int32)
    starts = jnp.stack([
        lax.dynamic_slice_in_dim(starts_all, source * local_rows, local_rows, 0)
        for source in sources
    ])
    sources = jnp.stack(sources).astype(jnp.int32)
    cosine, sine = rope_tables(sources[:, None] * local_rows + places - starts)
    info = jnp.concatenate([sources, starts[:, 0]])
    tables = (cosine, sine, starts, info)

    def scatter(sums):
        return lax.psum_scatter(sums, "dp", scatter_dimension=1, tiled=True)

    def scatter_direct(sums):
        if dp_size != 4:
            return scatter(sums)
        count = sums.shape[1] // dp_size
        parts = [
            lax.dynamic_slice_in_dim(sums, (dp_index ^ bits) * count, count, 1)
            for bits in range(dp_size)
        ]
        parts[1:] = [exchange(part, "dp", bits) for bits, part in enumerate(parts[1:], 1)]
        return sum(part.astype(F32) for part in parts).astype(BF16)

    def small_vector(scales, rate_one, rate_two):
        return jnp.concatenate([units_back(scales[0]), units_back(scales[1]), rate_one, rate_two])

    def attend_params(own, other):
        attend = jnp.concatenate(ordered(own, other), axis=2)
        return attend[:3].reshape(-1, attend.shape[2]), attend[3]

    first, second = layers
    own = attend_owns[0]
    first = (*attend_params(own, exchange(own, "section", 1)), *first)
    section_ref = section.astype(jnp.int32).reshape(1)
    grad = lax.dynamic_index_in_dim(cotangent, section, 0, False)
    _, hidden_second, stored_first, weights_first, later = layer_forward(
        hidden_low, hidden_low, first, tables, False, feed_owns[0], attend_owns[1]
    )
    second = (*attend_params(*later), *second)
    result, _, stored_second, weights_second, _ = layer_forward(
        hidden_second, hidden_second, second, tables, True, feed_owns[1]
    )
    parts, feed_second, attend_second, gains_second, small_second = layer_backward(
        stored_second, (grad,), False, second, tables, weights_second, section_ref
    )
    feed_second = scatter(feed_second)
    parts, attend_second = tie(parts, attend_second)
    attend_second = scatter(attend_second)

    def start_small(small_first):
        values = jnp.concatenate(
            [small_vector(*small_first), small_vector(*small_second), gains_second]
        )
        return values, exchange(values, "section", 1)

    def next_small(low, small, gains):
        low, (values, coming) = tie(low, small)
        values = jnp.concatenate([values + coming, gains])
        return low, (values, exchange(values, "dp", 1))

    def last_small(other, small):
        other, (values, coming) = tie(other, small)
        values, bit = values + coming, 2
        while 2 * bit < dp_size:
            values = values + exchange(values, "dp", bit)
            bit *= 2
        return other, (values, exchange(values, "dp", bit))

    parts, feed_first, attend_first, _, small = layer_backward(
        stored_first, parts, True, first, tables, weights_first, section_ref,
        (start_small, next_small, last_small),
    )
    feed_first = scatter(feed_first)
    attend_first, feed_second, attend_second, small = tie(
        attend_first, feed_second, attend_second, small
    )
    attend_first = scatter_direct(attend_first)
    grad = sum(part.astype(F32) for part in parts)

    reduced_first = (attend_first, feed_first)
    reduced_second = (attend_second, feed_second)
    squares = sum(
        jnp.sum(jnp.square(part.astype(F32))) for part in (*reduced_first, *reduced_second)
    )
    gradients = []
    for one, two, dim in zip(reduced_first, reduced_second, (2, 1)):
        own, other = jnp.where(is_first, one, two), jnp.where(is_first, two, one)
        other = exchange(other, "section", 1)
        gradients.append(jnp.concatenate(ordered(own, other), axis=dim))

    sums = small[0] + small[1]
    width_qk, width_rates = gains_second.shape[0], 2 * dp_size * mix_rates.shape[2]
    layer_sums = sums[: -2 * width_qk].reshape(2, -1)
    gain_first = sums[-width_qk:]
    gain_sums = jnp.stack([gain_first + exchange(gain_first, "section", 1), sums[-2 * width_qk : -width_qk]])
    scale_sums, rate_sums = layer_sums[:, :-width_rates], layer_sums[:, -width_rates:]
    rate_sums = sum_over(rate_sums, "mp").reshape(2, 2, -1)
    unit_grads = jnp.concatenate([gain_sums, scale_sums], axis=1)
    unit_grads = jnp.where(is_first, unit_grads[0], unit_grads[1])
    unit_grads = lax.dynamic_slice_in_dim(unit_grads, dp_index * units_here, units_here, 0)
    unit_grads = unit_grads[None, None]
    rates_here = mix_rates.shape[2]
    rate_grads = jnp.where(is_first, rate_sums[0], rate_sums[1])
    rate_grads = lax.dynamic_slice_in_dim(rate_grads, dp_index * rates_here, rates_here, 1)[None]

    turn = lambda array: jnp.swapaxes(array, 1, 2)
    attend_grad, feed_grad = gradients
    feed_in_grad = turn(feed_grad[:2])
    squares, attend_grad, feed_grad, feed_in_grad = tie(
        squares, attend_grad, feed_grad, feed_in_grad
    )
    leading = (mp_index == 0).astype(F32)
    squares = squares + jnp.sum(unit_grads * unit_grads)
    squares = squares + leading * jnp.sum(rate_grads * rate_grads)
    squares = squares.reshape(1)
    squares = squares + exchange(squares, "section", 1)
    squares = sum_over(sum_over(squares, "mp"), "dp")
    gradient_norm = jnp.sqrt(squares[0])
    factor = CLIP_NORM / jnp.maximum(gradient_norm, CLIP_NORM)

    to_send = jnp.where(is_first, result, grad)
    kept = jnp.where(is_first, grad, result)
    arrived = exchange(to_send, "section", 1)
    boundary_states = jnp.stack(ordered(kept, arrived))[None]

    scalar = factor.reshape(1)
    head_rows, width = attention_out.shape[1:]
    feed_units = feedforward_out.shape[1]
    rows, columns = min(32, head_rows), min(128, feed_units)
    updates = []
    new = adam_matrix(
        scalar, turn(attention_in[0]), turn(first_attention_in[0]), turn(second_attention_in[0]),
        attend_grad[:3], 2, (1, rows, width), lambda i, j: (i, j, 0), (3, head_rows // rows),
    )
    updates.extend(turn(part)[None] for part in new)
    updates.extend(adam_matrix(
        scalar, attention_out, first_attention_out, second_attention_out, attend_grad[3:],
        2, (1, rows, width), lambda i: (0, i, 0), (head_rows // rows,),
    ))
    new = adam_matrix(
        scalar, feedforward_in[0], first_feedforward_in[0], second_feedforward_in[0],
        feed_in_grad, 1, (1, width, columns), lambda i, j: (i, 0, j), (2, feed_units // columns),
    )
    updates.extend(part[None] for part in new)
    rows = min(64, feed_units)
    updates.extend(adam_matrix(
        scalar, feedforward_out, first_feedforward_out, second_feedforward_out, feed_grad[2:],
        2, (1, rows, width), lambda i: (0, i, 0), (feed_units // rows,),
    ))
    updates.extend(
        adam_update(
            unit_scales, first_unit_scales, second_unit_scales, unit_grads, factor, SCALE_RATE
        )
    )
    updates.extend(
        adam_update(
            mix_rates, first_mix_rates, second_mix_rates, rate_grads, factor, MIXING_RATE
        )
    )
    return (boundary_states, gradient_norm, *updates)


def solution(mesh):
    in_specs = (
        P("dp", "mp", None),
        P("dp", "mp", None),
        P("dp", None),
        P("section", None, None, ("mp", "dp")),
        P("section", ("mp", "dp"), None),
        P("section", None, None, ("mp", "dp")),
        P("section", ("mp", "dp"), None),
        P("section", "mp", "dp"),
        P("section", None, "dp"),
        P("section", None, None, ("mp", "dp")),
        P("section", None, None, ("mp", "dp")),
        P("section", ("mp", "dp"), None),
        P("section", ("mp", "dp"), None),
        P("section", None, None, ("mp", "dp")),
        P("section", None, None, ("mp", "dp")),
        P("section", ("mp", "dp"), None),
        P("section", ("mp", "dp"), None),
        P("section", "mp", "dp"),
        P("section", "mp", "dp"),
        P("section", None, "dp"),
        P("section", None, "dp"),
    )
    out_specs = (
        P("section", "dp", "mp", None),
        P(),
        P("section", None, None, ("mp", "dp")),
        P("section", None, None, ("mp", "dp")),
        P("section", None, None, ("mp", "dp")),
        P("section", ("mp", "dp"), None),
        P("section", ("mp", "dp"), None),
        P("section", ("mp", "dp"), None),
        P("section", None, None, ("mp", "dp")),
        P("section", None, None, ("mp", "dp")),
        P("section", None, None, ("mp", "dp")),
        P("section", ("mp", "dp"), None),
        P("section", ("mp", "dp"), None),
        P("section", ("mp", "dp"), None),
        P("section", "mp", "dp"),
        P("section", "mp", "dp"),
        P("section", "mp", "dp"),
        P("section", None, "dp"),
        P("section", None, "dp"),
        P("section", None, "dp"),
    )
    return jax.shard_map(
        per_device, mesh=mesh, in_specs=in_specs, out_specs=out_specs, check_vma=False
    )
```

```python
import functools
import math

import jax
import jax.numpy as jnp
from jax import lax
from jax.experimental import pallas as pl
from jax.experimental.pallas import tpu as pltpu
from jax.sharding import PartitionSpec as P

HD = 64
STEP = 10

NORM_EPSILON = 1e-06
ROPE_BASE = 10000.0
CLIP_NORM = 0.1
LEARN_RATE = 0.05
SCALE_RATE = 1.25
MIXING_RATE = 0.4
BETA_FIRST = 0.9
BETA_SECOND = 0.95
ADAM_EPSILON = 1e-08

BF16 = jnp.bfloat16
F32 = jnp.float32


def exchange(block, axis, bit):
    route = [(i, i ^ bit) for i in range(lax.axis_size(axis))]
    return lax.ppermute(block, axis, route)


def gray(place):
    return place ^ (place >> 1)


def ring_place(index, size):
    shift = 1
    while shift < size:
        index = index ^ (index >> shift)
        shift *= 2
    return index


def ring_step(block, axis):
    size = lax.axis_size(axis)
    route = []
    for place in range(size):
        route.append((gray(place), gray((place + 1) % size)))
        route.append((size + gray(place), size + gray((place - 1) % size)))
    return lax.ppermute(block, ("section", axis), route)


def ring_sources(axis):
    size = lax.axis_size(axis)
    place = ring_place(lax.axis_index(axis), size)
    way = 1 - 2 * lax.axis_index("section")
    return [gray((place - way * step + size) % size) for step in range(size)]


def spread_rows(block, axis="mp"):
    blocks = [block]
    for _ in range(lax.axis_size(axis) - 1):
        blocks.append(ring_step(blocks[-1], axis))
    return blocks


def sum_over(values, axis):
    bit = 1
    while bit < lax.axis_size(axis):
        values = values + exchange(values, axis, bit)
        bit *= 2
    return values


def gather_small(values, axis):
    index = lax.axis_index(axis)
    gathered = values[None]
    bit = 1
    while bit < lax.axis_size(axis):
        other = exchange(gathered, axis, bit)
        low = (index & bit) == 0
        gathered = jnp.concatenate(
            [jnp.where(low, gathered, other), jnp.where(low, other, gathered)], axis=0
        )
        bit *= 2
    return gathered


def unit_norm(values):
    return values * lax.rsqrt(jnp.sum(values * values, axis=-1, keepdims=True) + NORM_EPSILON)


def document_starts(doc_row):
    position = jnp.arange(doc_row.shape[-1], dtype=jnp.int32)
    change = jnp.concatenate([jnp.ones((1,), dtype=jnp.bool_), doc_row[1:] != doc_row[:-1]])
    return lax.cummax(jnp.where(change, position, 0), axis=0)


def rope_tables(offsets):
    half_width = HD // 2
    inverse = 1.0 / ROPE_BASE ** (jnp.arange(half_width, dtype=F32) * (2.0 / HD))
    angles = inverse[:, None] * offsets.astype(F32)[..., None, :]
    angles = jnp.concatenate([angles, angles], axis=-2)
    return jnp.cos(angles), jnp.sin(angles)


def mix_residual(hidden, branch, mixing):
    return unit_norm(hidden + mixing * (unit_norm(branch) - hidden))


NT = (((1,), (1,)), ((), ()))
TN = (((0,), (0,)), ((), ()))
NN = (((1,), (0,)), ((), ()))
VMEM = pltpu.VMEM
WHOLE, NEAR = "whole", "near"
SCALARS = pl.BlockSpec(memory_space=pltpu.SMEM)


def mul(left, right, dims=NN):
    return lax.dot_general(left, right, dims, preferred_element_type=F32)


def block_of(array):
    zeros = (0,) * len(array.shape)
    return pl.BlockSpec(array.shape, lambda *place: zeros)


def call(body, out_shape, in_specs, flops, moved, scratch=(), grid=(1,), out_specs=None, loose=()):
    def run(*args):
        specs = [
            block_of(arg) if spec in (WHOLE, NEAR) else spec for spec, arg in zip(in_specs, args)
        ]
        args = [
            arg if spec in (SCALARS, NEAR) else pltpu.with_memory_space_constraint(arg, pltpu.HBM)
            for spec, arg in zip(in_specs, args)
        ]
        return pl.pallas_call(
            body,
            out_shape=[
                out if at in loose else pltpu.HBM(out.shape, out.dtype)
                for at, out in enumerate(out_shape)
            ],
            grid=grid,
            in_specs=specs,
            out_specs=out_specs or [block_of(out) for out in out_shape],
            scratch_shapes=list(scratch),
            compiler_params=pltpu.CompilerParams(vmem_limit_bytes=50 << 20),
            cost_estimate=pl.CostEstimate(flops=flops, bytes_accessed=moved, transcendentals=0),
        )(*args)

    return run


def shape(dims, dtype):
    return jax.ShapeDtypeStruct(dims, dtype)


def turned(raw, cosine, sine):
    half = HD // 2
    first, second = raw[:half], raw[half:]
    return jnp.concatenate(
        [
            first * cosine[:half] - second * sine[:half],
            second * cosine[half:] + first * sine[half:],
        ],
        axis=0,
    )


def turned_back(grad, cosine, sine):
    half = HD // 2
    first, second = grad[:half], grad[half:]
    return jnp.concatenate(
        [
            first * cosine[:half] + second * sine[half:],
            second * cosine[half:] - first * sine[:half],
        ],
        axis=0,
    )


def rows_at(places):
    return [row for at in places for row in ((at,) if at < 3 else (3, 4))]


def side_by_side(refs):
    return refs[0][...] if len(refs) == 1 else jnp.concatenate([ref[...] for ref in refs], axis=0)


def project_kernel(places, *refs):
    count = len(rows_at(places))
    weight, cosine, sine, gains = refs[count : count + 4]
    tokens = cosine.shape[2]
    x, outs = side_by_side(refs[:count]), refs[count + 4 :]
    for n, at in enumerate(places):
        raw_out, query, keys, values = outs[4 * n : 4 * n + 4]
        width = query.shape[0]
        raw = mul(weight[...], x[n * tokens : (n + 1) * tokens], NT)
        raw_out[...] = raw[: 2 * width]
        values[...] = raw[2 * width :].astype(BF16)
        for part, out in ((0, query), (1, keys)):
            for top in range(0, width, HD):
                turn = turned(
                    raw[part * width + top : part * width + top + HD], cosine[at], sine[at]
                )
                scale = lax.rsqrt(jnp.sum(turn * turn, axis=0, keepdims=True) + NORM_EPSILON)
                head = (turn * scale * gains[top : top + HD]).astype(BF16)
                out[top : top + HD] = head * math.sqrt(HD) if part == 0 else head


def project_blocks(places, x, weight, cosine, sine, gains):
    tokens, depth, count = cosine.shape[2], weight.shape[1], len(places)
    width = weight.shape[0] // 3
    low = shape((width, tokens), BF16)
    outs = call(
        functools.partial(project_kernel, places),
        [shape((2 * width, tokens), F32), low, low, low] * count,
        [NEAR] * len(x) + [WHOLE] * 4,
        2 * tokens * depth * 3 * width * count,
        2 * 3 * width * depth,
    )(*x, weight, cosine, sine, gains)
    return [outs[4 * n : 4 * n + 4] for n in range(count)]


def near(info, at, other, tokens):
    return (info[other] <= info[at]) & ((info[other] + 1) * tokens > info[4 + at])


def seen(info, at, other, starts, tokens):
    key_place = info[other] * tokens + lax.broadcasted_iota(jnp.int32, (tokens, tokens), 0)
    query_place = info[at] * tokens + lax.broadcasted_iota(jnp.int32, (tokens, tokens), 1)
    return (key_place <= query_place) & (key_place >= starts)


def share_out(partial, value):
    partial[...] = value.astype(partial.dtype)


def partial_shape(at, tokens, depth):
    return shape((tokens, depth), BF16 if at else F32)


def attend_kernel(places, info, starts, *refs):
    count = len(places)
    query, rest = refs[:count], refs[count:]
    keys, values, weight, outs, (total, sums) = rest[:4], rest[4:8], rest[8], rest[9:-2], rest[-2:]
    width, tokens = query[0].shape
    for n, at in enumerate(places):
        attended, logsums, partial = outs[3 * n : 3 * n + 3]
        total[n] = jnp.zeros((width, tokens), F32)
        sums[n] = jnp.ones((8, tokens), F32)
        sums[n, : width // HD] = jnp.zeros((width // HD, tokens), F32)
        for other in range(4):

            @pl.when(near(info, at, other, tokens))
            def _():
                allowed = seen(info, at, other, starts[at : at + 1], tokens)
                for head in range(width // HD):
                    rows = slice(head * HD, head * HD + HD)
                    shares = jnp.exp(mul(keys[other][rows], query[n][rows], TN))
                    shares = jnp.where(allowed, shares, 0.0)
                    sums[n, head : head + 1] += jnp.sum(shares, axis=0, keepdims=True)
                    total[n, rows] += mul(values[other][rows], shares.astype(BF16))

        logsums[...] = jnp.log(sums[n])
        inverse = 1.0 / sums[n]
        for head in range(width // HD):
            rows = slice(head * HD, head * HD + HD)
            attended[rows] = (total[n, rows] * inverse[head : head + 1]).astype(BF16)
        share_out(partial, mul(attended[...], weight[...], TN))


def attend_blocks(places, info, starts, query, keys, values, weight):
    width, tokens = query[0].shape
    depth, count = weight.shape[1], len(places)
    outs = call(
        functools.partial(attend_kernel, places),
        [
            out
            for at in places
            for out in (
                shape((width, tokens), BF16),
                shape((8, tokens), F32),
                partial_shape(at, tokens, depth),
            )
        ],
        [SCALARS] + [WHOLE] * (10 + count),
        2 * tokens * (depth * width + 10 * tokens * 256) * count,
        2 * depth * width,
        [VMEM((count, width, tokens), F32), VMEM((count, 8, tokens), F32)],
        loose=[3 * n + 2 for n, at in enumerate(places) if at],
    )(info, starts, *[query[at] for at in places], *keys, *values, weight)
    return [outs[3 * n : 3 * n + 3] for n in range(count)]


def attend_back_kernel(info, starts, *refs):
    query, keys, values, attended, logsums, raw = (refs[4 * n : 4 * n + 4] for n in range(6))
    grads, (w_out, w_in, cosine, sine, gains) = refs[24:29], refs[29:34]
    low, partial, gain_grad = refs[34:38], refs[38:42], refs[42]
    pulled, deltas, grad_query, grad_keys, grad_values = refs[43:]
    width, tokens = query[0].shape
    heads = width // HD
    grad_query[...] = jnp.zeros_like(grad_query)
    grad_keys[...] = jnp.zeros_like(grad_keys)
    grad_values[...] = jnp.zeros_like(grad_values)
    deltas[...] = jnp.zeros_like(deltas)
    for at in range(4):
        rows = side_by_side([grads[row] for row in rows_at((at,))])
        grad = mul(w_out[...], rows, NT).astype(BF16)
        pulled[at] = grad
        product = grad.astype(F32) * attended[at][...].astype(F32)
        for head in range(heads):
            rows = slice(head * HD, head * HD + HD)
            deltas[at, head : head + 1] = jnp.sum(product[rows], axis=0, keepdims=True)
    for at in range(4):
        for other in range(4):

            @pl.when(near(info, at, other, tokens))
            def _():
                allowed = seen(info, at, other, starts[at : at + 1], tokens)
                for head in range(heads):
                    rows = slice(head * HD, head * HD + HD)
                    grad_rows, query_rows = pulled[at, rows], query[at][rows]
                    scores = mul(keys[other][rows], query_rows, TN) - logsums[at][head : head + 1]
                    shares = jnp.where(allowed, jnp.exp(scores), 0.0)
                    grad_shares = mul(values[other][rows], grad_rows, TN)
                    grad_scores = shares * (grad_shares - deltas[at, head : head + 1])
                    grad_scores = grad_scores.astype(BF16)
                    grad_values[other, rows] += mul(grad_rows, shares.astype(BF16), NT)
                    grad_keys[other, rows] += mul(query_rows, grad_scores, NT)
                    grad_query[at, rows] += mul(keys[other][rows], grad_scores)

    gain_total = [0.0] * heads
    for at in range(4):
        cos, sin = cosine[at], sine[at]
        for part, source, factor in ((0, grad_query, math.sqrt(HD)), (1, grad_keys, 1.0)):
            for head in range(heads):
                rows = slice(head * HD, head * HD + HD)
                turn = turned(raw[at][part * width + head * HD : part * width + head * HD + HD], cos, sin)
                scale = lax.rsqrt(jnp.sum(turn * turn, axis=0, keepdims=True) + NORM_EPSILON)
                unit = turn * scale
                grad = source[at, rows] * factor
                gain_total[head] = gain_total[head] + grad * unit
                grad = grad * gains[rows]
                grad = scale * (grad - unit * jnp.sum(unit * grad, axis=0, keepdims=True))
                low[at][part * width + head * HD : part * width + head * HD + HD] = turned_back(
                    grad, cos, sin
                ).astype(BF16)
        low[at][2 * width :] = grad_values[at].astype(BF16)
        share_out(partial[at], mul(low[at][...], w_in[...], TN))
    for head in range(heads):
        gain_grad[head * HD : head * HD + HD] = jnp.sum(gain_total[head], axis=1, keepdims=True)


def attend_back(info, starts, query, keys, values, attended, logsums, raw, grads,
                w_out, w_in, cosine, sine, gains):
    width, tokens = query[0].shape
    depth = w_out.shape[1]
    low = shape((3 * width, tokens), BF16)
    block = VMEM((4, width, tokens), F32)
    outs = call(
        attend_back_kernel,
        [low] * 4
        + [partial_shape(at, tokens, depth) for at in range(4)]
        + [shape((width, 1), F32)],
        [SCALARS] + [WHOLE] * 25 + [NEAR] * 5 + [WHOLE] * 5,
        2 * 4 * tokens * (depth * width * 4 + 60 * tokens * 256),
        2 * depth * width * 12,
        [VMEM((4, width, tokens), BF16), VMEM((4, 8, tokens), F32), block, block, block],
        loose=(5, 6, 7),
    )(info, starts, *query, *keys, *values, *attended, *logsums, *raw, *grads,
      w_out, w_in, cosine, sine, gains)
    return outs[:4], outs[4:8], outs[8]


CHUNK = 256
GATE_WIDTH = math.sqrt(1024)


def started(copies, arrived, first=0):
    copies = [
        pltpu.make_async_copy(source, target, arrived.at[first + n])
        for n, (source, target) in enumerate(copies)
    ]
    for copy in copies:
        copy.start()
    return copies


def fetch_weights(own, other, weights, arrived):
    half = own.shape[1]
    size = min(CHUNK, half)
    places = [(index, start) for index in range(2) for start in range(0, half, size)]
    copies = started(
        [
            ((own, other)[index].at[:, pl.ds(start, size)], weights.at[index, :, pl.ds(start, size)])
            for index, start in places
        ],
        arrived,
    )
    return [
        (copy, index, slice(start, start + size), slice(index * half + start, index * half + start + size))
        for copy, (index, start) in zip(copies, places)
    ]


def feed_kernel(given, count, *refs):
    x, refs = refs[:given], refs[given:]
    (own, other, scales_in), outs, partial = refs[:3], refs[3 : 3 * count + 3], refs[3 * count + 3 : 4 * count + 3]
    weights, scales, ups, gates, gated, gated_turned, arrived, came, left = refs[4 * count + 3 :]
    half, tokens = own.shape[1], ups.shape[0] // count
    (scales_copy,) = started([(scales_in, scales)], came)
    chunks = fetch_weights(own, other, weights, arrived)
    block = side_by_side(x)
    scales_copy.wait()
    leaving = []
    for copy, index, rows, units in chunks:
        copy.wait()
        up, gate = mul(block, weights[index, 0, rows], NT), mul(block, weights[index, 1, rows], NT)
        ups[:, units] = up.astype(BF16)
        gates[:, units] = gate.astype(BF16)
        z = gate * (scales[1:2, units] * GATE_WIDTH)
        silu = z * (0.5 + 0.5 * jnp.tanh(0.5 * z))
        mixed = (up * scales[0:1, units] * silu).astype(BF16)
        gated[:, units] = mixed
        gated_turned[units] = mixed.T
        if rows.stop == half:
            columns = pl.ds(index * half, half)
            for n in range(count):
                places = pl.ds(n * tokens, tokens)
                leaving += started(
                    [
                        (ups.at[places, columns], outs[3 * n].at[:, columns]),
                        (gates.at[places, columns], outs[3 * n + 1].at[:, columns]),
                        (gated_turned.at[columns, places], outs[3 * n + 2].at[columns]),
                    ],
                    left,
                    3 * (index * count + n),
                )
    total = mul(gated[:, :half], weights[0, 2]) + mul(gated[:, half:], weights[1, 2])
    for n in range(count):
        share_out(partial[n], total[n * tokens : (n + 1) * tokens])
    for copy in leaving:
        copy.wait()


def feed_back_kernel(given, count, *refs):
    g, refs = refs[:given], refs[given:]
    (own, other, scales_in), kept = refs[:3], refs[3 : 2 * count + 3]
    outs, scale_grad = refs[2 * count + 3 : 4 * count + 3], refs[4 * count + 3]
    partial = refs[4 * count + 4 : 5 * count + 4]
    weights, scales, ups, gates, low_up, low_gate, up_turned, gate_turned = refs[5 * count + 4 : -3]
    arrived, came, left = refs[-3:]
    half, tokens = own.shape[1], ups.shape[0] // count
    (scales_copy,) = started([(scales_in, scales)], came)
    chunks = fetch_weights(own, other, weights, arrived)
    coming = [
        started(
            [
                (ref.at[:, pl.ds(index * half, half)],
                 into.at[pl.ds(n * tokens, tokens), pl.ds(index * half, half)])
                for n in range(count)
                for ref, into in ((kept[2 * n], ups), (kept[2 * n + 1], gates))
            ],
            came,
            1 + 2 * count * index,
        )
        for index in range(2)
    ]
    block = side_by_side(g)
    scales_copy.wait()
    leaving = []
    for copy, index, rows, units in chunks:
        copy.wait()
        grad = mul(block, weights[index, 2, rows], NT)
        if rows.start == 0:
            for copy in coming[index]:
                copy.wait()
        up, gate = ups[:, units].astype(F32), gates[:, units].astype(F32)
        s_up, s_gate = scales[0:1, units], scales[1:2, units] * GATE_WIDTH
        z = gate * s_gate
        sigmoid = 0.5 + 0.5 * jnp.tanh(0.5 * z)
        silu = z * sigmoid
        grad_silu = grad * silu
        grad_z = grad * (up * s_up) * (sigmoid + silu * (1.0 - sigmoid))
        grad_up, grad_gate = (grad_silu * s_up).astype(BF16), (grad_z * s_gate).astype(BF16)
        low_up[:, units], low_gate[:, units] = grad_up, grad_gate
        up_turned[units], gate_turned[units] = grad_up.T, grad_gate.T
        scale_grad[0:1, units] = jnp.sum(grad_silu * up, axis=0, keepdims=True)
        scale_grad[1:2, units] = jnp.sum(grad_z * gate, axis=0, keepdims=True) * GATE_WIDTH
        if rows.stop == half:
            columns = pl.ds(index * half, half)
            for n in range(count):
                places = pl.ds(n * tokens, tokens)
                leaving += started(
                    [
                        (up_turned.at[columns, places], outs[2 * n].at[columns]),
                        (gate_turned.at[columns, places], outs[2 * n + 1].at[columns]),
                    ],
                    left,
                    2 * (index * count + n),
                )
    total = mul(low_up[:, :half], weights[0, 0]) + mul(low_up[:, half:], weights[1, 0])
    total = total + mul(low_gate[:, :half], weights[0, 1]) + mul(low_gate[:, half:], weights[1, 1])
    for n in range(count):
        share_out(partial[n], total[n * tokens : (n + 1) * tokens])
    for copy in leaving:
        copy.wait()


HELD = pl.BlockSpec(memory_space=pl.ANY)


def feed_call(body, places, x, weights, scales, kept, held, pair, low, turned_count):
    half, count = weights[0].shape[1], len(places)
    tokens, depth = sum(block.shape[0] for block in x) // count, x[0].shape[1]
    partial = [partial_shape(at, tokens, depth) for at in places]
    semaphores = pltpu.SemaphoreType.DMA
    return call(
        functools.partial(body, len(x), count),
        held + pair + partial,
        [NEAR] * len(x) + [HELD] * (3 + len(kept)),
        2 * 6 * tokens * depth * half * count,
        2 * 6 * depth * half,
        [VMEM((2, 3, half, depth), BF16), VMEM(scales.shape, F32)]
        + [VMEM((count * tokens, 2 * half), BF16)] * low
        + [VMEM((2 * half, count * tokens), BF16)] * turned_count
        + [
            semaphores((2 * half // min(CHUNK, half),)),
            semaphores((1 + 2 * len(kept),)),
            semaphores((2 * len(held),)),
        ],
        out_specs=[HELD] * len(held) + [block_of(out) for out in pair + partial],
        loose=[len(held + pair) + n for n, at in enumerate(places) if at],
    )(*x, *weights, scales, *kept)


def feed_blocks(places, x, weights, scales):
    count = len(places)
    dims = (sum(block.shape[0] for block in x) // count, 2 * weights[0].shape[1])
    held = [shape(dims, BF16), shape(dims, BF16), shape(dims[::-1], BF16)] * count
    outs = feed_call(feed_kernel, places, x, weights, scales, (), held, [], 3, 1)
    return [[*outs[3 * n : 3 * n + 3], outs[3 * count + n]] for n in range(count)]


def feed_back_blocks(places, g, weights, scales, ups, gates):
    count = len(places)
    held = [shape(ups[0].shape[::-1], BF16)] * (2 * count)
    pair = [shape((2, ups[0].shape[1]), F32)]
    kept = [array for at in places for array in (ups[at], gates[at])]
    outs = feed_call(feed_back_kernel, places, g, weights, scales, kept, held, pair, 4, 2)
    return [
        [*outs[2 * n : 2 * n + 2], outs[2 * count] if n == 0 else None, outs[2 * count + 1 + n]]
        for n in range(count)
    ]


def feed_grad_kernel(*refs):
    middle, mixed, (ups, gates, gated) = refs[:5], refs[5:10], (refs[10:14], refs[14:18], refs[18:22])
    outs = refs[22:]
    half = outs[0].shape[1]
    for row, (units, right) in enumerate(((ups, middle), (gates, middle), (gated, mixed))):
        right = side_by_side(right)
        for out, rows in ((outs[1], slice(half, 2 * half)), (outs[0], slice(0, half))):
            left = jnp.concatenate([block[rows] for block in units], axis=1)
            out[row] = mul(left, right).astype(BF16)


def feed_grads(middle, mixed, ups, gates, gated):
    units, tokens = ups[0].shape
    depth, half = middle[0].shape[1], units // 2
    return call(
        feed_grad_kernel,
        [shape((3, half, depth), BF16)] * 2,
        [WHOLE] * 5 + [NEAR] * 5 + [WHOLE] * 12,
        2 * 3 * 4 * tokens * units * depth,
        2 * 12 * tokens * (units + depth),
    )(*middle, *mixed, *ups, *gates, *gated)


def attend_grad_kernel(section, *refs):
    low, attended, hidden, grads = refs[:4], refs[4:8], refs[8:13], refs[13:18]
    own, other = refs[18:]
    width, half = attended[0].shape[0], own.shape[1]
    for lefts, rights, top in ((low, hidden, 0), (attended, grads, 3 * width)):
        right = side_by_side(rights)
        for start in range(0, lefts[0].shape[0], width):
            total = mul(
                jnp.concatenate([left[start : start + width] for left in lefts], axis=1), right
            )
            rows = slice(top + start, top + start + width)
            for place in range(2):
                columns = total[:, place * half : place * half + half]

                @pl.when(section[0] == place)
                def _():
                    own[rows] = columns

                @pl.when(section[0] != place)
                def _():
                    other[rows] = columns.astype(BF16)


def attend_grads(section, low, attended, hidden, grads):
    width, tokens = attended[0].shape
    depth = hidden[0].shape[1]
    return call(
        attend_grad_kernel,
        [shape((4 * width, depth // 2), F32), shape((4 * width, depth // 2), BF16)],
        [SCALARS] + [WHOLE] * 13 + [NEAR] * 5,
        2 * 4 * 4 * tokens * width * depth,
        2 * 16 * tokens * depth,
    )(section, *low, *attended, *hidden, *grads)


def adam_kernel(axis, factor, weight, first, second, gradient, first_out, second_out, weight_out):
    clipped = gradient[...].astype(F32) * factor[0]
    first_new = BETA_FIRST * first[...] + (1.0 - BETA_FIRST) * clipped
    second_new = BETA_SECOND * second[...] + (1.0 - BETA_SECOND) * clipped * clipped
    first_out[...] = first_new
    second_out[...] = second_new
    first_hat = first_new / (1.0 - BETA_FIRST**STEP)
    second_hat = second_new / (1.0 - BETA_SECOND**STEP)
    moved = weight[...] - LEARN_RATE * first_hat / (jnp.sqrt(second_hat) + ADAM_EPSILON)
    scale = lax.rsqrt(jnp.sum(moved * moved, axis=axis, keepdims=True) + NORM_EPSILON)
    weight_out[...] = moved * scale


def adam_matrix(factor, weight, first, second, gradient, axis, block, place, grid):
    spec = pl.BlockSpec(block, place)
    return call(
        functools.partial(adam_kernel, axis),
        [shape(weight.shape, F32)] * 3,
        [SCALARS] + [spec] * 4,
        20 * weight.size,
        28 * weight.size,
        grid=grid,
        out_specs=[spec] * 3,
    )(factor, weight, first, second, gradient)


def add_parts(parts):
    total = parts[0][...].astype(F32)
    for part in parts[1:]:
        total = total + part[...].astype(F32)
    return total


def mix_kernel(count, hidden, rate, *refs):
    branch_out, result, result_low = refs[count:]
    branch = add_parts(refs[:count])
    branch_out[...] = branch
    mixed = mix_residual(hidden[...].astype(F32), branch, rate[...])
    result[...] = mixed
    result_low[...] = mixed.astype(BF16)


def mix_block(hidden, rate, parts):
    dims = hidden.shape
    return call(
        functools.partial(mix_kernel, len(parts)),
        [shape(dims, F32), shape(dims, F32), shape(dims, BF16)],
        [WHOLE] * 2 + [WHOLE if part.dtype == F32 else NEAR for part in parts],
        10 * dims[0] * dims[1],
        8 * dims[0] * dims[1],
    )(hidden, rate, *parts)


def mix_back_kernel(count, rounded, hidden, branch, rate, *refs):
    grad_hidden, grad_branch, grad_rate = refs[count:]
    upstream = add_parts(refs[:count])
    if rounded:
        upstream = upstream.astype(BF16).astype(F32)
    h, b, r = hidden[...].astype(F32), branch[...], rate[...]
    scale = lax.rsqrt(jnp.sum(b * b, axis=-1, keepdims=True) + NORM_EPSILON)
    unit = b * scale
    apart = unit - h
    mixed = h + r * apart
    mixed_scale = lax.rsqrt(jnp.sum(mixed * mixed, axis=-1, keepdims=True) + NORM_EPSILON)
    mixed = mixed * mixed_scale
    grad = mixed_scale * (upstream - mixed * jnp.sum(mixed * upstream, axis=-1, keepdims=True))
    grad_rate[...] = jnp.sum(grad * apart, axis=0, keepdims=True)
    grad_unit = grad * r
    grad_hidden[...] = grad - grad_unit
    grad_unit = scale * (grad_unit - unit * jnp.sum(unit * grad_unit, axis=-1, keepdims=True))
    grad_branch[...] = grad_unit.astype(BF16)


def mix_back_block(hidden, branch, rate, parts, rounded=False):
    dims = hidden.shape
    return call(
        functools.partial(mix_back_kernel, len(parts), rounded),
        [shape(dims, F32), shape(dims, BF16), shape((1, dims[1]), F32)],
        [WHOLE] * 3 + [WHOLE if part.dtype == F32 else NEAR for part in parts],
        20 * dims[0] * dims[1],
        12 * dims[0] * dims[1],
    )(hidden, branch, rate, *parts)


def tie(*values):
    return lax.optimization_barrier(values)


def to(block, at):
    return exchange(block, "mp", at)


def pass_halves(first, second):
    half = first.shape[0] // 2
    return [to(second[:half], 1), to(first[half:], 2)]


def layer_forward(hidden, low, params, tables, tied, feed_own, later=None):
    attend_in, attend_out, gains, scales, mixing = params
    cosine, sine, starts, info = tables
    project = lambda *places: project_blocks(
        places, [blocks[row] for row in rows_at(places)], attend_in, cosine, sine, gains
    )
    blocks = [low, to(low, 1), to(low, 2)]
    if tied:
        heads = project(0)
        *blocks, heads = tie(*blocks, heads)
        blocks += pass_halves(*blocks[1:])
        heads += project(1, 2)
        *blocks, heads = tie(*blocks, heads)
        heads += project(3)
    else:
        blocks += pass_halves(*blocks[1:])
        heads = project(0, 1, 2, 3)
    raw, query, keys, values = zip(*heads)
    attend = lambda *places: attend_blocks(places, info, starts, query, keys, values, attend_out)
    far = attend(3)
    sent = [to(far[0][-1], 3)]
    near_blocks = attend(1, 2)
    sent += [to(block[-1], at) for at, block in zip((1, 2), near_blocks)]
    attended = attend(0) + near_blocks + far
    sent, attended[0], feed_own = tie(sent, attended[0], feed_own)
    feed_weights = (feed_own, exchange(feed_own, "section", 1))
    branch, middle, middle_low = mix_block(hidden, mixing[:1], (attended[0][-1], *sent))
    blocks_middle, fed, parts = feed_exchange(
        middle_low, lambda places, x: feed_blocks(places, x, feed_weights, scales)
    )
    fed, later = tie(fed, later)
    if later is not None:
        later = (later, exchange(later, "section", 1))
    mixed, result, result_low = mix_block(middle, mixing[1:], parts)
    ups, gates, gated, _ = zip(*fed)
    attended, logsums, _ = zip(*attended)
    stored = (
        (hidden, branch, blocks, raw, query, keys, values, attended, logsums),
        (middle, mixed, blocks_middle, ups, gates, gated),
    )
    return result, result_low, stored, feed_weights, later


def feed_exchange(block, work):
    blocks = [block, to(block, 1), to(block, 2)]
    done = work((0,), blocks[:1])
    *blocks, done = tie(*blocks, done)
    blocks += pass_halves(*blocks[1:])
    done += work((1, 2), blocks[1:3])
    sent = [to(done[at][-1], at) for at in (1, 2)]
    *blocks, done = tie(*blocks, done)
    done += work((3,), blocks[3:])
    sent.append(to(done[3][-1], 3))
    return blocks, done, (done[0][-1], *sent)


def layer_backward(stored, upstream, rounded, params, tables, feed_weights, section, hooks=()):
    attend_in, attend_out, gains, scales, mixing = params
    cosine, sine, starts, info = tables
    attend_stored, (middle, mixed, blocks_middle, ups, gates, gated) = stored
    hidden, branch, blocks_hidden, raw, query, keys, values, attended, logsums = attend_stored
    grad_middle, grad_mixed, rate_two = mix_back_block(
        middle, mixed, mixing[1:], upstream, rounded
    )
    blocks_mixed, done, parts = feed_exchange(
        grad_mixed, lambda places, g: feed_back_blocks(places, g, feed_weights, scales, ups, gates)
    )
    low_ups, low_gates, scale_grads, _ = zip(*done)
    own, other = feed_grads(blocks_middle, blocks_mixed, low_ups, low_gates, gated)
    parts, own, other = tie(parts, own, other)
    other = exchange(other, "section", 1)
    grad_hidden, grad_branch, rate_one = mix_back_block(
        hidden, branch, mixing[:1], (grad_middle, *parts)
    )
    grads = [grad_branch, to(grad_branch, 1), to(grad_branch, 2)]
    feed_sums = (own.astype(F32) + other.astype(F32)).astype(BF16)
    grads, _ = tie(grads, feed_sums)
    grads += pass_halves(*grads[1:])
    small = (scale_grads[0] + scale_grads[1] + scale_grads[3], rate_one[0], rate_two[0])
    if hooks:
        small = hooks[0](small)
    low, partial, gain_grad = attend_back(
        info, starts, query, keys, values, attended, logsums, raw, grads,
        attend_out, attend_in, cosine, sine, gains,
    )
    sent = [to(partial[at], at) for at in (3, 1, 2)]
    if hooks:
        low, small = hooks[1](low, small, gain_grad[:, 0])
    own, other = attend_grads(section, low, attended, blocks_hidden, grads)
    if hooks:
        other, small = hooks[2](other, small)
    other = exchange(other, "section", 1)
    attend_sums = (own + other.astype(F32)).astype(BF16).reshape(4, -1, own.shape[1])
    return (grad_hidden, partial[0], *sent), feed_sums, attend_sums, gain_grad[:, 0], small


def adam_update(weight, first, second, gradient, factor, rate):
    clipped = gradient * factor
    first_new = BETA_FIRST * first + (1.0 - BETA_FIRST) * clipped
    second_new = BETA_SECOND * second + (1.0 - BETA_SECOND) * clipped * clipped
    first_hat = first_new / (1.0 - BETA_FIRST**STEP)
    second_hat = second_new / (1.0 - BETA_SECOND**STEP)
    moved = weight - rate * first_hat / (jnp.sqrt(second_hat) + ADAM_EPSILON)
    return (first_new, second_new, moved)


def per_device(
    inputs,
    cotangent,
    doc_ids,
    attention_in,
    attention_out,
    feedforward_in,
    feedforward_out,
    unit_scales,
    mix_rates,
    first_attention_in,
    second_attention_in,
    first_attention_out,
    second_attention_out,
    first_feedforward_in,
    second_feedforward_in,
    first_feedforward_out,
    second_feedforward_out,
    first_unit_scales,
    second_unit_scales,
    first_mix_rates,
    second_mix_rates,
):
    section = lax.axis_index("section")
    is_first = section == 0
    dp_index = lax.axis_index("dp")
    dp_size = lax.axis_size("dp")
    local_rows = inputs.shape[1]

    def ordered(own, other):
        return jnp.where(is_first, own, other), jnp.where(is_first, other, own)

    def halves(array, dim):
        width = array.shape[dim] // 2
        own = lax.dynamic_slice_in_dim(array, section * width, width, dim)
        other = lax.dynamic_slice_in_dim(array, (1 - section) * width, width, dim)
        return own, other

    hidden_low = lax.dynamic_index_in_dim(inputs, section, 0, False)

    attend_rows = jnp.concatenate(
        [jnp.swapaxes(attention_in[0], 1, 2), attention_out], axis=0
    ).astype(BF16)
    small = jnp.concatenate([unit_scales.reshape(-1), mix_rates.reshape(-1)]).astype(BF16)
    def gather_direct(half):
        if dp_size != 4:
            whole = lax.all_gather(half, "dp", axis=1, tiled=True)
            return whole, whole
        count = half.shape[1]
        blocks = [half] + [exchange(half, "dp", bits) for bits in range(1, dp_size)]
        whole = jnp.zeros((half.shape[0], dp_size * count, half.shape[2]), BF16)
        for bits, block in enumerate(blocks):
            whole = lax.dynamic_update_slice_in_dim(whole, block, (dp_index ^ bits) * count, 1)
        return whole, blocks[1]

    own, other = halves(attend_rows, 2)
    attend_pieces = ordered(own, exchange(other, "section", 1))
    attend_pieces, hidden_low, small = tie(attend_pieces, hidden_low, small)
    attend_first, came = gather_direct(attend_pieces[0])
    feedforward_in_here, feedforward_out_here, attend_second, _ = tie(
        feedforward_in, feedforward_out, attend_pieces[1], came
    )
    feed_rows = jnp.concatenate(
        [jnp.swapaxes(feedforward_in_here[0].astype(BF16), 1, 2), feedforward_out_here.astype(BF16)], axis=0
    )
    own, other = halves(feed_rows, 1)
    feed_pieces = ordered(own, exchange(other, "section", 1))
    attend_owns = (attend_first, lax.all_gather(attend_second, "dp", axis=1, tiled=True))
    small = jnp.stack(ordered(small, exchange(small, "section", 1))).reshape(-1)
    small = gather_small(small, "dp").astype(F32)
    small = small.reshape(dp_size, 2, -1)
    units_here = unit_scales.shape[2]

    def units_apart(values):
        parts = values.reshape(dp_size, 2, -1)
        own, other = ordered(parts[:, 0], parts[:, 1])
        return jnp.concatenate([own.reshape(-1), other.reshape(-1)])

    def units_back(values):
        parts = values.reshape(2, dp_size, -1)
        own, other = ordered(parts[0], parts[1])
        return jnp.stack([own, other], axis=1).reshape(-1)

    layers, feed_owns = [], []
    for layer in range(2):
        feed_own = lax.all_gather(feed_pieces[layer], "dp", axis=1, tiled=True)
        units = small[:, layer, :units_here].reshape(-1)
        mixing = small[:, layer, units_here:].reshape(dp_size, 2, -1)
        mixing = jnp.swapaxes(mixing, 0, 1).reshape(2, -1)
        width_qk, width_ff = attend_owns[0].shape[1], 2 * feed_own.shape[1]
        layers.append((
            units[:width_qk, None],
            jnp.stack([
                units_apart(units[width_qk : width_qk + width_ff]),
                units_apart(units[width_qk + width_ff :]),
            ]),
            mixing,
        ))
        feed_owns.append(feed_own)

    doc_row = lax.dynamic_index_in_dim(doc_ids, section, 0, False)
    starts_all = document_starts(doc_row)
    mp_index = lax.axis_index("mp")
    sources = [mp_index ^ offset for offset in range(4)]
    places = jnp.arange(local_rows, dtype=jnp.int32)
    starts = jnp.stack([
        lax.dynamic_slice_in_dim(starts_all, source * local_rows, local_rows, 0)
        for source in sources
    ])
    sources = jnp.stack(sources).astype(jnp.int32)
    cosine, sine = rope_tables(sources[:, None] * local_rows + places - starts)
    info = jnp.concatenate([sources, starts[:, 0]])
    tables = (cosine, sine, starts, info)

    def scatter(sums):
        return lax.psum_scatter(sums, "dp", scatter_dimension=1, tiled=True)

    def scatter_direct(sums):
        if dp_size != 4:
            return scatter(sums)
        count = sums.shape[1] // dp_size
        parts = [
            lax.dynamic_slice_in_dim(sums, (dp_index ^ bits) * count, count, 1)
            for bits in range(dp_size)
        ]
        parts[1:] = [exchange(part, "dp", bits) for bits, part in enumerate(parts[1:], 1)]
        return sum(part.astype(F32) for part in parts).astype(BF16)

    def small_vector(scales, rate_one, rate_two):
        return jnp.concatenate([units_back(scales[0]), units_back(scales[1]), rate_one, rate_two])

    def attend_params(own, other):
        attend = jnp.concatenate(ordered(own, other), axis=2)
        return attend[:3].reshape(-1, attend.shape[2]), attend[3]

    first, second = layers
    own = attend_owns[0]
    first = (*attend_params(own, exchange(own, "section", 1)), *first)
    section_ref = section.astype(jnp.int32).reshape(1)
    grad = lax.dynamic_index_in_dim(cotangent, section, 0, False)
    _, hidden_second, stored_first, weights_first, later = layer_forward(
        hidden_low, hidden_low, first, tables, False, feed_owns[0], attend_owns[1]
    )
    second = (*attend_params(*later), *second)
    result, _, stored_second, weights_second, _ = layer_forward(
        hidden_second, hidden_second, second, tables, True, feed_owns[1]
    )
    parts, feed_second, attend_second, gains_second, small_second = layer_backward(
        stored_second, (grad,), False, second, tables, weights_second, section_ref
    )
    feed_second = scatter(feed_second)
    parts, attend_second = tie(parts, attend_second)
    attend_second = scatter(attend_second)

    def start_small(small_first):
        values = jnp.concatenate(
            [small_vector(*small_first), small_vector(*small_second), gains_second]
        )
        return values, exchange(values, "section", 1)

    def next_small(low, small, gains):
        low, (values, coming) = tie(low, small)
        values = jnp.concatenate([values + coming, gains])
        return low, (values, exchange(values, "dp", 1))

    def last_small(other, small):
        other, (values, coming) = tie(other, small)
        values, bit = values + coming, 2
        while 2 * bit < dp_size:
            values = values + exchange(values, "dp", bit)
            bit *= 2
        return other, (values, exchange(values, "dp", bit))

    parts, feed_first, attend_first, _, small = layer_backward(
        stored_first, parts, True, first, tables, weights_first, section_ref,
        (start_small, next_small, last_small),
    )
    feed_first = scatter(feed_first)
    attend_first, feed_second, attend_second, small = tie(
        attend_first, feed_second, attend_second, small
    )
    attend_first = scatter_direct(attend_first)

    reduced_first = (attend_first, feed_first)
    reduced_second = (attend_second, feed_second)
    squares = sum(
        jnp.sum(jnp.square(part.astype(F32))) for part in (*reduced_first, *reduced_second)
    )
    gradients = []
    for one, two, dim in zip(reduced_first, reduced_second, (2, 1)):
        own, other = jnp.where(is_first, one, two), jnp.where(is_first, two, one)
        other = exchange(other, "section", 1)
        gradients.append(jnp.concatenate(ordered(own, other), axis=dim))

    sums = small[0] + small[1]
    width_qk, width_rates = gains_second.shape[0], 2 * dp_size * mix_rates.shape[2]
    layer_sums = sums[: -2 * width_qk].reshape(2, -1)
    gain_first = sums[-width_qk:]
    gain_sums = jnp.stack([gain_first + exchange(gain_first, "section", 1), sums[-2 * width_qk : -width_qk]])
    scale_sums, rate_sums = layer_sums[:, :-width_rates], layer_sums[:, -width_rates:]
    rate_sums = sum_over(rate_sums, "mp").reshape(2, 2, -1)
    unit_grads = jnp.concatenate([gain_sums, scale_sums], axis=1)
    unit_grads = jnp.where(is_first, unit_grads[0], unit_grads[1])
    unit_grads = lax.dynamic_slice_in_dim(unit_grads, dp_index * units_here, units_here, 0)
    unit_grads = unit_grads[None, None]
    rates_here = mix_rates.shape[2]
    rate_grads = jnp.where(is_first, rate_sums[0], rate_sums[1])
    rate_grads = lax.dynamic_slice_in_dim(rate_grads, dp_index * rates_here, rates_here, 1)[None]

    turn = lambda array: jnp.swapaxes(array, 1, 2)
    attend_grad, feed_grad = gradients
    feed_in_grad = turn(feed_grad[:2])
    squares, attend_grad, feed_grad, feed_in_grad = tie(
        squares, attend_grad, feed_grad, feed_in_grad
    )
    leading = (mp_index == 0).astype(F32)
    squares = squares + jnp.sum(unit_grads * unit_grads)
    squares = squares + leading * jnp.sum(rate_grads * rate_grads)
    squares = squares.reshape(1)
    squares, parts = tie(squares + exchange(squares, "section", 1), parts)
    squares = sum_over(sum_over(squares, "mp"), "dp")
    gradient_norm = jnp.sqrt(squares[0])
    factor = CLIP_NORM / jnp.maximum(gradient_norm, CLIP_NORM)

    grad = sum(part.astype(F32) for part in parts)
    to_send = jnp.where(is_first, result, grad)
    kept = jnp.where(is_first, grad, result)
    arrived = exchange(to_send, "section", 1)
    boundary_states = jnp.stack(ordered(kept, arrived))[None]

    scalar = factor.reshape(1)
    head_rows, width = attention_out.shape[1:]
    feed_units = feedforward_out.shape[1]
    rows, columns = min(32, head_rows), min(128, feed_units)
    updates = []
    new = adam_matrix(
        scalar, turn(attention_in[0]), turn(first_attention_in[0]), turn(second_attention_in[0]),
        attend_grad[:3], 2, (1, rows, width), lambda i, j: (i, j, 0), (3, head_rows // rows),
    )
    updates.extend(turn(part)[None] for part in new)
    updates.extend(adam_matrix(
        scalar, attention_out, first_attention_out, second_attention_out, attend_grad[3:],
        2, (1, rows, width), lambda i: (0, i, 0), (head_rows // rows,),
    ))
    new = adam_matrix(
        scalar, feedforward_in[0], first_feedforward_in[0], second_feedforward_in[0],
        feed_in_grad, 1, (1, width, columns), lambda i, j: (i, 0, j), (2, feed_units // columns),
    )
    updates.extend(part[None] for part in new)
    rows = min(64, feed_units)
    updates.extend(adam_matrix(
        scalar, feedforward_out, first_feedforward_out, second_feedforward_out, feed_grad[2:],
        2, (1, rows, width), lambda i: (0, i, 0), (feed_units // rows,),
    ))
    updates.extend(
        adam_update(
            unit_scales, first_unit_scales, second_unit_scales, unit_grads, factor, SCALE_RATE
        )
    )
    updates.extend(
        adam_update(
            mix_rates, first_mix_rates, second_mix_rates, rate_grads, factor, MIXING_RATE
        )
    )
    return (boundary_states, gradient_norm, *updates)


def solution(mesh):
    in_specs = (
        P("dp", "mp", None),
        P("dp", "mp", None),
        P("dp", None),
        P("section", None, None, ("mp", "dp")),
        P("section", ("mp", "dp"), None),
        P("section", None, None, ("mp", "dp")),
        P("section", ("mp", "dp"), None),
        P("section", "mp", "dp"),
        P("section", None, "dp"),
        P("section", None, None, ("mp", "dp")),
        P("section", None, None, ("mp", "dp")),
        P("section", ("mp", "dp"), None),
        P("section", ("mp", "dp"), None),
        P("section", None, None, ("mp", "dp")),
        P("section", None, None, ("mp", "dp")),
        P("section", ("mp", "dp"), None),
        P("section", ("mp", "dp"), None),
        P("section", "mp", "dp"),
        P("section", "mp", "dp"),
        P("section", None, "dp"),
        P("section", None, "dp"),
    )
    out_specs = (
        P("section", "dp", "mp", None),
        P(),
        P("section", None, None, ("mp", "dp")),
        P("section", None, None, ("mp", "dp")),
        P("section", None, None, ("mp", "dp")),
        P("section", ("mp", "dp"), None),
        P("section", ("mp", "dp"), None),
        P("section", ("mp", "dp"), None),
        P("section", None, None, ("mp", "dp")),
        P("section", None, None, ("mp", "dp")),
        P("section", None, None, ("mp", "dp")),
        P("section", ("mp", "dp"), None),
        P("section", ("mp", "dp"), None),
        P("section", ("mp", "dp"), None),
        P("section", "mp", "dp"),
        P("section", "mp", "dp"),
        P("section", "mp", "dp"),
        P("section", None, "dp"),
        P("section", None, "dp"),
        P("section", None, "dp"),
    )
    return jax.shard_map(
        per_device, mesh=mesh, in_specs=in_specs, out_specs=out_specs, check_vma=False
    )
```

```python
import functools
import math

import jax
import jax.numpy as jnp
from jax import lax
from jax.experimental import pallas as pl
from jax.experimental.pallas import tpu as pltpu
from jax.sharding import PartitionSpec as P

HD = 64
STEP = 10

NORM_EPSILON = 1e-06
ROPE_BASE = 10000.0
CLIP_NORM = 0.1
LEARN_RATE = 0.05
SCALE_RATE = 1.25
MIXING_RATE = 0.4
BETA_FIRST = 0.9
BETA_SECOND = 0.95
ADAM_EPSILON = 1e-08

BF16 = jnp.bfloat16
F32 = jnp.float32


def exchange(block, axis, bit):
    route = [(i, i ^ bit) for i in range(lax.axis_size(axis))]
    return lax.ppermute(block, axis, route)


def gray(place):
    return place ^ (place >> 1)


def ring_place(index, size):
    shift = 1
    while shift < size:
        index = index ^ (index >> shift)
        shift *= 2
    return index


def ring_step(block, axis):
    size = lax.axis_size(axis)
    route = []
    for place in range(size):
        route.append((gray(place), gray((place + 1) % size)))
        route.append((size + gray(place), size + gray((place - 1) % size)))
    return lax.ppermute(block, ("section", axis), route)


def ring_sources(axis):
    size = lax.axis_size(axis)
    place = ring_place(lax.axis_index(axis), size)
    way = 1 - 2 * lax.axis_index("section")
    return [gray((place - way * step + size) % size) for step in range(size)]


def spread_rows(block, axis="mp"):
    blocks = [block]
    for _ in range(lax.axis_size(axis) - 1):
        blocks.append(ring_step(blocks[-1], axis))
    return blocks


def sum_over(values, axis):
    bit = 1
    while bit < lax.axis_size(axis):
        values = values + exchange(values, axis, bit)
        bit *= 2
    return values


def gather_small(values, axis):
    index = lax.axis_index(axis)
    gathered = values[None]
    bit = 1
    while bit < lax.axis_size(axis):
        other = exchange(gathered, axis, bit)
        low = (index & bit) == 0
        gathered = jnp.concatenate(
            [jnp.where(low, gathered, other), jnp.where(low, other, gathered)], axis=0
        )
        bit *= 2
    return gathered


def unit_norm(values):
    return values * lax.rsqrt(jnp.sum(values * values, axis=-1, keepdims=True) + NORM_EPSILON)


def document_starts(doc_row):
    position = jnp.arange(doc_row.shape[-1], dtype=jnp.int32)
    change = jnp.concatenate([jnp.ones((1,), dtype=jnp.bool_), doc_row[1:] != doc_row[:-1]])
    return lax.cummax(jnp.where(change, position, 0), axis=0)


def rope_tables(offsets):
    half_width = HD // 2
    inverse = 1.0 / ROPE_BASE ** (jnp.arange(half_width, dtype=F32) * (2.0 / HD))
    angles = inverse[:, None] * offsets.astype(F32)[..., None, :]
    angles = jnp.concatenate([angles, angles], axis=-2)
    return jnp.cos(angles), jnp.sin(angles)


def mix_residual(hidden, branch, mixing):
    return unit_norm(hidden + mixing * (unit_norm(branch) - hidden))


NT = (((1,), (1,)), ((), ()))
TN = (((0,), (0,)), ((), ()))
NN = (((1,), (0,)), ((), ()))
VMEM = pltpu.VMEM
WHOLE, NEAR = "whole", "near"
SCALARS = pl.BlockSpec(memory_space=pltpu.SMEM)


def mul(left, right, dims=NN):
    return lax.dot_general(left, right, dims, preferred_element_type=F32)


def block_of(array):
    zeros = (0,) * len(array.shape)
    return pl.BlockSpec(array.shape, lambda *place: zeros)


def call(body, out_shape, in_specs, flops, moved, scratch=(), grid=(1,), out_specs=None, loose=()):
    def run(*args):
        specs = [
            block_of(arg) if spec in (WHOLE, NEAR) else spec for spec, arg in zip(in_specs, args)
        ]
        args = [
            arg if spec in (SCALARS, NEAR) else pltpu.with_memory_space_constraint(arg, pltpu.HBM)
            for spec, arg in zip(in_specs, args)
        ]
        return pl.pallas_call(
            body,
            out_shape=[
                out if at in loose else pltpu.HBM(out.shape, out.dtype)
                for at, out in enumerate(out_shape)
            ],
            grid=grid,
            in_specs=specs,
            out_specs=out_specs or [block_of(out) for out in out_shape],
            scratch_shapes=list(scratch),
            compiler_params=pltpu.CompilerParams(vmem_limit_bytes=50 << 20),
            cost_estimate=pl.CostEstimate(flops=flops, bytes_accessed=moved, transcendentals=0),
        )(*args)

    return run


def shape(dims, dtype):
    return jax.ShapeDtypeStruct(dims, dtype)


def turned(raw, cosine, sine):
    half = HD // 2
    first, second = raw[:half], raw[half:]
    return jnp.concatenate(
        [
            first * cosine[:half] - second * sine[:half],
            second * cosine[half:] + first * sine[half:],
        ],
        axis=0,
    )


def turned_back(grad, cosine, sine):
    half = HD // 2
    first, second = grad[:half], grad[half:]
    return jnp.concatenate(
        [
            first * cosine[:half] + second * sine[half:],
            second * cosine[half:] - first * sine[:half],
        ],
        axis=0,
    )


def rows_at(places):
    return [row for at in places for row in ((at,) if at < 3 else (3, 4))]


def side_by_side(refs):
    return refs[0][...] if len(refs) == 1 else jnp.concatenate([ref[...] for ref in refs], axis=0)


def project_kernel(places, *refs):
    count = len(rows_at(places))
    weight, cosine, sine, gains = refs[count : count + 4]
    tokens = cosine.shape[2]
    x, outs = side_by_side(refs[:count]), refs[count + 4 :]
    for n, at in enumerate(places):
        raw_out, query, keys, values = outs[4 * n : 4 * n + 4]
        width = query.shape[0]
        raw = mul(weight[...], x[n * tokens : (n + 1) * tokens], NT)
        raw_out[...] = raw[: 2 * width]
        values[...] = raw[2 * width :].astype(BF16)
        for part, out in ((0, query), (1, keys)):
            for top in range(0, width, HD):
                turn = turned(
                    raw[part * width + top : part * width + top + HD], cosine[at], sine[at]
                )
                scale = lax.rsqrt(jnp.sum(turn * turn, axis=0, keepdims=True) + NORM_EPSILON)
                head = (turn * scale * gains[top : top + HD]).astype(BF16)
                out[top : top + HD] = head * math.sqrt(HD) if part == 0 else head


def project_blocks(places, x, weight, cosine, sine, gains):
    tokens, depth, count = cosine.shape[2], weight.shape[1], len(places)
    width = weight.shape[0] // 3
    low = shape((width, tokens), BF16)
    outs = call(
        functools.partial(project_kernel, places),
        [shape((2 * width, tokens), F32), low, low, low] * count,
        [NEAR] * len(x) + [WHOLE] * 4,
        2 * tokens * depth * 3 * width * count,
        2 * 3 * width * depth,
    )(*x, weight, cosine, sine, gains)
    return [outs[4 * n : 4 * n + 4] for n in range(count)]


def near(info, at, other, tokens):
    return (info[other] <= info[at]) & ((info[other] + 1) * tokens > info[4 + at])


def seen(info, at, other, starts, tokens):
    key_place = info[other] * tokens + lax.broadcasted_iota(jnp.int32, (tokens, tokens), 0)
    query_place = info[at] * tokens + lax.broadcasted_iota(jnp.int32, (tokens, tokens), 1)
    return (key_place <= query_place) & (key_place >= starts)


def share_out(partial, value):
    partial[...] = value.astype(partial.dtype)


def partial_shape(at, tokens, depth):
    return shape((tokens, depth), BF16 if at else F32)


def attend_kernel(places, info, starts, *refs):
    count = len(places)
    query, rest = refs[:count], refs[count:]
    keys, values, weight, outs, (total, sums) = rest[:4], rest[4:8], rest[8], rest[9:-2], rest[-2:]
    width, tokens = query[0].shape
    for n, at in enumerate(places):
        attended, logsums, partial = outs[3 * n : 3 * n + 3]
        total[n] = jnp.zeros((width, tokens), F32)
        sums[n] = jnp.ones((8, tokens), F32)
        sums[n, : width // HD] = jnp.zeros((width // HD, tokens), F32)
        for other in range(4):

            @pl.when(near(info, at, other, tokens))
            def _():
                allowed = seen(info, at, other, starts[at : at + 1], tokens)
                for head in range(width // HD):
                    rows = slice(head * HD, head * HD + HD)
                    shares = jnp.exp(mul(keys[other][rows], query[n][rows], TN))
                    shares = jnp.where(allowed, shares, 0.0)
                    sums[n, head : head + 1] += jnp.sum(shares, axis=0, keepdims=True)
                    total[n, rows] += mul(values[other][rows], shares.astype(BF16))

        logsums[...] = jnp.log(sums[n])
        inverse = 1.0 / sums[n]
        for head in range(width // HD):
            rows = slice(head * HD, head * HD + HD)
            attended[rows] = (total[n, rows] * inverse[head : head + 1]).astype(BF16)
        share_out(partial, mul(attended[...], weight[...], TN))


def attend_blocks(places, info, starts, query, keys, values, weight):
    width, tokens = query[0].shape
    depth, count = weight.shape[1], len(places)
    outs = call(
        functools.partial(attend_kernel, places),
        [
            out
            for at in places
            for out in (
                shape((width, tokens), BF16),
                shape((8, tokens), F32),
                partial_shape(at, tokens, depth),
            )
        ],
        [SCALARS] + [WHOLE] * (10 + count),
        2 * tokens * (depth * width + 10 * tokens * 256) * count,
        2 * depth * width,
        [VMEM((count, width, tokens), F32), VMEM((count, 8, tokens), F32)],
        loose=[3 * n + 2 for n, at in enumerate(places) if at],
    )(info, starts, *[query[at] for at in places], *keys, *values, weight)
    return [outs[3 * n : 3 * n + 3] for n in range(count)]


def attend_back_kernel(info, starts, *refs):
    query, keys, values, attended, logsums, raw = (refs[4 * n : 4 * n + 4] for n in range(6))
    grads, (w_out, w_in, cosine, sine, gains) = refs[24:29], refs[29:34]
    low, partial, gain_grad = refs[34:38], refs[38:42], refs[42]
    pulled, deltas, grad_query, grad_keys, grad_values = refs[43:]
    width, tokens = query[0].shape
    heads = width // HD
    grad_query[...] = jnp.zeros_like(grad_query)
    grad_keys[...] = jnp.zeros_like(grad_keys)
    grad_values[...] = jnp.zeros_like(grad_values)
    deltas[...] = jnp.zeros_like(deltas)
    for at in range(4):
        rows = side_by_side([grads[row] for row in rows_at((at,))])
        grad = mul(w_out[...], rows, NT).astype(BF16)
        pulled[at] = grad
        product = grad.astype(F32) * attended[at][...].astype(F32)
        for head in range(heads):
            rows = slice(head * HD, head * HD + HD)
            deltas[at, head : head + 1] = jnp.sum(product[rows], axis=0, keepdims=True)
    for at in range(4):
        for other in range(4):

            @pl.when(near(info, at, other, tokens))
            def _():
                allowed = seen(info, at, other, starts[at : at + 1], tokens)
                for head in range(heads):
                    rows = slice(head * HD, head * HD + HD)
                    grad_rows, query_rows = pulled[at, rows], query[at][rows]
                    scores = mul(keys[other][rows], query_rows, TN) - logsums[at][head : head + 1]
                    shares = jnp.where(allowed, jnp.exp(scores), 0.0)
                    grad_shares = mul(values[other][rows], grad_rows, TN)
                    grad_scores = shares * (grad_shares - deltas[at, head : head + 1])
                    grad_scores = grad_scores.astype(BF16)
                    grad_values[other, rows] += mul(grad_rows, shares.astype(BF16), NT)
                    grad_keys[other, rows] += mul(query_rows, grad_scores, NT)
                    grad_query[at, rows] += mul(keys[other][rows], grad_scores)

    gain_total = [0.0] * heads
    for at in range(4):
        cos, sin = cosine[at], sine[at]
        for part, source, factor in ((0, grad_query, math.sqrt(HD)), (1, grad_keys, 1.0)):
            for head in range(heads):
                rows = slice(head * HD, head * HD + HD)
                turn = turned(raw[at][part * width + head * HD : part * width + head * HD + HD], cos, sin)
                scale = lax.rsqrt(jnp.sum(turn * turn, axis=0, keepdims=True) + NORM_EPSILON)
                unit = turn * scale
                grad = source[at, rows] * factor
                gain_total[head] = gain_total[head] + grad * unit
                grad = grad * gains[rows]
                grad = scale * (grad - unit * jnp.sum(unit * grad, axis=0, keepdims=True))
                low[at][part * width + head * HD : part * width + head * HD + HD] = turned_back(
                    grad, cos, sin
                ).astype(BF16)
        low[at][2 * width :] = grad_values[at].astype(BF16)
        share_out(partial[at], mul(low[at][...], w_in[...], TN))
    for head in range(heads):
        gain_grad[head * HD : head * HD + HD] = jnp.sum(gain_total[head], axis=1, keepdims=True)


def attend_back(info, starts, query, keys, values, attended, logsums, raw, grads,
                w_out, w_in, cosine, sine, gains):
    width, tokens = query[0].shape
    depth = w_out.shape[1]
    low = shape((3 * width, tokens), BF16)
    block = VMEM((4, width, tokens), F32)
    outs = call(
        attend_back_kernel,
        [low] * 4
        + [partial_shape(at, tokens, depth) for at in range(4)]
        + [shape((width, 1), F32)],
        [SCALARS] + [WHOLE] * 25 + [NEAR] * 5 + [WHOLE] * 5,
        2 * 4 * tokens * (depth * width * 4 + 60 * tokens * 256),
        2 * depth * width * 12,
        [VMEM((4, width, tokens), BF16), VMEM((4, 8, tokens), F32), block, block, block],
        loose=(5, 6, 7),
    )(info, starts, *query, *keys, *values, *attended, *logsums, *raw, *grads,
      w_out, w_in, cosine, sine, gains)
    return outs[:4], outs[4:8], outs[8]


CHUNK = 256
GATE_WIDTH = math.sqrt(1024)


def started(copies, arrived, first=0):
    copies = [
        pltpu.make_async_copy(source, target, arrived.at[first + n])
        for n, (source, target) in enumerate(copies)
    ]
    for copy in copies:
        copy.start()
    return copies


def fetch_weights(own, other, weights, arrived):
    half = own.shape[1]
    size = min(CHUNK, half)
    places = [(index, start) for index in range(2) for start in range(0, half, size)]
    copies = started(
        [
            ((own, other)[index].at[:, pl.ds(start, size)], weights.at[index, :, pl.ds(start, size)])
            for index, start in places
        ],
        arrived,
    )
    return [
        (copy, index, slice(start, start + size), slice(index * half + start, index * half + start + size))
        for copy, (index, start) in zip(copies, places)
    ]


def feed_kernel(given, count, *refs):
    x, refs = refs[:given], refs[given:]
    (own, other, scales_in), outs, partial = refs[:3], refs[3 : 3 * count + 3], refs[3 * count + 3 : 4 * count + 3]
    weights, scales, ups, gates, gated, gated_turned, arrived, came, left = refs[4 * count + 3 :]
    half, tokens = own.shape[1], ups.shape[0] // count
    (scales_copy,) = started([(scales_in, scales)], came)
    chunks = fetch_weights(own, other, weights, arrived)
    block = side_by_side(x)
    scales_copy.wait()
    leaving = []
    for copy, index, rows, units in chunks:
        copy.wait()
        up, gate = mul(block, weights[index, 0, rows], NT), mul(block, weights[index, 1, rows], NT)
        ups[:, units] = up.astype(BF16)
        gates[:, units] = gate.astype(BF16)
        z = gate * (scales[1:2, units] * GATE_WIDTH)
        silu = z * (0.5 + 0.5 * jnp.tanh(0.5 * z))
        mixed = (up * scales[0:1, units] * silu).astype(BF16)
        gated[:, units] = mixed
        gated_turned[units] = mixed.T
        if rows.stop == half:
            columns = pl.ds(index * half, half)
            for n in range(count):
                places = pl.ds(n * tokens, tokens)
                leaving += started(
                    [
                        (ups.at[places, columns], outs[3 * n].at[:, columns]),
                        (gates.at[places, columns], outs[3 * n + 1].at[:, columns]),
                        (gated_turned.at[columns, places], outs[3 * n + 2].at[columns]),
                    ],
                    left,
                    3 * (index * count + n),
                )
    total = mul(gated[:, :half], weights[0, 2]) + mul(gated[:, half:], weights[1, 2])
    for n in range(count):
        share_out(partial[n], total[n * tokens : (n + 1) * tokens])
    for copy in leaving:
        copy.wait()


def feed_back_kernel(given, count, *refs):
    g, refs = refs[:given], refs[given:]
    (own, other, scales_in), kept = refs[:3], refs[3 : 2 * count + 3]
    outs, scale_grad = refs[2 * count + 3 : 4 * count + 3], refs[4 * count + 3]
    partial = refs[4 * count + 4 : 5 * count + 4]
    weights, scales, ups, gates, low_up, low_gate, up_turned, gate_turned = refs[5 * count + 4 : -3]
    arrived, came, left = refs[-3:]
    half, tokens = own.shape[1], ups.shape[0] // count
    (scales_copy,) = started([(scales_in, scales)], came)
    chunks = fetch_weights(own, other, weights, arrived)
    coming = [
        started(
            [
                (ref.at[:, pl.ds(index * half, half)],
                 into.at[pl.ds(n * tokens, tokens), pl.ds(index * half, half)])
                for n in range(count)
                for ref, into in ((kept[2 * n], ups), (kept[2 * n + 1], gates))
            ],
            came,
            1 + 2 * count * index,
        )
        for index in range(2)
    ]
    block = side_by_side(g)
    scales_copy.wait()
    leaving = []
    for copy, index, rows, units in chunks:
        copy.wait()
        grad = mul(block, weights[index, 2, rows], NT)
        if rows.start == 0:
            for copy in coming[index]:
                copy.wait()
        up, gate = ups[:, units].astype(F32), gates[:, units].astype(F32)
        s_up, s_gate = scales[0:1, units], scales[1:2, units] * GATE_WIDTH
        z = gate * s_gate
        sigmoid = 0.5 + 0.5 * jnp.tanh(0.5 * z)
        silu = z * sigmoid
        grad_silu = grad * silu
        grad_z = grad * (up * s_up) * (sigmoid + silu * (1.0 - sigmoid))
        grad_up, grad_gate = (grad_silu * s_up).astype(BF16), (grad_z * s_gate).astype(BF16)
        low_up[:, units], low_gate[:, units] = grad_up, grad_gate
        up_turned[units], gate_turned[units] = grad_up.T, grad_gate.T
        scale_grad[0:1, units] = jnp.sum(grad_silu * up, axis=0, keepdims=True)
        scale_grad[1:2, units] = jnp.sum(grad_z * gate, axis=0, keepdims=True) * GATE_WIDTH
        if rows.stop == half:
            columns = pl.ds(index * half, half)
            for n in range(count):
                places = pl.ds(n * tokens, tokens)
                leaving += started(
                    [
                        (up_turned.at[columns, places], outs[2 * n].at[columns]),
                        (gate_turned.at[columns, places], outs[2 * n + 1].at[columns]),
                    ],
                    left,
                    2 * (index * count + n),
                )
    total = mul(low_up[:, :half], weights[0, 0]) + mul(low_up[:, half:], weights[1, 0])
    total = total + mul(low_gate[:, :half], weights[0, 1]) + mul(low_gate[:, half:], weights[1, 1])
    for n in range(count):
        share_out(partial[n], total[n * tokens : (n + 1) * tokens])
    for copy in leaving:
        copy.wait()


HELD = pl.BlockSpec(memory_space=pl.ANY)


def feed_call(body, places, x, weights, scales, kept, held, pair, low, turned_count):
    half, count = weights[0].shape[1], len(places)
    tokens, depth = sum(block.shape[0] for block in x) // count, x[0].shape[1]
    partial = [partial_shape(at, tokens, depth) for at in places]
    semaphores = pltpu.SemaphoreType.DMA
    return call(
        functools.partial(body, len(x), count),
        held + pair + partial,
        [NEAR] * len(x) + [HELD] * (3 + len(kept)),
        2 * 6 * tokens * depth * half * count,
        2 * 6 * depth * half,
        [VMEM((2, 3, half, depth), BF16), VMEM(scales.shape, F32)]
        + [VMEM((count * tokens, 2 * half), BF16)] * low
        + [VMEM((2 * half, count * tokens), BF16)] * turned_count
        + [
            semaphores((2 * half // min(CHUNK, half),)),
            semaphores((1 + 2 * len(kept),)),
            semaphores((2 * len(held),)),
        ],
        out_specs=[HELD] * len(held) + [block_of(out) for out in pair + partial],
        loose=[len(held + pair) + n for n, at in enumerate(places) if at],
    )(*x, *weights, scales, *kept)


def feed_blocks(places, x, weights, scales):
    count = len(places)
    dims = (sum(block.shape[0] for block in x) // count, 2 * weights[0].shape[1])
    held = [shape(dims, BF16), shape(dims, BF16), shape(dims[::-1], BF16)] * count
    outs = feed_call(feed_kernel, places, x, weights, scales, (), held, [], 3, 1)
    return [[*outs[3 * n : 3 * n + 3], outs[3 * count + n]] for n in range(count)]


def feed_back_blocks(places, g, weights, scales, ups, gates):
    count = len(places)
    held = [shape(ups[0].shape[::-1], BF16)] * (2 * count)
    pair = [shape((2, ups[0].shape[1]), F32)]
    kept = [array for at in places for array in (ups[at], gates[at])]
    outs = feed_call(feed_back_kernel, places, g, weights, scales, kept, held, pair, 4, 2)
    return [
        [*outs[2 * n : 2 * n + 2], outs[2 * count] if n == 0 else None, outs[2 * count + 1 + n]]
        for n in range(count)
    ]


def feed_grad_kernel(has_other, *refs):
    middle, mixed, (ups, gates, gated) = refs[:5], refs[5:10], (refs[10:14], refs[14:18], refs[18:22])
    out = refs[-1]
    for row, (units, right) in enumerate(((ups, middle), (gates, middle), (gated, mixed))):
        left = jnp.concatenate([block[...] for block in units], axis=1)
        total = mul(left, side_by_side(right))
        if has_other:
            total = total + refs[22][row].astype(F32)
        out[row] = total.astype(BF16)


def feed_grads(half_at, middle, mixed, ups, gates, gated, other=None):
    units, tokens = ups[0].shape
    depth, half = middle[0].shape[1], units // 2
    part = pl.BlockSpec((half, tokens), lambda i: (half_at, 0))
    more = () if other is None else (other,)
    return call(
        functools.partial(feed_grad_kernel, bool(more)),
        [shape((3, half, depth), BF16)],
        [WHOLE] * 5 + [NEAR] * 5 + [part] * 12 + [NEAR] * len(more),
        2 * 3 * 4 * tokens * half * depth,
        2 * 12 * tokens * (half + depth),
    )(*middle, *mixed, *ups, *gates, *gated, *more)[0]


def attend_grad_kernel(section, *refs):
    low, attended, hidden, grads = refs[:4], refs[4:8], refs[8:13], refs[13:18]
    own, other = refs[18:]
    width, half = attended[0].shape[0], own.shape[1]
    for lefts, rights, top in ((low, hidden, 0), (attended, grads, 3 * width)):
        right = side_by_side(rights)
        for start in range(0, lefts[0].shape[0], width):
            total = mul(
                jnp.concatenate([left[start : start + width] for left in lefts], axis=1), right
            )
            rows = slice(top + start, top + start + width)
            for place in range(2):
                columns = total[:, place * half : place * half + half]

                @pl.when(section[0] == place)
                def _():
                    own[rows] = columns

                @pl.when(section[0] != place)
                def _():
                    other[rows] = columns.astype(BF16)


def attend_grads(section, low, attended, hidden, grads):
    width, tokens = attended[0].shape
    depth = hidden[0].shape[1]
    return call(
        attend_grad_kernel,
        [shape((4 * width, depth // 2), F32), shape((4 * width, depth // 2), BF16)],
        [SCALARS] + [WHOLE] * 13 + [NEAR] * 5,
        2 * 4 * 4 * tokens * width * depth,
        2 * 16 * tokens * depth,
    )(section, *low, *attended, *hidden, *grads)


def adam_kernel(axis, factor, weight, first, second, gradient, first_out, second_out, weight_out):
    clipped = gradient[...].astype(F32) * factor[0]
    first_new = BETA_FIRST * first[...] + (1.0 - BETA_FIRST) * clipped
    second_new = BETA_SECOND * second[...] + (1.0 - BETA_SECOND) * clipped * clipped
    first_out[...] = first_new
    second_out[...] = second_new
    first_hat = first_new / (1.0 - BETA_FIRST**STEP)
    second_hat = second_new / (1.0 - BETA_SECOND**STEP)
    moved = weight[...] - LEARN_RATE * first_hat / (jnp.sqrt(second_hat) + ADAM_EPSILON)
    scale = lax.rsqrt(jnp.sum(moved * moved, axis=axis, keepdims=True) + NORM_EPSILON)
    weight_out[...] = moved * scale


def adam_matrix(factor, weight, first, second, gradient, axis, block, place, grid):
    spec = pl.BlockSpec(block, place)
    return call(
        functools.partial(adam_kernel, axis),
        [shape(weight.shape, F32)] * 3,
        [SCALARS] + [spec] * 4,
        20 * weight.size,
        28 * weight.size,
        grid=grid,
        out_specs=[spec] * 3,
    )(factor, weight, first, second, gradient)


def add_parts(parts):
    total = parts[0][...].astype(F32)
    for part in parts[1:]:
        total = total + part[...].astype(F32)
    return total


def mix_kernel(count, hidden, rate, *refs):
    branch_out, result, result_low = refs[count:]
    branch = add_parts(refs[:count])
    branch_out[...] = branch
    mixed = mix_residual(hidden[...].astype(F32), branch, rate[...])
    result[...] = mixed
    result_low[...] = mixed.astype(BF16)


def mix_block(hidden, rate, parts):
    dims = hidden.shape
    return call(
        functools.partial(mix_kernel, len(parts)),
        [shape(dims, F32), shape(dims, F32), shape(dims, BF16)],
        [WHOLE] * 2 + [WHOLE if part.dtype == F32 else NEAR for part in parts],
        10 * dims[0] * dims[1],
        8 * dims[0] * dims[1],
    )(hidden, rate, *parts)


def mix_back_kernel(count, rounded, hidden, branch, rate, *refs):
    grad_hidden, grad_branch, grad_rate = refs[count:]
    upstream = add_parts(refs[:count])
    if rounded:
        upstream = upstream.astype(BF16).astype(F32)
    h, b, r = hidden[...].astype(F32), branch[...], rate[...]
    scale = lax.rsqrt(jnp.sum(b * b, axis=-1, keepdims=True) + NORM_EPSILON)
    unit = b * scale
    apart = unit - h
    mixed = h + r * apart
    mixed_scale = lax.rsqrt(jnp.sum(mixed * mixed, axis=-1, keepdims=True) + NORM_EPSILON)
    mixed = mixed * mixed_scale
    grad = mixed_scale * (upstream - mixed * jnp.sum(mixed * upstream, axis=-1, keepdims=True))
    grad_rate[...] = jnp.sum(grad * apart, axis=0, keepdims=True)
    grad_unit = grad * r
    grad_hidden[...] = grad - grad_unit
    grad_unit = scale * (grad_unit - unit * jnp.sum(unit * grad_unit, axis=-1, keepdims=True))
    grad_branch[...] = grad_unit.astype(BF16)


def mix_back_block(hidden, branch, rate, parts, rounded=False):
    dims = hidden.shape
    return call(
        functools.partial(mix_back_kernel, len(parts), rounded),
        [shape(dims, F32), shape(dims, BF16), shape((1, dims[1]), F32)],
        [WHOLE] * 3 + [WHOLE if part.dtype == F32 else NEAR for part in parts],
        20 * dims[0] * dims[1],
        12 * dims[0] * dims[1],
    )(hidden, branch, rate, *parts)


def tie(*values):
    return lax.optimization_barrier(values)


def to(block, at):
    return exchange(block, "mp", at)


def pass_halves(first, second):
    half = first.shape[0] // 2
    return [to(second[:half], 1), to(first[half:], 2)]


def layer_forward(hidden, low, params, tables, tied, feed_own, later=None):
    attend_in, attend_out, gains, scales, mixing = params
    cosine, sine, starts, info = tables
    project = lambda *places: project_blocks(
        places, [blocks[row] for row in rows_at(places)], attend_in, cosine, sine, gains
    )
    blocks = [low, to(low, 1), to(low, 2)]
    if tied:
        heads = project(0)
        *blocks, heads = tie(*blocks, heads)
        blocks += pass_halves(*blocks[1:])
        heads += project(1, 2)
        *blocks, heads = tie(*blocks, heads)
        heads += project(3)
    else:
        blocks += pass_halves(*blocks[1:])
        heads = project(0, 1, 2, 3)
    raw, query, keys, values = zip(*heads)
    attend = lambda *places: attend_blocks(places, info, starts, query, keys, values, attend_out)
    far = attend(3)
    sent = [to(far[0][-1], 3)]
    near_blocks = attend(1, 2)
    sent += [to(block[-1], at) for at, block in zip((1, 2), near_blocks)]
    attended = attend(0) + near_blocks + far
    sent, attended[0], feed_own = tie(sent, attended[0], feed_own)
    feed_weights = (feed_own, exchange(feed_own, "section", 1))
    branch, middle, middle_low = mix_block(hidden, mixing[:1], (attended[0][-1], *sent))
    blocks_middle, fed, parts = feed_exchange(
        middle_low, lambda places, x: feed_blocks(places, x, feed_weights, scales)
    )
    mixed, result, result_low = mix_block(middle, mixing[1:], parts)
    if later is not None:
        result_low, later = tie(result_low, later)
        later = (later, exchange(later, "section", 1))
    ups, gates, gated, _ = zip(*fed)
    attended, logsums, _ = zip(*attended)
    stored = (
        (hidden, branch, blocks, raw, query, keys, values, attended, logsums),
        (middle, mixed, blocks_middle, ups, gates, gated),
    )
    return result, result_low, stored, feed_weights, later


def feed_exchange(block, work):
    blocks = [block, to(block, 1), to(block, 2)]
    done = work((0,), blocks[:1])
    *blocks, done = tie(*blocks, done)
    blocks += pass_halves(*blocks[1:])
    done += work((1, 2), blocks[1:3])
    sent = [to(done[at][-1], at) for at in (1, 2)]
    *blocks, done = tie(*blocks, done)
    done += work((3,), blocks[3:])
    sent.append(to(done[3][-1], 3))
    return blocks, done, (done[0][-1], *sent)


def layer_backward(stored, upstream, rounded, params, tables, feed_weights, section, hooks=()):
    attend_in, attend_out, gains, scales, mixing = params
    cosine, sine, starts, info = tables
    attend_stored, (middle, mixed, blocks_middle, ups, gates, gated) = stored
    hidden, branch, blocks_hidden, raw, query, keys, values, attended, logsums = attend_stored
    grad_middle, grad_mixed, rate_two = mix_back_block(
        middle, mixed, mixing[1:], upstream, rounded
    )
    blocks_mixed, done, parts = feed_exchange(
        grad_mixed, lambda places, g: feed_back_blocks(places, g, feed_weights, scales, ups, gates)
    )
    low_ups, low_gates, scale_grads, _ = zip(*done)
    operands = (blocks_middle, blocks_mixed, low_ups, low_gates, gated)
    other = feed_grads(1, *operands)
    parts, other = tie(parts, other)
    other = exchange(other, "section", 1)
    grad_hidden, grad_branch, rate_one = mix_back_block(
        hidden, branch, mixing[:1], (grad_middle, *parts)
    )
    grads = [grad_branch, to(grad_branch, 1), to(grad_branch, 2)]
    feed_sums = feed_grads(0, *operands, other)
    grads, _ = tie(grads, feed_sums)
    grads += pass_halves(*grads[1:])
    small = (scale_grads[0] + scale_grads[1] + scale_grads[3], rate_one[0], rate_two[0])
    if hooks:
        small = hooks[0](small)
    low, partial, gain_grad = attend_back(
        info, starts, query, keys, values, attended, logsums, raw, grads,
        attend_out, attend_in, cosine, sine, gains,
    )
    sent = [to(partial[at], at) for at in (3, 1, 2)]
    if hooks:
        low, small = hooks[1](low, small, gain_grad[:, 0])
    own, other = attend_grads(section, low, attended, blocks_hidden, grads)
    if hooks:
        other, small = hooks[2](other, small)
    other = exchange(other, "section", 1)
    attend_sums = (own + other.astype(F32)).astype(BF16).reshape(4, -1, own.shape[1])
    return (grad_hidden, partial[0], *sent), feed_sums, attend_sums, gain_grad[:, 0], small


def adam_update(weight, first, second, gradient, factor, rate):
    clipped = gradient * factor
    first_new = BETA_FIRST * first + (1.0 - BETA_FIRST) * clipped
    second_new = BETA_SECOND * second + (1.0 - BETA_SECOND) * clipped * clipped
    first_hat = first_new / (1.0 - BETA_FIRST**STEP)
    second_hat = second_new / (1.0 - BETA_SECOND**STEP)
    moved = weight - rate * first_hat / (jnp.sqrt(second_hat) + ADAM_EPSILON)
    return (first_new, second_new, moved)


def per_device(
    inputs,
    cotangent,
    doc_ids,
    attention_in,
    attention_out,
    feedforward_in,
    feedforward_out,
    unit_scales,
    mix_rates,
    first_attention_in,
    second_attention_in,
    first_attention_out,
    second_attention_out,
    first_feedforward_in,
    second_feedforward_in,
    first_feedforward_out,
    second_feedforward_out,
    first_unit_scales,
    second_unit_scales,
    first_mix_rates,
    second_mix_rates,
):
    section = lax.axis_index("section")
    is_first = section == 0
    dp_index = lax.axis_index("dp")
    dp_size = lax.axis_size("dp")
    local_rows = inputs.shape[1]

    def ordered(own, other):
        return jnp.where(is_first, own, other), jnp.where(is_first, other, own)

    def halves(array, dim):
        width = array.shape[dim] // 2
        own = lax.dynamic_slice_in_dim(array, section * width, width, dim)
        other = lax.dynamic_slice_in_dim(array, (1 - section) * width, width, dim)
        return own, other

    hidden_low = lax.dynamic_index_in_dim(inputs, section, 0, False)

    attend_rows = jnp.concatenate(
        [jnp.swapaxes(attention_in[0], 1, 2), attention_out], axis=0
    ).astype(BF16)
    small = jnp.concatenate([unit_scales.reshape(-1), mix_rates.reshape(-1)]).astype(BF16)
    def gather_ring(half):
        if dp_size != 4:
            whole = lax.all_gather(half, "dp", axis=1, tiled=True)
            return whole, whole
        blocks, count = spread_rows(half, "dp"), half.shape[1]
        whole = jnp.zeros((half.shape[0], dp_size * count, half.shape[2]), BF16)
        for source, block in zip(ring_sources("dp"), blocks):
            whole = lax.dynamic_update_slice_in_dim(whole, block, source * count, 1)
        return whole, blocks[-2]

    own, other = halves(attend_rows, 2)
    attend_pieces = ordered(own, exchange(other, "section", 1))
    attend_pieces, feedforward_in_here, feedforward_out_here = tie(
        attend_pieces, feedforward_in, feedforward_out
    )
    feed_rows = jnp.concatenate(
        [jnp.swapaxes(feedforward_in_here[0].astype(BF16), 1, 2), feedforward_out_here.astype(BF16)], axis=0
    )
    own, other = halves(feed_rows, 1)
    feed_pieces = ordered(own, exchange(other, "section", 1))
    attend_first, came = gather_ring(attend_pieces[0])
    attend_second, *feed_pieces, _ = tie(attend_pieces[1], *feed_pieces, came)
    attend_owns = (attend_first, lax.all_gather(attend_second, "dp", axis=1, tiled=True))
    small = jnp.stack(ordered(small, exchange(small, "section", 1))).reshape(-1)
    small = gather_small(small, "dp").astype(F32)
    small = small.reshape(dp_size, 2, -1)
    units_here = unit_scales.shape[2]

    def units_apart(values):
        parts = values.reshape(dp_size, 2, -1)
        own, other = ordered(parts[:, 0], parts[:, 1])
        return jnp.concatenate([own.reshape(-1), other.reshape(-1)])

    def units_back(values):
        parts = values.reshape(2, dp_size, -1)
        own, other = ordered(parts[0], parts[1])
        return jnp.stack([own, other], axis=1).reshape(-1)

    layers, feed_owns = [], []
    for layer in range(2):
        feed_own = lax.all_gather(feed_pieces[layer], "dp", axis=1, tiled=True)
        units = small[:, layer, :units_here].reshape(-1)
        mixing = small[:, layer, units_here:].reshape(dp_size, 2, -1)
        mixing = jnp.swapaxes(mixing, 0, 1).reshape(2, -1)
        width_qk, width_ff = attend_owns[0].shape[1], 2 * feed_own.shape[1]
        layers.append((
            units[:width_qk, None],
            jnp.stack([
                units_apart(units[width_qk : width_qk + width_ff]),
                units_apart(units[width_qk + width_ff :]),
            ]),
            mixing,
        ))
        feed_owns.append(feed_own)

    doc_row = lax.dynamic_index_in_dim(doc_ids, section, 0, False)
    starts_all = document_starts(doc_row)
    mp_index = lax.axis_index("mp")
    sources = [mp_index ^ offset for offset in range(4)]
    places = jnp.arange(local_rows, dtype=jnp.int32)
    starts = jnp.stack([
        lax.dynamic_slice_in_dim(starts_all, source * local_rows, local_rows, 0)
        for source in sources
    ])
    sources = jnp.stack(sources).astype(jnp.int32)
    cosine, sine = rope_tables(sources[:, None] * local_rows + places - starts)
    info = jnp.concatenate([sources, starts[:, 0]])
    tables = (cosine, sine, starts, info)

    def scatter(sums):
        return lax.psum_scatter(sums, "dp", scatter_dimension=1, tiled=True)

    def scatter_direct(sums):
        if dp_size != 4:
            return scatter(sums)
        count = sums.shape[1] // dp_size
        parts = [
            lax.dynamic_slice_in_dim(sums, (dp_index ^ bits) * count, count, 1)
            for bits in range(dp_size)
        ]
        parts[1:] = [exchange(part, "dp", bits) for bits, part in enumerate(parts[1:], 1)]
        return sum(part.astype(F32) for part in parts).astype(BF16)

    def small_vector(scales, rate_one, rate_two):
        return jnp.concatenate([units_back(scales[0]), units_back(scales[1]), rate_one, rate_two])

    def attend_params(own, other):
        attend = jnp.concatenate(ordered(own, other), axis=2)
        return attend[:3].reshape(-1, attend.shape[2]), attend[3]

    first, second = layers
    own = attend_owns[0]
    first = (*attend_params(own, exchange(own, "section", 1)), *first)
    section_ref = section.astype(jnp.int32).reshape(1)
    grad = lax.dynamic_index_in_dim(cotangent, section, 0, False)
    _, hidden_second, stored_first, weights_first, later = layer_forward(
        hidden_low, hidden_low, first, tables, False, feed_owns[0], attend_owns[1]
    )
    second = (*attend_params(*later), *second)
    result, _, stored_second, weights_second, _ = layer_forward(
        hidden_second, hidden_second, second, tables, True, feed_owns[1]
    )
    parts, feed_second, attend_second, gains_second, small_second = layer_backward(
        stored_second, (grad,), False, second, tables, weights_second, section_ref
    )
    feed_second = scatter(feed_second)
    parts, attend_second = tie(parts, attend_second)
    attend_second = scatter(attend_second)

    def start_small(small_first):
        values = jnp.concatenate(
            [small_vector(*small_first), small_vector(*small_second), gains_second]
        )
        return values, exchange(values, "section", 1)

    def next_small(low, small, gains):
        low, (values, coming) = tie(low, small)
        values = jnp.concatenate([values + coming, gains])
        return low, (values, exchange(values, "dp", 1))

    def last_small(other, small):
        other, (values, coming) = tie(other, small)
        values, bit = values + coming, 2
        while 2 * bit < dp_size:
            values = values + exchange(values, "dp", bit)
            bit *= 2
        return other, (values, exchange(values, "dp", bit))

    parts, feed_first, attend_first, _, small = layer_backward(
        stored_first, parts, True, first, tables, weights_first, section_ref,
        (start_small, next_small, last_small),
    )
    feed_first = scatter(feed_first)
    attend_first, feed_second, attend_second, small = tie(
        attend_first, feed_second, attend_second, small
    )
    attend_first = scatter_direct(attend_first)

    reduced_first = (attend_first, feed_first)
    reduced_second = (attend_second, feed_second)
    squares = sum(
        jnp.sum(jnp.square(part.astype(F32))) for part in (*reduced_first, *reduced_second)
    )
    gradients = []
    for one, two, dim in zip(reduced_first, reduced_second, (2, 1)):
        own, other = jnp.where(is_first, one, two), jnp.where(is_first, two, one)
        other = exchange(other, "section", 1)
        gradients.append(jnp.concatenate(ordered(own, other), axis=dim))

    sums = small[0] + small[1]
    width_qk, width_rates = gains_second.shape[0], 2 * dp_size * mix_rates.shape[2]
    layer_sums = sums[: -2 * width_qk].reshape(2, -1)
    gain_first = sums[-width_qk:]
    gain_sums = jnp.stack([gain_first + exchange(gain_first, "section", 1), sums[-2 * width_qk : -width_qk]])
    scale_sums, rate_sums = layer_sums[:, :-width_rates], layer_sums[:, -width_rates:]
    rate_sums = sum_over(rate_sums, "mp").reshape(2, 2, -1)
    unit_grads = jnp.concatenate([gain_sums, scale_sums], axis=1)
    unit_grads = jnp.where(is_first, unit_grads[0], unit_grads[1])
    unit_grads = lax.dynamic_slice_in_dim(unit_grads, dp_index * units_here, units_here, 0)
    unit_grads = unit_grads[None, None]
    rates_here = mix_rates.shape[2]
    rate_grads = jnp.where(is_first, rate_sums[0], rate_sums[1])
    rate_grads = lax.dynamic_slice_in_dim(rate_grads, dp_index * rates_here, rates_here, 1)[None]

    turn = lambda array: jnp.swapaxes(array, 1, 2)
    attend_grad, feed_grad = gradients
    feed_in_grad = turn(feed_grad[:2])
    squares, attend_grad, feed_grad, feed_in_grad = tie(
        squares, attend_grad, feed_grad, feed_in_grad
    )
    leading = (mp_index == 0).astype(F32)
    squares = squares + jnp.sum(unit_grads * unit_grads)
    squares = squares + leading * jnp.sum(rate_grads * rate_grads)
    squares = squares.reshape(1)
    squares, parts = tie(squares, parts)
    squares = squares + exchange(squares, "section", 1)
    squares = sum_over(sum_over(squares, "mp"), "dp")
    gradient_norm = jnp.sqrt(squares[0])
    factor = CLIP_NORM / jnp.maximum(gradient_norm, CLIP_NORM)

    grad = sum(part.astype(F32) for part in parts)
    to_send = jnp.where(is_first, result, grad)
    kept = jnp.where(is_first, grad, result)
    arrived = exchange(to_send, "section", 1)
    boundary_states = jnp.stack(ordered(kept, arrived))[None]

    scalar = factor.reshape(1)
    head_rows, width = attention_out.shape[1:]
    feed_units = feedforward_out.shape[1]
    rows, columns = min(32, head_rows), min(128, feed_units)
    updates = []
    new = adam_matrix(
        scalar, turn(attention_in[0]), turn(first_attention_in[0]), turn(second_attention_in[0]),
        attend_grad[:3], 2, (1, rows, width), lambda i, j: (i, j, 0), (3, head_rows // rows),
    )
    updates.extend(turn(part)[None] for part in new)
    updates.extend(adam_matrix(
        scalar, attention_out, first_attention_out, second_attention_out, attend_grad[3:],
        2, (1, rows, width), lambda i: (0, i, 0), (head_rows // rows,),
    ))
    new = adam_matrix(
        scalar, feedforward_in[0], first_feedforward_in[0], second_feedforward_in[0],
        feed_in_grad, 1, (1, width, columns), lambda i, j: (i, 0, j), (2, feed_units // columns),
    )
    updates.extend(part[None] for part in new)
    rows = min(64, feed_units)
    updates.extend(adam_matrix(
        scalar, feedforward_out, first_feedforward_out, second_feedforward_out, feed_grad[2:],
        2, (1, rows, width), lambda i: (0, i, 0), (feed_units // rows,),
    ))
    updates.extend(
        adam_update(
            unit_scales, first_unit_scales, second_unit_scales, unit_grads, factor, SCALE_RATE
        )
    )
    updates.extend(
        adam_update(
            mix_rates, first_mix_rates, second_mix_rates, rate_grads, factor, MIXING_RATE
        )
    )
    return (boundary_states, gradient_norm, *updates)


def solution(mesh):
    in_specs = (
        P("dp", "mp", None),
        P("dp", "mp", None),
        P("dp", None),
        P("section", None, None, ("mp", "dp")),
        P("section", ("mp", "dp"), None),
        P("section", None, None, ("mp", "dp")),
        P("section", ("mp", "dp"), None),
        P("section", "mp", "dp"),
        P("section", None, "dp"),
        P("section", None, None, ("mp", "dp")),
        P("section", None, None, ("mp", "dp")),
        P("section", ("mp", "dp"), None),
        P("section", ("mp", "dp"), None),
        P("section", None, None, ("mp", "dp")),
        P("section", None, None, ("mp", "dp")),
        P("section", ("mp", "dp"), None),
        P("section", ("mp", "dp"), None),
        P("section", "mp", "dp"),
        P("section", "mp", "dp"),
        P("section", None, "dp"),
        P("section", None, "dp"),
    )
    out_specs = (
        P("section", "dp", "mp", None),
        P(),
        P("section", None, None, ("mp", "dp")),
        P("section", None, None, ("mp", "dp")),
        P("section", None, None, ("mp", "dp")),
        P("section", ("mp", "dp"), None),
        P("section", ("mp", "dp"), None),
        P("section", ("mp", "dp"), None),
        P("section", None, None, ("mp", "dp")),
        P("section", None, None, ("mp", "dp")),
        P("section", None, None, ("mp", "dp")),
        P("section", ("mp", "dp"), None),
        P("section", ("mp", "dp"), None),
        P("section", ("mp", "dp"), None),
        P("section", "mp", "dp"),
        P("section", "mp", "dp"),
        P("section", "mp", "dp"),
        P("section", None, "dp"),
        P("section", None, "dp"),
        P("section", None, "dp"),
    )
    return jax.shard_map(
        per_device, mesh=mesh, in_specs=in_specs, out_specs=out_specs, check_vma=False
    )
```

```python
import functools
import math

import jax
import jax.numpy as jnp
from jax import lax
from jax.experimental import pallas as pl
from jax.experimental.pallas import tpu as pltpu
from jax.sharding import PartitionSpec as P

HD = 64
STEP = 10

NORM_EPSILON = 1e-06
ROPE_BASE = 10000.0
CLIP_NORM = 0.1
LEARN_RATE = 0.05
SCALE_RATE = 1.25
MIXING_RATE = 0.4
BETA_FIRST = 0.9
BETA_SECOND = 0.95
ADAM_EPSILON = 1e-08

BF16 = jnp.bfloat16
F32 = jnp.float32


def exchange(block, axis, bit):
    route = [(i, i ^ bit) for i in range(lax.axis_size(axis))]
    return lax.ppermute(block, axis, route)


def gray(place):
    return place ^ (place >> 1)


def ring_place(index, size):
    shift = 1
    while shift < size:
        index = index ^ (index >> shift)
        shift *= 2
    return index


def ring_step(block, axis):
    size = lax.axis_size(axis)
    route = []
    for place in range(size):
        route.append((gray(place), gray((place + 1) % size)))
        route.append((size + gray(place), size + gray((place - 1) % size)))
    return lax.ppermute(block, ("section", axis), route)


def ring_sources(axis):
    size = lax.axis_size(axis)
    place = ring_place(lax.axis_index(axis), size)
    way = 1 - 2 * lax.axis_index("section")
    return [gray((place - way * step + size) % size) for step in range(size)]


def spread_rows(block, axis="mp"):
    blocks = [block]
    for _ in range(lax.axis_size(axis) - 1):
        blocks.append(ring_step(blocks[-1], axis))
    return blocks


def sum_over(values, axis):
    bit = 1
    while bit < lax.axis_size(axis):
        values = values + exchange(values, axis, bit)
        bit *= 2
    return values


def gather_small(values, axis):
    index = lax.axis_index(axis)
    gathered = values[None]
    bit = 1
    while bit < lax.axis_size(axis):
        other = exchange(gathered, axis, bit)
        low = (index & bit) == 0
        gathered = jnp.concatenate(
            [jnp.where(low, gathered, other), jnp.where(low, other, gathered)], axis=0
        )
        bit *= 2
    return gathered


def unit_norm(values):
    return values * lax.rsqrt(jnp.sum(values * values, axis=-1, keepdims=True) + NORM_EPSILON)


def document_starts(doc_row):
    position = jnp.arange(doc_row.shape[-1], dtype=jnp.int32)
    change = jnp.concatenate([jnp.ones((1,), dtype=jnp.bool_), doc_row[1:] != doc_row[:-1]])
    return lax.cummax(jnp.where(change, position, 0), axis=0)


def rope_tables(offsets):
    half_width = HD // 2
    inverse = 1.0 / ROPE_BASE ** (jnp.arange(half_width, dtype=F32) * (2.0 / HD))
    angles = inverse[:, None] * offsets.astype(F32)[..., None, :]
    angles = jnp.concatenate([angles, angles], axis=-2)
    return jnp.cos(angles), jnp.sin(angles)


def mix_residual(hidden, branch, mixing):
    return unit_norm(hidden + mixing * (unit_norm(branch) - hidden))


NT = (((1,), (1,)), ((), ()))
TN = (((0,), (0,)), ((), ()))
NN = (((1,), (0,)), ((), ()))
VMEM = pltpu.VMEM
WHOLE, NEAR = "whole", "near"
SCALARS = pl.BlockSpec(memory_space=pltpu.SMEM)


def mul(left, right, dims=NN):
    return lax.dot_general(left, right, dims, preferred_element_type=F32)


def block_of(array):
    zeros = (0,) * len(array.shape)
    return pl.BlockSpec(array.shape, lambda *place: zeros)


def call(body, out_shape, in_specs, flops, moved, scratch=(), grid=(1,), out_specs=None, loose=()):
    def run(*args):
        specs = [
            block_of(arg) if spec in (WHOLE, NEAR) else spec for spec, arg in zip(in_specs, args)
        ]
        args = [
            arg if spec in (SCALARS, NEAR) else pltpu.with_memory_space_constraint(arg, pltpu.HBM)
            for spec, arg in zip(in_specs, args)
        ]
        return pl.pallas_call(
            body,
            out_shape=[
                out if at in loose else pltpu.HBM(out.shape, out.dtype)
                for at, out in enumerate(out_shape)
            ],
            grid=grid,
            in_specs=specs,
            out_specs=out_specs or [block_of(out) for out in out_shape],
            scratch_shapes=list(scratch),
            compiler_params=pltpu.CompilerParams(vmem_limit_bytes=50 << 20),
            cost_estimate=pl.CostEstimate(flops=flops, bytes_accessed=moved, transcendentals=0),
        )(*args)

    return run


def shape(dims, dtype):
    return jax.ShapeDtypeStruct(dims, dtype)


def turned(raw, cosine, sine):
    half = HD // 2
    first, second = raw[:half], raw[half:]
    return jnp.concatenate(
        [
            first * cosine[:half] - second * sine[:half],
            second * cosine[half:] + first * sine[half:],
        ],
        axis=0,
    )


def turned_back(grad, cosine, sine):
    half = HD // 2
    first, second = grad[:half], grad[half:]
    return jnp.concatenate(
        [
            first * cosine[:half] + second * sine[half:],
            second * cosine[half:] - first * sine[:half],
        ],
        axis=0,
    )


def rows_at(places):
    return [row for at in places for row in ((at,) if at < 3 else (3, 4))]


def side_by_side(refs):
    return refs[0][...] if len(refs) == 1 else jnp.concatenate([ref[...] for ref in refs], axis=0)


def project_kernel(places, *refs):
    count = len(rows_at(places))
    weight, cosine, sine, gains = refs[count : count + 4]
    tokens = cosine.shape[2]
    x, outs = side_by_side(refs[:count]), refs[count + 4 :]
    for n, at in enumerate(places):
        raw_out, query, keys, values = outs[4 * n : 4 * n + 4]
        width = query.shape[0]
        raw = mul(weight[...], x[n * tokens : (n + 1) * tokens], NT)
        raw_out[...] = raw[: 2 * width]
        values[...] = raw[2 * width :].astype(BF16)
        for part, out in ((0, query), (1, keys)):
            for top in range(0, width, HD):
                turn = turned(
                    raw[part * width + top : part * width + top + HD], cosine[at], sine[at]
                )
                scale = lax.rsqrt(jnp.sum(turn * turn, axis=0, keepdims=True) + NORM_EPSILON)
                head = (turn * scale * gains[top : top + HD]).astype(BF16)
                out[top : top + HD] = head * math.sqrt(HD) if part == 0 else head


def project_blocks(places, x, weight, cosine, sine, gains):
    tokens, depth, count = cosine.shape[2], weight.shape[1], len(places)
    width = weight.shape[0] // 3
    low = shape((width, tokens), BF16)
    outs = call(
        functools.partial(project_kernel, places),
        [shape((2 * width, tokens), F32), low, low, low] * count,
        [NEAR] * len(x) + [WHOLE] * 4,
        2 * tokens * depth * 3 * width * count,
        2 * 3 * width * depth,
    )(*x, weight, cosine, sine, gains)
    return [outs[4 * n : 4 * n + 4] for n in range(count)]


def near(info, at, other, tokens):
    return (info[other] <= info[at]) & ((info[other] + 1) * tokens > info[4 + at])


def seen(info, at, other, starts, tokens):
    key_place = info[other] * tokens + lax.broadcasted_iota(jnp.int32, (tokens, tokens), 0)
    query_place = info[at] * tokens + lax.broadcasted_iota(jnp.int32, (tokens, tokens), 1)
    return (key_place <= query_place) & (key_place >= starts)


def share_out(partial, value):
    partial[...] = value.astype(partial.dtype)


def partial_shape(at, tokens, depth):
    return shape((tokens, depth), BF16 if at else F32)


def attend_kernel(places, info, starts, *refs):
    count = len(places)
    query, rest = refs[:count], refs[count:]
    keys, values, weight, outs, (total, sums) = rest[:4], rest[4:8], rest[8], rest[9:-2], rest[-2:]
    width, tokens = query[0].shape
    for n, at in enumerate(places):
        attended, logsums, partial = outs[3 * n : 3 * n + 3]
        total[n] = jnp.zeros((width, tokens), F32)
        sums[n] = jnp.ones((8, tokens), F32)
        sums[n, : width // HD] = jnp.zeros((width // HD, tokens), F32)
        for other in range(4):

            @pl.when(near(info, at, other, tokens))
            def _():
                allowed = seen(info, at, other, starts[at : at + 1], tokens)
                for head in range(width // HD):
                    rows = slice(head * HD, head * HD + HD)
                    shares = jnp.exp(mul(keys[other][rows], query[n][rows], TN))
                    shares = jnp.where(allowed, shares, 0.0)
                    sums[n, head : head + 1] += jnp.sum(shares, axis=0, keepdims=True)
                    total[n, rows] += mul(values[other][rows], shares.astype(BF16))

        logsums[...] = jnp.log(sums[n])
        inverse = 1.0 / sums[n]
        for head in range(width // HD):
            rows = slice(head * HD, head * HD + HD)
            attended[rows] = (total[n, rows] * inverse[head : head + 1]).astype(BF16)
        share_out(partial, mul(attended[...], weight[...], TN))


def attend_blocks(places, info, starts, query, keys, values, weight):
    width, tokens = query[0].shape
    depth, count = weight.shape[1], len(places)
    outs = call(
        functools.partial(attend_kernel, places),
        [
            out
            for at in places
            for out in (
                shape((width, tokens), BF16),
                shape((8, tokens), F32),
                partial_shape(at, tokens, depth),
            )
        ],
        [SCALARS] + [WHOLE] * (10 + count),
        2 * tokens * (depth * width + 10 * tokens * 256) * count,
        2 * depth * width,
        [VMEM((count, width, tokens), F32), VMEM((count, 8, tokens), F32)],
        loose=[3 * n + 2 for n, at in enumerate(places) if at],
    )(info, starts, *[query[at] for at in places], *keys, *values, weight)
    return [outs[3 * n : 3 * n + 3] for n in range(count)]


def attend_back_kernel(info, starts, *refs):
    query, keys, values, attended, logsums, raw = (refs[4 * n : 4 * n + 4] for n in range(6))
    grads, (w_out, w_in, cosine, sine, gains) = refs[24:29], refs[29:34]
    low, partial, gain_grad = refs[34:38], refs[38:42], refs[42]
    pulled, deltas, grad_query, grad_keys, grad_values = refs[43:]
    width, tokens = query[0].shape
    heads = width // HD
    grad_query[...] = jnp.zeros_like(grad_query)
    grad_keys[...] = jnp.zeros_like(grad_keys)
    grad_values[...] = jnp.zeros_like(grad_values)
    deltas[...] = jnp.zeros_like(deltas)
    for at in range(4):
        rows = side_by_side([grads[row] for row in rows_at((at,))])
        grad = mul(w_out[...], rows, NT).astype(BF16)
        pulled[at] = grad
        product = grad.astype(F32) * attended[at][...].astype(F32)
        for head in range(heads):
            rows = slice(head * HD, head * HD + HD)
            deltas[at, head : head + 1] = jnp.sum(product[rows], axis=0, keepdims=True)
    for at in range(4):
        for other in range(4):

            @pl.when(near(info, at, other, tokens))
            def _():
                allowed = seen(info, at, other, starts[at : at + 1], tokens)
                for head in range(heads):
                    rows = slice(head * HD, head * HD + HD)
                    grad_rows, query_rows = pulled[at, rows], query[at][rows]
                    scores = mul(keys[other][rows], query_rows, TN) - logsums[at][head : head + 1]
                    shares = jnp.where(allowed, jnp.exp(scores), 0.0)
                    grad_shares = mul(values[other][rows], grad_rows, TN)
                    grad_scores = shares * (grad_shares - deltas[at, head : head + 1])
                    grad_scores = grad_scores.astype(BF16)
                    grad_values[other, rows] += mul(grad_rows, shares.astype(BF16), NT)
                    grad_keys[other, rows] += mul(query_rows, grad_scores, NT)
                    grad_query[at, rows] += mul(keys[other][rows], grad_scores)

    gain_total = [0.0] * heads
    for at in range(4):
        cos, sin = cosine[at], sine[at]
        for part, source, factor in ((0, grad_query, math.sqrt(HD)), (1, grad_keys, 1.0)):
            for head in range(heads):
                rows = slice(head * HD, head * HD + HD)
                turn = turned(raw[at][part * width + head * HD : part * width + head * HD + HD], cos, sin)
                scale = lax.rsqrt(jnp.sum(turn * turn, axis=0, keepdims=True) + NORM_EPSILON)
                unit = turn * scale
                grad = source[at, rows] * factor
                gain_total[head] = gain_total[head] + grad * unit
                grad = grad * gains[rows]
                grad = scale * (grad - unit * jnp.sum(unit * grad, axis=0, keepdims=True))
                low[at][part * width + head * HD : part * width + head * HD + HD] = turned_back(
                    grad, cos, sin
                ).astype(BF16)
        low[at][2 * width :] = grad_values[at].astype(BF16)
        share_out(partial[at], mul(low[at][...], w_in[...], TN))
    for head in range(heads):
        gain_grad[head * HD : head * HD + HD] = jnp.sum(gain_total[head], axis=1, keepdims=True)


def attend_back(info, starts, query, keys, values, attended, logsums, raw, grads,
                w_out, w_in, cosine, sine, gains):
    width, tokens = query[0].shape
    depth = w_out.shape[1]
    low = shape((3 * width, tokens), BF16)
    block = VMEM((4, width, tokens), F32)
    outs = call(
        attend_back_kernel,
        [low] * 4
        + [partial_shape(at, tokens, depth) for at in range(4)]
        + [shape((width, 1), F32)],
        [SCALARS] + [WHOLE] * 25 + [NEAR] * 5 + [WHOLE] * 5,
        2 * 4 * tokens * (depth * width * 4 + 60 * tokens * 256),
        2 * depth * width * 12,
        [VMEM((4, width, tokens), BF16), VMEM((4, 8, tokens), F32), block, block, block],
        loose=(5, 6, 7),
    )(info, starts, *query, *keys, *values, *attended, *logsums, *raw, *grads,
      w_out, w_in, cosine, sine, gains)
    return outs[:4], outs[4:8], outs[8]


CHUNK = 256
GATE_WIDTH = math.sqrt(1024)


def started(copies, arrived, first=0):
    copies = [
        pltpu.make_async_copy(source, target, arrived.at[first + n])
        for n, (source, target) in enumerate(copies)
    ]
    for copy in copies:
        copy.start()
    return copies


def fetch_weights(own, other, weights, arrived):
    half = own.shape[1]
    size = min(CHUNK, half)
    places = [(index, start) for index in range(2) for start in range(0, half, size)]
    copies = started(
        [
            ((own, other)[index].at[:, pl.ds(start, size)], weights.at[index, :, pl.ds(start, size)])
            for index, start in places
        ],
        arrived,
    )
    return [
        (copy, index, slice(start, start + size), slice(index * half + start, index * half + start + size))
        for copy, (index, start) in zip(copies, places)
    ]


def feed_kernel(given, count, *refs):
    x, refs = refs[:given], refs[given:]
    (own, other, scales_in), outs, partial = refs[:3], refs[3 : 3 * count + 3], refs[3 * count + 3 : 4 * count + 3]
    weights, scales, ups, gates, gated, gated_turned, arrived, came, left = refs[4 * count + 3 :]
    half, tokens = own.shape[1], ups.shape[0] // count
    (scales_copy,) = started([(scales_in, scales)], came)
    chunks = fetch_weights(own, other, weights, arrived)
    block = side_by_side(x)
    scales_copy.wait()
    leaving = []
    for copy, index, rows, units in chunks:
        copy.wait()
        up, gate = mul(block, weights[index, 0, rows], NT), mul(block, weights[index, 1, rows], NT)
        ups[:, units] = up.astype(BF16)
        gates[:, units] = gate.astype(BF16)
        z = gate * (scales[1:2, units] * GATE_WIDTH)
        silu = z * (0.5 + 0.5 * jnp.tanh(0.5 * z))
        mixed = (up * scales[0:1, units] * silu).astype(BF16)
        gated[:, units] = mixed
        gated_turned[units] = mixed.T
        if rows.stop == half:
            columns = pl.ds(index * half, half)
            for n in range(count):
                places = pl.ds(n * tokens, tokens)
                leaving += started(
                    [
                        (ups.at[places, columns], outs[3 * n].at[:, columns]),
                        (gates.at[places, columns], outs[3 * n + 1].at[:, columns]),
                        (gated_turned.at[columns, places], outs[3 * n + 2].at[columns]),
                    ],
                    left,
                    3 * (index * count + n),
                )
    total = mul(gated[:, :half], weights[0, 2]) + mul(gated[:, half:], weights[1, 2])
    for n in range(count):
        share_out(partial[n], total[n * tokens : (n + 1) * tokens])
    for copy in leaving:
        copy.wait()


def feed_back_kernel(given, count, *refs):
    g, refs = refs[:given], refs[given:]
    (own, other, scales_in), kept = refs[:3], refs[3 : 2 * count + 3]
    outs, scale_grad = refs[2 * count + 3 : 4 * count + 3], refs[4 * count + 3]
    partial = refs[4 * count + 4 : 5 * count + 4]
    weights, scales, ups, gates, low_up, low_gate, up_turned, gate_turned = refs[5 * count + 4 : -3]
    arrived, came, left = refs[-3:]
    half, tokens = own.shape[1], ups.shape[0] // count
    (scales_copy,) = started([(scales_in, scales)], came)
    chunks = fetch_weights(own, other, weights, arrived)
    coming = [
        started(
            [
                (ref.at[:, pl.ds(index * half, half)],
                 into.at[pl.ds(n * tokens, tokens), pl.ds(index * half, half)])
                for n in range(count)
                for ref, into in ((kept[2 * n], ups), (kept[2 * n + 1], gates))
            ],
            came,
            1 + 2 * count * index,
        )
        for index in range(2)
    ]
    block = side_by_side(g)
    scales_copy.wait()
    leaving = []
    for copy, index, rows, units in chunks:
        copy.wait()
        grad = mul(block, weights[index, 2, rows], NT)
        if rows.start == 0:
            for copy in coming[index]:
                copy.wait()
        up, gate = ups[:, units].astype(F32), gates[:, units].astype(F32)
        s_up, s_gate = scales[0:1, units], scales[1:2, units] * GATE_WIDTH
        z = gate * s_gate
        sigmoid = 0.5 + 0.5 * jnp.tanh(0.5 * z)
        silu = z * sigmoid
        grad_silu = grad * silu
        grad_z = grad * (up * s_up) * (sigmoid + silu * (1.0 - sigmoid))
        grad_up, grad_gate = (grad_silu * s_up).astype(BF16), (grad_z * s_gate).astype(BF16)
        low_up[:, units], low_gate[:, units] = grad_up, grad_gate
        up_turned[units], gate_turned[units] = grad_up.T, grad_gate.T
        scale_grad[0:1, units] = jnp.sum(grad_silu * up, axis=0, keepdims=True)
        scale_grad[1:2, units] = jnp.sum(grad_z * gate, axis=0, keepdims=True) * GATE_WIDTH
        if rows.stop == half:
            columns = pl.ds(index * half, half)
            for n in range(count):
                places = pl.ds(n * tokens, tokens)
                leaving += started(
                    [
                        (up_turned.at[columns, places], outs[2 * n].at[columns]),
                        (gate_turned.at[columns, places], outs[2 * n + 1].at[columns]),
                    ],
                    left,
                    2 * (index * count + n),
                )
    total = mul(low_up[:, :half], weights[0, 0]) + mul(low_up[:, half:], weights[1, 0])
    total = total + mul(low_gate[:, :half], weights[0, 1]) + mul(low_gate[:, half:], weights[1, 1])
    for n in range(count):
        share_out(partial[n], total[n * tokens : (n + 1) * tokens])
    for copy in leaving:
        copy.wait()


HELD = pl.BlockSpec(memory_space=pl.ANY)


def feed_call(body, places, x, weights, scales, kept, held, pair, low, turned_count):
    half, count = weights[0].shape[1], len(places)
    tokens, depth = sum(block.shape[0] for block in x) // count, x[0].shape[1]
    partial = [partial_shape(at, tokens, depth) for at in places]
    semaphores = pltpu.SemaphoreType.DMA
    return call(
        functools.partial(body, len(x), count),
        held + pair + partial,
        [NEAR] * len(x) + [HELD] * (3 + len(kept)),
        2 * 6 * tokens * depth * half * count,
        2 * 6 * depth * half,
        [VMEM((2, 3, half, depth), BF16), VMEM(scales.shape, F32)]
        + [VMEM((count * tokens, 2 * half), BF16)] * low
        + [VMEM((2 * half, count * tokens), BF16)] * turned_count
        + [
            semaphores((2 * half // min(CHUNK, half),)),
            semaphores((1 + 2 * len(kept),)),
            semaphores((2 * len(held),)),
        ],
        out_specs=[HELD] * len(held) + [block_of(out) for out in pair + partial],
        loose=[len(held + pair) + n for n, at in enumerate(places) if at],
    )(*x, *weights, scales, *kept)


def feed_blocks(places, x, weights, scales):
    count = len(places)
    dims = (sum(block.shape[0] for block in x) // count, 2 * weights[0].shape[1])
    held = [shape(dims, BF16), shape(dims, BF16), shape(dims[::-1], BF16)] * count
    outs = feed_call(feed_kernel, places, x, weights, scales, (), held, [], 3, 1)
    return [[*outs[3 * n : 3 * n + 3], outs[3 * count + n]] for n in range(count)]


def feed_back_blocks(places, g, weights, scales, ups, gates):
    count = len(places)
    held = [shape(ups[0].shape[::-1], BF16)] * (2 * count)
    pair = [shape((2, ups[0].shape[1]), F32)]
    kept = [array for at in places for array in (ups[at], gates[at])]
    outs = feed_call(feed_back_kernel, places, g, weights, scales, kept, held, pair, 4, 2)
    return [
        [*outs[2 * n : 2 * n + 2], outs[2 * count] if n == 0 else None, outs[2 * count + 1 + n]]
        for n in range(count)
    ]


def feed_grad_kernel(has_other, *refs):
    middle, mixed, (ups, gates, gated) = refs[:5], refs[5:10], (refs[10:14], refs[14:18], refs[18:22])
    out = refs[-1]
    for row, (units, right) in enumerate(((ups, middle), (gates, middle), (gated, mixed))):
        left = jnp.concatenate([block[...] for block in units], axis=1)
        total = mul(left, side_by_side(right))
        if has_other:
            total = total + refs[22][row].astype(F32)
        out[row] = total.astype(BF16)


def feed_grads(half_at, middle, mixed, ups, gates, gated, other=None):
    units, tokens = ups[0].shape
    depth, half = middle[0].shape[1], units // 2
    part = pl.BlockSpec((half, tokens), lambda i: (half_at, 0))
    more = () if other is None else (other,)
    return call(
        functools.partial(feed_grad_kernel, bool(more)),
        [shape((3, half, depth), BF16)],
        [WHOLE] * 5 + [NEAR] * 5 + [part] * 12 + [NEAR] * len(more),
        2 * 3 * 4 * tokens * half * depth,
        2 * 12 * tokens * (half + depth),
    )(*middle, *mixed, *ups, *gates, *gated, *more)[0]


def attend_grad_kernel(section, *refs):
    low, attended, hidden, grads = refs[:4], refs[4:8], refs[8:13], refs[13:18]
    own, other = refs[18:]
    width, half = attended[0].shape[0], own.shape[1]
    for lefts, rights, top in ((low, hidden, 0), (attended, grads, 3 * width)):
        right = side_by_side(rights)
        for start in range(0, lefts[0].shape[0], width):
            total = mul(
                jnp.concatenate([left[start : start + width] for left in lefts], axis=1), right
            )
            rows = slice(top + start, top + start + width)
            for place in range(2):
                columns = total[:, place * half : place * half + half]

                @pl.when(section[0] == place)
                def _():
                    own[rows] = columns

                @pl.when(section[0] != place)
                def _():
                    other[rows] = columns.astype(BF16)


def attend_grads(section, low, attended, hidden, grads):
    width, tokens = attended[0].shape
    depth = hidden[0].shape[1]
    return call(
        attend_grad_kernel,
        [shape((4 * width, depth // 2), F32), shape((4 * width, depth // 2), BF16)],
        [SCALARS] + [WHOLE] * 13 + [NEAR] * 5,
        2 * 4 * 4 * tokens * width * depth,
        2 * 16 * tokens * depth,
    )(section, *low, *attended, *hidden, *grads)


def adam_kernel(axis, gradient_of, section, factor, weight, first, second, *refs):
    first_out, second_out, weight_out = refs[4:]
    clipped = gradient_of(section[0] == 0, [ref[...].astype(F32) for ref in refs[:4]]) * factor[0]
    first_new = BETA_FIRST * first[...] + (1.0 - BETA_FIRST) * clipped
    second_new = BETA_SECOND * second[...] + (1.0 - BETA_SECOND) * clipped * clipped
    first_out[...] = first_new
    second_out[...] = second_new
    first_hat = first_new / (1.0 - BETA_FIRST**STEP)
    second_hat = second_new / (1.0 - BETA_SECOND**STEP)
    moved = weight[...] - LEARN_RATE * first_hat / (jnp.sqrt(second_hat) + ADAM_EPSILON)
    scale = lax.rsqrt(jnp.sum(moved * moved, axis=axis, keepdims=True) + NORM_EPSILON)
    weight_out[...] = moved * scale


def adam_matrix(section, factor, arrays, halves, axis, gradient_of, block, half_block, place,
                half_place, grid):
    spec, half_spec = pl.BlockSpec(block, place), pl.BlockSpec(half_block, half_place)
    dims, size = arrays[0].shape, arrays[0].size
    return call(
        functools.partial(adam_kernel, axis, gradient_of),
        [shape(dims, F32)] * 3,
        [SCALARS] * 2 + [spec] * 3 + [half_spec] * 4,
        20 * size,
        28 * size,
        grid=grid,
        out_specs=[spec] * 3,
    )(section, factor, *arrays, *halves)


def half_of(is_first, parts, low_half):
    here, there = jnp.where(is_first, parts[0], parts[1]), jnp.where(is_first, parts[2], parts[3])
    return jnp.where(is_first == low_half, here, there)


def by_columns(is_first, parts):
    return jnp.concatenate(
        [half_of(is_first, parts, True), half_of(is_first, parts, False)], axis=2
    )


def by_rows(steps, is_first, parts):
    return half_of(is_first, parts, pl.program_id(0) < steps)


def by_rows_turned(apart, is_first, parts):
    if apart:
        return half_of(is_first, parts, pl.program_id(1) == 0)[0].T[None]
    both = [half_of(is_first, parts, low)[0] for low in (True, False)]
    return jnp.concatenate(both, axis=0).T[None]


def add_parts(parts):
    total = parts[0][...].astype(F32)
    for part in parts[1:]:
        total = total + part[...].astype(F32)
    return total


def mix_kernel(count, hidden, rate, *refs):
    branch_out, result, result_low = refs[count:]
    branch = add_parts(refs[:count])
    branch_out[...] = branch
    mixed = mix_residual(hidden[...].astype(F32), branch, rate[...])
    result[...] = mixed
    result_low[...] = mixed.astype(BF16)


def mix_block(hidden, rate, parts):
    dims = hidden.shape
    return call(
        functools.partial(mix_kernel, len(parts)),
        [shape(dims, F32), shape(dims, F32), shape(dims, BF16)],
        [WHOLE] * 2 + [WHOLE if part.dtype == F32 else NEAR for part in parts],
        10 * dims[0] * dims[1],
        8 * dims[0] * dims[1],
    )(hidden, rate, *parts)


def mix_back_kernel(count, rounded, hidden, branch, rate, *refs):
    grad_hidden, grad_branch, grad_rate = refs[count:]
    upstream = add_parts(refs[:count])
    if rounded:
        upstream = upstream.astype(BF16).astype(F32)
    h, b, r = hidden[...].astype(F32), branch[...], rate[...]
    scale = lax.rsqrt(jnp.sum(b * b, axis=-1, keepdims=True) + NORM_EPSILON)
    unit = b * scale
    apart = unit - h
    mixed = h + r * apart
    mixed_scale = lax.rsqrt(jnp.sum(mixed * mixed, axis=-1, keepdims=True) + NORM_EPSILON)
    mixed = mixed * mixed_scale
    grad = mixed_scale * (upstream - mixed * jnp.sum(mixed * upstream, axis=-1, keepdims=True))
    grad_rate[...] = jnp.sum(grad * apart, axis=0, keepdims=True)
    grad_unit = grad * r
    grad_hidden[...] = grad - grad_unit
    grad_unit = scale * (grad_unit - unit * jnp.sum(unit * grad_unit, axis=-1, keepdims=True))
    grad_branch[...] = grad_unit.astype(BF16)


def mix_back_block(hidden, branch, rate, parts, rounded=False):
    dims = hidden.shape
    return call(
        functools.partial(mix_back_kernel, len(parts), rounded),
        [shape(dims, F32), shape(dims, BF16), shape((1, dims[1]), F32)],
        [WHOLE] * 3 + [WHOLE if part.dtype == F32 else NEAR for part in parts],
        20 * dims[0] * dims[1],
        12 * dims[0] * dims[1],
    )(hidden, branch, rate, *parts)


def tie(*values):
    return lax.optimization_barrier(values)


def to(block, at):
    return exchange(block, "mp", at)


def pass_halves(first, second):
    half = first.shape[0] // 2
    return [to(second[:half], 1), to(first[half:], 2)]


def layer_forward(hidden, low, params, tables, tied, feed_own, later=None):
    attend_in, attend_out, gains, scales, mixing = params
    cosine, sine, starts, info = tables
    project = lambda *places: project_blocks(
        places, [blocks[row] for row in rows_at(places)], attend_in, cosine, sine, gains
    )
    blocks = [low, to(low, 1), to(low, 2)]
    if tied:
        heads = project(0)
        *blocks, heads = tie(*blocks, heads)
        blocks += pass_halves(*blocks[1:])
        heads += project(1, 2)
        *blocks, heads = tie(*blocks, heads)
        heads += project(3)
    else:
        blocks += pass_halves(*blocks[1:])
        heads = project(0, 1, 2, 3)
    raw, query, keys, values = zip(*heads)
    attend = lambda *places: attend_blocks(places, info, starts, query, keys, values, attend_out)
    far = attend(3)
    sent = [to(far[0][-1], 3)]
    near_blocks = attend(1, 2)
    sent += [to(block[-1], at) for at, block in zip((1, 2), near_blocks)]
    attended = attend(0) + near_blocks + far
    sent, attended[0], feed_own = tie(sent, attended[0], feed_own)
    feed_weights = (feed_own, exchange(feed_own, "section", 1))
    branch, middle, middle_low = mix_block(hidden, mixing[:1], (attended[0][-1], *sent))
    blocks_middle, fed, parts = feed_exchange(
        middle_low, lambda places, x: feed_blocks(places, x, feed_weights, scales)
    )
    mixed, result, result_low = mix_block(middle, mixing[1:], parts)
    if later is not None:
        result_low, later = tie(result_low, later)
        later = (later, exchange(later, "section", 1))
    ups, gates, gated, _ = zip(*fed)
    attended, logsums, _ = zip(*attended)
    stored = (
        (hidden, branch, blocks, raw, query, keys, values, attended, logsums),
        (middle, mixed, blocks_middle, ups, gates, gated),
    )
    return result, result_low, stored, feed_weights, later


def feed_exchange(block, work):
    blocks = [block, to(block, 1), to(block, 2)]
    done = work((0,), blocks[:1])
    *blocks, done = tie(*blocks, done)
    blocks += pass_halves(*blocks[1:])
    done += work((1, 2), blocks[1:3])
    sent = [to(done[at][-1], at) for at in (1, 2)]
    *blocks, done = tie(*blocks, done)
    done += work((3,), blocks[3:])
    sent.append(to(done[3][-1], 3))
    return blocks, done, (done[0][-1], *sent)


def layer_backward(stored, upstream, rounded, params, tables, feed_weights, section, hooks=()):
    attend_in, attend_out, gains, scales, mixing = params
    cosine, sine, starts, info = tables
    attend_stored, (middle, mixed, blocks_middle, ups, gates, gated) = stored
    hidden, branch, blocks_hidden, raw, query, keys, values, attended, logsums = attend_stored
    grad_middle, grad_mixed, rate_two = mix_back_block(
        middle, mixed, mixing[1:], upstream, rounded
    )
    blocks_mixed, done, parts = feed_exchange(
        grad_mixed, lambda places, g: feed_back_blocks(places, g, feed_weights, scales, ups, gates)
    )
    low_ups, low_gates, scale_grads, _ = zip(*done)
    operands = (blocks_middle, blocks_mixed, low_ups, low_gates, gated)
    other = feed_grads(1, *operands)
    parts, other = tie(parts, other)
    other = exchange(other, "section", 1)
    grad_hidden, grad_branch, rate_one = mix_back_block(
        hidden, branch, mixing[:1], (grad_middle, *parts)
    )
    grads = [grad_branch, to(grad_branch, 1), to(grad_branch, 2)]
    feed_sums = feed_grads(0, *operands, other)
    grads, _ = tie(grads, feed_sums)
    grads += pass_halves(*grads[1:])
    small = (scale_grads[0] + scale_grads[1] + scale_grads[3], rate_one[0], rate_two[0])
    if hooks:
        small = hooks[0](small)
    low, partial, gain_grad = attend_back(
        info, starts, query, keys, values, attended, logsums, raw, grads,
        attend_out, attend_in, cosine, sine, gains,
    )
    sent = [to(partial[at], at) for at in (3, 1, 2)]
    if hooks:
        low, small = hooks[1](low, small, gain_grad[:, 0])
    own, other = attend_grads(section, low, attended, blocks_hidden, grads)
    if hooks:
        other, small = hooks[2](other, small)
    other = exchange(other, "section", 1)
    attend_sums = (own + other.astype(F32)).astype(BF16).reshape(4, -1, own.shape[1])
    return (grad_hidden, partial[0], *sent), feed_sums, attend_sums, gain_grad[:, 0], small


def adam_update(weight, first, second, gradient, factor, rate):
    clipped = gradient * factor
    first_new = BETA_FIRST * first + (1.0 - BETA_FIRST) * clipped
    second_new = BETA_SECOND * second + (1.0 - BETA_SECOND) * clipped * clipped
    first_hat = first_new / (1.0 - BETA_FIRST**STEP)
    second_hat = second_new / (1.0 - BETA_SECOND**STEP)
    moved = weight - rate * first_hat / (jnp.sqrt(second_hat) + ADAM_EPSILON)
    return (first_new, second_new, moved)


def per_device(
    inputs,
    cotangent,
    doc_ids,
    attention_in,
    attention_out,
    feedforward_in,
    feedforward_out,
    unit_scales,
    mix_rates,
    first_attention_in,
    second_attention_in,
    first_attention_out,
    second_attention_out,
    first_feedforward_in,
    second_feedforward_in,
    first_feedforward_out,
    second_feedforward_out,
    first_unit_scales,
    second_unit_scales,
    first_mix_rates,
    second_mix_rates,
):
    section = lax.axis_index("section")
    is_first = section == 0
    dp_index = lax.axis_index("dp")
    dp_size = lax.axis_size("dp")
    local_rows = inputs.shape[1]

    def ordered(own, other):
        return jnp.where(is_first, own, other), jnp.where(is_first, other, own)

    def halves(array, dim):
        width = array.shape[dim] // 2
        own = lax.dynamic_slice_in_dim(array, section * width, width, dim)
        other = lax.dynamic_slice_in_dim(array, (1 - section) * width, width, dim)
        return own, other

    hidden_low = lax.dynamic_index_in_dim(inputs, section, 0, False)

    attend_rows = jnp.concatenate(
        [jnp.swapaxes(attention_in[0], 1, 2), attention_out], axis=0
    ).astype(BF16)
    small = jnp.concatenate([unit_scales.reshape(-1), mix_rates.reshape(-1)]).astype(BF16)
    def gather_ring(half):
        if dp_size != 4:
            whole = lax.all_gather(half, "dp", axis=1, tiled=True)
            return whole, whole
        blocks, count = spread_rows(half, "dp"), half.shape[1]
        whole = jnp.zeros((half.shape[0], dp_size * count, half.shape[2]), BF16)
        for source, block in zip(ring_sources("dp"), blocks):
            whole = lax.dynamic_update_slice_in_dim(whole, block, source * count, 1)
        return whole, blocks[-2]

    own, other = halves(attend_rows, 2)
    attend_pieces = ordered(own, exchange(other, "section", 1))
    attend_pieces, feedforward_in_here, feedforward_out_here = tie(
        attend_pieces, feedforward_in, feedforward_out
    )
    feed_rows = jnp.concatenate(
        [jnp.swapaxes(feedforward_in_here[0].astype(BF16), 1, 2), feedforward_out_here.astype(BF16)], axis=0
    )
    own, other = halves(feed_rows, 1)
    feed_pieces = ordered(own, exchange(other, "section", 1))
    attend_first, came = gather_ring(attend_pieces[0])
    attend_second, *feed_pieces, _ = tie(attend_pieces[1], *feed_pieces, came)
    attend_owns = (attend_first, lax.all_gather(attend_second, "dp", axis=1, tiled=True))
    small = jnp.stack(ordered(small, exchange(small, "section", 1))).reshape(-1)
    small = gather_small(small, "dp").astype(F32)
    small = small.reshape(dp_size, 2, -1)
    units_here = unit_scales.shape[2]

    def units_apart(values):
        parts = values.reshape(dp_size, 2, -1)
        own, other = ordered(parts[:, 0], parts[:, 1])
        return jnp.concatenate([own.reshape(-1), other.reshape(-1)])

    def units_back(values):
        parts = values.reshape(2, dp_size, -1)
        own, other = ordered(parts[0], parts[1])
        return jnp.stack([own, other], axis=1).reshape(-1)

    layers, feed_owns = [], []
    for layer in range(2):
        feed_own = lax.all_gather(feed_pieces[layer], "dp", axis=1, tiled=True)
        units = small[:, layer, :units_here].reshape(-1)
        mixing = small[:, layer, units_here:].reshape(dp_size, 2, -1)
        mixing = jnp.swapaxes(mixing, 0, 1).reshape(2, -1)
        width_qk, width_ff = attend_owns[0].shape[1], 2 * feed_own.shape[1]
        layers.append((
            units[:width_qk, None],
            jnp.stack([
                units_apart(units[width_qk : width_qk + width_ff]),
                units_apart(units[width_qk + width_ff :]),
            ]),
            mixing,
        ))
        feed_owns.append(feed_own)

    doc_row = lax.dynamic_index_in_dim(doc_ids, section, 0, False)
    starts_all = document_starts(doc_row)
    mp_index = lax.axis_index("mp")
    sources = [mp_index ^ offset for offset in range(4)]
    places = jnp.arange(local_rows, dtype=jnp.int32)
    starts = jnp.stack([
        lax.dynamic_slice_in_dim(starts_all, source * local_rows, local_rows, 0)
        for source in sources
    ])
    sources = jnp.stack(sources).astype(jnp.int32)
    cosine, sine = rope_tables(sources[:, None] * local_rows + places - starts)
    info = jnp.concatenate([sources, starts[:, 0]])
    tables = (cosine, sine, starts, info)

    def scatter(sums):
        return lax.psum_scatter(sums, "dp", scatter_dimension=1, tiled=True)

    def scatter_direct(sums):
        if dp_size != 4:
            return scatter(sums)
        count = sums.shape[1] // dp_size
        parts = [
            lax.dynamic_slice_in_dim(sums, (dp_index ^ bits) * count, count, 1)
            for bits in range(dp_size)
        ]
        parts[1:] = [exchange(part, "dp", bits) for bits, part in enumerate(parts[1:], 1)]
        return sum(part.astype(F32) for part in parts).astype(BF16)

    def small_vector(scales, rate_one, rate_two):
        return jnp.concatenate([units_back(scales[0]), units_back(scales[1]), rate_one, rate_two])

    def attend_params(own, other):
        attend = jnp.concatenate(ordered(own, other), axis=2)
        return attend[:3].reshape(-1, attend.shape[2]), attend[3]

    first, second = layers
    own = attend_owns[0]
    first = (*attend_params(own, exchange(own, "section", 1)), *first)
    section_ref = section.astype(jnp.int32).reshape(1)
    grad = lax.dynamic_index_in_dim(cotangent, section, 0, False)
    _, hidden_second, stored_first, weights_first, later = layer_forward(
        hidden_low, hidden_low, first, tables, False, feed_owns[0], attend_owns[1]
    )
    second = (*attend_params(*later), *second)
    result, _, stored_second, weights_second, _ = layer_forward(
        hidden_second, hidden_second, second, tables, True, feed_owns[1]
    )
    parts, feed_second, attend_second, gains_second, small_second = layer_backward(
        stored_second, (grad,), False, second, tables, weights_second, section_ref
    )
    feed_second = scatter(feed_second)
    parts, attend_second = tie(parts, attend_second)
    attend_second = scatter(attend_second)

    width_qk, width_rates = gains_second.shape[0], 2 * dp_size * mix_rates.shape[2]

    def start_small(small_first):
        values = jnp.stack([small_vector(*small_first), small_vector(*small_second)])
        values = jnp.concatenate([values.reshape(-1), gains_second])
        values = values + exchange(values, "section", 1)
        values, gains = values[:-width_qk].reshape(2, -1), values[-width_qk:]
        rates = sum_over(values[:, -width_rates:], "mp")
        return jnp.concatenate([values[:, :-width_rates], rates], axis=1), gains

    def next_small(low, small, gains):
        low, (values, gains_two) = tie(low, small)
        return low, (jnp.concatenate([values.reshape(-1), gains_two, gains]),)

    def last_small(other, small):
        other, (values,) = tie(other, small)
        bit = 1
        while 2 * bit < dp_size:
            values = values + exchange(values, "dp", bit)
            bit *= 2
        return other, (values, exchange(values, "dp", bit))

    parts, feed_first, attend_first, _, small = layer_backward(
        stored_first, parts, True, first, tables, weights_first, section_ref,
        (start_small, next_small, last_small),
    )
    feed_first = scatter(feed_first)
    sent_second = [
        lax.ppermute(part, "section", [(0, 1)]) for part in (attend_second, feed_second)
    ]
    attend_first, feed_second, attend_second, small, sent_second = tie(
        attend_first, feed_second, attend_second, small, sent_second
    )
    attend_first = scatter_direct(attend_first)

    reduced_first = (attend_first, feed_first)
    reduced_second = (attend_second, feed_second)
    squares = sum(
        jnp.sum(jnp.square(part.astype(F32))) for part in (*reduced_first, *reduced_second)
    )
    halves_of = [
        (one, two, lax.ppermute(one, "section", [(1, 0)]), theirs)
        for one, two, theirs in zip(reduced_first, reduced_second, sent_second)
    ]

    sums = small[0] + small[1]
    layer_sums = sums[: -2 * width_qk].reshape(2, -1)
    gain_first = sums[-width_qk:]
    gain_sums = jnp.stack([gain_first + exchange(gain_first, "section", 1), sums[-2 * width_qk : -width_qk]])
    scale_sums, rate_sums = layer_sums[:, :-width_rates], layer_sums[:, -width_rates:]
    rate_sums = rate_sums.reshape(2, 2, -1)
    unit_grads = jnp.concatenate([gain_sums, scale_sums], axis=1)
    unit_grads = jnp.where(is_first, unit_grads[0], unit_grads[1])
    unit_grads = lax.dynamic_slice_in_dim(unit_grads, dp_index * units_here, units_here, 0)
    unit_grads = unit_grads[None, None]
    rates_here = mix_rates.shape[2]
    rate_grads = jnp.where(is_first, rate_sums[0], rate_sums[1])
    rate_grads = lax.dynamic_slice_in_dim(rate_grads, dp_index * rates_here, rates_here, 1)[None]

    turn = lambda array: jnp.swapaxes(array, 1, 2)
    leading = (mp_index == 0).astype(F32)
    squares = squares + jnp.sum(unit_grads * unit_grads)
    squares = squares + leading * jnp.sum(rate_grads * rate_grads)
    squares = squares.reshape(1)
    squares, parts = tie(squares, parts)
    squares = squares + exchange(squares, "section", 1)
    squares = sum_over(sum_over(squares, "mp"), "dp")
    gradient_norm = jnp.sqrt(squares[0])
    factor = CLIP_NORM / jnp.maximum(gradient_norm, CLIP_NORM)

    grad = sum(part.astype(F32) for part in parts)
    to_send = jnp.where(is_first, result, grad)
    kept = jnp.where(is_first, grad, result)
    arrived = exchange(to_send, "section", 1)
    boundary_states = jnp.stack(ordered(kept, arrived))[None]

    scalar = factor.reshape(1)
    head_rows, width = attention_out.shape[1:]
    feed_units = feedforward_out.shape[1]
    rows = min(32, head_rows)
    updates = []
    attend_halves, feed_halves = halves_of
    unit_half = feed_units // 2
    apart = unit_half % 128 == 0
    turned = (
        (1, width, unit_half if apart else feed_units), (1, unit_half, width),
        lambda i, j: (i, 0, j), lambda i, j: (i, 0, 0), (2, 2 if apart else 1),
    )
    update = functools.partial(adam_matrix, section_ref, scalar)
    new = update(
        [turn(array[0]) for array in (attention_in, first_attention_in, second_attention_in)],
        attend_halves, 2, by_columns, (1, rows, width), (1, rows, width // 2),
        lambda i, j: (i, j, 0), lambda i, j: (i, j, 0), (3, head_rows // rows),
    )
    updates.extend(turn(part)[None] for part in new)
    updates.extend(update(
        (attention_out, first_attention_out, second_attention_out),
        attend_halves, 2, by_columns, (1, rows, width), (1, rows, width // 2),
        lambda i: (0, i, 0), lambda i: (3, i, 0), (head_rows // rows,),
    ))
    new = update(
        [array[0] for array in (feedforward_in, first_feedforward_in, second_feedforward_in)],
        feed_halves, 1, functools.partial(by_rows_turned, apart), *turned,
    )
    updates.extend(part[None] for part in new)
    steps = max(1, feed_units // 128)
    rows = feed_units // 2 // steps
    updates.extend(update(
        (feedforward_out, first_feedforward_out, second_feedforward_out),
        feed_halves, 2, functools.partial(by_rows, steps), (1, rows, width), (1, rows, width),
        lambda i: (0, i, 0), lambda i: (2, i % steps, 0), (2 * steps,),
    ))
    updates.extend(
        adam_update(
            unit_scales, first_unit_scales, second_unit_scales, unit_grads, factor, SCALE_RATE
        )
    )
    updates.extend(
        adam_update(
            mix_rates, first_mix_rates, second_mix_rates, rate_grads, factor, MIXING_RATE
        )
    )
    return (boundary_states, gradient_norm, *updates)


def solution(mesh):
    in_specs = (
        P("dp", "mp", None),
        P("dp", "mp", None),
        P("dp", None),
        P("section", None, None, ("mp", "dp")),
        P("section", ("mp", "dp"), None),
        P("section", None, None, ("mp", "dp")),
        P("section", ("mp", "dp"), None),
        P("section", "mp", "dp"),
        P("section", None, "dp"),
        P("section", None, None, ("mp", "dp")),
        P("section", None, None, ("mp", "dp")),
        P("section", ("mp", "dp"), None),
        P("section", ("mp", "dp"), None),
        P("section", None, None, ("mp", "dp")),
        P("section", None, None, ("mp", "dp")),
        P("section", ("mp", "dp"), None),
        P("section", ("mp", "dp"), None),
        P("section", "mp", "dp"),
        P("section", "mp", "dp"),
        P("section", None, "dp"),
        P("section", None, "dp"),
    )
    out_specs = (
        P("section", "dp", "mp", None),
        P(),
        P("section", None, None, ("mp", "dp")),
        P("section", None, None, ("mp", "dp")),
        P("section", None, None, ("mp", "dp")),
        P("section", ("mp", "dp"), None),
        P("section", ("mp", "dp"), None),
        P("section", ("mp", "dp"), None),
        P("section", None, None, ("mp", "dp")),
        P("section", None, None, ("mp", "dp")),
        P("section", None, None, ("mp", "dp")),
        P("section", ("mp", "dp"), None),
        P("section", ("mp", "dp"), None),
        P("section", ("mp", "dp"), None),
        P("section", "mp", "dp"),
        P("section", "mp", "dp"),
        P("section", "mp", "dp"),
        P("section", None, "dp"),
        P("section", None, "dp"),
        P("section", None, "dp"),
    )
    return jax.shard_map(
        per_device, mesh=mesh, in_specs=in_specs, out_specs=out_specs, check_vma=False
    )
```

```python
import functools
import math

import jax
import jax.numpy as jnp
from jax import lax
from jax.experimental import pallas as pl
from jax.experimental.pallas import tpu as pltpu
from jax.sharding import PartitionSpec as P

HD = 64
STEP = 10

NORM_EPSILON = 1e-06
ROPE_BASE = 10000.0
CLIP_NORM = 0.1
LEARN_RATE = 0.05
SCALE_RATE = 1.25
MIXING_RATE = 0.4
BETA_FIRST = 0.9
BETA_SECOND = 0.95
ADAM_EPSILON = 1e-08

BF16 = jnp.bfloat16
F32 = jnp.float32


def exchange(block, axis, bit):
    route = [(i, i ^ bit) for i in range(lax.axis_size(axis))]
    return lax.ppermute(block, axis, route)


def gray(place):
    return place ^ (place >> 1)


def ring_place(index, size):
    shift = 1
    while shift < size:
        index = index ^ (index >> shift)
        shift *= 2
    return index


def ring_step(block, axis):
    size = lax.axis_size(axis)
    route = []
    for place in range(size):
        route.append((gray(place), gray((place + 1) % size)))
        route.append((size + gray(place), size + gray((place - 1) % size)))
    return lax.ppermute(block, ("section", axis), route)


def ring_sources(axis):
    size = lax.axis_size(axis)
    place = ring_place(lax.axis_index(axis), size)
    way = 1 - 2 * lax.axis_index("section")
    return [gray((place - way * step + size) % size) for step in range(size)]


def spread_rows(block, axis="mp"):
    blocks = [block]
    for _ in range(lax.axis_size(axis) - 1):
        blocks.append(ring_step(blocks[-1], axis))
    return blocks


def sum_over(values, axis):
    bit = 1
    while bit < lax.axis_size(axis):
        values = values + exchange(values, axis, bit)
        bit *= 2
    return values


def gather_small(values, axis):
    index = lax.axis_index(axis)
    gathered = values[None]
    bit = 1
    while bit < lax.axis_size(axis):
        other = exchange(gathered, axis, bit)
        low = (index & bit) == 0
        gathered = jnp.concatenate(
            [jnp.where(low, gathered, other), jnp.where(low, other, gathered)], axis=0
        )
        bit *= 2
    return gathered


def unit_norm(values):
    return values * lax.rsqrt(jnp.sum(values * values, axis=-1, keepdims=True) + NORM_EPSILON)


def document_starts(doc_row):
    position = jnp.arange(doc_row.shape[-1], dtype=jnp.int32)
    change = jnp.concatenate([jnp.ones((1,), dtype=jnp.bool_), doc_row[1:] != doc_row[:-1]])
    return lax.cummax(jnp.where(change, position, 0), axis=0)


def rope_tables(offsets):
    half_width = HD // 2
    inverse = 1.0 / ROPE_BASE ** (jnp.arange(half_width, dtype=F32) * (2.0 / HD))
    angles = inverse[:, None] * offsets.astype(F32)[..., None, :]
    angles = jnp.concatenate([angles, angles], axis=-2)
    return jnp.cos(angles), jnp.sin(angles)


def mix_residual(hidden, branch, mixing):
    return unit_norm(hidden + mixing * (unit_norm(branch) - hidden))


NT = (((1,), (1,)), ((), ()))
TN = (((0,), (0,)), ((), ()))
NN = (((1,), (0,)), ((), ()))
VMEM = pltpu.VMEM
WHOLE, NEAR = "whole", "near"
SCALARS = pl.BlockSpec(memory_space=pltpu.SMEM)


def mul(left, right, dims=NN):
    return lax.dot_general(left, right, dims, preferred_element_type=F32)


def block_of(array):
    zeros = (0,) * len(array.shape)
    return pl.BlockSpec(array.shape, lambda *place: zeros)


def call(body, out_shape, in_specs, flops, moved, scratch=(), grid=(1,), out_specs=None, loose=()):
    def run(*args):
        specs = [
            block_of(arg) if spec in (WHOLE, NEAR) else spec for spec, arg in zip(in_specs, args)
        ]
        args = [
            arg if spec in (SCALARS, NEAR) else pltpu.with_memory_space_constraint(arg, pltpu.HBM)
            for spec, arg in zip(in_specs, args)
        ]
        return pl.pallas_call(
            body,
            out_shape=[
                out if at in loose else pltpu.HBM(out.shape, out.dtype)
                for at, out in enumerate(out_shape)
            ],
            grid=grid,
            in_specs=specs,
            out_specs=out_specs or [block_of(out) for out in out_shape],
            scratch_shapes=list(scratch),
            compiler_params=pltpu.CompilerParams(vmem_limit_bytes=50 << 20),
            cost_estimate=pl.CostEstimate(flops=flops, bytes_accessed=moved, transcendentals=0),
        )(*args)

    return run


def shape(dims, dtype):
    return jax.ShapeDtypeStruct(dims, dtype)


def turned(raw, cosine, sine):
    half = HD // 2
    first, second = raw[:half], raw[half:]
    return jnp.concatenate(
        [
            first * cosine[:half] - second * sine[:half],
            second * cosine[half:] + first * sine[half:],
        ],
        axis=0,
    )


def turned_back(grad, cosine, sine):
    half = HD // 2
    first, second = grad[:half], grad[half:]
    return jnp.concatenate(
        [
            first * cosine[:half] + second * sine[half:],
            second * cosine[half:] - first * sine[:half],
        ],
        axis=0,
    )


def rows_at(places):
    return [row for at in places for row in ((at,) if at < 3 else (3, 4))]


def side_by_side(refs):
    return refs[0][...] if len(refs) == 1 else jnp.concatenate([ref[...] for ref in refs], axis=0)


def project_kernel(places, *refs):
    count = len(rows_at(places))
    weight, cosine, sine, gains = refs[count : count + 4]
    tokens = cosine.shape[2]
    x, outs = side_by_side(refs[:count]), refs[count + 4 :]
    for n, at in enumerate(places):
        raw_out, query, keys, values = outs[4 * n : 4 * n + 4]
        width = query.shape[0]
        raw = mul(weight[...], x[n * tokens : (n + 1) * tokens], NT)
        raw_out[...] = raw[: 2 * width]
        values[...] = raw[2 * width :].astype(BF16)
        for part, out in ((0, query), (1, keys)):
            for top in range(0, width, HD):
                turn = turned(
                    raw[part * width + top : part * width + top + HD], cosine[at], sine[at]
                )
                scale = lax.rsqrt(jnp.sum(turn * turn, axis=0, keepdims=True) + NORM_EPSILON)
                head = (turn * scale * gains[top : top + HD]).astype(BF16)
                out[top : top + HD] = head * math.sqrt(HD) if part == 0 else head


def project_blocks(places, x, weight, cosine, sine, gains):
    tokens, depth, count = cosine.shape[2], weight.shape[1], len(places)
    width = weight.shape[0] // 3
    low = shape((width, tokens), BF16)
    outs = call(
        functools.partial(project_kernel, places),
        [shape((2 * width, tokens), F32), low, low, low] * count,
        [NEAR] * len(x) + [WHOLE] * 4,
        2 * tokens * depth * 3 * width * count,
        2 * 3 * width * depth,
    )(*x, weight, cosine, sine, gains)
    return [outs[4 * n : 4 * n + 4] for n in range(count)]


def near(info, at, other, tokens):
    return (info[other] <= info[at]) & ((info[other] + 1) * tokens > info[4 + at])


def seen(info, at, other, starts, tokens):
    key_place = info[other] * tokens + lax.broadcasted_iota(jnp.int32, (tokens, tokens), 0)
    query_place = info[at] * tokens + lax.broadcasted_iota(jnp.int32, (tokens, tokens), 1)
    return (key_place <= query_place) & (key_place >= starts)


def share_out(partial, value):
    partial[...] = value.astype(partial.dtype)


def partial_shape(at, tokens, depth):
    return shape((tokens, depth), BF16 if at else F32)


def attend_kernel(places, info, starts, *refs):
    count = len(places)
    query, rest = refs[:count], refs[count:]
    keys, values, weight, outs, (total, sums) = rest[:4], rest[4:8], rest[8], rest[9:-2], rest[-2:]
    width, tokens = query[0].shape
    for n, at in enumerate(places):
        attended, logsums, partial = outs[3 * n : 3 * n + 3]
        total[n] = jnp.zeros((width, tokens), F32)
        sums[n] = jnp.ones((8, tokens), F32)
        sums[n, : width // HD] = jnp.zeros((width // HD, tokens), F32)
        for other in range(4):

            @pl.when(near(info, at, other, tokens))
            def _():
                allowed = seen(info, at, other, starts[at : at + 1], tokens)
                for head in range(width // HD):
                    rows = slice(head * HD, head * HD + HD)
                    shares = jnp.exp(mul(keys[other][rows], query[n][rows], TN))
                    shares = jnp.where(allowed, shares, 0.0)
                    sums[n, head : head + 1] += jnp.sum(shares, axis=0, keepdims=True)
                    total[n, rows] += mul(values[other][rows], shares.astype(BF16))

        logsums[...] = jnp.log(sums[n])
        inverse = 1.0 / sums[n]
        for head in range(width // HD):
            rows = slice(head * HD, head * HD + HD)
            attended[rows] = (total[n, rows] * inverse[head : head + 1]).astype(BF16)
        share_out(partial, mul(attended[...], weight[...], TN))


def attend_blocks(places, info, starts, query, keys, values, weight):
    width, tokens = query[0].shape
    depth, count = weight.shape[1], len(places)
    outs = call(
        functools.partial(attend_kernel, places),
        [
            out
            for at in places
            for out in (
                shape((width, tokens), BF16),
                shape((8, tokens), F32),
                partial_shape(at, tokens, depth),
            )
        ],
        [SCALARS] + [WHOLE] * (10 + count),
        2 * tokens * (depth * width + 10 * tokens * 256) * count,
        2 * depth * width,
        [VMEM((count, width, tokens), F32), VMEM((count, 8, tokens), F32)],
        loose=[3 * n + 2 for n, at in enumerate(places) if at],
    )(info, starts, *[query[at] for at in places], *keys, *values, weight)
    return [outs[3 * n : 3 * n + 3] for n in range(count)]


def attend_back_kernel(info, starts, *refs):
    query, keys, values, attended, logsums, raw = (refs[4 * n : 4 * n + 4] for n in range(6))
    grads, (w_out, w_in, cosine, sine, gains) = refs[24:29], refs[29:34]
    low, partial, gain_grad = refs[34:38], refs[38:42], refs[42]
    pulled, deltas, grad_query, grad_keys, grad_values = refs[43:]
    width, tokens = query[0].shape
    heads = width // HD
    grad_query[...] = jnp.zeros_like(grad_query)
    grad_keys[...] = jnp.zeros_like(grad_keys)
    grad_values[...] = jnp.zeros_like(grad_values)
    deltas[...] = jnp.zeros_like(deltas)
    for at in range(4):
        rows = side_by_side([grads[row] for row in rows_at((at,))])
        grad = mul(w_out[...], rows, NT).astype(BF16)
        pulled[at] = grad
        product = grad.astype(F32) * attended[at][...].astype(F32)
        for head in range(heads):
            rows = slice(head * HD, head * HD + HD)
            deltas[at, head : head + 1] = jnp.sum(product[rows], axis=0, keepdims=True)
    for at in range(4):
        for other in range(4):

            @pl.when(near(info, at, other, tokens))
            def _():
                allowed = seen(info, at, other, starts[at : at + 1], tokens)
                for head in range(heads):
                    rows = slice(head * HD, head * HD + HD)
                    grad_rows, query_rows = pulled[at, rows], query[at][rows]
                    scores = mul(keys[other][rows], query_rows, TN) - logsums[at][head : head + 1]
                    shares = jnp.where(allowed, jnp.exp(scores), 0.0)
                    grad_shares = mul(values[other][rows], grad_rows, TN)
                    grad_scores = shares * (grad_shares - deltas[at, head : head + 1])
                    grad_scores = grad_scores.astype(BF16)
                    grad_values[other, rows] += mul(grad_rows, shares.astype(BF16), NT)
                    grad_keys[other, rows] += mul(query_rows, grad_scores, NT)
                    grad_query[at, rows] += mul(keys[other][rows], grad_scores)

    gain_total = [0.0] * heads
    for at in range(4):
        cos, sin = cosine[at], sine[at]
        for part, source, factor in ((0, grad_query, math.sqrt(HD)), (1, grad_keys, 1.0)):
            for head in range(heads):
                rows = slice(head * HD, head * HD + HD)
                turn = turned(raw[at][part * width + head * HD : part * width + head * HD + HD], cos, sin)
                scale = lax.rsqrt(jnp.sum(turn * turn, axis=0, keepdims=True) + NORM_EPSILON)
                unit = turn * scale
                grad = source[at, rows] * factor
                gain_total[head] = gain_total[head] + grad * unit
                grad = grad * gains[rows]
                grad = scale * (grad - unit * jnp.sum(unit * grad, axis=0, keepdims=True))
                low[at][part * width + head * HD : part * width + head * HD + HD] = turned_back(
                    grad, cos, sin
                ).astype(BF16)
        low[at][2 * width :] = grad_values[at].astype(BF16)
        share_out(partial[at], mul(low[at][...], w_in[...], TN))
    for head in range(heads):
        gain_grad[head * HD : head * HD + HD] = jnp.sum(gain_total[head], axis=1, keepdims=True)


def attend_back(info, starts, query, keys, values, attended, logsums, raw, grads,
                w_out, w_in, cosine, sine, gains):
    width, tokens = query[0].shape
    depth = w_out.shape[1]
    low = shape((3 * width, tokens), BF16)
    block = VMEM((4, width, tokens), F32)
    outs = call(
        attend_back_kernel,
        [low] * 4
        + [partial_shape(at, tokens, depth) for at in range(4)]
        + [shape((width, 1), F32)],
        [SCALARS] + [WHOLE] * 25 + [NEAR] * 5 + [WHOLE] * 5,
        2 * 4 * tokens * (depth * width * 4 + 60 * tokens * 256),
        2 * depth * width * 12,
        [VMEM((4, width, tokens), BF16), VMEM((4, 8, tokens), F32), block, block, block],
        loose=(5, 6, 7),
    )(info, starts, *query, *keys, *values, *attended, *logsums, *raw, *grads,
      w_out, w_in, cosine, sine, gains)
    return outs[:4], outs[4:8], outs[8]


CHUNK = 256
GATE_WIDTH = math.sqrt(1024)


def started(copies, arrived, first=0):
    copies = [
        pltpu.make_async_copy(source, target, arrived.at[first + n])
        for n, (source, target) in enumerate(copies)
    ]
    for copy in copies:
        copy.start()
    return copies


def fetch_weights(own, other, weights, arrived):
    half = own.shape[1]
    size = min(CHUNK, half)
    places = [(index, start) for index in range(2) for start in range(0, half, size)]
    copies = started(
        [
            ((own, other)[index].at[:, pl.ds(start, size)], weights.at[index, :, pl.ds(start, size)])
            for index, start in places
        ],
        arrived,
    )
    return [
        (copy, index, slice(start, start + size), slice(index * half + start, index * half + start + size))
        for copy, (index, start) in zip(copies, places)
    ]


def feed_kernel(given, count, *refs):
    x, refs = refs[:given], refs[given:]
    (own, other, scales_in), outs, partial = refs[:3], refs[3 : 3 * count + 3], refs[3 * count + 3 : 4 * count + 3]
    weights, scales, ups, gates, gated, gated_turned, arrived, came, left = refs[4 * count + 3 :]
    half, tokens = own.shape[1], ups.shape[0] // count
    (scales_copy,) = started([(scales_in, scales)], came)
    chunks = fetch_weights(own, other, weights, arrived)
    block = side_by_side(x)
    scales_copy.wait()
    leaving = []
    for copy, index, rows, units in chunks:
        copy.wait()
        up, gate = mul(block, weights[index, 0, rows], NT), mul(block, weights[index, 1, rows], NT)
        ups[:, units] = up.astype(BF16)
        gates[:, units] = gate.astype(BF16)
        z = gate * (scales[1:2, units] * GATE_WIDTH)
        silu = z * (0.5 + 0.5 * jnp.tanh(0.5 * z))
        mixed = (up * scales[0:1, units] * silu).astype(BF16)
        gated[:, units] = mixed
        gated_turned[units] = mixed.T
        if rows.stop == half:
            columns = pl.ds(index * half, half)
            for n in range(count):
                places = pl.ds(n * tokens, tokens)
                leaving += started(
                    [
                        (ups.at[places, columns], outs[3 * n].at[:, columns]),
                        (gates.at[places, columns], outs[3 * n + 1].at[:, columns]),
                        (gated_turned.at[columns, places], outs[3 * n + 2].at[columns]),
                    ],
                    left,
                    3 * (index * count + n),
                )
    total = mul(gated[:, :half], weights[0, 2]) + mul(gated[:, half:], weights[1, 2])
    for n in range(count):
        share_out(partial[n], total[n * tokens : (n + 1) * tokens])
    for copy in leaving:
        copy.wait()


def feed_back_kernel(given, count, *refs):
    g, refs = refs[:given], refs[given:]
    (own, other, scales_in), kept = refs[:3], refs[3 : 2 * count + 3]
    outs, scale_grad = refs[2 * count + 3 : 4 * count + 3], refs[4 * count + 3]
    partial = refs[4 * count + 4 : 5 * count + 4]
    weights, scales, ups, gates, low_up, low_gate, up_turned, gate_turned = refs[5 * count + 4 : -3]
    arrived, came, left = refs[-3:]
    half, tokens = own.shape[1], ups.shape[0] // count
    (scales_copy,) = started([(scales_in, scales)], came)
    chunks = fetch_weights(own, other, weights, arrived)
    coming = [
        started(
            [
                (ref.at[:, pl.ds(index * half, half)],
                 into.at[pl.ds(n * tokens, tokens), pl.ds(index * half, half)])
                for n in range(count)
                for ref, into in ((kept[2 * n], ups), (kept[2 * n + 1], gates))
            ],
            came,
            1 + 2 * count * index,
        )
        for index in range(2)
    ]
    block = side_by_side(g)
    scales_copy.wait()
    leaving = []
    for copy, index, rows, units in chunks:
        copy.wait()
        grad = mul(block, weights[index, 2, rows], NT)
        if rows.start == 0:
            for copy in coming[index]:
                copy.wait()
        up, gate = ups[:, units].astype(F32), gates[:, units].astype(F32)
        s_up, s_gate = scales[0:1, units], scales[1:2, units] * GATE_WIDTH
        z = gate * s_gate
        sigmoid = 0.5 + 0.5 * jnp.tanh(0.5 * z)
        silu = z * sigmoid
        grad_silu = grad * silu
        grad_z = grad * (up * s_up) * (sigmoid + silu * (1.0 - sigmoid))
        grad_up, grad_gate = (grad_silu * s_up).astype(BF16), (grad_z * s_gate).astype(BF16)
        low_up[:, units], low_gate[:, units] = grad_up, grad_gate
        up_turned[units], gate_turned[units] = grad_up.T, grad_gate.T
        scale_grad[0:1, units] = jnp.sum(grad_silu * up, axis=0, keepdims=True)
        scale_grad[1:2, units] = jnp.sum(grad_z * gate, axis=0, keepdims=True) * GATE_WIDTH
        if rows.stop == half:
            columns = pl.ds(index * half, half)
            for n in range(count):
                places = pl.ds(n * tokens, tokens)
                leaving += started(
                    [
                        (up_turned.at[columns, places], outs[2 * n].at[columns]),
                        (gate_turned.at[columns, places], outs[2 * n + 1].at[columns]),
                    ],
                    left,
                    2 * (index * count + n),
                )
    total = mul(low_up[:, :half], weights[0, 0]) + mul(low_up[:, half:], weights[1, 0])
    total = total + mul(low_gate[:, :half], weights[0, 1]) + mul(low_gate[:, half:], weights[1, 1])
    for n in range(count):
        share_out(partial[n], total[n * tokens : (n + 1) * tokens])
    for copy in leaving:
        copy.wait()


HELD = pl.BlockSpec(memory_space=pl.ANY)


def feed_call(body, places, x, weights, scales, kept, held, pair, low, turned_count):
    half, count = weights[0].shape[1], len(places)
    tokens, depth = sum(block.shape[0] for block in x) // count, x[0].shape[1]
    partial = [partial_shape(at, tokens, depth) for at in places]
    semaphores = pltpu.SemaphoreType.DMA
    return call(
        functools.partial(body, len(x), count),
        held + pair + partial,
        [NEAR] * len(x) + [HELD] * (3 + len(kept)),
        2 * 6 * tokens * depth * half * count,
        2 * 6 * depth * half,
        [VMEM((2, 3, half, depth), BF16), VMEM(scales.shape, F32)]
        + [VMEM((count * tokens, 2 * half), BF16)] * low
        + [VMEM((2 * half, count * tokens), BF16)] * turned_count
        + [
            semaphores((2 * half // min(CHUNK, half),)),
            semaphores((1 + 2 * len(kept),)),
            semaphores((2 * len(held),)),
        ],
        out_specs=[HELD] * len(held) + [block_of(out) for out in pair + partial],
        loose=[len(held + pair) + n for n, at in enumerate(places) if at],
    )(*x, *weights, scales, *kept)


def feed_blocks(places, x, weights, scales):
    count = len(places)
    dims = (sum(block.shape[0] for block in x) // count, 2 * weights[0].shape[1])
    held = [shape(dims, BF16), shape(dims, BF16), shape(dims[::-1], BF16)] * count
    outs = feed_call(feed_kernel, places, x, weights, scales, (), held, [], 3, 1)
    return [[*outs[3 * n : 3 * n + 3], outs[3 * count + n]] for n in range(count)]


def feed_back_blocks(places, g, weights, scales, ups, gates):
    count = len(places)
    held = [shape(ups[0].shape[::-1], BF16)] * (2 * count)
    pair = [shape((2, ups[0].shape[1]), F32)]
    kept = [array for at in places for array in (ups[at], gates[at])]
    outs = feed_call(feed_back_kernel, places, g, weights, scales, kept, held, pair, 4, 2)
    return [
        [*outs[2 * n : 2 * n + 2], outs[2 * count] if n == 0 else None, outs[2 * count + 1 + n]]
        for n in range(count)
    ]


def feed_grad_kernel(has_other, *refs):
    middle, mixed, (ups, gates, gated) = refs[:5], refs[5:10], (refs[10:14], refs[14:18], refs[18:22])
    out = refs[-1]
    for row, (units, right) in enumerate(((ups, middle), (gates, middle), (gated, mixed))):
        left = jnp.concatenate([block[...] for block in units], axis=1)
        total = mul(left, side_by_side(right))
        if has_other:
            total = total + refs[22][row].astype(F32)
        out[row] = total.astype(BF16)


def feed_grads(half_at, middle, mixed, ups, gates, gated, other=None):
    units, tokens = ups[0].shape
    depth, half = middle[0].shape[1], units // 2
    part = pl.BlockSpec((half, tokens), lambda i: (half_at, 0))
    more = () if other is None else (other,)
    return call(
        functools.partial(feed_grad_kernel, bool(more)),
        [shape((3, half, depth), BF16)],
        [WHOLE] * 5 + [NEAR] * 5 + [part] * 12 + [NEAR] * len(more),
        2 * 3 * 4 * tokens * half * depth,
        2 * 12 * tokens * (half + depth),
    )(*middle, *mixed, *ups, *gates, *gated, *more)[0]


def attend_grad_kernel(section, *refs):
    low, attended, hidden, grads = refs[:4], refs[4:8], refs[8:13], refs[13:18]
    own, other = refs[18:]
    width, half = attended[0].shape[0], own.shape[1]
    for lefts, rights, top in ((low, hidden, 0), (attended, grads, 3 * width)):
        right = side_by_side(rights)
        for start in range(0, lefts[0].shape[0], width):
            total = mul(
                jnp.concatenate([left[start : start + width] for left in lefts], axis=1), right
            )
            rows = slice(top + start, top + start + width)
            for place in range(2):
                columns = total[:, place * half : place * half + half]

                @pl.when(section[0] == place)
                def _():
                    own[rows] = columns

                @pl.when(section[0] != place)
                def _():
                    other[rows] = columns.astype(BF16)


def attend_grads(section, low, attended, hidden, grads):
    width, tokens = attended[0].shape
    depth = hidden[0].shape[1]
    return call(
        attend_grad_kernel,
        [shape((4 * width, depth // 2), F32), shape((4 * width, depth // 2), BF16)],
        [SCALARS] + [WHOLE] * 13 + [NEAR] * 5,
        2 * 4 * 4 * tokens * width * depth,
        2 * 16 * tokens * depth,
    )(section, *low, *attended, *hidden, *grads)


def adam_kernel(axis, gradient_of, section, factor, weight, first, second, *refs):
    first_out, second_out, weight_out = refs[4:]
    clipped = gradient_of(section[0] == 0, [ref[...].astype(F32) for ref in refs[:4]]) * factor[0]
    first_new = BETA_FIRST * first[...] + (1.0 - BETA_FIRST) * clipped
    second_new = BETA_SECOND * second[...] + (1.0 - BETA_SECOND) * clipped * clipped
    first_out[...] = first_new
    second_out[...] = second_new
    first_hat = first_new / (1.0 - BETA_FIRST**STEP)
    second_hat = second_new / (1.0 - BETA_SECOND**STEP)
    moved = weight[...] - LEARN_RATE * first_hat / (jnp.sqrt(second_hat) + ADAM_EPSILON)
    scale = lax.rsqrt(jnp.sum(moved * moved, axis=axis, keepdims=True) + NORM_EPSILON)
    weight_out[...] = moved * scale


def adam_matrix(section, factor, arrays, halves, axis, gradient_of, block, half_block, place,
                half_place, grid):
    spec, half_spec = pl.BlockSpec(block, place), pl.BlockSpec(half_block, half_place)
    dims, size = arrays[0].shape, arrays[0].size
    return call(
        functools.partial(adam_kernel, axis, gradient_of),
        [shape(dims, F32)] * 3,
        [SCALARS] * 2 + [spec] * 3 + [half_spec] * 4,
        20 * size,
        28 * size,
        grid=grid,
        out_specs=[spec] * 3,
    )(section, factor, *arrays, *halves)


def half_of(is_first, parts, low_half):
    here, there = jnp.where(is_first, parts[0], parts[1]), jnp.where(is_first, parts[2], parts[3])
    return jnp.where(is_first == low_half, here, there)


def by_columns(is_first, parts):
    return jnp.concatenate(
        [half_of(is_first, parts, True), half_of(is_first, parts, False)], axis=2
    )


def by_rows(is_first, parts):
    return half_of(is_first, parts, pl.program_id(0) == 0)


def by_rows_turned(is_first, parts):
    both = [half_of(is_first, parts, low)[0] for low in (True, False)]
    return jnp.concatenate(both, axis=0).T[None]


def add_parts(parts):
    total = parts[0][...].astype(F32)
    for part in parts[1:]:
        total = total + part[...].astype(F32)
    return total


def mix_kernel(count, hidden, rate, *refs):
    branch_out, result, result_low = refs[count:]
    branch = add_parts(refs[:count])
    branch_out[...] = branch
    mixed = mix_residual(hidden[...].astype(F32), branch, rate[...])
    result[...] = mixed
    result_low[...] = mixed.astype(BF16)


def mix_block(hidden, rate, parts):
    dims = hidden.shape
    return call(
        functools.partial(mix_kernel, len(parts)),
        [shape(dims, F32), shape(dims, F32), shape(dims, BF16)],
        [WHOLE] * 2 + [WHOLE if part.dtype == F32 else NEAR for part in parts],
        10 * dims[0] * dims[1],
        8 * dims[0] * dims[1],
    )(hidden, rate, *parts)


def mix_back_kernel(count, rounded, hidden, branch, rate, *refs):
    grad_hidden, grad_branch, grad_rate = refs[count:]
    upstream = add_parts(refs[:count])
    if rounded:
        upstream = upstream.astype(BF16).astype(F32)
    h, b, r = hidden[...].astype(F32), branch[...], rate[...]
    scale = lax.rsqrt(jnp.sum(b * b, axis=-1, keepdims=True) + NORM_EPSILON)
    unit = b * scale
    apart = unit - h
    mixed = h + r * apart
    mixed_scale = lax.rsqrt(jnp.sum(mixed * mixed, axis=-1, keepdims=True) + NORM_EPSILON)
    mixed = mixed * mixed_scale
    grad = mixed_scale * (upstream - mixed * jnp.sum(mixed * upstream, axis=-1, keepdims=True))
    grad_rate[...] = jnp.sum(grad * apart, axis=0, keepdims=True)
    grad_unit = grad * r
    grad_hidden[...] = grad - grad_unit
    grad_unit = scale * (grad_unit - unit * jnp.sum(unit * grad_unit, axis=-1, keepdims=True))
    grad_branch[...] = grad_unit.astype(BF16)


def mix_back_block(hidden, branch, rate, parts, rounded=False):
    dims = hidden.shape
    return call(
        functools.partial(mix_back_kernel, len(parts), rounded),
        [shape(dims, F32), shape(dims, BF16), shape((1, dims[1]), F32)],
        [WHOLE] * 3 + [WHOLE if part.dtype == F32 else NEAR for part in parts],
        20 * dims[0] * dims[1],
        12 * dims[0] * dims[1],
    )(hidden, branch, rate, *parts)


def tie(*values):
    return lax.optimization_barrier(values)


def to(block, at):
    return exchange(block, "mp", at)


def pass_halves(first, second):
    half = first.shape[0] // 2
    return [to(second[:half], 1), to(first[half:], 2)]


def layer_forward(hidden, low, params, tables, tied, feed_own, later=None):
    attend_in, attend_out, gains, scales, mixing = params
    cosine, sine, starts, info = tables
    project = lambda *places: project_blocks(
        places, [blocks[row] for row in rows_at(places)], attend_in, cosine, sine, gains
    )
    blocks = [low, to(low, 1), to(low, 2)]
    if tied:
        heads = project(0)
        *blocks, heads = tie(*blocks, heads)
        blocks += pass_halves(*blocks[1:])
        heads += project(1, 2)
        *blocks, heads = tie(*blocks, heads)
        heads += project(3)
    else:
        blocks += pass_halves(*blocks[1:])
        heads = project(0, 1, 2, 3)
    raw, query, keys, values = zip(*heads)
    attend = lambda *places: attend_blocks(places, info, starts, query, keys, values, attend_out)
    far = attend(3)
    sent = [to(far[0][-1], 3)]
    near_blocks = attend(1, 2)
    sent += [to(block[-1], at) for at, block in zip((1, 2), near_blocks)]
    attended = attend(0) + near_blocks + far
    sent, attended[0], feed_own = tie(sent, attended[0], feed_own)
    feed_weights = (feed_own, exchange(feed_own, "section", 1))
    branch, middle, middle_low = mix_block(hidden, mixing[:1], (attended[0][-1], *sent))
    blocks_middle, fed, parts = feed_exchange(
        middle_low, lambda places, x: feed_blocks(places, x, feed_weights, scales)
    )
    mixed, result, result_low = mix_block(middle, mixing[1:], parts)
    if later is not None:
        result_low, later = tie(result_low, later)
        later = (later, exchange(later, "section", 1))
    ups, gates, gated, _ = zip(*fed)
    attended, logsums, _ = zip(*attended)
    stored = (
        (hidden, branch, blocks, raw, query, keys, values, attended, logsums),
        (middle, mixed, blocks_middle, ups, gates, gated),
    )
    return result, result_low, stored, feed_weights, later


def feed_exchange(block, work):
    blocks = [block, to(block, 1), to(block, 2)]
    done = work((0,), blocks[:1])
    *blocks, done = tie(*blocks, done)
    blocks += pass_halves(*blocks[1:])
    done += work((1, 2), blocks[1:3])
    sent = [to(done[at][-1], at) for at in (1, 2)]
    *blocks, done = tie(*blocks, done)
    done += work((3,), blocks[3:])
    sent.append(to(done[3][-1], 3))
    return blocks, done, (done[0][-1], *sent)


def layer_backward(stored, upstream, rounded, params, tables, feed_weights, section, hooks=()):
    attend_in, attend_out, gains, scales, mixing = params
    cosine, sine, starts, info = tables
    attend_stored, (middle, mixed, blocks_middle, ups, gates, gated) = stored
    hidden, branch, blocks_hidden, raw, query, keys, values, attended, logsums = attend_stored
    grad_middle, grad_mixed, rate_two = mix_back_block(
        middle, mixed, mixing[1:], upstream, rounded
    )
    blocks_mixed, done, parts = feed_exchange(
        grad_mixed, lambda places, g: feed_back_blocks(places, g, feed_weights, scales, ups, gates)
    )
    low_ups, low_gates, scale_grads, _ = zip(*done)
    operands = (blocks_middle, blocks_mixed, low_ups, low_gates, gated)
    other = feed_grads(1, *operands)
    parts, other = tie(parts, other)
    other = exchange(other, "section", 1)
    grad_hidden, grad_branch, rate_one = mix_back_block(
        hidden, branch, mixing[:1], (grad_middle, *parts)
    )
    grads = [grad_branch, to(grad_branch, 1), to(grad_branch, 2)]
    low_ups, _ = tie(low_ups, grad_branch)
    feed_sums = feed_grads(0, blocks_middle, blocks_mixed, low_ups, low_gates, gated, other)
    grads, _ = tie(grads, feed_sums)
    grads += pass_halves(*grads[1:])
    small = (scale_grads[0] + scale_grads[1] + scale_grads[3], rate_one[0], rate_two[0])
    if hooks:
        small, _ = tie(small, feed_sums)
        small = hooks[0](small)
    low, partial, gain_grad = attend_back(
        info, starts, query, keys, values, attended, logsums, raw, grads,
        attend_out, attend_in, cosine, sine, gains,
    )
    sent = [to(partial[at], at) for at in (3, 1, 2)]
    if hooks:
        low, small = hooks[1](low, small, gain_grad[:, 0])
    own, other = attend_grads(section, low, attended, blocks_hidden, grads)
    if hooks:
        other, small = hooks[2](other, small)
    other = exchange(other, "section", 1)
    attend_sums = (own + other.astype(F32)).astype(BF16).reshape(4, -1, own.shape[1])
    return (grad_hidden, partial[0], *sent), feed_sums, attend_sums, gain_grad[:, 0], small


def adam_update(weight, first, second, gradient, factor, rate):
    clipped = gradient * factor
    first_new = BETA_FIRST * first + (1.0 - BETA_FIRST) * clipped
    second_new = BETA_SECOND * second + (1.0 - BETA_SECOND) * clipped * clipped
    first_hat = first_new / (1.0 - BETA_FIRST**STEP)
    second_hat = second_new / (1.0 - BETA_SECOND**STEP)
    moved = weight - rate * first_hat / (jnp.sqrt(second_hat) + ADAM_EPSILON)
    return (first_new, second_new, moved)


def per_device(
    inputs,
    cotangent,
    doc_ids,
    attention_in,
    attention_out,
    feedforward_in,
    feedforward_out,
    unit_scales,
    mix_rates,
    first_attention_in,
    second_attention_in,
    first_attention_out,
    second_attention_out,
    first_feedforward_in,
    second_feedforward_in,
    first_feedforward_out,
    second_feedforward_out,
    first_unit_scales,
    second_unit_scales,
    first_mix_rates,
    second_mix_rates,
):
    section = lax.axis_index("section")
    is_first = section == 0
    dp_index = lax.axis_index("dp")
    dp_size = lax.axis_size("dp")
    local_rows = inputs.shape[1]

    def ordered(own, other):
        return jnp.where(is_first, own, other), jnp.where(is_first, other, own)

    def halves(array, dim):
        width = array.shape[dim] // 2
        own = lax.dynamic_slice_in_dim(array, section * width, width, dim)
        other = lax.dynamic_slice_in_dim(array, (1 - section) * width, width, dim)
        return own, other

    hidden_low = lax.dynamic_index_in_dim(inputs, section, 0, False)

    attend_rows = jnp.concatenate(
        [jnp.swapaxes(attention_in[0], 1, 2), attention_out], axis=0
    ).astype(BF16)
    small = jnp.concatenate([unit_scales.reshape(-1), mix_rates.reshape(-1)]).astype(BF16)
    def gather_ring(half):
        if dp_size != 4:
            whole = lax.all_gather(half, "dp", axis=1, tiled=True)
            return whole, whole
        blocks, count = spread_rows(half, "dp"), half.shape[1]
        whole = jnp.zeros((half.shape[0], dp_size * count, half.shape[2]), BF16)
        for source, block in zip(ring_sources("dp"), blocks):
            whole = lax.dynamic_update_slice_in_dim(whole, block, source * count, 1)
        return whole, blocks[-2]

    own, other = halves(attend_rows, 2)
    attend_pieces = ordered(own, exchange(other, "section", 1))
    attend_pieces, feedforward_in_here, feedforward_out_here = tie(
        attend_pieces, feedforward_in, feedforward_out
    )
    feed_rows = jnp.concatenate(
        [jnp.swapaxes(feedforward_in_here[0].astype(BF16), 1, 2), feedforward_out_here.astype(BF16)], axis=0
    )
    own, other = halves(feed_rows, 1)
    feed_pieces = ordered(own, exchange(other, "section", 1))
    attend_first, came = gather_ring(attend_pieces[0])
    attend_second, *feed_pieces, _ = tie(attend_pieces[1], *feed_pieces, came)
    attend_owns = (attend_first, lax.all_gather(attend_second, "dp", axis=1, tiled=True))
    small = jnp.stack(ordered(small, exchange(small, "section", 1))).reshape(-1)
    small = gather_small(small, "dp").astype(F32)
    small = small.reshape(dp_size, 2, -1)
    units_here = unit_scales.shape[2]

    def units_apart(values):
        parts = values.reshape(dp_size, 2, -1)
        own, other = ordered(parts[:, 0], parts[:, 1])
        return jnp.concatenate([own.reshape(-1), other.reshape(-1)])

    def units_back(values):
        parts = values.reshape(2, dp_size, -1)
        own, other = ordered(parts[0], parts[1])
        return jnp.stack([own, other], axis=1).reshape(-1)

    layers, feed_owns = [], []
    for layer in range(2):
        feed_own = lax.all_gather(feed_pieces[layer], "dp", axis=1, tiled=True)
        units = small[:, layer, :units_here].reshape(-1)
        mixing = small[:, layer, units_here:].reshape(dp_size, 2, -1)
        mixing = jnp.swapaxes(mixing, 0, 1).reshape(2, -1)
        width_qk, width_ff = attend_owns[0].shape[1], 2 * feed_own.shape[1]
        layers.append((
            units[:width_qk, None],
            jnp.stack([
                units_apart(units[width_qk : width_qk + width_ff]),
                units_apart(units[width_qk + width_ff :]),
            ]),
            mixing,
        ))
        feed_owns.append(feed_own)

    doc_row = lax.dynamic_index_in_dim(doc_ids, section, 0, False)
    starts_all = document_starts(doc_row)
    mp_index = lax.axis_index("mp")
    sources = [mp_index ^ offset for offset in range(4)]
    places = jnp.arange(local_rows, dtype=jnp.int32)
    starts = jnp.stack([
        lax.dynamic_slice_in_dim(starts_all, source * local_rows, local_rows, 0)
        for source in sources
    ])
    sources = jnp.stack(sources).astype(jnp.int32)
    cosine, sine = rope_tables(sources[:, None] * local_rows + places - starts)
    info = jnp.concatenate([sources, starts[:, 0]])
    tables = (cosine, sine, starts, info)

    def scatter(sums):
        return lax.psum_scatter(sums, "dp", scatter_dimension=1, tiled=True)

    def scatter_direct(sums):
        if dp_size != 4:
            return scatter(sums)
        count = sums.shape[1] // dp_size
        parts = [
            lax.dynamic_slice_in_dim(sums, (dp_index ^ bits) * count, count, 1)
            for bits in range(dp_size)
        ]
        parts[1:] = [exchange(part, "dp", bits) for bits, part in enumerate(parts[1:], 1)]
        return sum(part.astype(F32) for part in parts).astype(BF16)

    def small_vector(scales, rate_one, rate_two):
        return jnp.concatenate([units_back(scales[0]), units_back(scales[1]), rate_one, rate_two])

    def attend_params(own, other):
        attend = jnp.concatenate(ordered(own, other), axis=2)
        return attend[:3].reshape(-1, attend.shape[2]), attend[3]

    first, second = layers
    own = attend_owns[0]
    first = (*attend_params(own, exchange(own, "section", 1)), *first)
    section_ref = section.astype(jnp.int32).reshape(1)
    grad = lax.dynamic_index_in_dim(cotangent, section, 0, False)
    _, hidden_second, stored_first, weights_first, later = layer_forward(
        hidden_low, hidden_low, first, tables, False, feed_owns[0], attend_owns[1]
    )
    second = (*attend_params(*later), *second)
    result, _, stored_second, weights_second, _ = layer_forward(
        hidden_second, hidden_second, second, tables, True, feed_owns[1]
    )
    parts, feed_second, attend_second, gains_second, small_second = layer_backward(
        stored_second, (grad,), False, second, tables, weights_second, section_ref
    )
    feed_second = scatter(feed_second)
    parts, attend_second = tie(parts, attend_second)
    attend_second = scatter(attend_second)

    width_qk, width_rates = gains_second.shape[0], 2 * dp_size * mix_rates.shape[2]

    def start_small(small_first):
        values = jnp.stack([small_vector(*small_first), small_vector(*small_second)])
        values = jnp.concatenate([values.reshape(-1), gains_second])
        values = values + exchange(values, "section", 1)
        values, gains = values[:-width_qk].reshape(2, -1), values[-width_qk:]
        rates = sum_over(values[:, -width_rates:], "mp")
        return jnp.concatenate([values[:, :-width_rates], rates], axis=1), gains

    def next_small(low, small, gains):
        low, (values, gains_two) = tie(low, small)
        return low, (jnp.concatenate([values.reshape(-1), gains_two, gains]),)

    def last_small(other, small):
        other, (values,) = tie(other, small)
        bit = 1
        while 2 * bit < dp_size:
            values = values + exchange(values, "dp", bit)
            bit *= 2
        return other, (values, exchange(values, "dp", bit))

    parts, feed_first, attend_first, _, small = layer_backward(
        stored_first, parts, True, first, tables, weights_first, section_ref,
        (start_small, next_small, last_small),
    )
    feed_first = scatter(feed_first)
    sent_second = [
        lax.ppermute(part, "section", [(0, 1)]) for part in (attend_second, feed_second)
    ]
    attend_first, feed_second, attend_second, small, sent_second = tie(
        attend_first, feed_second, attend_second, small, sent_second
    )
    attend_first = scatter_direct(attend_first)

    reduced_first = (attend_first, feed_first)
    reduced_second = (attend_second, feed_second)
    squares = sum(
        jnp.sum(jnp.square(part.astype(F32))) for part in (*reduced_first, *reduced_second)
    )
    halves_of = [
        (one, two, lax.ppermute(one, "section", [(1, 0)]), theirs)
        for one, two, theirs in zip(reduced_first, reduced_second, sent_second)
    ]

    sums = small[0] + small[1]
    layer_sums = sums[: -2 * width_qk].reshape(2, -1)
    gain_first = sums[-width_qk:]
    gain_sums = jnp.stack([gain_first + exchange(gain_first, "section", 1), sums[-2 * width_qk : -width_qk]])
    scale_sums, rate_sums = layer_sums[:, :-width_rates], layer_sums[:, -width_rates:]
    rate_sums = rate_sums.reshape(2, 2, -1)
    unit_grads = jnp.concatenate([gain_sums, scale_sums], axis=1)
    unit_grads = jnp.where(is_first, unit_grads[0], unit_grads[1])
    unit_grads = lax.dynamic_slice_in_dim(unit_grads, dp_index * units_here, units_here, 0)
    unit_grads = unit_grads[None, None]
    rates_here = mix_rates.shape[2]
    rate_grads = jnp.where(is_first, rate_sums[0], rate_sums[1])
    rate_grads = lax.dynamic_slice_in_dim(rate_grads, dp_index * rates_here, rates_here, 1)[None]

    turn = lambda array: jnp.swapaxes(array, 1, 2)
    leading = (mp_index == 0).astype(F32)
    squares = squares + jnp.sum(unit_grads * unit_grads)
    squares = squares + leading * jnp.sum(rate_grads * rate_grads)
    squares = squares.reshape(1)
    squares, parts = tie(squares, parts)
    squares = squares + exchange(squares, "section", 1)
    squares = sum_over(sum_over(squares, "mp"), "dp")
    gradient_norm = jnp.sqrt(squares[0])
    factor = CLIP_NORM / jnp.maximum(gradient_norm, CLIP_NORM)

    grad = sum(part.astype(F32) for part in parts)
    to_send = jnp.where(is_first, result, grad)
    kept = jnp.where(is_first, grad, result)
    arrived = exchange(to_send, "section", 1)
    boundary_states = jnp.stack(ordered(kept, arrived))[None]

    scalar = factor.reshape(1)
    head_rows, width = attention_out.shape[1:]
    feed_units = feedforward_out.shape[1]
    rows = min(64, head_rows)
    updates = []
    attend_halves, feed_halves = halves_of
    unit_half = feed_units // 2
    turned = (
        (1, width, feed_units), (1, unit_half, width), lambda i: (i, 0, 0), lambda i: (i, 0, 0), (2,)
    )
    update = functools.partial(adam_matrix, section_ref, scalar)
    new = update(
        [turn(array[0]) for array in (attention_in, first_attention_in, second_attention_in)],
        attend_halves, 2, by_columns, (1, rows, width), (1, rows, width // 2),
        lambda i, j: (i, j, 0), lambda i, j: (i, j, 0), (3, head_rows // rows),
    )
    updates.extend(turn(part)[None] for part in new)
    updates.extend(update(
        (attention_out, first_attention_out, second_attention_out),
        attend_halves, 2, by_columns, (1, rows, width), (1, rows, width // 2),
        lambda i: (0, i, 0), lambda i: (3, i, 0), (head_rows // rows,),
    ))
    new = update(
        [array[0] for array in (feedforward_in, first_feedforward_in, second_feedforward_in)],
        feed_halves, 1, by_rows_turned, *turned,
    )
    updates.extend(part[None] for part in new)
    updates.extend(update(
        (feedforward_out, first_feedforward_out, second_feedforward_out),
        feed_halves, 2, by_rows, (1, unit_half, width), (1, unit_half, width),
        lambda i: (0, i, 0), lambda i: (2, 0, 0), (2,),
    ))
    updates.extend(
        adam_update(
            unit_scales, first_unit_scales, second_unit_scales, unit_grads, factor, SCALE_RATE
        )
    )
    updates.extend(
        adam_update(
            mix_rates, first_mix_rates, second_mix_rates, rate_grads, factor, MIXING_RATE
        )
    )
    return (boundary_states, gradient_norm, *updates)


def solution(mesh):
    in_specs = (
        P("dp", "mp", None),
        P("dp", "mp", None),
        P("dp", None),
        P("section", None, None, ("mp", "dp")),
        P("section", ("mp", "dp"), None),
        P("section", None, None, ("mp", "dp")),
        P("section", ("mp", "dp"), None),
        P("section", "mp", "dp"),
        P("section", None, "dp"),
        P("section", None, None, ("mp", "dp")),
        P("section", None, None, ("mp", "dp")),
        P("section", ("mp", "dp"), None),
        P("section", ("mp", "dp"), None),
        P("section", None, None, ("mp", "dp")),
        P("section", None, None, ("mp", "dp")),
        P("section", ("mp", "dp"), None),
        P("section", ("mp", "dp"), None),
        P("section", "mp", "dp"),
        P("section", "mp", "dp"),
        P("section", None, "dp"),
        P("section", None, "dp"),
    )
    out_specs = (
        P("section", "dp", "mp", None),
        P(),
        P("section", None, None, ("mp", "dp")),
        P("section", None, None, ("mp", "dp")),
        P("section", None, None, ("mp", "dp")),
        P("section", ("mp", "dp"), None),
        P("section", ("mp", "dp"), None),
        P("section", ("mp", "dp"), None),
        P("section", None, None, ("mp", "dp")),
        P("section", None, None, ("mp", "dp")),
        P("section", None, None, ("mp", "dp")),
        P("section", ("mp", "dp"), None),
        P("section", ("mp", "dp"), None),
        P("section", ("mp", "dp"), None),
        P("section", "mp", "dp"),
        P("section", "mp", "dp"),
        P("section", "mp", "dp"),
        P("section", None, "dp"),
        P("section", None, "dp"),
        P("section", None, "dp"),
    )
    return jax.shard_map(
        per_device, mesh=mesh, in_specs=in_specs, out_specs=out_specs, check_vma=False
    )
```

```python
import functools
import math

import jax
import jax.numpy as jnp
from jax import lax
from jax.experimental import pallas as pl
from jax.experimental.pallas import tpu as pltpu
from jax.sharding import PartitionSpec as P

HD = 64
STEP = 10

NORM_EPSILON = 1e-06
ROPE_BASE = 10000.0
CLIP_NORM = 0.1
LEARN_RATE = 0.05
SCALE_RATE = 1.25
MIXING_RATE = 0.4
BETA_FIRST = 0.9
BETA_SECOND = 0.95
ADAM_EPSILON = 1e-08

BF16 = jnp.bfloat16
F32 = jnp.float32


def exchange(block, axis, bit):
    route = [(i, i ^ bit) for i in range(lax.axis_size(axis))]
    return lax.ppermute(block, axis, route)


def gray(place):
    return place ^ (place >> 1)


def ring_place(index, size):
    shift = 1
    while shift < size:
        index = index ^ (index >> shift)
        shift *= 2
    return index


def ring_step(block, axis):
    size = lax.axis_size(axis)
    route = []
    for place in range(size):
        route.append((gray(place), gray((place + 1) % size)))
        route.append((size + gray(place), size + gray((place - 1) % size)))
    return lax.ppermute(block, ("section", axis), route)


def ring_sources(axis):
    size = lax.axis_size(axis)
    place = ring_place(lax.axis_index(axis), size)
    way = 1 - 2 * lax.axis_index("section")
    return [gray((place - way * step + size) % size) for step in range(size)]


def spread_rows(block, axis="mp"):
    blocks = [block]
    for _ in range(lax.axis_size(axis) - 1):
        blocks.append(ring_step(blocks[-1], axis))
    return blocks


def sum_over(values, axis):
    bit = 1
    while bit < lax.axis_size(axis):
        values = values + exchange(values, axis, bit)
        bit *= 2
    return values


def gather_small(values, axis):
    index = lax.axis_index(axis)
    gathered = values[None]
    bit = 1
    while bit < lax.axis_size(axis):
        other = exchange(gathered, axis, bit)
        low = (index & bit) == 0
        gathered = jnp.concatenate(
            [jnp.where(low, gathered, other), jnp.where(low, other, gathered)], axis=0
        )
        bit *= 2
    return gathered


def unit_norm(values):
    return values * lax.rsqrt(jnp.sum(values * values, axis=-1, keepdims=True) + NORM_EPSILON)


def document_starts(doc_row):
    position = jnp.arange(doc_row.shape[-1], dtype=jnp.int32)
    change = jnp.concatenate([jnp.ones((1,), dtype=jnp.bool_), doc_row[1:] != doc_row[:-1]])
    return lax.cummax(jnp.where(change, position, 0), axis=0)


def rope_tables(offsets):
    half_width = HD // 2
    inverse = 1.0 / ROPE_BASE ** (jnp.arange(half_width, dtype=F32) * (2.0 / HD))
    angles = inverse[:, None] * offsets.astype(F32)[..., None, :]
    angles = jnp.concatenate([angles, angles], axis=-2)
    return jnp.cos(angles), jnp.sin(angles)


def mix_residual(hidden, branch, mixing):
    return unit_norm(hidden + mixing * (unit_norm(branch) - hidden))


NT = (((1,), (1,)), ((), ()))
TN = (((0,), (0,)), ((), ()))
NN = (((1,), (0,)), ((), ()))
VMEM = pltpu.VMEM
WHOLE, NEAR = "whole", "near"
SCALARS = pl.BlockSpec(memory_space=pltpu.SMEM)


def mul(left, right, dims=NN):
    return lax.dot_general(left, right, dims, preferred_element_type=F32)


def block_of(array):
    zeros = (0,) * len(array.shape)
    return pl.BlockSpec(array.shape, lambda *place: zeros)


def call(body, out_shape, in_specs, flops, moved, scratch=(), grid=(1,), out_specs=None, loose=()):
    def run(*args):
        specs = [
            block_of(arg) if spec in (WHOLE, NEAR) else spec for spec, arg in zip(in_specs, args)
        ]
        args = [
            arg if spec in (SCALARS, NEAR) else pltpu.with_memory_space_constraint(arg, pltpu.HBM)
            for spec, arg in zip(in_specs, args)
        ]
        return pl.pallas_call(
            body,
            out_shape=[
                out if at in loose else pltpu.HBM(out.shape, out.dtype)
                for at, out in enumerate(out_shape)
            ],
            grid=grid,
            in_specs=specs,
            out_specs=out_specs or [block_of(out) for out in out_shape],
            scratch_shapes=list(scratch),
            compiler_params=pltpu.CompilerParams(vmem_limit_bytes=50 << 20),
            cost_estimate=pl.CostEstimate(flops=flops, bytes_accessed=moved, transcendentals=0),
        )(*args)

    return run


def shape(dims, dtype):
    return jax.ShapeDtypeStruct(dims, dtype)


def turned(raw, cosine, sine):
    half = HD // 2
    first, second = raw[:half], raw[half:]
    return jnp.concatenate(
        [
            first * cosine[:half] - second * sine[:half],
            second * cosine[half:] + first * sine[half:],
        ],
        axis=0,
    )


def turned_back(grad, cosine, sine):
    half = HD // 2
    first, second = grad[:half], grad[half:]
    return jnp.concatenate(
        [
            first * cosine[:half] + second * sine[half:],
            second * cosine[half:] - first * sine[:half],
        ],
        axis=0,
    )


def rows_at(places):
    return [row for at in places for row in ((at,) if at < 3 else (3, 4))]


def side_by_side(refs):
    return refs[0][...] if len(refs) == 1 else jnp.concatenate([ref[...] for ref in refs], axis=0)


def project_kernel(places, *refs):
    count = len(rows_at(places))
    weight, cosine, sine, gains = refs[count : count + 4]
    tokens = cosine.shape[2]
    x, outs = side_by_side(refs[:count]), refs[count + 4 :]
    for n, at in enumerate(places):
        raw_out, query, keys, values = outs[4 * n : 4 * n + 4]
        width = query.shape[0]
        raw = mul(weight[...], x[n * tokens : (n + 1) * tokens], NT)
        raw_out[...] = raw[: 2 * width]
        values[...] = raw[2 * width :].astype(BF16)
        for part, out in ((0, query), (1, keys)):
            for top in range(0, width, HD):
                turn = turned(
                    raw[part * width + top : part * width + top + HD], cosine[at], sine[at]
                )
                scale = lax.rsqrt(jnp.sum(turn * turn, axis=0, keepdims=True) + NORM_EPSILON)
                head = (turn * scale * gains[top : top + HD]).astype(BF16)
                out[top : top + HD] = head * math.sqrt(HD) if part == 0 else head


def project_blocks(places, x, weight, cosine, sine, gains):
    tokens, depth, count = cosine.shape[2], weight.shape[1], len(places)
    width = weight.shape[0] // 3
    low = shape((width, tokens), BF16)
    outs = call(
        functools.partial(project_kernel, places),
        [shape((2 * width, tokens), F32), low, low, low] * count,
        [NEAR] * len(x) + [WHOLE] * 4,
        2 * tokens * depth * 3 * width * count,
        2 * 3 * width * depth,
    )(*x, weight, cosine, sine, gains)
    return [outs[4 * n : 4 * n + 4] for n in range(count)]


def near(info, at, other, tokens):
    return (info[other] <= info[at]) & ((info[other] + 1) * tokens > info[4 + at])


def seen(info, at, other, starts, tokens):
    key_place = info[other] * tokens + lax.broadcasted_iota(jnp.int32, (tokens, tokens), 0)
    query_place = info[at] * tokens + lax.broadcasted_iota(jnp.int32, (tokens, tokens), 1)
    return (key_place <= query_place) & (key_place >= starts)


def share_out(partial, value):
    partial[...] = value.astype(partial.dtype)


def partial_shape(at, tokens, depth):
    return shape((tokens, depth), BF16 if at else F32)


def attend_kernel(places, info, starts, *refs):
    count = len(places)
    query, rest = refs[:count], refs[count:]
    keys, values, weight, outs, (total, sums) = rest[:4], rest[4:8], rest[8], rest[9:-2], rest[-2:]
    width, tokens = query[0].shape
    for n, at in enumerate(places):
        attended, logsums, partial = outs[3 * n : 3 * n + 3]
        total[n] = jnp.zeros((width, tokens), F32)
        sums[n] = jnp.ones((8, tokens), F32)
        sums[n, : width // HD] = jnp.zeros((width // HD, tokens), F32)
        for other in range(4):

            @pl.when(near(info, at, other, tokens))
            def _():
                allowed = seen(info, at, other, starts[at : at + 1], tokens)
                for head in range(width // HD):
                    rows = slice(head * HD, head * HD + HD)
                    shares = jnp.exp(mul(keys[other][rows], query[n][rows], TN))
                    shares = jnp.where(allowed, shares, 0.0)
                    sums[n, head : head + 1] += jnp.sum(shares, axis=0, keepdims=True)
                    total[n, rows] += mul(values[other][rows], shares.astype(BF16))

        logsums[...] = jnp.log(sums[n])
        inverse = 1.0 / sums[n]
        for head in range(width // HD):
            rows = slice(head * HD, head * HD + HD)
            attended[rows] = (total[n, rows] * inverse[head : head + 1]).astype(BF16)
        share_out(partial, mul(attended[...], weight[...], TN))


def attend_blocks(places, info, starts, query, keys, values, weight):
    width, tokens = query[0].shape
    depth, count = weight.shape[1], len(places)
    outs = call(
        functools.partial(attend_kernel, places),
        [
            out
            for at in places
            for out in (
                shape((width, tokens), BF16),
                shape((8, tokens), F32),
                partial_shape(at, tokens, depth),
            )
        ],
        [SCALARS] + [WHOLE] * (10 + count),
        2 * tokens * (depth * width + 10 * tokens * 256) * count,
        2 * depth * width,
        [VMEM((count, width, tokens), F32), VMEM((count, 8, tokens), F32)],
        loose=[3 * n + 2 for n, at in enumerate(places) if at],
    )(info, starts, *[query[at] for at in places], *keys, *values, weight)
    return [outs[3 * n : 3 * n + 3] for n in range(count)]


def attend_back_kernel(info, starts, *refs):
    query, keys, values, attended, logsums, raw = (refs[4 * n : 4 * n + 4] for n in range(6))
    grads, (w_out, w_in, cosine, sine, gains) = refs[24:29], refs[29:34]
    low, partial, gain_grad = refs[34:38], refs[38:42], refs[42]
    pulled, deltas, grad_query, grad_keys, grad_values = refs[43:]
    width, tokens = query[0].shape
    heads = width // HD
    grad_query[...] = jnp.zeros_like(grad_query)
    grad_keys[...] = jnp.zeros_like(grad_keys)
    grad_values[...] = jnp.zeros_like(grad_values)
    deltas[...] = jnp.zeros_like(deltas)
    for at in range(4):
        rows = side_by_side([grads[row] for row in rows_at((at,))])
        grad = mul(w_out[...], rows, NT).astype(BF16)
        pulled[at] = grad
        product = grad.astype(F32) * attended[at][...].astype(F32)
        for head in range(heads):
            rows = slice(head * HD, head * HD + HD)
            deltas[at, head : head + 1] = jnp.sum(product[rows], axis=0, keepdims=True)
    for at in range(4):
        for other in range(4):

            @pl.when(near(info, at, other, tokens))
            def _():
                allowed = seen(info, at, other, starts[at : at + 1], tokens)
                for head in range(heads):
                    rows = slice(head * HD, head * HD + HD)
                    grad_rows, query_rows = pulled[at, rows], query[at][rows]
                    scores = mul(keys[other][rows], query_rows, TN) - logsums[at][head : head + 1]
                    shares = jnp.where(allowed, jnp.exp(scores), 0.0)
                    grad_shares = mul(values[other][rows], grad_rows, TN)
                    grad_scores = shares * (grad_shares - deltas[at, head : head + 1])
                    grad_scores = grad_scores.astype(BF16)
                    grad_values[other, rows] += mul(grad_rows, shares.astype(BF16), NT)
                    grad_keys[other, rows] += mul(query_rows, grad_scores, NT)
                    grad_query[at, rows] += mul(keys[other][rows], grad_scores)

    gain_total = [0.0] * heads
    for at in range(4):
        cos, sin = cosine[at], sine[at]
        for part, source, factor in ((0, grad_query, math.sqrt(HD)), (1, grad_keys, 1.0)):
            for head in range(heads):
                rows = slice(head * HD, head * HD + HD)
                turn = turned(raw[at][part * width + head * HD : part * width + head * HD + HD], cos, sin)
                scale = lax.rsqrt(jnp.sum(turn * turn, axis=0, keepdims=True) + NORM_EPSILON)
                unit = turn * scale
                grad = source[at, rows] * factor
                gain_total[head] = gain_total[head] + grad * unit
                grad = grad * gains[rows]
                grad = scale * (grad - unit * jnp.sum(unit * grad, axis=0, keepdims=True))
                low[at][part * width + head * HD : part * width + head * HD + HD] = turned_back(
                    grad, cos, sin
                ).astype(BF16)
        low[at][2 * width :] = grad_values[at].astype(BF16)
        share_out(partial[at], mul(low[at][...], w_in[...], TN))
    for head in range(heads):
        gain_grad[head * HD : head * HD + HD] = jnp.sum(gain_total[head], axis=1, keepdims=True)


def attend_back(info, starts, query, keys, values, attended, logsums, raw, grads,
                w_out, w_in, cosine, sine, gains):
    width, tokens = query[0].shape
    depth = w_out.shape[1]
    low = shape((3 * width, tokens), BF16)
    block = VMEM((4, width, tokens), F32)
    outs = call(
        attend_back_kernel,
        [low] * 4
        + [partial_shape(at, tokens, depth) for at in range(4)]
        + [shape((width, 1), F32)],
        [SCALARS] + [WHOLE] * 25 + [NEAR] * 5 + [WHOLE] * 5,
        2 * 4 * tokens * (depth * width * 4 + 60 * tokens * 256),
        2 * depth * width * 12,
        [VMEM((4, width, tokens), BF16), VMEM((4, 8, tokens), F32), block, block, block],
        loose=(5, 6, 7),
    )(info, starts, *query, *keys, *values, *attended, *logsums, *raw, *grads,
      w_out, w_in, cosine, sine, gains)
    return outs[:4], outs[4:8], outs[8]


CHUNK = 256
GATE_WIDTH = math.sqrt(1024)


def started(copies, arrived, first=0):
    copies = [
        pltpu.make_async_copy(source, target, arrived.at[first + n])
        for n, (source, target) in enumerate(copies)
    ]
    for copy in copies:
        copy.start()
    return copies


def fetch_weights(own, other, weights, arrived):
    half = own.shape[1]
    size = min(CHUNK, half)
    places = [(index, start) for index in range(2) for start in range(0, half, size)]
    copies = started(
        [
            ((own, other)[index].at[:, pl.ds(start, size)], weights.at[index, :, pl.ds(start, size)])
            for index, start in places
        ],
        arrived,
    )
    return [
        (copy, index, slice(start, start + size), slice(index * half + start, index * half + start + size))
        for copy, (index, start) in zip(copies, places)
    ]


def feed_kernel(given, count, *refs):
    x, refs = refs[:given], refs[given:]
    (own, other, scales_in), outs, partial = refs[:3], refs[3 : 3 * count + 3], refs[3 * count + 3 : 4 * count + 3]
    weights, scales, ups, gates, gated, gated_turned, arrived, came, left = refs[4 * count + 3 :]
    half, tokens = own.shape[1], ups.shape[0] // count
    (scales_copy,) = started([(scales_in, scales)], came)
    chunks = fetch_weights(own, other, weights, arrived)
    block = side_by_side(x)
    scales_copy.wait()
    leaving = []
    for copy, index, rows, units in chunks:
        copy.wait()
        up, gate = mul(block, weights[index, 0, rows], NT), mul(block, weights[index, 1, rows], NT)
        ups[:, units] = up.astype(BF16)
        gates[:, units] = gate.astype(BF16)
        z = gate * (scales[1:2, units] * GATE_WIDTH)
        silu = z * (0.5 + 0.5 * jnp.tanh(0.5 * z))
        mixed = (up * scales[0:1, units] * silu).astype(BF16)
        gated[:, units] = mixed
        gated_turned[units] = mixed.T
        if rows.stop == half:
            columns = pl.ds(index * half, half)
            for n in range(count):
                places = pl.ds(n * tokens, tokens)
                leaving += started(
                    [
                        (ups.at[places, columns], outs[3 * n].at[:, columns]),
                        (gates.at[places, columns], outs[3 * n + 1].at[:, columns]),
                        (gated_turned.at[columns, places], outs[3 * n + 2].at[columns]),
                    ],
                    left,
                    3 * (index * count + n),
                )
    total = mul(gated[:, :half], weights[0, 2]) + mul(gated[:, half:], weights[1, 2])
    for n in range(count):
        share_out(partial[n], total[n * tokens : (n + 1) * tokens])
    for copy in leaving:
        copy.wait()


def feed_back_kernel(given, count, *refs):
    g, refs = refs[:given], refs[given:]
    (own, other, scales_in), kept = refs[:3], refs[3 : 2 * count + 3]
    outs, scale_grad = refs[2 * count + 3 : 4 * count + 3], refs[4 * count + 3]
    partial = refs[4 * count + 4 : 5 * count + 4]
    weights, scales, ups, gates, low_up, low_gate, up_turned, gate_turned = refs[5 * count + 4 : -3]
    arrived, came, left = refs[-3:]
    half, tokens = own.shape[1], ups.shape[0] // count
    (scales_copy,) = started([(scales_in, scales)], came)
    chunks = fetch_weights(own, other, weights, arrived)
    coming = [
        started(
            [
                (ref.at[:, pl.ds(index * half, half)],
                 into.at[pl.ds(n * tokens, tokens), pl.ds(index * half, half)])
                for n in range(count)
                for ref, into in ((kept[2 * n], ups), (kept[2 * n + 1], gates))
            ],
            came,
            1 + 2 * count * index,
        )
        for index in range(2)
    ]
    block = side_by_side(g)
    scales_copy.wait()
    leaving = []
    for copy, index, rows, units in chunks:
        copy.wait()
        grad = mul(block, weights[index, 2, rows], NT)
        if rows.start == 0:
            for copy in coming[index]:
                copy.wait()
        up, gate = ups[:, units].astype(F32), gates[:, units].astype(F32)
        s_up, s_gate = scales[0:1, units], scales[1:2, units] * GATE_WIDTH
        z = gate * s_gate
        sigmoid = 0.5 + 0.5 * jnp.tanh(0.5 * z)
        silu = z * sigmoid
        grad_silu = grad * silu
        grad_z = grad * (up * s_up) * (sigmoid + silu * (1.0 - sigmoid))
        grad_up, grad_gate = (grad_silu * s_up).astype(BF16), (grad_z * s_gate).astype(BF16)
        low_up[:, units], low_gate[:, units] = grad_up, grad_gate
        up_turned[units], gate_turned[units] = grad_up.T, grad_gate.T
        scale_grad[0:1, units] = jnp.sum(grad_silu * up, axis=0, keepdims=True)
        scale_grad[1:2, units] = jnp.sum(grad_z * gate, axis=0, keepdims=True) * GATE_WIDTH
        if rows.stop == half:
            columns = pl.ds(index * half, half)
            for n in range(count):
                places = pl.ds(n * tokens, tokens)
                leaving += started(
                    [
                        (up_turned.at[columns, places], outs[2 * n].at[columns]),
                        (gate_turned.at[columns, places], outs[2 * n + 1].at[columns]),
                    ],
                    left,
                    2 * (index * count + n),
                )
    total = mul(low_up[:, :half], weights[0, 0]) + mul(low_up[:, half:], weights[1, 0])
    total = total + mul(low_gate[:, :half], weights[0, 1]) + mul(low_gate[:, half:], weights[1, 1])
    for n in range(count):
        share_out(partial[n], total[n * tokens : (n + 1) * tokens])
    for copy in leaving:
        copy.wait()


HELD = pl.BlockSpec(memory_space=pl.ANY)


def feed_call(body, places, x, weights, scales, kept, held, pair, low, turned_count):
    half, count = weights[0].shape[1], len(places)
    tokens, depth = sum(block.shape[0] for block in x) // count, x[0].shape[1]
    partial = [partial_shape(at, tokens, depth) for at in places]
    semaphores = pltpu.SemaphoreType.DMA
    return call(
        functools.partial(body, len(x), count),
        held + pair + partial,
        [NEAR] * len(x) + [HELD] * (3 + len(kept)),
        2 * 6 * tokens * depth * half * count,
        2 * 6 * depth * half,
        [VMEM((2, 3, half, depth), BF16), VMEM(scales.shape, F32)]
        + [VMEM((count * tokens, 2 * half), BF16)] * low
        + [VMEM((2 * half, count * tokens), BF16)] * turned_count
        + [
            semaphores((2 * half // min(CHUNK, half),)),
            semaphores((1 + 2 * len(kept),)),
            semaphores((2 * len(held),)),
        ],
        out_specs=[HELD] * len(held) + [block_of(out) for out in pair + partial],
        loose=[len(held + pair) + n for n, at in enumerate(places) if at],
    )(*x, *weights, scales, *kept)


def feed_blocks(places, x, weights, scales):
    count = len(places)
    dims = (sum(block.shape[0] for block in x) // count, 2 * weights[0].shape[1])
    held = [shape(dims, BF16), shape(dims, BF16), shape(dims[::-1], BF16)] * count
    outs = feed_call(feed_kernel, places, x, weights, scales, (), held, [], 3, 1)
    return [[*outs[3 * n : 3 * n + 3], outs[3 * count + n]] for n in range(count)]


def feed_back_blocks(places, g, weights, scales, ups, gates):
    count = len(places)
    held = [shape(ups[0].shape[::-1], BF16)] * (2 * count)
    pair = [shape((2, ups[0].shape[1]), F32)]
    kept = [array for at in places for array in (ups[at], gates[at])]
    outs = feed_call(feed_back_kernel, places, g, weights, scales, kept, held, pair, 4, 2)
    return [
        [*outs[2 * n : 2 * n + 2], outs[2 * count] if n == 0 else None, outs[2 * count + 1 + n]]
        for n in range(count)
    ]


def feed_grad_kernel(has_other, *refs):
    middle, mixed, (ups, gates, gated) = refs[:5], refs[5:10], (refs[10:14], refs[14:18], refs[18:22])
    out = refs[-1]
    for row, (units, right) in enumerate(((ups, middle), (gates, middle), (gated, mixed))):
        left = jnp.concatenate([block[...] for block in units], axis=1)
        total = mul(left, side_by_side(right))
        if has_other:
            total = total + refs[22][row].astype(F32)
        out[row] = total.astype(BF16)


def feed_grads(half_at, middle, mixed, ups, gates, gated, other=None):
    units, tokens = ups[0].shape
    depth, half = middle[0].shape[1], units // 2
    part = pl.BlockSpec((half, tokens), lambda i: (half_at, 0))
    more = () if other is None else (other,)
    return call(
        functools.partial(feed_grad_kernel, bool(more)),
        [shape((3, half, depth), BF16)],
        [WHOLE] * 5 + [NEAR] * 5 + [part] * 12 + [NEAR] * len(more),
        2 * 3 * 4 * tokens * half * depth,
        2 * 12 * tokens * (half + depth),
    )(*middle, *mixed, *ups, *gates, *gated, *more)[0]


def attend_grad_kernel(section, *refs):
    low, attended, hidden, grads = refs[:4], refs[4:8], refs[8:13], refs[13:18]
    own, other = refs[18:]
    width, half = attended[0].shape[0], own.shape[1]
    for lefts, rights, top in ((low, hidden, 0), (attended, grads, 3 * width)):
        right = side_by_side(rights)
        for start in range(0, lefts[0].shape[0], width):
            total = mul(
                jnp.concatenate([left[start : start + width] for left in lefts], axis=1), right
            )
            rows = slice(top + start, top + start + width)
            for place in range(2):
                columns = total[:, place * half : place * half + half]

                @pl.when(section[0] == place)
                def _():
                    own[rows] = columns

                @pl.when(section[0] != place)
                def _():
                    other[rows] = columns.astype(BF16)


def attend_grads(section, low, attended, hidden, grads):
    width, tokens = attended[0].shape
    depth = hidden[0].shape[1]
    return call(
        attend_grad_kernel,
        [shape((4 * width, depth // 2), F32), shape((4 * width, depth // 2), BF16)],
        [SCALARS] + [WHOLE] * 13 + [NEAR] * 5,
        2 * 4 * 4 * tokens * width * depth,
        2 * 16 * tokens * depth,
    )(section, *low, *attended, *hidden, *grads)


def adam_kernel(axis, gradient_of, section, factor, weight, first, second, *refs):
    first_out, second_out, weight_out = refs[4:]
    clipped = gradient_of(section[0] == 0, [ref[...].astype(F32) for ref in refs[:4]]) * factor[0]
    first_new = BETA_FIRST * first[...] + (1.0 - BETA_FIRST) * clipped
    second_new = BETA_SECOND * second[...] + (1.0 - BETA_SECOND) * clipped * clipped
    first_out[...] = first_new
    second_out[...] = second_new
    first_hat = first_new / (1.0 - BETA_FIRST**STEP)
    second_hat = second_new / (1.0 - BETA_SECOND**STEP)
    moved = weight[...] - LEARN_RATE * first_hat / (jnp.sqrt(second_hat) + ADAM_EPSILON)
    scale = lax.rsqrt(jnp.sum(moved * moved, axis=axis, keepdims=True) + NORM_EPSILON)
    weight_out[...] = moved * scale


def adam_matrix(section, factor, arrays, halves, axis, gradient_of, block, half_block, place,
                half_place, grid):
    spec, half_spec = pl.BlockSpec(block, place), pl.BlockSpec(half_block, half_place)
    dims, size = arrays[0].shape, arrays[0].size
    return call(
        functools.partial(adam_kernel, axis, gradient_of),
        [shape(dims, F32)] * 3,
        [SCALARS] * 2 + [spec] * 3 + [half_spec] * 4,
        20 * size,
        28 * size,
        grid=grid,
        out_specs=[spec] * 3,
    )(section, factor, *arrays, *halves)


def half_of(is_first, parts, low_half):
    here, there = jnp.where(is_first, parts[0], parts[1]), jnp.where(is_first, parts[2], parts[3])
    return jnp.where(is_first == low_half, here, there)


def by_columns(is_first, parts):
    return jnp.concatenate(
        [half_of(is_first, parts, True), half_of(is_first, parts, False)], axis=2
    )


def by_rows(is_first, parts):
    return half_of(is_first, parts, pl.program_id(0) == 0)


def by_rows_turned(is_first, parts):
    both = [half_of(is_first, parts, low)[0] for low in (True, False)]
    return jnp.concatenate(both, axis=0).T[None]


def add_parts(parts):
    total = parts[0][...].astype(F32)
    for part in parts[1:]:
        total = total + part[...].astype(F32)
    return total


def mix_kernel(count, hidden, rate, *refs):
    branch_out, result, result_low = refs[count:]
    branch = add_parts(refs[:count])
    branch_out[...] = branch
    mixed = mix_residual(hidden[...].astype(F32), branch, rate[...])
    result[...] = mixed
    result_low[...] = mixed.astype(BF16)


def mix_block(hidden, rate, parts):
    dims = hidden.shape
    return call(
        functools.partial(mix_kernel, len(parts)),
        [shape(dims, F32), shape(dims, F32), shape(dims, BF16)],
        [WHOLE] * 2 + [WHOLE if part.dtype == F32 else NEAR for part in parts],
        10 * dims[0] * dims[1],
        8 * dims[0] * dims[1],
    )(hidden, rate, *parts)


def mix_back_kernel(count, rounded, hidden, branch, rate, *refs):
    grad_hidden, grad_branch, grad_rate = refs[count:]
    upstream = add_parts(refs[:count])
    if rounded:
        upstream = upstream.astype(BF16).astype(F32)
    h, b, r = hidden[...].astype(F32), branch[...], rate[...]
    scale = lax.rsqrt(jnp.sum(b * b, axis=-1, keepdims=True) + NORM_EPSILON)
    unit = b * scale
    apart = unit - h
    mixed = h + r * apart
    mixed_scale = lax.rsqrt(jnp.sum(mixed * mixed, axis=-1, keepdims=True) + NORM_EPSILON)
    mixed = mixed * mixed_scale
    grad = mixed_scale * (upstream - mixed * jnp.sum(mixed * upstream, axis=-1, keepdims=True))
    grad_rate[...] = jnp.sum(grad * apart, axis=0, keepdims=True)
    grad_unit = grad * r
    grad_hidden[...] = grad - grad_unit
    grad_unit = scale * (grad_unit - unit * jnp.sum(unit * grad_unit, axis=-1, keepdims=True))
    grad_branch[...] = grad_unit.astype(BF16)


def mix_back_block(hidden, branch, rate, parts, rounded=False):
    dims = hidden.shape
    return call(
        functools.partial(mix_back_kernel, len(parts), rounded),
        [shape(dims, F32), shape(dims, BF16), shape((1, dims[1]), F32)],
        [WHOLE] * 3 + [WHOLE if part.dtype == F32 else NEAR for part in parts],
        20 * dims[0] * dims[1],
        12 * dims[0] * dims[1],
    )(hidden, branch, rate, *parts)


def tie(*values):
    return lax.optimization_barrier(values)


def to(block, at):
    return exchange(block, "mp", at)


def pass_halves(first, second):
    half = first.shape[0] // 2
    return [to(second[:half], 1), to(first[half:], 2)]


def layer_forward(hidden, low, params, tables, tied, feed_own, later=None):
    attend_in, attend_out, gains, scales, mixing = params
    cosine, sine, starts, info = tables
    project = lambda *places: project_blocks(
        places, [blocks[row] for row in rows_at(places)], attend_in, cosine, sine, gains
    )
    blocks = [low, to(low, 1), to(low, 2)]
    if tied:
        heads = project(0)
        *blocks, heads = tie(*blocks, heads)
        blocks += pass_halves(*blocks[1:])
        heads += project(1, 2)
        *blocks, heads = tie(*blocks, heads)
        heads += project(3)
    else:
        blocks += pass_halves(*blocks[1:])
        heads = project(0, 1, 2, 3)
    raw, query, keys, values = zip(*heads)
    attend = lambda *places: attend_blocks(places, info, starts, query, keys, values, attend_out)
    far = attend(3)
    sent = [to(far[0][-1], 3)]
    near_blocks = attend(1, 2)
    sent += [to(block[-1], at) for at, block in zip((1, 2), near_blocks)]
    attended = attend(0) + near_blocks + far
    sent, attended[0], feed_own = tie(sent, attended[0], feed_own)
    feed_weights = (feed_own, exchange(feed_own, "section", 1))
    branch, middle, middle_low = mix_block(hidden, mixing[:1], (attended[0][-1], *sent))
    blocks_middle, fed, parts = feed_exchange(
        middle_low, lambda places, x: feed_blocks(places, x, feed_weights, scales)
    )
    mixed, result, result_low = mix_block(middle, mixing[1:], parts)
    if later is not None:
        result_low, later = tie(result_low, later)
        later = (later, exchange(later, "section", 1))
    ups, gates, gated, _ = zip(*fed)
    attended, logsums, _ = zip(*attended)
    stored = (
        (hidden, branch, blocks, raw, query, keys, values, attended, logsums),
        (middle, mixed, blocks_middle, ups, gates, gated),
    )
    return result, result_low, stored, feed_weights, later


def feed_exchange(block, work):
    blocks = [block, to(block, 1), to(block, 2)]
    done = work((0,), blocks[:1])
    *blocks, done = tie(*blocks, done)
    blocks += pass_halves(*blocks[1:])
    done += work((1, 2), blocks[1:3])
    sent = [to(done[at][-1], at) for at in (1, 2)]
    *blocks, done = tie(*blocks, done)
    done += work((3,), blocks[3:])
    sent.append(to(done[3][-1], 3))
    return blocks, done, (done[0][-1], *sent)


def layer_backward(stored, upstream, rounded, params, tables, feed_weights, section, hooks=()):
    attend_in, attend_out, gains, scales, mixing = params
    cosine, sine, starts, info = tables
    attend_stored, (middle, mixed, blocks_middle, ups, gates, gated) = stored
    hidden, branch, blocks_hidden, raw, query, keys, values, attended, logsums = attend_stored
    grad_middle, grad_mixed, rate_two = mix_back_block(
        middle, mixed, mixing[1:], upstream, rounded
    )
    blocks_mixed, done, parts = feed_exchange(
        grad_mixed, lambda places, g: feed_back_blocks(places, g, feed_weights, scales, ups, gates)
    )
    low_ups, low_gates, scale_grads, _ = zip(*done)
    operands = (blocks_middle, blocks_mixed, low_ups, low_gates, gated)
    other = feed_grads(1, *operands)
    parts, other = tie(parts, other)
    other = exchange(other, "section", 1)
    grad_hidden, grad_branch, rate_one = mix_back_block(
        hidden, branch, mixing[:1], (grad_middle, *parts)
    )
    grads = [grad_branch, to(grad_branch, 1), to(grad_branch, 2)]
    low_ups, _ = tie(low_ups, grad_branch)
    feed_sums = feed_grads(0, blocks_middle, blocks_mixed, low_ups, low_gates, gated, other)
    grads, _ = tie(grads, feed_sums)
    small = (scale_grads[0] + scale_grads[1] + scale_grads[3], rate_one[0], rate_two[0])
    grads += pass_halves(*grads[1:])
    if hooks:
        small, grads = tie(small, grads)
        small = hooks[0](small)
    low, partial, gain_grad = attend_back(
        info, starts, query, keys, values, attended, logsums, raw, grads,
        attend_out, attend_in, cosine, sine, gains,
    )
    sent = [to(partial[at], at) for at in (3, 1, 2)]
    if hooks:
        low, small = hooks[1](low, small, gain_grad[:, 0])
    own, other = attend_grads(section, low, attended, blocks_hidden, grads)
    if hooks:
        other, small = hooks[2](other, small)
    other = exchange(other, "section", 1)
    attend_sums = (own + other.astype(F32)).astype(BF16).reshape(4, -1, own.shape[1])
    return (grad_hidden, partial[0], *sent), feed_sums, attend_sums, gain_grad[:, 0], small


def adam_update(weight, first, second, gradient, factor, rate):
    clipped = gradient * factor
    first_new = BETA_FIRST * first + (1.0 - BETA_FIRST) * clipped
    second_new = BETA_SECOND * second + (1.0 - BETA_SECOND) * clipped * clipped
    first_hat = first_new / (1.0 - BETA_FIRST**STEP)
    second_hat = second_new / (1.0 - BETA_SECOND**STEP)
    moved = weight - rate * first_hat / (jnp.sqrt(second_hat) + ADAM_EPSILON)
    return (first_new, second_new, moved)


def per_device(
    inputs,
    cotangent,
    doc_ids,
    attention_in,
    attention_out,
    feedforward_in,
    feedforward_out,
    unit_scales,
    mix_rates,
    first_attention_in,
    second_attention_in,
    first_attention_out,
    second_attention_out,
    first_feedforward_in,
    second_feedforward_in,
    first_feedforward_out,
    second_feedforward_out,
    first_unit_scales,
    second_unit_scales,
    first_mix_rates,
    second_mix_rates,
):
    section = lax.axis_index("section")
    is_first = section == 0
    dp_index = lax.axis_index("dp")
    dp_size = lax.axis_size("dp")
    local_rows = inputs.shape[1]

    def ordered(own, other):
        return jnp.where(is_first, own, other), jnp.where(is_first, other, own)

    def halves(array, dim):
        width = array.shape[dim] // 2
        own = lax.dynamic_slice_in_dim(array, section * width, width, dim)
        other = lax.dynamic_slice_in_dim(array, (1 - section) * width, width, dim)
        return own, other

    hidden_low = lax.dynamic_index_in_dim(inputs, section, 0, False)

    attend_rows = jnp.concatenate(
        [jnp.swapaxes(attention_in[0], 1, 2), attention_out], axis=0
    ).astype(BF16)
    small = jnp.concatenate([unit_scales.reshape(-1), mix_rates.reshape(-1)]).astype(BF16)
    def gather_ring(half):
        if dp_size != 4:
            whole = lax.all_gather(half, "dp", axis=1, tiled=True)
            return whole, whole
        blocks, count = spread_rows(half, "dp"), half.shape[1]
        whole = jnp.zeros((half.shape[0], dp_size * count, half.shape[2]), BF16)
        for source, block in zip(ring_sources("dp"), blocks):
            whole = lax.dynamic_update_slice_in_dim(whole, block, source * count, 1)
        return whole, blocks[-2]

    own, other = halves(attend_rows, 2)
    attend_pieces = ordered(own, exchange(other, "section", 1))
    attend_pieces, feedforward_in_here, feedforward_out_here = tie(
        attend_pieces, feedforward_in, feedforward_out
    )
    feed_rows = jnp.concatenate(
        [jnp.swapaxes(feedforward_in_here[0].astype(BF16), 1, 2), feedforward_out_here.astype(BF16)], axis=0
    )
    own, other = halves(feed_rows, 1)
    feed_pieces = ordered(own, exchange(other, "section", 1))
    attend_first, came = gather_ring(attend_pieces[0])
    attend_second, *feed_pieces, _ = tie(attend_pieces[1], *feed_pieces, came)
    attend_owns = (attend_first, lax.all_gather(attend_second, "dp", axis=1, tiled=True))
    small = jnp.stack(ordered(small, exchange(small, "section", 1))).reshape(-1)
    small = gather_small(small, "dp").astype(F32)
    small = small.reshape(dp_size, 2, -1)
    units_here = unit_scales.shape[2]

    def units_apart(values):
        parts = values.reshape(dp_size, 2, -1)
        own, other = ordered(parts[:, 0], parts[:, 1])
        return jnp.concatenate([own.reshape(-1), other.reshape(-1)])

    def units_back(values):
        parts = values.reshape(2, dp_size, -1)
        own, other = ordered(parts[0], parts[1])
        return jnp.stack([own, other], axis=1).reshape(-1)

    layers, feed_owns = [], []
    for layer in range(2):
        feed_own = lax.all_gather(feed_pieces[layer], "dp", axis=1, tiled=True)
        units = small[:, layer, :units_here].reshape(-1)
        mixing = small[:, layer, units_here:].reshape(dp_size, 2, -1)
        mixing = jnp.swapaxes(mixing, 0, 1).reshape(2, -1)
        width_qk, width_ff = attend_owns[0].shape[1], 2 * feed_own.shape[1]
        layers.append((
            units[:width_qk, None],
            jnp.stack([
                units_apart(units[width_qk : width_qk + width_ff]),
                units_apart(units[width_qk + width_ff :]),
            ]),
            mixing,
        ))
        feed_owns.append(feed_own)

    doc_row = lax.dynamic_index_in_dim(doc_ids, section, 0, False)
    starts_all = document_starts(doc_row)
    mp_index = lax.axis_index("mp")
    sources = [mp_index ^ offset for offset in range(4)]
    places = jnp.arange(local_rows, dtype=jnp.int32)
    starts = jnp.stack([
        lax.dynamic_slice_in_dim(starts_all, source * local_rows, local_rows, 0)
        for source in sources
    ])
    sources = jnp.stack(sources).astype(jnp.int32)
    cosine, sine = rope_tables(sources[:, None] * local_rows + places - starts)
    info = jnp.concatenate([sources, starts[:, 0]])
    tables = (cosine, sine, starts, info)

    def scatter(sums):
        return lax.psum_scatter(sums, "dp", scatter_dimension=1, tiled=True)

    def scatter_direct(sums):
        if dp_size != 4:
            return scatter(sums), sums
        count = sums.shape[1] // dp_size
        parts = [
            lax.dynamic_slice_in_dim(sums, (dp_index ^ bits) * count, count, 1)
            for bits in range(dp_size)
        ]
        parts[1:] = [exchange(part, "dp", bits) for bits, part in enumerate(parts[1:], 1)]
        return sum(part.astype(F32) for part in tie(*parts)).astype(BF16), parts[1]

    def small_vector(scales, rate_one, rate_two):
        return jnp.concatenate([units_back(scales[0]), units_back(scales[1]), rate_one, rate_two])

    def attend_params(own, other):
        attend = jnp.concatenate(ordered(own, other), axis=2)
        return attend[:3].reshape(-1, attend.shape[2]), attend[3]

    first, second = layers
    own = attend_owns[0]
    first = (*attend_params(own, exchange(own, "section", 1)), *first)
    section_ref = section.astype(jnp.int32).reshape(1)
    grad = lax.dynamic_index_in_dim(cotangent, section, 0, False)
    _, hidden_second, stored_first, weights_first, later = layer_forward(
        hidden_low, hidden_low, first, tables, False, feed_owns[0], attend_owns[1]
    )
    second = (*attend_params(*later), *second)
    result, _, stored_second, weights_second, _ = layer_forward(
        hidden_second, hidden_second, second, tables, True, feed_owns[1]
    )
    parts, feed_second, attend_second, gains_second, small_second = layer_backward(
        stored_second, (grad,), False, second, tables, weights_second, section_ref
    )
    feed_second = scatter(feed_second)
    parts, attend_second = tie(parts, attend_second)
    attend_second = scatter(attend_second)

    width_qk, width_rates = gains_second.shape[0], 2 * dp_size * mix_rates.shape[2]

    def start_small(small_first):
        values = jnp.concatenate(
            [small_vector(*small_first), small_vector(*small_second), gains_second]
        )
        return values, exchange(values, "section", 1)

    def next_small(low, small, gains):
        low, (values, coming) = tie(low, small)
        return low, (jnp.concatenate([values + coming, gains]),)

    def last_small(other, small):
        other, (values,) = tie(other, small)
        return other, (values, exchange(values, "dp", 1))

    parts, feed_first, attend_first, _, small = layer_backward(
        stored_first, parts, True, first, tables, weights_first, section_ref,
        (start_small, next_small, last_small),
    )
    feed_first = scatter(feed_first)
    sent_second = [
        lax.ppermute(part, "section", [(0, 1)]) for part in (attend_second, feed_second)
    ]
    attend_first, came = scatter_direct(attend_first)
    small, _ = tie(small, came)
    sums, bit = small[0] + small[1], 2
    while bit < dp_size:
        sums = sums + exchange(sums, "dp", bit)
        bit *= 2

    reduced_first = (attend_first, feed_first)
    reduced_second = (attend_second, feed_second)
    squares = sum(
        jnp.sum(jnp.square(part.astype(F32))) for part in (*reduced_first, *reduced_second)
    )
    halves_of = [
        (one, two, lax.ppermute(one, "section", [(1, 0)]), theirs)
        for one, two, theirs in zip(reduced_first, reduced_second, sent_second)
    ]

    layer_sums = sums[: -2 * width_qk].reshape(2, -1)
    gain_first = sums[-width_qk:]
    gain_sums = jnp.stack([gain_first + exchange(gain_first, "section", 1), sums[-2 * width_qk : -width_qk]])
    scale_sums, rate_sums = layer_sums[:, :-width_rates], layer_sums[:, -width_rates:]
    near_rates, *far_rates = [rate_sums] + [to(rate_sums, at) for at in (1, 2, 3)]
    rate_sums = ((near_rates + far_rates[0]) + (far_rates[1] + far_rates[2])).reshape(2, 2, -1)
    unit_grads = jnp.concatenate([gain_sums, scale_sums], axis=1)
    unit_grads = jnp.where(is_first, unit_grads[0], unit_grads[1])
    unit_grads = lax.dynamic_slice_in_dim(unit_grads, dp_index * units_here, units_here, 0)
    unit_grads = unit_grads[None, None]
    rates_here = mix_rates.shape[2]
    rate_grads = jnp.where(is_first, rate_sums[0], rate_sums[1])
    rate_grads = lax.dynamic_slice_in_dim(rate_grads, dp_index * rates_here, rates_here, 1)[None]

    turn = lambda array: jnp.swapaxes(array, 1, 2)
    leading = (mp_index == 0).astype(F32)
    squares = squares + jnp.sum(unit_grads * unit_grads)
    squares = squares + leading * jnp.sum(rate_grads * rate_grads)
    squares = squares.reshape(1)
    squares = sum_over(squares + exchange(squares, "section", 1), "mp")
    squares, parts = tie(squares, parts)
    squares = sum_over(squares, "dp")
    gradient_norm = jnp.sqrt(squares[0])
    factor = CLIP_NORM / jnp.maximum(gradient_norm, CLIP_NORM)

    grad = sum(part.astype(F32) for part in parts)
    to_send = jnp.where(is_first, result, grad)
    kept = jnp.where(is_first, grad, result)
    arrived = exchange(to_send, "section", 1)
    boundary_states = jnp.stack(ordered(kept, arrived))[None]

    scalar = factor.reshape(1)
    head_rows, width = attention_out.shape[1:]
    feed_units = feedforward_out.shape[1]
    rows = min(64, head_rows)
    updates = []
    attend_halves, feed_halves = halves_of
    unit_half = feed_units // 2
    turned = (
        (1, width, feed_units), (1, unit_half, width), lambda i: (i, 0, 0), lambda i: (i, 0, 0), (2,)
    )
    update = functools.partial(adam_matrix, section_ref, scalar)
    new = update(
        [turn(array[0]) for array in (attention_in, first_attention_in, second_attention_in)],
        attend_halves, 2, by_columns, (1, rows, width), (1, rows, width // 2),
        lambda i, j: (i, j, 0), lambda i, j: (i, j, 0), (3, head_rows // rows),
    )
    updates.extend(turn(part)[None] for part in new)
    updates.extend(update(
        (attention_out, first_attention_out, second_attention_out),
        attend_halves, 2, by_columns, (1, rows, width), (1, rows, width // 2),
        lambda i: (0, i, 0), lambda i: (3, i, 0), (head_rows // rows,),
    ))
    new = update(
        [array[0] for array in (feedforward_in, first_feedforward_in, second_feedforward_in)],
        feed_halves, 1, by_rows_turned, *turned,
    )
    updates.extend(part[None] for part in new)
    updates.extend(update(
        (feedforward_out, first_feedforward_out, second_feedforward_out),
        feed_halves, 2, by_rows, (1, unit_half, width), (1, unit_half, width),
        lambda i: (0, i, 0), lambda i: (2, 0, 0), (2,),
    ))
    updates.extend(
        adam_update(
            unit_scales, first_unit_scales, second_unit_scales, unit_grads, factor, SCALE_RATE
        )
    )
    updates.extend(
        adam_update(
            mix_rates, first_mix_rates, second_mix_rates, rate_grads, factor, MIXING_RATE
        )
    )
    return (boundary_states, gradient_norm, *updates)


def solution(mesh):
    in_specs = (
        P("dp", "mp", None),
        P("dp", "mp", None),
        P("dp", None),
        P("section", None, None, ("mp", "dp")),
        P("section", ("mp", "dp"), None),
        P("section", None, None, ("mp", "dp")),
        P("section", ("mp", "dp"), None),
        P("section", "mp", "dp"),
        P("section", None, "dp"),
        P("section", None, None, ("mp", "dp")),
        P("section", None, None, ("mp", "dp")),
        P("section", ("mp", "dp"), None),
        P("section", ("mp", "dp"), None),
        P("section", None, None, ("mp", "dp")),
        P("section", None, None, ("mp", "dp")),
        P("section", ("mp", "dp"), None),
        P("section", ("mp", "dp"), None),
        P("section", "mp", "dp"),
        P("section", "mp", "dp"),
        P("section", None, "dp"),
        P("section", None, "dp"),
    )
    out_specs = (
        P("section", "dp", "mp", None),
        P(),
        P("section", None, None, ("mp", "dp")),
        P("section", None, None, ("mp", "dp")),
        P("section", None, None, ("mp", "dp")),
        P("section", ("mp", "dp"), None),
        P("section", ("mp", "dp"), None),
        P("section", ("mp", "dp"), None),
        P("section", None, None, ("mp", "dp")),
        P("section", None, None, ("mp", "dp")),
        P("section", None, None, ("mp", "dp")),
        P("section", ("mp", "dp"), None),
        P("section", ("mp", "dp"), None),
        P("section", ("mp", "dp"), None),
        P("section", "mp", "dp"),
        P("section", "mp", "dp"),
        P("section", "mp", "dp"),
        P("section", None, "dp"),
        P("section", None, "dp"),
        P("section", None, "dp"),
    )
    return jax.shard_map(
        per_device, mesh=mesh, in_specs=in_specs, out_specs=out_specs, check_vma=False
    )
```

```python
import functools
import math

import jax
import jax.numpy as jnp
from jax import lax
from jax.experimental import pallas as pl
from jax.experimental.pallas import tpu as pltpu
from jax.sharding import PartitionSpec as P

HD = 64
STEP = 10

NORM_EPSILON = 1e-06
ROPE_BASE = 10000.0
CLIP_NORM = 0.1
LEARN_RATE = 0.05
SCALE_RATE = 1.25
MIXING_RATE = 0.4
BETA_FIRST = 0.9
BETA_SECOND = 0.95
ADAM_EPSILON = 1e-08

BF16 = jnp.bfloat16
F32 = jnp.float32


def exchange(block, axis, bit):
    route = [(i, i ^ bit) for i in range(lax.axis_size(axis))]
    return lax.ppermute(block, axis, route)


def gray(place):
    return place ^ (place >> 1)


def ring_place(index, size):
    shift = 1
    while shift < size:
        index = index ^ (index >> shift)
        shift *= 2
    return index


def ring_step(block, axis):
    size = lax.axis_size(axis)
    route = []
    for place in range(size):
        route.append((gray(place), gray((place + 1) % size)))
        route.append((size + gray(place), size + gray((place - 1) % size)))
    return lax.ppermute(block, ("section", axis), route)


def ring_sources(axis):
    size = lax.axis_size(axis)
    place = ring_place(lax.axis_index(axis), size)
    way = 1 - 2 * lax.axis_index("section")
    return [gray((place - way * step + size) % size) for step in range(size)]


def spread_rows(block, axis="mp"):
    blocks = [block]
    for _ in range(lax.axis_size(axis) - 1):
        blocks.append(ring_step(blocks[-1], axis))
    return blocks


def sum_over(values, axis):
    bit = 1
    while bit < lax.axis_size(axis):
        values = values + exchange(values, axis, bit)
        bit *= 2
    return values


def gather_small(values, axis):
    index = lax.axis_index(axis)
    gathered = values[None]
    bit = 1
    while bit < lax.axis_size(axis):
        other = exchange(gathered, axis, bit)
        low = (index & bit) == 0
        gathered = jnp.concatenate(
            [jnp.where(low, gathered, other), jnp.where(low, other, gathered)], axis=0
        )
        bit *= 2
    return gathered


def unit_norm(values):
    return values * lax.rsqrt(jnp.sum(values * values, axis=-1, keepdims=True) + NORM_EPSILON)


def document_starts(doc_row):
    position = jnp.arange(doc_row.shape[-1], dtype=jnp.int32)
    change = jnp.concatenate([jnp.ones((1,), dtype=jnp.bool_), doc_row[1:] != doc_row[:-1]])
    return lax.cummax(jnp.where(change, position, 0), axis=0)


def rope_tables(offsets):
    half_width = HD // 2
    inverse = 1.0 / ROPE_BASE ** (jnp.arange(half_width, dtype=F32) * (2.0 / HD))
    angles = inverse[:, None] * offsets.astype(F32)[..., None, :]
    angles = jnp.concatenate([angles, angles], axis=-2)
    return jnp.cos(angles), jnp.sin(angles)


def mix_residual(hidden, branch, mixing):
    return unit_norm(hidden + mixing * (unit_norm(branch) - hidden))


NT = (((1,), (1,)), ((), ()))
TN = (((0,), (0,)), ((), ()))
NN = (((1,), (0,)), ((), ()))
VMEM = pltpu.VMEM
WHOLE, NEAR = "whole", "near"
SCALARS = pl.BlockSpec(memory_space=pltpu.SMEM)


def mul(left, right, dims=NN):
    return lax.dot_general(left, right, dims, preferred_element_type=F32)


def block_of(array):
    zeros = (0,) * len(array.shape)
    return pl.BlockSpec(array.shape, lambda *place: zeros)


def call(body, out_shape, in_specs, flops, moved, scratch=(), grid=(1,), out_specs=None, loose=()):
    def run(*args):
        specs = [
            block_of(arg) if spec in (WHOLE, NEAR) else spec for spec, arg in zip(in_specs, args)
        ]
        args = [
            arg if spec in (SCALARS, NEAR) else pltpu.with_memory_space_constraint(arg, pltpu.HBM)
            for spec, arg in zip(in_specs, args)
        ]
        return pl.pallas_call(
            body,
            out_shape=[
                out if at in loose else pltpu.HBM(out.shape, out.dtype)
                for at, out in enumerate(out_shape)
            ],
            grid=grid,
            in_specs=specs,
            out_specs=out_specs or [block_of(out) for out in out_shape],
            scratch_shapes=list(scratch),
            compiler_params=pltpu.CompilerParams(vmem_limit_bytes=50 << 20),
            cost_estimate=pl.CostEstimate(flops=flops, bytes_accessed=moved, transcendentals=0),
        )(*args)

    return run


def shape(dims, dtype):
    return jax.ShapeDtypeStruct(dims, dtype)


def turned(raw, cosine, sine):
    half = HD // 2
    first, second = raw[:half], raw[half:]
    return jnp.concatenate(
        [
            first * cosine[:half] - second * sine[:half],
            second * cosine[half:] + first * sine[half:],
        ],
        axis=0,
    )


def turned_back(grad, cosine, sine):
    half = HD // 2
    first, second = grad[:half], grad[half:]
    return jnp.concatenate(
        [
            first * cosine[:half] + second * sine[half:],
            second * cosine[half:] - first * sine[:half],
        ],
        axis=0,
    )


def rows_at(places):
    return [row for at in places for row in ((at,) if at < 3 else (3, 4))]


def side_by_side(refs):
    return refs[0][...] if len(refs) == 1 else jnp.concatenate([ref[...] for ref in refs], axis=0)


def project_kernel(places, *refs):
    count = len(rows_at(places))
    weight, cosine, sine, gains = refs[count : count + 4]
    tokens = cosine.shape[2]
    x, outs = side_by_side(refs[:count]), refs[count + 4 :]
    for n, at in enumerate(places):
        raw_out, query, keys, values = outs[4 * n : 4 * n + 4]
        width = query.shape[0]
        raw = mul(weight[...], x[n * tokens : (n + 1) * tokens], NT)
        raw_out[...] = raw[: 2 * width]
        values[...] = raw[2 * width :].astype(BF16)
        for part, out in ((0, query), (1, keys)):
            for top in range(0, width, HD):
                turn = turned(
                    raw[part * width + top : part * width + top + HD], cosine[at], sine[at]
                )
                scale = lax.rsqrt(jnp.sum(turn * turn, axis=0, keepdims=True) + NORM_EPSILON)
                head = (turn * scale * gains[top : top + HD]).astype(BF16)
                out[top : top + HD] = head * math.sqrt(HD) if part == 0 else head


def project_blocks(places, x, weight, cosine, sine, gains):
    tokens, depth, count = cosine.shape[2], weight.shape[1], len(places)
    width = weight.shape[0] // 3
    low = shape((width, tokens), BF16)
    outs = call(
        functools.partial(project_kernel, places),
        [shape((2 * width, tokens), F32), low, low, low] * count,
        [NEAR] * len(x) + [WHOLE] * 4,
        2 * tokens * depth * 3 * width * count,
        2 * 3 * width * depth,
    )(*x, weight, cosine, sine, gains)
    return [outs[4 * n : 4 * n + 4] for n in range(count)]


def near(info, at, other, tokens):
    return (info[other] <= info[at]) & ((info[other] + 1) * tokens > info[4 + at])


def seen(info, at, other, starts, tokens):
    key_place = info[other] * tokens + lax.broadcasted_iota(jnp.int32, (tokens, tokens), 0)
    query_place = info[at] * tokens + lax.broadcasted_iota(jnp.int32, (tokens, tokens), 1)
    return (key_place <= query_place) & (key_place >= starts)


def share_out(partial, value):
    partial[...] = value.astype(partial.dtype)


def partial_shape(at, tokens, depth):
    return shape((tokens, depth), BF16 if at else F32)


def attend_kernel(places, info, starts, *refs):
    count = len(places)
    query, rest = refs[:count], refs[count:]
    keys, values, weight, outs, (total, sums) = rest[:4], rest[4:8], rest[8], rest[9:-2], rest[-2:]
    width, tokens = query[0].shape
    for n, at in enumerate(places):
        attended, logsums, partial = outs[3 * n : 3 * n + 3]
        total[n] = jnp.zeros((width, tokens), F32)
        sums[n] = jnp.ones((8, tokens), F32)
        sums[n, : width // HD] = jnp.zeros((width // HD, tokens), F32)
        for other in range(4):

            @pl.when(near(info, at, other, tokens))
            def _():
                allowed = seen(info, at, other, starts[at : at + 1], tokens)
                for head in range(width // HD):
                    rows = slice(head * HD, head * HD + HD)
                    shares = jnp.exp(mul(keys[other][rows], query[n][rows], TN))
                    shares = jnp.where(allowed, shares, 0.0)
                    sums[n, head : head + 1] += jnp.sum(shares, axis=0, keepdims=True)
                    total[n, rows] += mul(values[other][rows], shares.astype(BF16))

        logsums[...] = jnp.log(sums[n])
        inverse = 1.0 / sums[n]
        for head in range(width // HD):
            rows = slice(head * HD, head * HD + HD)
            attended[rows] = (total[n, rows] * inverse[head : head + 1]).astype(BF16)
        share_out(partial, mul(attended[...], weight[...], TN))


def attend_blocks(places, info, starts, query, keys, values, weight):
    width, tokens = query[0].shape
    depth, count = weight.shape[1], len(places)
    outs = call(
        functools.partial(attend_kernel, places),
        [
            out
            for at in places
            for out in (
                shape((width, tokens), BF16),
                shape((8, tokens), F32),
                partial_shape(at, tokens, depth),
            )
        ],
        [SCALARS] + [WHOLE] * (10 + count),
        2 * tokens * (depth * width + 10 * tokens * 256) * count,
        2 * depth * width,
        [VMEM((count, width, tokens), F32), VMEM((count, 8, tokens), F32)],
        loose=[3 * n + 2 for n, at in enumerate(places) if at],
    )(info, starts, *[query[at] for at in places], *keys, *values, weight)
    return [outs[3 * n : 3 * n + 3] for n in range(count)]


def attend_back_kernel(info, starts, *refs):
    query, keys, values, attended, logsums, raw = (refs[4 * n : 4 * n + 4] for n in range(6))
    grads, (w_out, w_in, cosine, sine, gains) = refs[24:29], refs[29:34]
    low, partial, gain_grad = refs[34:38], refs[38:42], refs[42]
    pulled, deltas, grad_query, grad_keys, grad_values = refs[43:]
    width, tokens = query[0].shape
    heads = width // HD
    grad_query[...] = jnp.zeros_like(grad_query)
    grad_keys[...] = jnp.zeros_like(grad_keys)
    grad_values[...] = jnp.zeros_like(grad_values)
    deltas[...] = jnp.zeros_like(deltas)
    for at in range(4):
        rows = side_by_side([grads[row] for row in rows_at((at,))])
        grad = mul(w_out[...], rows, NT).astype(BF16)
        pulled[at] = grad
        product = grad.astype(F32) * attended[at][...].astype(F32)
        for head in range(heads):
            rows = slice(head * HD, head * HD + HD)
            deltas[at, head : head + 1] = jnp.sum(product[rows], axis=0, keepdims=True)
    for at in range(4):
        for other in range(4):

            @pl.when(near(info, at, other, tokens))
            def _():
                allowed = seen(info, at, other, starts[at : at + 1], tokens)
                for head in range(heads):
                    rows = slice(head * HD, head * HD + HD)
                    grad_rows, query_rows = pulled[at, rows], query[at][rows]
                    scores = mul(keys[other][rows], query_rows, TN) - logsums[at][head : head + 1]
                    shares = jnp.where(allowed, jnp.exp(scores), 0.0)
                    grad_shares = mul(values[other][rows], grad_rows, TN)
                    grad_scores = shares * (grad_shares - deltas[at, head : head + 1])
                    grad_scores = grad_scores.astype(BF16)
                    grad_values[other, rows] += mul(grad_rows, shares.astype(BF16), NT)
                    grad_keys[other, rows] += mul(query_rows, grad_scores, NT)
                    grad_query[at, rows] += mul(keys[other][rows], grad_scores)

    gain_total = [0.0] * heads
    for at in range(4):
        cos, sin = cosine[at], sine[at]
        for part, source, factor in ((0, grad_query, math.sqrt(HD)), (1, grad_keys, 1.0)):
            for head in range(heads):
                rows = slice(head * HD, head * HD + HD)
                turn = turned(raw[at][part * width + head * HD : part * width + head * HD + HD], cos, sin)
                scale = lax.rsqrt(jnp.sum(turn * turn, axis=0, keepdims=True) + NORM_EPSILON)
                unit = turn * scale
                grad = source[at, rows] * factor
                gain_total[head] = gain_total[head] + grad * unit
                grad = grad * gains[rows]
                grad = scale * (grad - unit * jnp.sum(unit * grad, axis=0, keepdims=True))
                low[at][part * width + head * HD : part * width + head * HD + HD] = turned_back(
                    grad, cos, sin
                ).astype(BF16)
        low[at][2 * width :] = grad_values[at].astype(BF16)
        share_out(partial[at], mul(low[at][...], w_in[...], TN))
    for head in range(heads):
        gain_grad[head * HD : head * HD + HD] = jnp.sum(gain_total[head], axis=1, keepdims=True)


def attend_back(info, starts, query, keys, values, attended, logsums, raw, grads,
                w_out, w_in, cosine, sine, gains):
    width, tokens = query[0].shape
    depth = w_out.shape[1]
    low = shape((3 * width, tokens), BF16)
    block = VMEM((4, width, tokens), F32)
    outs = call(
        attend_back_kernel,
        [low] * 4
        + [partial_shape(at, tokens, depth) for at in range(4)]
        + [shape((width, 1), F32)],
        [SCALARS] + [WHOLE] * 25 + [NEAR] * 5 + [WHOLE] * 5,
        2 * 4 * tokens * (depth * width * 4 + 60 * tokens * 256),
        2 * depth * width * 12,
        [VMEM((4, width, tokens), BF16), VMEM((4, 8, tokens), F32), block, block, block],
        loose=(5, 6, 7),
    )(info, starts, *query, *keys, *values, *attended, *logsums, *raw, *grads,
      w_out, w_in, cosine, sine, gains)
    return outs[:4], outs[4:8], outs[8]


CHUNK = 256
GATE_WIDTH = math.sqrt(1024)


def started(copies, arrived, first=0):
    copies = [
        pltpu.make_async_copy(source, target, arrived.at[first + n])
        for n, (source, target) in enumerate(copies)
    ]
    for copy in copies:
        copy.start()
    return copies


def fetch_weights(own, other, weights, arrived):
    half = own.shape[1]
    size = min(CHUNK, half)
    places = [(index, start) for index in range(2) for start in range(0, half, size)]
    copies = started(
        [
            ((own, other)[index].at[:, pl.ds(start, size)], weights.at[index, :, pl.ds(start, size)])
            for index, start in places
        ],
        arrived,
    )
    return [
        (copy, index, slice(start, start + size), slice(index * half + start, index * half + start + size))
        for copy, (index, start) in zip(copies, places)
    ]


def feed_kernel(given, count, *refs):
    x, refs = refs[:given], refs[given:]
    (own, other, scales_in), outs, partial = refs[:3], refs[3 : 3 * count + 3], refs[3 * count + 3 : 4 * count + 3]
    weights, scales, ups, gates, gated, gated_turned, arrived, came, left = refs[4 * count + 3 :]
    half, tokens = own.shape[1], ups.shape[0] // count
    (scales_copy,) = started([(scales_in, scales)], came)
    chunks = fetch_weights(own, other, weights, arrived)
    block = side_by_side(x)
    scales_copy.wait()
    leaving = []
    for copy, index, rows, units in chunks:
        copy.wait()
        up, gate = mul(block, weights[index, 0, rows], NT), mul(block, weights[index, 1, rows], NT)
        ups[:, units] = up.astype(BF16)
        gates[:, units] = gate.astype(BF16)
        z = gate * (scales[1:2, units] * GATE_WIDTH)
        silu = z * (0.5 + 0.5 * jnp.tanh(0.5 * z))
        mixed = (up * scales[0:1, units] * silu).astype(BF16)
        gated[:, units] = mixed
        gated_turned[units] = mixed.T
        if rows.stop == half:
            columns = pl.ds(index * half, half)
            for n in range(count):
                places = pl.ds(n * tokens, tokens)
                leaving += started(
                    [
                        (ups.at[places, columns], outs[3 * n].at[:, columns]),
                        (gates.at[places, columns], outs[3 * n + 1].at[:, columns]),
                        (gated_turned.at[columns, places], outs[3 * n + 2].at[columns]),
                    ],
                    left,
                    3 * (index * count + n),
                )
    total = mul(gated[:, :half], weights[0, 2]) + mul(gated[:, half:], weights[1, 2])
    for n in range(count):
        share_out(partial[n], total[n * tokens : (n + 1) * tokens])
    for copy in leaving:
        copy.wait()


def feed_back_kernel(given, count, *refs):
    g, refs = refs[:given], refs[given:]
    (own, other, scales_in), kept = refs[:3], refs[3 : 2 * count + 3]
    outs, scale_grad = refs[2 * count + 3 : 4 * count + 3], refs[4 * count + 3]
    partial = refs[4 * count + 4 : 5 * count + 4]
    weights, scales, ups, gates, low_up, low_gate, up_turned, gate_turned = refs[5 * count + 4 : -3]
    arrived, came, left = refs[-3:]
    half, tokens = own.shape[1], ups.shape[0] // count
    (scales_copy,) = started([(scales_in, scales)], came)
    chunks = fetch_weights(own, other, weights, arrived)
    coming = [
        started(
            [
                (ref.at[:, pl.ds(index * half, half)],
                 into.at[pl.ds(n * tokens, tokens), pl.ds(index * half, half)])
                for n in range(count)
                for ref, into in ((kept[2 * n], ups), (kept[2 * n + 1], gates))
            ],
            came,
            1 + 2 * count * index,
        )
        for index in range(2)
    ]
    block = side_by_side(g)
    scales_copy.wait()
    leaving = []
    for copy, index, rows, units in chunks:
        copy.wait()
        grad = mul(block, weights[index, 2, rows], NT)
        if rows.start == 0:
            for copy in coming[index]:
                copy.wait()
        up, gate = ups[:, units].astype(F32), gates[:, units].astype(F32)
        s_up, s_gate = scales[0:1, units], scales[1:2, units] * GATE_WIDTH
        z = gate * s_gate
        sigmoid = 0.5 + 0.5 * jnp.tanh(0.5 * z)
        silu = z * sigmoid
        grad_silu = grad * silu
        grad_z = grad * (up * s_up) * (sigmoid + silu * (1.0 - sigmoid))
        grad_up, grad_gate = (grad_silu * s_up).astype(BF16), (grad_z * s_gate).astype(BF16)
        low_up[:, units], low_gate[:, units] = grad_up, grad_gate
        up_turned[units], gate_turned[units] = grad_up.T, grad_gate.T
        scale_grad[0:1, units] = jnp.sum(grad_silu * up, axis=0, keepdims=True)
        scale_grad[1:2, units] = jnp.sum(grad_z * gate, axis=0, keepdims=True) * GATE_WIDTH
        if rows.stop == half:
            columns = pl.ds(index * half, half)
            for n in range(count):
                places = pl.ds(n * tokens, tokens)
                leaving += started(
                    [
                        (up_turned.at[columns, places], outs[2 * n].at[columns]),
                        (gate_turned.at[columns, places], outs[2 * n + 1].at[columns]),
                    ],
                    left,
                    2 * (index * count + n),
                )
    total = mul(low_up[:, :half], weights[0, 0]) + mul(low_up[:, half:], weights[1, 0])
    total = total + mul(low_gate[:, :half], weights[0, 1]) + mul(low_gate[:, half:], weights[1, 1])
    for n in range(count):
        share_out(partial[n], total[n * tokens : (n + 1) * tokens])
    for copy in leaving:
        copy.wait()


HELD = pl.BlockSpec(memory_space=pl.ANY)


def feed_call(body, places, x, weights, scales, kept, held, pair, low, turned_count):
    half, count = weights[0].shape[1], len(places)
    tokens, depth = sum(block.shape[0] for block in x) // count, x[0].shape[1]
    partial = [partial_shape(at, tokens, depth) for at in places]
    semaphores = pltpu.SemaphoreType.DMA
    return call(
        functools.partial(body, len(x), count),
        held + pair + partial,
        [NEAR] * len(x) + [HELD] * (3 + len(kept)),
        2 * 6 * tokens * depth * half * count,
        2 * 6 * depth * half,
        [VMEM((2, 3, half, depth), BF16), VMEM(scales.shape, F32)]
        + [VMEM((count * tokens, 2 * half), BF16)] * low
        + [VMEM((2 * half, count * tokens), BF16)] * turned_count
        + [
            semaphores((2 * half // min(CHUNK, half),)),
            semaphores((1 + 2 * len(kept),)),
            semaphores((2 * len(held),)),
        ],
        out_specs=[HELD] * len(held) + [block_of(out) for out in pair + partial],
        loose=[len(held + pair) + n for n, at in enumerate(places) if at],
    )(*x, *weights, scales, *kept)


def feed_blocks(places, x, weights, scales):
    count = len(places)
    dims = (sum(block.shape[0] for block in x) // count, 2 * weights[0].shape[1])
    held = [shape(dims, BF16), shape(dims, BF16), shape(dims[::-1], BF16)] * count
    outs = feed_call(feed_kernel, places, x, weights, scales, (), held, [], 3, 1)
    return [[*outs[3 * n : 3 * n + 3], outs[3 * count + n]] for n in range(count)]


def feed_back_blocks(places, g, weights, scales, ups, gates):
    count = len(places)
    held = [shape(ups[0].shape[::-1], BF16)] * (2 * count)
    pair = [shape((2, ups[0].shape[1]), F32)]
    kept = [array for at in places for array in (ups[at], gates[at])]
    outs = feed_call(feed_back_kernel, places, g, weights, scales, kept, held, pair, 4, 2)
    return [
        [*outs[2 * n : 2 * n + 2], outs[2 * count] if n == 0 else None, outs[2 * count + 1 + n]]
        for n in range(count)
    ]


def feed_grad_kernel(has_other, *refs):
    middle, mixed, (ups, gates, gated) = refs[:5], refs[5:10], (refs[10:14], refs[14:18], refs[18:22])
    out = refs[-1]
    for row, (units, right) in enumerate(((ups, middle), (gates, middle), (gated, mixed))):
        left = jnp.concatenate([block[...] for block in units], axis=1)
        total = mul(left, side_by_side(right))
        if has_other:
            total = total + refs[22][row].astype(F32)
        out[row] = total.astype(BF16)


def feed_grads(half_at, middle, mixed, ups, gates, gated, other=None):
    units, tokens = ups[0].shape
    depth, half = middle[0].shape[1], units // 2
    part = pl.BlockSpec((half, tokens), lambda i: (half_at, 0))
    more = () if other is None else (other,)
    return call(
        functools.partial(feed_grad_kernel, bool(more)),
        [shape((3, half, depth), BF16)],
        [WHOLE] * 5 + [NEAR] * 5 + [part] * 12 + [NEAR] * len(more),
        2 * 3 * 4 * tokens * half * depth,
        2 * 12 * tokens * (half + depth),
    )(*middle, *mixed, *ups, *gates, *gated, *more)[0]


def attend_grad_kernel(section, *refs):
    low, attended, hidden, grads = refs[:4], refs[4:8], refs[8:13], refs[13:18]
    own, other = refs[18:]
    width, half = attended[0].shape[0], own.shape[1]
    for lefts, rights, top in ((low, hidden, 0), (attended, grads, 3 * width)):
        right = side_by_side(rights)
        for start in range(0, lefts[0].shape[0], width):
            total = mul(
                jnp.concatenate([left[start : start + width] for left in lefts], axis=1), right
            )
            rows = slice(top + start, top + start + width)
            for place in range(2):
                columns = total[:, place * half : place * half + half]

                @pl.when(section[0] == place)
                def _():
                    own[rows] = columns

                @pl.when(section[0] != place)
                def _():
                    other[rows] = columns.astype(BF16)


def attend_grads(section, low, attended, hidden, grads):
    width, tokens = attended[0].shape
    depth = hidden[0].shape[1]
    return call(
        attend_grad_kernel,
        [shape((4 * width, depth // 2), F32), shape((4 * width, depth // 2), BF16)],
        [SCALARS] + [WHOLE] * 13 + [NEAR] * 5,
        2 * 4 * 4 * tokens * width * depth,
        2 * 16 * tokens * depth,
    )(section, *low, *attended, *hidden, *grads)


def adam_kernel(axis, gradient_of, section, factor, weight, first, second, *refs):
    first_out, second_out, weight_out = refs[4:]
    clipped = gradient_of(section[0] == 0, [ref[...].astype(F32) for ref in refs[:4]]) * factor[0]
    first_new = BETA_FIRST * first[...] + (1.0 - BETA_FIRST) * clipped
    second_new = BETA_SECOND * second[...] + (1.0 - BETA_SECOND) * clipped * clipped
    first_out[...] = first_new
    second_out[...] = second_new
    first_hat = first_new / (1.0 - BETA_FIRST**STEP)
    second_hat = second_new / (1.0 - BETA_SECOND**STEP)
    moved = weight[...] - LEARN_RATE * first_hat / (jnp.sqrt(second_hat) + ADAM_EPSILON)
    scale = lax.rsqrt(jnp.sum(moved * moved, axis=axis, keepdims=True) + NORM_EPSILON)
    weight_out[...] = moved * scale


def adam_matrix(section, factor, arrays, halves, axis, gradient_of, block, half_block, place,
                half_place, grid):
    spec, half_spec = pl.BlockSpec(block, place), pl.BlockSpec(half_block, half_place)
    dims, size = arrays[0].shape, arrays[0].size
    return call(
        functools.partial(adam_kernel, axis, gradient_of),
        [shape(dims, F32)] * 3,
        [SCALARS] * 2 + [spec] * 3 + [half_spec] * 4,
        20 * size,
        28 * size,
        grid=grid,
        out_specs=[spec] * 3,
    )(section, factor, *arrays, *halves)


def half_of(is_first, parts, low_half):
    here, there = jnp.where(is_first, parts[0], parts[1]), jnp.where(is_first, parts[2], parts[3])
    return jnp.where(is_first == low_half, here, there)


def by_columns(is_first, parts):
    return jnp.concatenate(
        [half_of(is_first, parts, True), half_of(is_first, parts, False)], axis=2
    )


def by_rows(is_first, parts):
    return half_of(is_first, parts, pl.program_id(0) == 0)


def by_rows_turned(is_first, parts):
    both = [half_of(is_first, parts, low)[0] for low in (True, False)]
    return jnp.concatenate(both, axis=0).T[None]


def add_parts(parts):
    total = parts[0][...].astype(F32)
    for part in parts[1:]:
        total = total + part[...].astype(F32)
    return total


def mix_kernel(count, hidden, rate, *refs):
    branch_out, result, result_low = refs[count:]
    branch = add_parts(refs[:count])
    branch_out[...] = branch
    mixed = mix_residual(hidden[...].astype(F32), branch, rate[...])
    result[...] = mixed
    result_low[...] = mixed.astype(BF16)


def mix_block(hidden, rate, parts):
    dims = hidden.shape
    return call(
        functools.partial(mix_kernel, len(parts)),
        [shape(dims, F32), shape(dims, F32), shape(dims, BF16)],
        [WHOLE] * 2 + [WHOLE if part.dtype == F32 else NEAR for part in parts],
        10 * dims[0] * dims[1],
        8 * dims[0] * dims[1],
    )(hidden, rate, *parts)


def mix_back_kernel(count, rounded, hidden, branch, rate, *refs):
    grad_hidden, grad_branch, grad_rate = refs[count:]
    upstream = add_parts(refs[:count])
    if rounded:
        upstream = upstream.astype(BF16).astype(F32)
    h, b, r = hidden[...].astype(F32), branch[...], rate[...]
    scale = lax.rsqrt(jnp.sum(b * b, axis=-1, keepdims=True) + NORM_EPSILON)
    unit = b * scale
    apart = unit - h
    mixed = h + r * apart
    mixed_scale = lax.rsqrt(jnp.sum(mixed * mixed, axis=-1, keepdims=True) + NORM_EPSILON)
    mixed = mixed * mixed_scale
    grad = mixed_scale * (upstream - mixed * jnp.sum(mixed * upstream, axis=-1, keepdims=True))
    grad_rate[...] = jnp.sum(grad * apart, axis=0, keepdims=True)
    grad_unit = grad * r
    grad_hidden[...] = grad - grad_unit
    grad_unit = scale * (grad_unit - unit * jnp.sum(unit * grad_unit, axis=-1, keepdims=True))
    grad_branch[...] = grad_unit.astype(BF16)


def mix_back_block(hidden, branch, rate, parts, rounded=False):
    dims = hidden.shape
    return call(
        functools.partial(mix_back_kernel, len(parts), rounded),
        [shape(dims, F32), shape(dims, BF16), shape((1, dims[1]), F32)],
        [WHOLE] * 3 + [WHOLE if part.dtype == F32 else NEAR for part in parts],
        20 * dims[0] * dims[1],
        12 * dims[0] * dims[1],
    )(hidden, branch, rate, *parts)


def tie(*values):
    return lax.optimization_barrier(values)


def to(block, at):
    return exchange(block, "mp", at)


def pass_halves(first, second):
    half = first.shape[0] // 2
    return [to(second[:half], 1), to(first[half:], 2)]


def layer_forward(hidden, low, params, tables, tied, feed_own, later=None):
    attend_in, attend_out, gains, scales, mixing = params
    cosine, sine, starts, info = tables
    project = lambda *places: project_blocks(
        places, [blocks[row] for row in rows_at(places)], attend_in, cosine, sine, gains
    )
    blocks = [low, to(low, 1), to(low, 2)]
    if tied:
        heads = project(0)
        *blocks, heads = tie(*blocks, heads)
        blocks += pass_halves(*blocks[1:])
        heads += project(1, 2)
        *blocks, heads = tie(*blocks, heads)
        heads += project(3)
    else:
        blocks += pass_halves(*blocks[1:])
        heads = project(0, 1, 2, 3)
    raw, query, keys, values = zip(*heads)
    attend = lambda *places: attend_blocks(places, info, starts, query, keys, values, attend_out)
    far = attend(3)
    sent = [to(far[0][-1], 3)]
    near_blocks = attend(1, 2)
    sent += [to(block[-1], at) for at, block in zip((1, 2), near_blocks)]
    attended = attend(0) + near_blocks + far
    sent, attended[0], feed_own = tie(sent, attended[0], feed_own)
    feed_weights = (feed_own, exchange(feed_own, "section", 1))
    branch, middle, middle_low = mix_block(hidden, mixing[:1], (attended[0][-1], *sent))
    blocks_middle, fed, parts = feed_exchange(
        middle_low, lambda places, x: feed_blocks(places, x, feed_weights, scales)
    )
    mixed, result, result_low = mix_block(middle, mixing[1:], parts)
    if later is not None:
        result_low, later = tie(result_low, later)
        later = (later, exchange(later, "section", 1))
    ups, gates, gated, _ = zip(*fed)
    attended, logsums, _ = zip(*attended)
    stored = (
        (hidden, branch, blocks, raw, query, keys, values, attended, logsums),
        (middle, mixed, blocks_middle, ups, gates, gated),
    )
    return result, result_low, stored, feed_weights, later


def feed_exchange(block, work):
    blocks = [block, to(block, 1), to(block, 2)]
    done = work((0,), blocks[:1])
    *blocks, done = tie(*blocks, done)
    blocks += pass_halves(*blocks[1:])
    done += work((1, 2), blocks[1:3])
    sent = [to(done[at][-1], at) for at in (1, 2)]
    *blocks, done = tie(*blocks, done)
    done += work((3,), blocks[3:])
    sent.append(to(done[3][-1], 3))
    return blocks, done, (done[0][-1], *sent)


def layer_backward(stored, upstream, rounded, params, tables, feed_weights, section, hooks=()):
    attend_in, attend_out, gains, scales, mixing = params
    cosine, sine, starts, info = tables
    attend_stored, (middle, mixed, blocks_middle, ups, gates, gated) = stored
    hidden, branch, blocks_hidden, raw, query, keys, values, attended, logsums = attend_stored
    grad_middle, grad_mixed, rate_two = mix_back_block(
        middle, mixed, mixing[1:], upstream, rounded
    )
    blocks_mixed, done, parts = feed_exchange(
        grad_mixed, lambda places, g: feed_back_blocks(places, g, feed_weights, scales, ups, gates)
    )
    low_ups, low_gates, scale_grads, _ = zip(*done)
    operands = (blocks_middle, blocks_mixed, low_ups, low_gates, gated)
    other = feed_grads(1, *operands)
    parts, other = tie(parts, other)
    other = exchange(other, "section", 1)
    grad_hidden, grad_branch, rate_one = mix_back_block(
        hidden, branch, mixing[:1], (grad_middle, *parts)
    )
    grads = [grad_branch, to(grad_branch, 1), to(grad_branch, 2)]
    low_ups, _ = tie(low_ups, grad_branch)
    feed_sums = feed_grads(0, blocks_middle, blocks_mixed, low_ups, low_gates, gated, other)
    grads, _ = tie(grads, feed_sums)
    small = (scale_grads[0] + scale_grads[1] + scale_grads[3], rate_one[0], rate_two[0])
    grads += pass_halves(*grads[1:])
    if hooks:
        small, grads = tie(small, grads)
        small = hooks[0](small)
    low, partial, gain_grad = attend_back(
        info, starts, query, keys, values, attended, logsums, raw, grads,
        attend_out, attend_in, cosine, sine, gains,
    )
    sent = [to(partial[at], at) for at in (3, 1, 2)]
    if hooks:
        low, small = hooks[1](low, small, gain_grad[:, 0])
    own, other = attend_grads(section, low, attended, blocks_hidden, grads)
    if hooks:
        other, small = hooks[2](other, small)
    other = exchange(other, "section", 1)
    attend_sums = (own + other.astype(F32)).astype(BF16).reshape(4, -1, own.shape[1])
    return (grad_hidden, partial[0], *sent), feed_sums, attend_sums, gain_grad[:, 0], small


def adam_update(weight, first, second, gradient, factor, rate):
    clipped = gradient * factor
    first_new = BETA_FIRST * first + (1.0 - BETA_FIRST) * clipped
    second_new = BETA_SECOND * second + (1.0 - BETA_SECOND) * clipped * clipped
    first_hat = first_new / (1.0 - BETA_FIRST**STEP)
    second_hat = second_new / (1.0 - BETA_SECOND**STEP)
    moved = weight - rate * first_hat / (jnp.sqrt(second_hat) + ADAM_EPSILON)
    return (first_new, second_new, moved)


def per_device(
    inputs,
    cotangent,
    doc_ids,
    attention_in,
    attention_out,
    feedforward_in,
    feedforward_out,
    unit_scales,
    mix_rates,
    first_attention_in,
    second_attention_in,
    first_attention_out,
    second_attention_out,
    first_feedforward_in,
    second_feedforward_in,
    first_feedforward_out,
    second_feedforward_out,
    first_unit_scales,
    second_unit_scales,
    first_mix_rates,
    second_mix_rates,
):
    section = lax.axis_index("section")
    is_first = section == 0
    dp_index = lax.axis_index("dp")
    dp_size = lax.axis_size("dp")
    local_rows = inputs.shape[1]

    def ordered(own, other):
        return jnp.where(is_first, own, other), jnp.where(is_first, other, own)

    def halves(array, dim):
        width = array.shape[dim] // 2
        own = lax.dynamic_slice_in_dim(array, section * width, width, dim)
        other = lax.dynamic_slice_in_dim(array, (1 - section) * width, width, dim)
        return own, other

    hidden_low = lax.dynamic_index_in_dim(inputs, section, 0, False)

    attend_rows = jnp.concatenate(
        [jnp.swapaxes(attention_in[0], 1, 2), attention_out], axis=0
    ).astype(BF16)
    small = jnp.concatenate([unit_scales.reshape(-1), mix_rates.reshape(-1)]).astype(BF16)
    def gather_ring(half):
        if dp_size != 4:
            whole = lax.all_gather(half, "dp", axis=1, tiled=True)
            return whole, whole
        blocks, count = spread_rows(half, "dp"), half.shape[1]
        whole = jnp.zeros((half.shape[0], dp_size * count, half.shape[2]), BF16)
        for source, block in zip(ring_sources("dp"), blocks):
            whole = lax.dynamic_update_slice_in_dim(whole, block, source * count, 1)
        return whole, blocks[-2]

    own, other = halves(attend_rows, 2)
    attend_pieces = ordered(own, exchange(other, "section", 1))
    attend_pieces, feedforward_in_here, feedforward_out_here = tie(
        attend_pieces, feedforward_in, feedforward_out
    )
    feed_rows = jnp.concatenate(
        [jnp.swapaxes(feedforward_in_here[0].astype(BF16), 1, 2), feedforward_out_here.astype(BF16)], axis=0
    )
    own, other = halves(feed_rows, 1)
    feed_pieces = ordered(own, exchange(other, "section", 1))
    attend_first, came = gather_ring(attend_pieces[0])
    attend_second, *feed_pieces, _ = tie(attend_pieces[1], *feed_pieces, came)
    attend_owns = (attend_first, lax.all_gather(attend_second, "dp", axis=1, tiled=True))
    small = jnp.stack(ordered(small, exchange(small, "section", 1))).reshape(-1)
    small = gather_small(small, "dp").astype(F32)
    small = small.reshape(dp_size, 2, -1)
    units_here = unit_scales.shape[2]

    def units_apart(values):
        parts = values.reshape(dp_size, 2, -1)
        own, other = ordered(parts[:, 0], parts[:, 1])
        return jnp.concatenate([own.reshape(-1), other.reshape(-1)])

    def units_back(values):
        parts = values.reshape(2, dp_size, -1)
        own, other = ordered(parts[0], parts[1])
        return jnp.stack([own, other], axis=1).reshape(-1)

    layers, feed_owns = [], []
    for layer in range(2):
        feed_own = lax.all_gather(feed_pieces[layer], "dp", axis=1, tiled=True)
        units = small[:, layer, :units_here].reshape(-1)
        mixing = small[:, layer, units_here:].reshape(dp_size, 2, -1)
        mixing = jnp.swapaxes(mixing, 0, 1).reshape(2, -1)
        width_qk, width_ff = attend_owns[0].shape[1], 2 * feed_own.shape[1]
        layers.append((
            units[:width_qk, None],
            jnp.stack([
                units_apart(units[width_qk : width_qk + width_ff]),
                units_apart(units[width_qk + width_ff :]),
            ]),
            mixing,
        ))
        feed_owns.append(feed_own)

    doc_row = lax.dynamic_index_in_dim(doc_ids, section, 0, False)
    starts_all = document_starts(doc_row)
    mp_index = lax.axis_index("mp")
    sources = [mp_index ^ offset for offset in range(4)]
    places = jnp.arange(local_rows, dtype=jnp.int32)
    starts = jnp.stack([
        lax.dynamic_slice_in_dim(starts_all, source * local_rows, local_rows, 0)
        for source in sources
    ])
    sources = jnp.stack(sources).astype(jnp.int32)
    cosine, sine = rope_tables(sources[:, None] * local_rows + places - starts)
    info = jnp.concatenate([sources, starts[:, 0]])
    tables = (cosine, sine, starts, info)

    def scatter(sums):
        return lax.psum_scatter(sums, "dp", scatter_dimension=1, tiled=True)

    def scatter_direct(sums):
        if dp_size != 4:
            return scatter(sums), sums
        count = sums.shape[1] // dp_size
        parts = [
            lax.dynamic_slice_in_dim(sums, (dp_index ^ bits) * count, count, 1)
            for bits in range(dp_size)
        ]
        parts[1:] = [exchange(part, "dp", bits) for bits, part in enumerate(parts[1:], 1)]
        return sum(part.astype(F32) for part in tie(*parts)).astype(BF16), parts[1]

    def small_vector(scales, rate_one, rate_two):
        return jnp.concatenate([units_back(scales[0]), units_back(scales[1]), rate_one, rate_two])

    def attend_params(own, other):
        attend = jnp.concatenate(ordered(own, other), axis=2)
        return attend[:3].reshape(-1, attend.shape[2]), attend[3]

    first, second = layers
    own = attend_owns[0]
    first = (*attend_params(own, exchange(own, "section", 1)), *first)
    section_ref = section.astype(jnp.int32).reshape(1)
    grad = lax.dynamic_index_in_dim(cotangent, section, 0, False)
    _, hidden_second, stored_first, weights_first, later = layer_forward(
        hidden_low, hidden_low, first, tables, False, feed_owns[0], attend_owns[1]
    )
    second = (*attend_params(*later), *second)
    result, _, stored_second, weights_second, _ = layer_forward(
        hidden_second, hidden_second, second, tables, True, feed_owns[1]
    )
    parts, feed_second, attend_second, gains_second, small_second = layer_backward(
        stored_second, (grad,), False, second, tables, weights_second, section_ref
    )
    feed_second = scatter(feed_second)
    parts, attend_second = tie(parts, attend_second)
    attend_second = scatter(attend_second)

    width_qk, width_rates = gains_second.shape[0], 2 * dp_size * mix_rates.shape[2]

    def start_small(small_first):
        values = jnp.concatenate(
            [small_vector(*small_first), small_vector(*small_second), gains_second]
        )
        return values, exchange(values, "section", 1)

    def next_small(low, small, gains):
        low, (values, coming) = tie(low, small)
        return low, (jnp.concatenate([values + coming, gains]),)

    def last_small(other, small):
        other, (values,) = tie(other, small)
        bit = 1
        while 2 * bit < dp_size:
            values = values + exchange(values, "dp", bit)
            bit *= 2
        return other, (values, exchange(values, "dp", bit))

    parts, feed_first, attend_first, _, small = layer_backward(
        stored_first, parts, True, first, tables, weights_first, section_ref,
        (start_small, next_small, last_small),
    )
    feed_first = scatter(feed_first)
    sent_second = [
        lax.ppermute(part, "section", [(0, 1)]) for part in (attend_second, feed_second)
    ]
    attend_first, feed_second, attend_second, small, sent_second = tie(
        attend_first, feed_second, attend_second, small, sent_second
    )
    attend_first, came = scatter_direct(attend_first)
    (sums, coming), _ = tie(small, came)
    sums = sums + coming

    reduced_first = (attend_first, feed_first)
    reduced_second = (attend_second, feed_second)
    squares = sum(
        jnp.sum(jnp.square(part.astype(F32))) for part in (*reduced_first, *reduced_second)
    )
    halves_of = [
        (one, two, lax.ppermute(one, "section", [(1, 0)]), theirs)
        for one, two, theirs in zip(reduced_first, reduced_second, sent_second)
    ]

    layer_sums = sums[: -2 * width_qk].reshape(2, -1)
    gain_first = sums[-width_qk:]
    gain_sums = jnp.stack([gain_first + exchange(gain_first, "section", 1), sums[-2 * width_qk : -width_qk]])
    scale_sums, rate_sums = layer_sums[:, :-width_rates], layer_sums[:, -width_rates:]
    near_rates, *far_rates = [rate_sums] + [to(rate_sums, at) for at in (1, 2, 3)]
    rate_sums = ((near_rates + far_rates[0]) + (far_rates[1] + far_rates[2])).reshape(2, 2, -1)
    unit_grads = jnp.concatenate([gain_sums, scale_sums], axis=1)
    unit_grads = jnp.where(is_first, unit_grads[0], unit_grads[1])
    unit_grads = lax.dynamic_slice_in_dim(unit_grads, dp_index * units_here, units_here, 0)
    unit_grads = unit_grads[None, None]
    rates_here = mix_rates.shape[2]
    rate_grads = jnp.where(is_first, rate_sums[0], rate_sums[1])
    rate_grads = lax.dynamic_slice_in_dim(rate_grads, dp_index * rates_here, rates_here, 1)[None]

    turn = lambda array: jnp.swapaxes(array, 1, 2)
    leading = (mp_index == 0).astype(F32)
    squares = squares + jnp.sum(unit_grads * unit_grads)
    squares = squares + leading * jnp.sum(rate_grads * rate_grads)
    squares = squares.reshape(1)
    squares, parts = tie(squares, parts)
    squares = squares + exchange(squares, "section", 1)
    squares = sum_over(sum_over(squares, "mp"), "dp")
    gradient_norm = jnp.sqrt(squares[0])
    factor = CLIP_NORM / jnp.maximum(gradient_norm, CLIP_NORM)

    grad = sum(part.astype(F32) for part in parts)
    to_send = jnp.where(is_first, result, grad)
    kept = jnp.where(is_first, grad, result)
    arrived = exchange(to_send, "section", 1)
    boundary_states = jnp.stack(ordered(kept, arrived))[None]

    scalar = factor.reshape(1)
    head_rows, width = attention_out.shape[1:]
    feed_units = feedforward_out.shape[1]
    rows = min(64, head_rows)
    updates = []
    attend_halves, feed_halves = halves_of
    unit_half = feed_units // 2
    turned = (
        (1, width, feed_units), (1, unit_half, width), lambda i: (i, 0, 0), lambda i: (i, 0, 0), (2,)
    )
    update = functools.partial(adam_matrix, section_ref, scalar)
    new = update(
        [turn(array[0]) for array in (attention_in, first_attention_in, second_attention_in)],
        attend_halves, 2, by_columns, (1, rows, width), (1, rows, width // 2),
        lambda i, j: (i, j, 0), lambda i, j: (i, j, 0), (3, head_rows // rows),
    )
    updates.extend(turn(part)[None] for part in new)
    updates.extend(update(
        (attention_out, first_attention_out, second_attention_out),
        attend_halves, 2, by_columns, (1, rows, width), (1, rows, width // 2),
        lambda i: (0, i, 0), lambda i: (3, i, 0), (head_rows // rows,),
    ))
    new = update(
        [array[0] for array in (feedforward_in, first_feedforward_in, second_feedforward_in)],
        feed_halves, 1, by_rows_turned, *turned,
    )
    updates.extend(part[None] for part in new)
    updates.extend(update(
        (feedforward_out, first_feedforward_out, second_feedforward_out),
        feed_halves, 2, by_rows, (1, unit_half, width), (1, unit_half, width),
        lambda i: (0, i, 0), lambda i: (2, 0, 0), (2,),
    ))
    updates.extend(
        adam_update(
            unit_scales, first_unit_scales, second_unit_scales, unit_grads, factor, SCALE_RATE
        )
    )
    updates.extend(
        adam_update(
            mix_rates, first_mix_rates, second_mix_rates, rate_grads, factor, MIXING_RATE
        )
    )
    return (boundary_states, gradient_norm, *updates)


def solution(mesh):
    in_specs = (
        P("dp", "mp", None),
        P("dp", "mp", None),
        P("dp", None),
        P("section", None, None, ("mp", "dp")),
        P("section", ("mp", "dp"), None),
        P("section", None, None, ("mp", "dp")),
        P("section", ("mp", "dp"), None),
        P("section", "mp", "dp"),
        P("section", None, "dp"),
        P("section", None, None, ("mp", "dp")),
        P("section", None, None, ("mp", "dp")),
        P("section", ("mp", "dp"), None),
        P("section", ("mp", "dp"), None),
        P("section", None, None, ("mp", "dp")),
        P("section", None, None, ("mp", "dp")),
        P("section", ("mp", "dp"), None),
        P("section", ("mp", "dp"), None),
        P("section", "mp", "dp"),
        P("section", "mp", "dp"),
        P("section", None, "dp"),
        P("section", None, "dp"),
    )
    out_specs = (
        P("section", "dp", "mp", None),
        P(),
        P("section", None, None, ("mp", "dp")),
        P("section", None, None, ("mp", "dp")),
        P("section", None, None, ("mp", "dp")),
        P("section", ("mp", "dp"), None),
        P("section", ("mp", "dp"), None),
        P("section", ("mp", "dp"), None),
        P("section", None, None, ("mp", "dp")),
        P("section", None, None, ("mp", "dp")),
        P("section", None, None, ("mp", "dp")),
        P("section", ("mp", "dp"), None),
        P("section", ("mp", "dp"), None),
        P("section", ("mp", "dp"), None),
        P("section", "mp", "dp"),
        P("section", "mp", "dp"),
        P("section", "mp", "dp"),
        P("section", None, "dp"),
        P("section", None, "dp"),
        P("section", None, "dp"),
    )
    return jax.shard_map(
        per_device, mesh=mesh, in_specs=in_specs, out_specs=out_specs, check_vma=False
    )
```
